32 devices in a mesh: expert: 4 (over z), context: 4 (over y, x), tensor: 2 (over core).
Axes of the slice: x: 2, y: 2, z: 4, core: 2. Of those that a mesh axis runs over, the one named last changes fastest.
Arguments:
- tokens_in: bfloat16 [8192, 768], P(('expert', 'context', 'tensor')), may hold values from -6 to 6
- gain_attn: bfloat16 [768], replicated, may hold values from 0.5 to 1.5
- w_qkv: bfloat16 [768, 2304], replicated, may hold values from -1 to 1
- rel_bias: bfloat16 [12, 32], P('context'), may hold values from -4 to 4
- w_out: bfloat16 [768, 768], replicated, may hold values from -0.875 to 0.875
- gain_ffn: bfloat16 [768], replicated, may hold values from 0.5 to 1.5
- w_router: bfloat16 [768, 16], replicated, may hold values from -0.15625 to 0.15625
- w_up: bfloat16 [16, 768, 3072], P(('expert', 'context')), may hold values from -0.21875 to 0.21875
- w_down: bfloat16 [16, 3072, 768], P(('expert', 'context')), may hold values from -1.25 to 1.25
- segments: int32 [4, 2048], P('expert'), may hold values from 0 to 2, as said below
- routes: int32 [8192, 1], P(('expert', 'context', 'tensor')), may hold values from 0 to 15; in each aligned block of 256 rows (0 to 255, 256 to 511, ...) at most 40 rows name the same one
- cotangent: bfloat16 [8192, 768], P(('expert', 'context', 'tensor')), may hold values from -6 to 6
Outputs:
- mixed_out: bfloat16 [8192, 768], P(('expert', 'context', 'tensor'))
- grad_tokens: bfloat16 [8192, 768], P(('expert', 'context', 'tensor'))
- grad_gain_attn: float32 [768], P(('expert', 'context', 'tensor'))
- grad_qkv: float32 [768, 2304], P(('expert', 'context', 'tensor'))
- grad_rel: float32 [12, 32], P('context')
- grad_out: float32 [768, 768], P(None, ('expert', 'context', 'tensor'))
- grad_gain_ffn: float32 [768], P(('expert', 'context', 'tensor'))
- grad_router: float32 [768, 16], P(('expert', 'context', 'tensor'))
- grad_up: float32 [16, 768, 3072], P(('expert', 'context'), None, 'tensor')
- grad_down: float32 [16, 3072, 768], P(('expert', 'context'), 'tensor')
The draws below stay inside these ranges and needn't reach their ends.
Inputs may be any that keep to these rules, and one draw needn't show every extreme that they name: `segments`: each row does not fall, starts at 0 and holds 0, 1 and 2; segment 1 begins within the first 256 positions and ends within the last 256. `routes`: within the 256 rows of one device no expert is named more than 40 times.
All inputs are finite; a program needn't handle non-finite values.
Results may differ from the reference program's by a relative error of at most 0.014.
Values may be sent and summed in bfloat16 or wider, within the bound.
No kernel may reach another device: no remote copies, remote signals or barrier semaphores. Data moves between devices by JAX's collectives and lax.ppermute only.
A program may use at most 256 MiB of HBM per device.

```python
import math
import jax
import jax.numpy as jnp
import numpy as np
from jax import lax

D = 768
H = 12
DH = 64
FF = 3072
BUCKETS = 32
TOK_DEV = 256
EXPERTS = 16
LEN = 2048
SEQS = 4
TOKENS = 8192
CAP = 20
MOST = 40


def draw_segments(key, part):
    key = jax.random.fold_in(key, 11)
    opening_key, closing_key = jax.random.split(key)
    opening = jax.random.randint(opening_key, (SEQS, 1), 1, TOK_DEV, dtype=jnp.int32)
    closing = jax.random.randint(closing_key, (SEQS, 1), LEN - TOK_DEV + 1, LEN, dtype=jnp.int32)
    position = jnp.arange(LEN, dtype=jnp.int32)[None, :]
    return (position >= opening).astype(jnp.int32) + (position >= closing).astype(jnp.int32)


def draw_w_qkv(key, part):
    key = jax.random.fold_in(key, 23)
    values = jnp.clip(jax.random.normal(key, (D, 3 * D), jnp.float32), -6.0, 6.0) * D ** (-0.5)
    column = jnp.arange(3 * D, dtype=jnp.int32)[None, :]
    factor = jnp.where(column < D, 0.125, 1.0).astype(jnp.float32)
    return (values * factor).astype(jnp.bfloat16)


def with_spikes(drawn, key, source, target, blocks, factor):
    owner, partner = [(jnp.arange(drawn.shape[axis_at]) // (drawn.shape[axis_at] // blocks)).reshape([-1 if axis == axis_at else 1 for axis in range(drawn.ndim)]) for axis_at in (source, target)]
    chosen = jax.random.permutation(key, blocks)[partner]
    strong = (owner == chosen) | (owner == (partner + blocks // 2) % blocks)
    return jnp.where(strong, factor * drawn, drawn)


def level_of(key, dims, cuts, smallest, high):
    loudness, own = 1.0, jax.random.fold_in(key, 6)
    for dim, shards_of in cuts:
        steps = jnp.exp(jax.random.uniform(jax.random.fold_in(own, dim), (shards_of,), jnp.float32, smallest / len(cuts), high / len(cuts)))
        loudness = loudness * jnp.repeat(steps, dims[dim] // shards_of).reshape([-1 if axis == dim else 1 for axis in range(len(dims))])
    return loudness


def shared_out(own_key, own, number, rows, count, top, limit, skew):
    order = jax.random.permutation(own_key, count)
    heavy_load, common = shares(count, rows * top, limit, skew, True), shares(count, rows * top, limit, skew, False)
    places = jnp.arange(count)

    def named(sizes, turn):
        used = int((sizes > 0).sum())
        fixed = max(1, used // 4)
        shifted = fixed + (places - fixed + turn * (used - fixed)) % max(1, count - fixed)
        return jnp.zeros((count,), jnp.int32).at[order[jnp.where(places < fixed, places, shifted)]].set(jnp.asarray(sizes, jnp.int32))

    sizes = jnp.where(number % 4 == 0, named(heavy_load, number // 4), named(common, number - number // 4 - 1))
    mixed = jax.random.permutation(jax.random.fold_in(own, 3), count)
    source_of, taker = mixed[0:count // 2 * 2:2], mixed[1:count // 2 * 2:2]
    room = jnp.minimum(sizes[source_of] - 1, limit - sizes[taker]) // 2
    room = jnp.where((source_of == order[0]) | (taker == order[0]) | (sizes[taker] == 0), 0, jnp.maximum(room, 0))
    shifted = jax.random.randint(jax.random.fold_in(own, 4), (count // 2,), 0, 1 << 20) % (room + 1)
    sizes = sizes.at[source_of].add(-shifted).at[taker].add(shifted)
    labels = jnp.searchsorted(jnp.cumsum(sizes), jnp.arange(rows * top), side="right").astype(jnp.int32)
    table = labels.reshape(top, rows).T
    table = table[jax.random.permutation(jax.random.fold_in(own, 1), rows)]
    turn = jax.random.randint(jax.random.fold_in(own, 2), (rows, 1), 0, top)
    return jnp.take_along_axis(table, (jnp.arange(top)[None, :] + turn) % top, axis=1)


def shares(count, total, bound, skew, full):
    weights = [(1 << 20) // math.isqrt(grade ** skew) + 1 for grade in range(1, count + 1)]
    largest = bound if full else min(bound, max(-(-total // count), total * weights[0] // sum(weights)))
    least = 1 if total - largest >= count - 1 else 0
    given, spare = [largest] + [least] * (count - 1), total - largest - least * (count - 1)
    while spare > 0:
        free = [i for i in range(1, count) if given[i] < largest] or [i for i in range(1, count) if given[i] < bound]
        mass, budget = sum([weights[i] for i in free]), spare
        for i in free:
            more = min(bound - given[i], max(1, budget * weights[i] // mass), spare)
            given[i] = given[i] + more
            spare = spare - more
    return np.array(given)


def centred(key, dims, spread, limit, shards=(), kind=jnp.bfloat16):
    drawn = jax.random.normal(key, dims, jnp.float32) * spread
    if len(shards) > 0:
        drawn = level_of(key, dims, shards, -0.22, 0.18) * drawn
    return jnp.clip(drawn, min=-limit, max=limit).astype(kind)


def gaussian_with(rng, dims, width, limit, pieces, heavy, kind=jnp.bfloat16):
    values = width * jax.random.normal(rng, dims, jnp.float32)
    if pieces:
        values = values * level_of(rng, dims, pieces, -0.22, 0.18)
    return jnp.clip(with_spikes(values, jax.random.fold_in(rng, 3), *heavy), -limit, limit).astype(kind)


def setup_inputs(seed: int = 0) -> dict:
    splits = jax.random.split(jax.random.key(seed), 13)
    tokens_in = gaussian_with(splits[0], (TOKENS, D), 1.0, 6.0, ((0, 32),), (0, 1, 32, 2.75))
    gain_attn = jnp.clip(1.0 + 0.1 * jax.random.normal(splits[1], (D,), jnp.float32), 0.5, 1.5).astype(jnp.bfloat16)
    w_qkv = draw_w_qkv(jax.random.fold_in(splits[12], 71), 0)
    rel_bias = centred(splits[3], (H, BUCKETS), 1.0, 4.0, ((0, 4),))
    w_out = centred(splits[4], (D, D), (D // 16) ** -0.5, 0.875)
    gain_ffn = jnp.clip(1.0 + 0.1 * jax.random.normal(splits[5], (D,), jnp.float32), 0.5, 1.5).astype(jnp.bfloat16)
    w_router = centred(splits[6], (D, EXPERTS), (2 * D) ** -0.5, 0.15625)
    w_up = centred(splits[7], (EXPERTS, D, FF), D ** -0.5, 0.21875, ((0, 16),))
    w_down = centred(splits[8], (EXPERTS, FF, D), (max(1, FF // (EXPERTS * EXPERTS // 2))) ** -0.5, 1.25, ((0, 16),))
    segments = draw_segments(jax.random.fold_in(splits[12], 71), 0)
    routes_keys = jax.random.split(jax.random.fold_in(splits[10], 1), TOKENS // TOK_DEV)
    routes_turns = jax.random.permutation(jax.random.fold_in(splits[10], 3), TOKENS // TOK_DEV)
    routes = jax.vmap(lambda own, number: shared_out(jax.random.fold_in(splits[10], 2), own, number, TOK_DEV, EXPERTS, 1, MOST, 2))(routes_keys, routes_turns).reshape((TOKENS, 1))
    cotangent = gaussian_with(splits[11], (TOKENS, D), 1.0, 6.0, ((0, 32),), (0, 1, 32, 2.75))
    return {"tokens_in": tokens_in, "gain_attn": gain_attn, "w_qkv": w_qkv, "rel_bias": rel_bias, "w_out": w_out, "gain_ffn": gain_ffn, "w_router": w_router, "w_up": w_up, "w_down": w_down, "segments": segments, "routes": routes, "cotangent": cotangent}


@jax.custom_vjp
def low(v):
    return lax.optimization_barrier(v.astype(jnp.bfloat16)).astype(jnp.float32)

@jax.custom_vjp
def low_back(v):
    return v

def low_keep(v):
    return (low(v), None)

def low_pass(kept, grad):
    return (grad,)

def back_keep(v):
    return (v, None)

def back_low(kept, grad):
    return (low(grad),)
low.defvjp(low_keep, low_pass)
low_back.defvjp(back_keep, back_low)
EPSILON = 1e-06
THRESHOLDS = (12, 16, 23, 32, 46, 64, 91)
HIGHEST = lax.Precision.HIGHEST

def bucket_of(offset):
    distance = jnp.abs(offset)
    beyond = jnp.zeros_like(distance)
    for threshold in THRESHOLDS:
        beyond = beyond + (distance >= threshold).astype(jnp.int32)
    nearby = jnp.where(distance < 8, distance, 8 + beyond)
    return nearby + 16 * (offset > 0).astype(jnp.int32)

def rms_norm(values, scaling):
    return values * lax.rsqrt(lax.optimization_barrier(jnp.mean(values * values, axis=-1, keepdims=True)) + EPSILON) * scaling

def attend_block(query_block, first_row, key_rows, value_rows, segment_row, rel_bias):
    height = query_block.shape[0]
    query_place = first_row + jnp.arange(height, dtype=jnp.int32)
    key_place = jnp.arange(key_rows.shape[0], dtype=jnp.int32)
    buckets = bucket_of(key_place[None, :] - query_place[:, None])
    bias_block = rel_bias[:, buckets]
    raw_scores = jnp.einsum('qhd,khd->hqk', query_block, key_rows, precision=HIGHEST) + bias_block
    scores = low_back(raw_scores)
    query_docs = lax.dynamic_slice_in_dim(segment_row, first_row, height)
    same_doc = query_docs[:, None] == segment_row[None, :]
    masked = jnp.where(same_doc[None], scores, -1e+30)
    row_max = lax.optimization_barrier(jnp.max(masked, axis=-1, keepdims=True))
    weights = jnp.exp(masked - row_max)
    prob_rows = weights / lax.optimization_barrier(jnp.sum(weights, axis=-1, keepdims=True))
    return jnp.einsum('hqk,khd->qhd', low(prob_rows), value_rows, precision=HIGHEST)

def attend_sequence(query_rows, key_rows, value_rows, segment_row, rel_bias):
    blocks = query_rows.shape[0] // TOK_DEV
    shaped = query_rows.reshape((blocks, TOK_DEV) + query_rows.shape[1:])
    starts = jnp.arange(blocks, dtype=jnp.int32) * TOK_DEV
    checked = jax.checkpoint(attend_block)
    result = lax.map(lambda element: checked(element[0], element[1], key_rows, value_rows, segment_row, rel_bias), (shaped, starts))
    return result.reshape(query_rows.shape)

def expert_pass(element):
    rows_in, first_weight, second_weight = element
    hidden = low_back(jnp.dot(rows_in, first_weight, precision=HIGHEST))
    active = low(jax.nn.gelu(hidden, approximate=False))
    return low(low_back(jnp.dot(active, second_weight, precision=HIGHEST)))

def forward(tokens, gain_attn, w_qkv, rel_bias, w_out, gain_ffn, w_router, w_up, w_down, segments, routes):
    normed = low(rms_norm(tokens, gain_attn))
    projected = jnp.dot(normed, w_qkv, precision=HIGHEST).reshape(TOKENS, 3, H, DH)
    queries = low(low_back(projected[:, 0])).reshape(SEQS, LEN, H, DH)
    key_all = low(low_back(projected[:, 1])).reshape(SEQS, LEN, H, DH)
    value_all = low(low_back(projected[:, 2])).reshape(SEQS, LEN, H, DH)
    attended = lax.map(lambda element: attend_sequence(element[0], element[1], element[2], element[3], rel_bias), (queries, key_all, value_all, segments))
    attended = low(low_back(attended.reshape(TOKENS, D)))
    residual = tokens + low_back(jnp.dot(attended, w_out, precision=HIGHEST))
    normed_ffn = low(rms_norm(residual, gain_ffn))
    logits = low_back(jnp.dot(normed_ffn, w_router, precision=HIGHEST))
    router = jax.nn.softmax(logits, axis=-1)
    chosen = routes[:, 0]
    onehot = chosen[:, None] == jnp.arange(EXPERTS, dtype=jnp.int32)[None, :]
    gate_value = lax.optimization_barrier(jnp.sum(jnp.where(onehot, router, 0.0), axis=-1))
    sources = TOKENS // TOK_DEV
    owner_marks = onehot.astype(jnp.int32).reshape(sources, TOK_DEV, EXPERTS)
    slot_rank = lax.optimization_barrier(jnp.sum((jnp.cumsum(owner_marks, axis=1) - 1) * owner_marks, axis=-1)).reshape(TOKENS)
    kept_mask = slot_rank < CAP
    anchor = jnp.arange(TOKENS, dtype=jnp.int32) // TOK_DEV
    column = jnp.where(kept_mask, anchor * CAP + slot_rank, sources * CAP)
    sent_rows = low_back(normed_ffn)
    slot_table = jnp.zeros((EXPERTS, sources * CAP + 1, D), jnp.float32).at[chosen, column].set(sent_rows)
    outputs = lax.map(jax.checkpoint(expert_pass), (slot_table[:, :sources * CAP], w_up, w_down))
    padded = jnp.concatenate([outputs, jnp.zeros((EXPERTS, 1, D), jnp.float32)], axis=1)
    returned = padded[chosen, column]
    return residual + jnp.where(kept_mask, gate_value, 0.0)[:, None] * returned

def reference(tokens_in, gain_attn, w_qkv, rel_bias, w_out, gain_ffn, w_router, w_up, w_down, segments, routes, cotangent):
    floats = tuple((array_in.astype(jnp.float32) for array_in in (tokens_in, gain_attn, w_qkv, rel_bias, w_out, gain_ffn, w_router, w_up, w_down)))

    def wrapped(*params):
        return forward(*params, segments, routes)
    mixed_out, pullback = jax.vjp(wrapped, *floats)
    gradients = pullback(cotangent.astype(jnp.float32))
    return (mixed_out.astype(jnp.bfloat16), gradients[0].astype(jnp.bfloat16), gradients[1], gradients[2], gradients[3], gradients[4], gradients[5], gradients[6], gradients[7], gradients[8])
```

```python
import functools

import jax
import jax.numpy as jnp
from jax import lax
from jax.experimental import pallas as pl
from jax.experimental.pallas import tpu as pltpu
from jax.sharding import PartitionSpec as P

EPSILON = 1e-06
THRESHOLDS = (12, 16, 23, 32, 46, 64, 91)
FAR_LEFT = 15
FAR_RIGHT = 31
EXCLUDED = -1e30
LANES = 128
BF16 = jnp.bfloat16
F32 = jnp.float32
VMEM_LIMIT = 56 * 1024 * 1024


def bucket_of(offset):
    distance = jnp.abs(offset)
    beyond = jnp.zeros_like(distance)
    for threshold in THRESHOLDS:
        beyond = beyond + (distance >= threshold).astype(jnp.int32)
    nearby = jnp.where(distance < 8, distance, 8 + beyond)
    return nearby + 16 * (offset > 0).astype(jnp.int32)


def nn(left, right):
    return lax.dot_general(left, right, (((1,), (0,)), ((), ())), preferred_element_type=F32)


def nt(left, right):
    return lax.dot_general(left, right, (((1,), (1,)), ((), ())), preferred_element_type=F32)


def tn(left, right):
    return lax.dot_general(left, right, (((0,), (0,)), ((), ())), preferred_element_type=F32)


def iota(shape, axis):
    return lax.broadcasted_iota(jnp.int32, shape, axis)


def three_terms(values):
    high = values.astype(BF16).astype(F32)
    middle = (values - high).astype(BF16).astype(F32)
    return high, middle, values - high - middle


def call(body, out_shape, cost, smem=(), count=0):
    specs = [
        pl.BlockSpec(memory_space=pltpu.SMEM if i in smem else pltpu.VMEM) for i in range(count)
    ]
    return functools.partial(
        pl.pallas_call,
        body,
        out_shape=out_shape,
        in_specs=specs,
        cost_estimate=pl.CostEstimate(flops=cost[0], bytes_accessed=cost[1], transcendentals=0),
        compiler_params=pltpu.CompilerParams(vmem_limit_bytes=VMEM_LIMIT),
    )


def shape(dims, kind=BF16):
    return jax.ShapeDtypeStruct(dims, kind)


def project_body(tokens_ref, gain_ref, w_ref, kv_ref, q_ref, normed_ref):
    groups, height, width = q_ref.shape
    features = tokens_ref.shape[1]
    tokens = tokens_ref[...].astype(F32)
    inverse = lax.rsqrt(jnp.mean(tokens * tokens, axis=-1, keepdims=True) + EPSILON)
    normed = (tokens * inverse * gain_ref[...].astype(F32)).astype(BF16)
    normed_ref[...] = normed
    for part in range(3):
        product = nn(normed, w_ref[:, part * features : (part + 1) * features]).astype(BF16)
        for group in range(groups):
            piece = product[:, group * width : (group + 1) * width]
            if part == 0:
                q_ref[group] = piece
            else:
                kv_ref[group, :, (part - 1) * width : part * width] = piece


def forward_body(
    place_ref,
    bias_ref,
    q_ref,
    kv_own_ref,
    kv_other_ref,
    seg_col_ref,
    seg_row_ref,
    strip_ref,
    attended_ref,
    exact_ref,
    kaug_ref,
    vaug_ref,
    qaug_ref,
    vt_ref,
    score_ref,
):
    blocks, height, width = q_ref.shape
    heads, head_size = exact_ref.shape[1], exact_ref.shape[2]
    spans = kaug_ref.shape[1] // height
    place = place_ref[0]
    lane = iota((height, LANES), 1)
    pick_v = (
        iota((head_size + 16, LANES), 0) == iota((head_size + 16, LANES), 1)
    ).astype(BF16)
    eye = (iota((LANES, LANES), 0) == iota((LANES, LANES), 1)).astype(BF16)
    zero_half = jnp.zeros((height, LANES - head_size), BF16)
    ones_half = jnp.where(iota((height, LANES - head_size), 1) < 3, 1.0, 0.0).astype(BF16)
    extra_lane = iota((height, LANES - head_size), 1)
    extra_row = iota((LANES - head_size, height), 0)
    for block in range(blocks):
        for own in (True, False):
            source = kv_own_ref if own else kv_other_ref
            span = 2 * block + (place if own else 1 - place)
            first = pl.multiple_of(span * height, height)
            docs = seg_col_ref[pl.ds(first, height), :]
            extra = jnp.where(extra_lane < 3, jnp.where(docs == extra_lane, 0.0, EXCLUDED), 0.0)
            extra = jnp.where(extra_lane - 3 == span, 1.0, extra)
            extra = jnp.where((extra_lane >= 11) & (extra_lane < 14), 1.0, extra).astype(BF16)
            for head in range(heads):
                k_part = source[block, :, head * head_size : (head + 1) * head_size]
                v_part = source[
                    block, :, width + head * head_size : width + (head + 1) * head_size
                ]
                kaug_ref[head, pl.ds(first, height), :] = jnp.concatenate([k_part, extra], axis=1)
                v_full = jnp.concatenate([v_part, ones_half], axis=1)
                vaug_ref[head, pl.ds(first, height), :] = v_full
                vt_ref[head, span] = nt(pick_v, v_full).astype(BF16)
        span = 2 * block + place
        docs = seg_row_ref[pl.ds(span, 1), :]
        same = jnp.where(docs == extra_row, 1.0, 0.0)
        apart = extra_row - 3 - span
        for head in range(heads):
            q_part = q_ref[block, :, head * head_size : (head + 1) * head_size]
            q_turned = nt(eye, jnp.concatenate([q_part, zero_half], axis=1))
            far = jnp.where(
                apart <= -2,
                bias_ref[head, FAR_LEFT],
                jnp.where(apart >= 2, bias_ref[head, FAR_RIGHT], 0.0),
            )
            extra = jnp.where(
                extra_row < 3, same, jnp.where(extra_row < 3 + spans, far, 0.0)
            )
            qaug_ref[head, block] = jnp.concatenate([q_turned[:head_size], extra], axis=0).astype(
                BF16
            )

    def step(index, carried):
        block = index // heads
        head = index % heads
        span = 2 * block + place
        queries = qaug_ref[head, block]
        for at in range(spans):
            score_ref[(at + 1) * height : (at + 2) * height] = nn(
                kaug_ref[head, at * height : (at + 1) * height, :], queries
            )
        near = pl.ds(pl.multiple_of(span * height, height), 3 * height)
        score_ref[near, :] = score_ref[near, :] + strip_ref[head, height : 4 * height, :]
        row_max = jnp.max(score_ref[height : 2 * height], axis=0, keepdims=True)
        for at in range(1, spans):
            row_max = jnp.maximum(
                row_max,
                jnp.max(score_ref[(at + 1) * height : (at + 2) * height], axis=0, keepdims=True),
            )
        total = jnp.zeros((head_size + 16, height), F32)
        for at in range(spans):
            weights = jnp.exp(score_ref[(at + 1) * height : (at + 2) * height] - row_max)
            total = total + nn(vt_ref[head, at], weights.astype(BF16))
        denominator = total[head_size : head_size + 1]
        result = total[:head_size] * (1.0 / denominator)
        attended_ref[block, head] = result.astype(BF16)
        exact_ref[block, head] = result
        high, middle, low = three_terms(-(row_max + jnp.log(denominator)))
        row = iota((16, height), 0)
        terms = jnp.where(row == 11, high, jnp.where(row == 12, middle, low))
        held = qaug_ref[head, block, head_size : head_size + 16, :].astype(F32)
        qaug_ref[head, block, head_size : head_size + 16, :] = jnp.where(
            (row >= 11) & (row < 14), terms, held
        ).astype(BF16)
        return carried

    lax.fori_loop(0, blocks * heads, step, 0)


def backward_body(
    place_ref,
    kaug_ref,
    vaug_ref,
    qaug_ref,
    exact_ref,
    grad_ref,
    strip_ref,
    dq_ref,
    own_ref,
    other_ref,
    diag_ref,
    far_ref,
    kt_ref,
    dkv_ref,
    turned_ref,
):
    blocks, heads, head_size, height = exact_ref.shape
    spans = kaug_ref.shape[1] // height
    width = heads * head_size
    place = place_ref[0]
    tall = head_size + 16
    row, column = iota((tall, LANES), 0), iota((tall, LANES), 1)
    pick_k = (
        ((row < head_size) & (row == column))
        | ((row >= head_size) & (row < head_size + spans) & (row + 3 == column))
    ).astype(BF16)
    for head in range(heads):
        for at in range(spans):
            kt_ref[head, at] = nt(
                pick_k, kaug_ref[head, at * height : (at + 1) * height, :]
            ).astype(BF16)
    dkv_ref[...] = jnp.zeros_like(dkv_ref)
    diag_ref[...] = jnp.zeros_like(diag_ref)
    far_ref[...] = jnp.zeros_like(far_ref)

    def step(index, carried):
        block = index // heads
        head = index % heads
        span = 2 * block + place
        start = jnp.clip(span - 1, 0, spans - 3)
        queries = qaug_ref[head, block]
        grads = grad_ref[block, head]
        delta = jnp.sum(grads.astype(F32) * exact_ref[block, head], axis=0, keepdims=True)
        high, middle, low = three_terms(-delta)
        extra_row = iota((LANES - head_size, height), 0)
        extra = jnp.where(
            extra_row == 0,
            high,
            jnp.where(extra_row == 1, middle, jnp.where(extra_row == 2, low, 0.0)),
        ).astype(BF16)
        grads_extra = jnp.concatenate([grads, extra], axis=0)
        blank = jnp.zeros((head_size, height), BF16)
        sides = jnp.concatenate(
            [
                jnp.concatenate([queries[:head_size], blank], axis=1),
                jnp.concatenate([blank, grads], axis=1),
            ],
            axis=0,
        )
        dq_total = jnp.zeros((tall, height), F32)
        far_total = jnp.zeros((tall, height), F32)
        for at in range(spans):
            near = at < 3
            key_span = (start + at) if near else ((start + at) & (spans - 1))
            first = pl.multiple_of(key_span * height, height)
            keys = kaug_ref[head, pl.ds(first, height), :]
            exponent = nn(keys, queries)
            if near:
                level = pl.multiple_of((key_span - span + 2) * height, height)
                exponent = exponent + strip_ref[head, pl.ds(level, height), :]
            probs = jnp.exp(exponent)
            grad_probs = nn(vaug_ref[head, pl.ds(first, height), :], grads_extra)
            grad_scores = (probs * grad_probs).astype(BF16)
            if near:
                diag_ref[head, pl.ds(level, height), :] = diag_ref[
                    head, pl.ds(level, height), :
                ] + grad_scores.astype(F32)
            both = jnp.concatenate([grad_scores, probs.astype(BF16)], axis=1)
            dkv_ref[head, pl.ds(first, height), :] = dkv_ref[
                head, pl.ds(first, height), :
            ] + nt(both, sides)
            turned = nn(kt_ref[head, key_span], grad_scores)
            if near:
                dq_total = dq_total + turned
            else:
                far_total = far_total + turned
        dq_total = dq_total + far_total
        turned_ref[pl.ds(pl.multiple_of(head * head_size, head_size), head_size), :] = dq_total[
            :head_size
        ]
        sums = far_total[head_size : head_size + spans]
        span_row = iota((spans, height), 0)
        far_ref[head, 0] = far_ref[head, 0] + jnp.where(span_row < start, sums, 0.0)
        far_ref[head, 1] = far_ref[head, 1] + jnp.where(span_row >= start + 3, sums, 0.0)

        @pl.when(head == heads - 1)
        def _():
            dq_ref[block] = jnp.transpose(turned_ref[...]).astype(BF16)

        return carried

    lax.fori_loop(0, blocks * heads, step, 0)
    for block in range(blocks):
        for target, parity in ((own_ref, place), (other_ref, 1 - place)):
            first = pl.multiple_of((2 * block + parity) * height, height)
            for head in range(heads):
                both = dkv_ref[head, pl.ds(first, height), :].astype(BF16)
                target[block, :, head * head_size : (head + 1) * head_size] = both[:, :head_size]
                target[
                    block, :, width + head * head_size : width + (head + 1) * head_size
                ] = both[:, head_size:]


def diagonal_body(diag_ref, far_ref, out_ref):
    heads, rows, height = diag_ref.shape
    total_rows = rows + 2 * height
    lane = iota((total_rows, height), 1)
    offset = iota((total_rows, LANES), 0) - 3 * height
    table = (bucket_of(offset) == iota((total_rows, LANES), 1)).astype(F32)
    lane_out = iota((1, LANES), 1)
    for head in range(heads):
        blank = jnp.zeros((height, height), F32)
        values = jnp.concatenate([blank, diag_ref[head], blank], axis=0)
        moved = 1
        while moved < height:
            values = jnp.where(
                (lane & moved) != 0, pltpu.roll(values, total_rows - moved, 0), values
            )
            moved *= 2
        sums = jnp.sum(values, axis=1, keepdims=True)
        by_bucket = jnp.sum(sums * table, axis=0, keepdims=True)
        left = jnp.sum(far_ref[head, 0])
        right = jnp.sum(far_ref[head, 1])
        by_bucket = by_bucket + jnp.where(lane_out == FAR_LEFT, left, 0.0)
        out_ref[head] = by_bucket + jnp.where(lane_out == FAR_RIGHT, right, 0.0)


def finish_body(tokens_ref, gain_ref, w_ref, gp_ref, residual_ref, out_ref, joined_ref):
    groups, height, wide = gp_ref.shape
    width = wide // 3
    features = tokens_ref.shape[1]
    for group in range(groups):
        joined_ref[:, group * width : (group + 1) * width] = gp_ref[group, :, 2 * width :]
        for part in range(2):
            at = (part + 1) * features + group * width
            joined_ref[:, at : at + width] = gp_ref[group, :, part * width : (part + 1) * width]
    grad_normed = nt(joined_ref[...], w_ref[...])
    tokens = tokens_ref[...].astype(F32)
    inverse = lax.rsqrt(jnp.mean(tokens * tokens, axis=-1, keepdims=True) + EPSILON)
    unit = tokens * inverse
    grad_unit = grad_normed * gain_ref[...].astype(F32)
    grad = inverse * (grad_unit - unit * jnp.mean(grad_unit * unit, axis=-1, keepdims=True))
    out_ref[...] = (residual_ref[...] + grad).astype(BF16)


def exchange(moving, axis):
    return lax.all_to_all(moving, axis, split_axis=0, concat_axis=0, tiled=True)


def bias_strip(rel_bias, height):
    reach = iota((5 * height, height), 0) - iota((5 * height, height), 1) - 2 * height
    table = rel_bias.astype(F32)
    buckets = bucket_of(reach)
    tile = iota((5 * height, height), 0) // height
    strips = []
    for head in range(table.shape[0]):
        strip = jnp.zeros((5 * height, height), F32)
        for bucket in range(table.shape[1]):
            strip = jnp.where(buckets == bucket, table[head, bucket], strip)
        strips.append(jnp.where((tile == 0) | (tile == 4), 0.0, strip))
    return jnp.stack(strips)


def per_device(
    tokens_in,
    gain_attn,
    w_qkv,
    rel_bias,
    w_out,
    gain_ffn,
    w_router,
    w_up,
    w_down,
    segments,
    routes,
    cotangent,
):
    context_size = lax.axis_size("context")
    tensor_size = lax.axis_size("tensor")
    expert_size = lax.axis_size("expert")
    height, features = tokens_in.shape
    heads = rel_bias.shape[0]
    width = features // context_size
    head_size = width // heads
    length = segments.shape[1]
    spans = length // height
    experts_all = expert_size * context_size
    capacity = max(2, 5 * height // (4 * experts_all))
    rows_each = -(-capacity // 8) * 8
    place = lax.axis_index("tensor")
    place_arg = place.reshape(1).astype(jnp.int32)
    partner = [(0, 1), (1, 0)]
    blocks = context_size

    def swap(moving):
        return lax.ppermute(moving, "tensor", partner)

    gain_row = gain_attn.reshape(1, features)
    kv_out, q_out, normed = call(
        project_body,
        [
            shape((blocks, height, 2 * width)),
            shape((blocks, height, width)),
            shape((height, features)),
        ],
        (6 * height * features * features, 8 * features * features),
        count=3,
    )()(tokens_in, gain_row, w_qkv)
    kv_own = exchange(kv_out, "context")
    kv_other = swap(kv_own)
    q_own = exchange(q_out, "context")
    normed_rows = lax.all_gather(normed, "context", axis=0, tiled=True)
    strip = bias_strip(rel_bias, height)
    bias32 = rel_bias.astype(F32)
    attention_flops = 4 * heads * blocks * height * length * head_size
    attended_heads, exact, kaug, vaug, qaug = call(
        forward_body,
        [
            shape((blocks, heads, head_size, height)),
            shape((blocks, heads, head_size, height), F32),
            shape((heads, length, LANES)),
            shape((heads, length, LANES)),
            shape((heads, blocks, LANES, height)),
        ],
        (4 * attention_flops, 8 * features * features),
        smem=(0, 1),
        count=8,
    )(
        scratch_shapes=[
            pltpu.VMEM((heads, spans, head_size + 16, height), BF16),
            pltpu.VMEM(((spans + 2) * height, height), F32),
        ]
    )(
        place_arg,
        bias32,
        q_own,
        kv_own,
        kv_other,
        segments.reshape(length, 1),
        segments.reshape(spans, height),
        strip,
    )
    attended_t = exchange(attended_heads.reshape(blocks, width, height), "context").reshape(
        features, height
    )
    tokens = tokens_in.astype(F32)
    residual = tokens + tn(attended_t, w_out)
    inverse_ffn = lax.rsqrt(jnp.mean(residual * residual, axis=-1, keepdims=True) + EPSILON)
    unit_ffn = residual * inverse_ffn
    normed_ffn = (unit_ffn * gain_ffn.astype(F32)).astype(BF16)
    logits = nn(normed_ffn, w_router)
    router = jax.nn.softmax(logits, axis=-1)
    chosen = routes[:, 0]
    onehot = chosen[:, None] == jnp.arange(experts_all, dtype=jnp.int32)[None, :]
    gate_value = jnp.sum(jnp.where(onehot, router, 0.0), axis=-1)
    earlier = (iota((height, height), 0) > iota((height, height), 1)).astype(BF16)
    before = nn(earlier, onehot.astype(BF16))
    slot_rank = jnp.sum(jnp.where(onehot, before, 0.0), axis=-1).astype(jnp.int32)
    slot_of = jnp.where(slot_rank < capacity, chosen * rows_each + slot_rank, -1)
    dispatch = (
        jnp.arange(experts_all * rows_each, dtype=jnp.int32)[:, None] == slot_of[None, :]
    ).astype(BF16)
    grad_mixed = cotangent.astype(F32)
    grad_expert = (gate_value[:, None] * grad_mixed).astype(BF16)
    slots = experts_all * rows_each
    both_rows = jnp.concatenate([normed_ffn, grad_expert], axis=1)
    outgoing = nn(dispatch, both_rows).astype(BF16)
    incoming = exchange(
        outgoing.reshape(experts_all, rows_each, 2 * features), ("expert", "context")
    ).reshape(slots, 2 * features)
    rows_in, grad_produced = incoming[:, :features], incoming[:, features:]
    hidden = nn(rows_in, w_up[0])
    gelu, gelu_pull = jax.vjp(lambda pre_act: jax.nn.gelu(pre_act, approximate=False), hidden)
    active = gelu.astype(BF16)
    produced = nn(active, w_down[0]).astype(BF16)
    grad_active = nt(grad_produced, w_down[0])
    grad_hidden = gelu_pull(grad_active)[0].astype(BF16)
    grad_incoming = nt(grad_hidden, w_up[0]).astype(BF16)
    returned = exchange(
        jnp.concatenate([produced, grad_incoming], axis=1).reshape(
            experts_all, rows_each, 2 * features
        ),
        ("expert", "context"),
    ).reshape(slots, 2 * features)
    half = w_up.shape[2] // tensor_size

    def share(values):
        mine = lax.dynamic_slice_in_dim(values, place * half, half, 1)
        theirs = lax.dynamic_slice_in_dim(values, (1 - place) * half, half, 1)
        return jnp.concatenate([mine, swap(theirs)], axis=0)

    all_in = jnp.concatenate([incoming, swap(incoming)], axis=0)
    grad_up = tn(all_in[:, :features], share(grad_hidden))
    grad_down = tn(share(active), all_in[:, features:])
    back = tn(dispatch, returned)
    gathered_back, grad_sent = back[:, :features], back[:, features:]
    mixed_out = (residual + gate_value[:, None] * gathered_back).astype(BF16)
    grad_gate = jnp.sum(grad_mixed * gathered_back, axis=-1)
    grad_logits = (
        router * (jnp.where(onehot, grad_gate[:, None], 0.0) - (gate_value * grad_gate)[:, None])
    ).astype(BF16)
    grad_normed_ffn = grad_sent + nt(grad_logits, w_router)
    grad_unit = grad_normed_ffn * gain_ffn.astype(F32)
    grad_residual = grad_mixed + inverse_ffn * (
        grad_unit - unit_ffn * jnp.mean(grad_unit * unit_ffn, axis=-1, keepdims=True)
    )
    grad_branch = grad_residual.astype(BF16)
    grad_attended = nt(w_out, grad_branch).astype(BF16)
    grad_heads = exchange(grad_attended.reshape(blocks, width, height), "context").reshape(
        blocks, heads, head_size, height
    )
    grad_gain_ffn = jnp.sum(grad_normed_ffn * unit_ffn, axis=0)
    grad_router = tn(normed_ffn, grad_logits)
    grad_out_t = nt(grad_branch.T, attended_t)
    pieces = features // (experts_all * tensor_size)

    def scatter(partial):
        columns = partial.shape[1]
        shaped = partial.astype(BF16).reshape(experts_all, tensor_size, pieces, columns)
        mine = lax.dynamic_index_in_dim(shaped, place, 1, keepdims=False)
        theirs = lax.dynamic_index_in_dim(shaped, 1 - place, 1, keepdims=False)
        summed = (mine.astype(F32) + swap(theirs).astype(F32)).astype(BF16)
        return exchange(summed, ("expert", "context"))

    packed = jnp.concatenate([grad_out_t, grad_router, grad_gain_ffn[:, None]], axis=1)
    reduced = jnp.sum(scatter(packed).astype(F32), axis=0)
    dq, dkv_own, dkv_other, diag, far = call(
        backward_body,
        [
            shape((blocks, height, width)),
            shape((blocks, height, 2 * width)),
            shape((blocks, height, 2 * width)),
            shape((heads, 5 * height, height), F32),
            shape((heads, 2, spans, height), F32),
        ],
        (6 * attention_flops, 8 * features * features),
        smem=(0,),
        count=7,
    )(
        scratch_shapes=[
            pltpu.VMEM((heads, spans, head_size + 16, height), BF16),
            pltpu.VMEM((heads, length, LANES), F32),
            pltpu.VMEM((width, height), F32),
        ]
    )(place_arg, kaug, vaug, qaug, exact, grad_heads, strip)
    summed_kv = (dkv_own.astype(F32) + swap(dkv_other).astype(F32)).astype(BF16)
    group_grads = jnp.concatenate([summed_kv, dq], axis=2)
    grad_projected = exchange(group_grads, "context")
    group_qkv = tn(normed_rows, group_grads.reshape(blocks * height, 3 * width))
    landed = scatter(group_qkv).astype(F32).reshape(expert_size, context_size, pieces, 3 * width)
    mine_qkv = jnp.sum(landed, axis=0)
    grad_qkv = jnp.concatenate(
        [mine_qkv[c, :, 2 * width :] for c in range(context_size)]
        + [mine_qkv[c, :, :width] for c in range(context_size)]
        + [mine_qkv[c, :, width : 2 * width] for c in range(context_size)],
        axis=1,
    )
    first_piece = (
        (lax.axis_index("expert") * context_size + lax.axis_index("context")) * tensor_size + place
    ) * pieces
    own_w = lax.dynamic_slice_in_dim(w_qkv, first_piece, pieces, 0).astype(F32)
    own_gain = lax.dynamic_slice_in_dim(gain_attn, first_piece, pieces, 0).astype(F32)
    grad_gain_attn = jnp.sum(own_w * grad_qkv, axis=1) / own_gain
    (grad_tokens,) = call(
        finish_body,
        [shape((height, features))],
        (6 * height * features * features, 8 * features * features),
        count=5,
    )(scratch_shapes=[pltpu.VMEM((height, 3 * features), BF16)])(
        tokens_in, gain_row, w_qkv, grad_projected, grad_residual
    )
    (by_bucket,) = call(
        diagonal_body,
        [shape((heads, 1, LANES), F32)],
        (10 * heads * 7 * height * height, 4 * heads * 5 * height * height),
        count=2,
    )()(diag, far)
    grad_rel = lax.psum(by_bucket[:, 0, : rel_bias.shape[1]], ("expert", "tensor"))
    return (
        mixed_out,
        grad_tokens,
        grad_gain_attn,
        grad_qkv,
        grad_rel,
        reduced[:, :features].T,
        reduced[:, features + experts_all],
        reduced[:, features : features + experts_all],
        grad_up[None],
        grad_down[None],
    )


def solution(mesh):
    rows = ("expert", "context", "tensor")
    in_specs = (
        P(rows, None),
        P(),
        P(),
        P("context", None),
        P(),
        P(),
        P(),
        P(("expert", "context"), None, None),
        P(("expert", "context"), None, None),
        P("expert", None),
        P(rows, None),
        P(rows, None),
    )
    out_specs = (
        P(rows, None),
        P(rows, None),
        P(rows),
        P(rows, None),
        P("context", None),
        P(None, rows),
        P(rows),
        P(rows, None),
        P(("expert", "context"), None, "tensor"),
        P(("expert", "context"), "tensor", None),
    )
    return jax.shard_map(
        per_device, mesh=mesh, in_specs=in_specs, out_specs=out_specs, check_vma=False
    )
```

```python
import functools

import jax
import jax.numpy as jnp
from jax import lax
from jax.experimental import pallas as pl
from jax.experimental.pallas import tpu as pltpu
from jax.sharding import PartitionSpec as P

EPSILON = 1e-06
THRESHOLDS = (12, 16, 23, 32, 46, 64, 91)
FAR_LEFT = 15
FAR_RIGHT = 31
EXCLUDED = -1e30
LANES = 128
BF16 = jnp.bfloat16
F32 = jnp.float32
VMEM_LIMIT = 56 * 1024 * 1024
SMALL_LIMIT = 32 * 1024 * 1024
EXPERT_LIMIT = 40 * 1024 * 1024
CHUNK = 512


def bucket_of(offset):
    distance = jnp.abs(offset)
    beyond = jnp.zeros_like(distance)
    for threshold in THRESHOLDS:
        beyond = beyond + (distance >= threshold).astype(jnp.int32)
    nearby = jnp.where(distance < 8, distance, 8 + beyond)
    return nearby + 16 * (offset > 0).astype(jnp.int32)


def nn(left, right):
    return lax.dot_general(left, right, (((1,), (0,)), ((), ())), preferred_element_type=F32)


def nt(left, right):
    return lax.dot_general(left, right, (((1,), (1,)), ((), ())), preferred_element_type=F32)


def tn(left, right):
    return lax.dot_general(left, right, (((0,), (0,)), ((), ())), preferred_element_type=F32)


def iota(shape, axis):
    return lax.broadcasted_iota(jnp.int32, shape, axis)


def three_terms(values):
    high = values.astype(BF16).astype(F32)
    middle = (values - high).astype(BF16).astype(F32)
    return high, middle, values - high - middle


def specs_for(count, smem=()):
    return [
        pl.BlockSpec(memory_space=pltpu.SMEM if i in smem else pltpu.VMEM) for i in range(count)
    ]


def run(body, out_shape, args, scratch=(), smem=(), flops=0, moved=0, limit=VMEM_LIMIT):
    return pl.pallas_call(
        body,
        out_shape=out_shape,
        in_specs=specs_for(len(args), smem),
        scratch_shapes=list(scratch),
        cost_estimate=pl.CostEstimate(flops=flops, bytes_accessed=moved, transcendentals=0),
        compiler_params=pltpu.CompilerParams(vmem_limit_bytes=limit),
    )(*args)


def shape(dims, kind=BF16):
    return jax.ShapeDtypeStruct(dims, kind)


def project_body(groups, place_ref, tokens_ref, gain_ref, w_ref, *refs):
    kv_refs, q_refs, normed_ref = refs[:groups], refs[groups : 2 * groups], refs[2 * groups]
    kv_all, q_all = refs[2 * groups + 1 :]
    width, height = q_refs[0].shape
    features = tokens_ref.shape[1]
    group = place_ref[1]
    tokens = tokens_ref[...].astype(F32)
    inverse = lax.rsqrt(jnp.mean(tokens * tokens, axis=-1, keepdims=True) + EPSILON)
    normed = (tokens * inverse * gain_ref[...].astype(F32)).astype(BF16)
    normed_ref[...] = normed
    for part in range(2):
        first = (part + 1) * features
        product = nn(normed, w_ref[:, first : first + features]).astype(BF16)
        for at in range(groups):
            kv_all[at ^ group, :, part * width : (part + 1) * width] = product[
                :, at * width : (at + 1) * width
            ]
    turned = jnp.transpose(nn(normed, w_ref[:, :features])).astype(BF16)
    for at in range(groups):
        q_all[at ^ group] = turned[at * width : (at + 1) * width]
    for at in range(groups):
        kv_refs[at][...] = kv_all[at]
        q_refs[at][...] = q_all[at]


def strip_body(table_ref, *strip_refs):
    rows, height = strip_refs[0].shape
    used = rows - height
    offset = iota((used, LANES), 0) - 2 * height
    onehot = (bucket_of(offset) == iota((used, LANES), 1)).astype(BF16)
    lane = iota((used, height), 1)
    blank = jnp.zeros((height, height), F32)
    for head, strip_ref in enumerate(strip_refs):
        values = nn(onehot, table_ref[head])
        moved = 1
        while moved < height:
            values = jnp.where((lane & moved) != 0, pltpu.roll(values, moved, 0), values)
            moved *= 2
        strip_ref[:height] = blank
        strip_ref[height:used] = values[height:]
        strip_ref[used:] = blank


def forward_body(groups, heads, head, place_ref, bias_ref, *refs):
    q_refs, kv_refs, far_refs = (refs[i * groups : (i + 1) * groups] for i in range(3))
    seg_col_ref, seg_row_ref, strip_ref = refs[3 * groups : 3 * groups + 3]
    out_refs = refs[3 * groups + 3 : 4 * groups + 3]
    exact_ref, kaug_ref, vaug_ref, qaug_ref, vt_ref, score_ref, out_all = refs[4 * groups + 3 :]
    head_size, height = out_refs[0].shape
    width = heads * head_size
    spans = kaug_ref.shape[0] // height
    place, group = place_ref[0], place_ref[1]
    rest = LANES - head_size
    tall = head_size + 16
    pick_v = (iota((tall, LANES), 0) == iota((tall, LANES), 1)).astype(BF16)
    extra_lane = iota((height, rest), 1)
    ones_half = jnp.where(extra_lane < 3, 1.0, 0.0).astype(BF16)
    extra_row = iota((rest, height), 0)
    first_k, first_v = head * head_size, width + head * head_size
    for at in range(groups):
        block = at ^ group
        for source, parity in ((kv_refs[at], place), (far_refs[at], 1 - place)):
            span = 2 * block + parity
            first = pl.multiple_of(span * height, height)
            docs = seg_col_ref[pl.ds(first, height), :]
            extra = jnp.where(extra_lane < 3, jnp.where(docs == extra_lane, 0.0, EXCLUDED), 0.0)
            extra = jnp.where(extra_lane - 3 == span, 1.0, extra)
            extra = jnp.where((extra_lane >= 11) & (extra_lane < 14), 1.0, extra).astype(BF16)
            k_part = source[:, first_k : first_k + head_size]
            v_part = source[:, first_v : first_v + head_size]
            kaug_ref[pl.ds(first, height), :] = jnp.concatenate([k_part, extra], axis=1)
            v_full = jnp.concatenate([v_part, ones_half], axis=1)
            vaug_ref[pl.ds(first, height), :] = v_full
            vt_ref[span] = nt(pick_v, v_full).astype(BF16)
        span = 2 * block + place
        docs = seg_row_ref[pl.ds(span, 1), :]
        apart = extra_row - 3 - span
        far = jnp.where(
            apart <= -2,
            bias_ref[head, FAR_LEFT],
            jnp.where(apart >= 2, bias_ref[head, FAR_RIGHT], 0.0),
        )
        extra = jnp.where(
            extra_row < 3,
            jnp.where(docs == extra_row, 1.0, 0.0),
            jnp.where(extra_row < 3 + spans, far, 0.0),
        )
        qaug_ref[at] = jnp.concatenate(
            [q_refs[at][first_k : first_k + head_size, :], extra.astype(BF16)], axis=0
        )

    def step(at, carried):
        span = 2 * (at ^ group) + place
        queries = qaug_ref[at]
        for key in range(spans):
            score_ref[(key + 1) * height : (key + 2) * height] = nn(
                kaug_ref[key * height : (key + 1) * height, :], queries
            )
        near = pl.ds(pl.multiple_of(span * height, height), 3 * height)
        score_ref[near, :] = score_ref[near, :] + strip_ref[height : 4 * height, :]
        row_max = jnp.max(score_ref[height : 2 * height], axis=0, keepdims=True)
        for key in range(1, spans):
            row_max = jnp.maximum(
                row_max,
                jnp.max(score_ref[(key + 1) * height : (key + 2) * height], axis=0, keepdims=True),
            )
        total = jnp.zeros((tall, height), F32)
        for key in range(spans):
            weights = jnp.exp(score_ref[(key + 1) * height : (key + 2) * height] - row_max)
            total = total + nn(vt_ref[key], weights.astype(BF16))
        denominator = total[head_size : head_size + 1]
        result = total[:head_size] * (1.0 / denominator)
        out_all[at] = result.astype(BF16)
        exact_ref[at] = result
        high, middle, low = three_terms(-(row_max + jnp.log(denominator)))
        row = iota((16, height), 0)
        terms = jnp.where(row == 11, high, jnp.where(row == 12, middle, low))
        held = qaug_ref[at, head_size:tall, :].astype(F32)
        qaug_ref[at, head_size:tall, :] = jnp.where((row >= 11) & (row < 14), terms, held).astype(
            BF16
        )
        return carried

    lax.fori_loop(0, groups, step, 0)
    for at in range(groups):
        out_refs[at][...] = out_all[at]


def backward_body(
    groups, place_ref, kaug_ref, vaug_ref, qaug_ref, exact_ref, strip_ref, *refs
):
    grad_refs, dq_refs = refs[:groups], refs[groups : 2 * groups]
    own_ref, other_ref, diag_ref, far_ref, kt_ref, dkv_ref, grad_all, dq_all = refs[2 * groups :]
    head_size, height = grad_refs[0].shape
    spans = kaug_ref.shape[0] // height
    place, group = place_ref[0], place_ref[1]
    tall = head_size + 16
    row, column = iota((tall, LANES), 0), iota((tall, LANES), 1)
    pick_k = (
        ((row < head_size) & (row == column))
        | ((row >= head_size) & (row < head_size + spans) & (row + 3 == column))
    ).astype(BF16)
    for key in range(spans):
        kt_ref[key] = nt(pick_k, kaug_ref[key * height : (key + 1) * height, :]).astype(BF16)
    for at in range(groups):
        grad_all[at] = grad_refs[at][...]
    dkv_ref[...] = jnp.zeros_like(dkv_ref)
    diag_ref[...] = jnp.zeros_like(diag_ref)
    far_ref[...] = jnp.zeros_like(far_ref)
    extra_row = iota((LANES - head_size, height), 0)
    blank = jnp.zeros((head_size, height), BF16)
    span_row = iota((spans, height), 0)

    def step(at, carried):
        span = 2 * (at ^ group) + place
        start = jnp.clip(span - 1, 0, spans - 3)
        queries = qaug_ref[at]
        grads = grad_all[at]
        delta = jnp.sum(grads.astype(F32) * exact_ref[at], axis=0, keepdims=True)
        high, middle, low = three_terms(-delta)
        extra = jnp.where(
            extra_row == 0,
            high,
            jnp.where(extra_row == 1, middle, jnp.where(extra_row == 2, low, 0.0)),
        ).astype(BF16)
        grads_extra = jnp.concatenate([grads, extra], axis=0)
        sides = jnp.concatenate(
            [
                jnp.concatenate([queries[:head_size], blank], axis=1),
                jnp.concatenate([blank, grads], axis=1),
            ],
            axis=0,
        )
        dq_total = jnp.zeros((tall, height), F32)
        far_total = jnp.zeros((tall, height), F32)
        for step_at in range(spans):
            near = step_at < 3
            key_span = (start + step_at) if near else ((start + step_at) & (spans - 1))
            first = pl.multiple_of(key_span * height, height)
            exponent = nn(kaug_ref[pl.ds(first, height), :], queries)
            if near:
                level = pl.multiple_of((key_span - span + 2) * height, height)
                exponent = exponent + strip_ref[pl.ds(level, height), :]
            probs = jnp.exp(exponent)
            grad_probs = nn(vaug_ref[pl.ds(first, height), :], grads_extra)
            grad_scores = (probs * grad_probs).astype(BF16)
            if near:
                diag_ref[pl.ds(level, height), :] = diag_ref[
                    pl.ds(level, height), :
                ] + grad_scores.astype(F32)
            both = jnp.concatenate([grad_scores, probs.astype(BF16)], axis=1)
            dkv_ref[pl.ds(first, height), :] = dkv_ref[pl.ds(first, height), :] + nt(both, sides)
            turned = nn(kt_ref[key_span], grad_scores)
            if near:
                dq_total = dq_total + turned
            else:
                far_total = far_total + turned
        dq_all[at] = (dq_total + far_total)[:head_size].astype(BF16)
        sums = far_total[head_size : head_size + spans]
        far_ref[0] = far_ref[0] + jnp.where(span_row < start, sums, 0.0)
        far_ref[1] = far_ref[1] + jnp.where(span_row >= start + 3, sums, 0.0)
        return carried

    lax.fori_loop(0, groups, step, 0)
    for at in range(groups):
        dq_refs[at][...] = dq_all[at]
        for target, parity in ((own_ref, place), (other_ref, 1 - place)):
            first = pl.multiple_of((2 * (at ^ group) + parity) * height, height)
            target[at] = dkv_ref[pl.ds(first, height), :].astype(BF16)


def pair_body(own_ref, other_ref, *out_refs):
    for at, out_ref in enumerate(out_refs):
        out_ref[...] = (own_ref[at].astype(F32) + other_ref[at].astype(F32)).astype(BF16)


def diagonal_body(heads, *refs):
    out_ref = refs[2 * heads]
    rows, height = refs[0].shape
    total_rows = rows + 2 * height
    lane = iota((total_rows, height), 1)
    offset = iota((total_rows, LANES), 0) - 3 * height
    table = (bucket_of(offset) == iota((total_rows, LANES), 1)).astype(F32)
    lane_out = iota((1, LANES), 1)
    blank = jnp.zeros((height, height), F32)
    for head in range(heads):
        diag_ref, far_ref = refs[head], refs[heads + head]
        values = jnp.concatenate([blank, diag_ref[...], blank], axis=0)
        moved = 1
        while moved < height:
            values = jnp.where(
                (lane & moved) != 0, pltpu.roll(values, total_rows - moved, 0), values
            )
            moved *= 2
        sums = jnp.sum(values, axis=1, keepdims=True)
        by_bucket = jnp.sum(sums * table, axis=0, keepdims=True)
        by_bucket = by_bucket + jnp.where(lane_out == FAR_LEFT, jnp.sum(far_ref[0]), 0.0)
        out_ref[head] = by_bucket + jnp.where(lane_out == FAR_RIGHT, jnp.sum(far_ref[1]), 0.0)


def route_body(
    groups,
    heads,
    capacity,
    rows_each,
    place_ref,
    tokens_ref,
    w_out_ref,
    gain_ref,
    w_router_ref,
    route_col_ref,
    route_row_ref,
    cotangent_ref,
    *refs,
):
    pieces = refs[: groups * heads]
    residual_ref, normed_ref, router_ref, sent_ref, grad_sent_ref, attended_ref = refs[
        groups * heads :
    ]
    height = tokens_ref.shape[0]
    experts = w_router_ref.shape[1]
    slots = sent_ref.shape[0]
    head_size = pieces[0].shape[0]
    group = place_ref[1]
    for at in range(groups):
        for head in range(heads):
            first = pl.multiple_of(((at ^ group) * heads + head) * head_size, head_size)
            attended_ref[pl.ds(first, head_size), :] = pieces[head * groups + at][...]
    residual = tokens_ref[...].astype(F32) + tn(attended_ref[...], w_out_ref[...])
    residual_ref[...] = residual
    inverse = lax.rsqrt(jnp.mean(residual * residual, axis=-1, keepdims=True) + EPSILON)
    normed = (residual * inverse * gain_ref[...].astype(F32)).astype(BF16)
    normed_ref[...] = normed
    logits = nn(normed, w_router_ref[...])
    powers = jnp.exp(logits - jnp.max(logits, axis=-1, keepdims=True))
    router = powers / jnp.sum(powers, axis=-1, keepdims=True)
    router_ref[...] = router
    onehot = iota((height, experts), 1) == route_col_ref[...]
    gate = jnp.sum(jnp.where(onehot, router, 0.0), axis=-1, keepdims=True)
    grad_expert = (gate * cotangent_ref[...].astype(F32)).astype(BF16)
    chosen = route_row_ref[...]
    marks = iota((experts, height), 0) == chosen
    earlier = (iota((height, height), 0) < iota((height, height), 1)).astype(BF16)
    before = nn(jnp.where(marks, 1.0, 0.0).astype(BF16), earlier)
    rank = jnp.sum(jnp.where(marks, before, 0.0), axis=0, keepdims=True).astype(jnp.int32)
    slot = jnp.where(rank < capacity, chosen * rows_each + rank, -1)
    dispatch = jnp.where(iota((slots, height), 0) == slot, 1.0, 0.0).astype(BF16)
    sent_ref[...] = nn(dispatch, normed).astype(BF16)
    grad_sent_ref[...] = nn(dispatch, grad_expert).astype(BF16)


def combine_body(
    groups,
    heads,
    capacity,
    rows_each,
    place_ref,
    produced_ref,
    grad_back_ref,
    residual_ref,
    router_ref,
    route_col_ref,
    cotangent_ref,
    gain_ref,
    w_router_ref,
    w_out_ref,
    mixed_ref,
    grad_residual_ref,
    branch_ref,
    logits_ref,
    gain_out_ref,
    *refs,
):
    pieces, turned_ref = refs[: groups * heads], refs[groups * heads]
    height, experts = router_ref.shape
    slots = produced_ref.shape[0]
    head_size = pieces[0].shape[0]
    group = place_ref[1]
    chosen = route_col_ref[...]
    onehot = iota((height, experts), 1) == chosen
    earlier = (iota((height, height), 0) > iota((height, height), 1)).astype(BF16)
    before = nn(earlier, jnp.where(onehot, 1.0, 0.0).astype(BF16))
    rank = jnp.sum(jnp.where(onehot, before, 0.0), axis=1, keepdims=True).astype(jnp.int32)
    slot = jnp.where(rank < capacity, chosen * rows_each + rank, -1)
    combine = jnp.where(iota((height, slots), 1) == slot, 1.0, 0.0).astype(BF16)
    router = router_ref[...]
    gate = jnp.sum(jnp.where(onehot, router, 0.0), axis=-1, keepdims=True)
    residual = residual_ref[...]
    inverse = lax.rsqrt(jnp.mean(residual * residual, axis=-1, keepdims=True) + EPSILON)
    unit = residual * inverse
    grad_mixed = cotangent_ref[...].astype(F32)
    gathered = nn(combine, produced_ref[...])
    mixed_ref[...] = (residual + gate * gathered).astype(BF16)
    grad_gate = jnp.sum(grad_mixed * gathered, axis=-1, keepdims=True)
    grad_logits = (router * (jnp.where(onehot, grad_gate, 0.0) - gate * grad_gate)).astype(BF16)
    grad_normed = nn(combine, grad_back_ref[...]) + nt(grad_logits, w_router_ref[...])
    grad_unit = grad_normed * gain_ref[...].astype(F32)
    grad_residual = grad_mixed + inverse * (
        grad_unit - unit * jnp.mean(grad_unit * unit, axis=-1, keepdims=True)
    )
    branch = grad_residual.astype(BF16)
    turned_ref[...] = nt(w_out_ref[...], branch).astype(BF16)
    for at in range(groups):
        for head in range(heads):
            first = pl.multiple_of(((at ^ group) * heads + head) * head_size, head_size)
            pieces[head * groups + at][...] = turned_ref[pl.ds(first, head_size), :]
    grad_residual_ref[...] = grad_residual
    branch_ref[...] = branch
    spare = logits_ref.shape[1] - experts
    logits_ref[...] = jnp.concatenate([grad_logits, jnp.zeros((height, spare), BF16)], axis=1)
    sums = jnp.sum(grad_normed * unit, axis=0, keepdims=True)
    gain_out_ref[...] = jnp.broadcast_to(sums, gain_out_ref.shape)


def split_rows(place, source_ref, mine_ref, other_ref):
    experts_all, pieces, columns = mine_ref.shape
    for parity in range(2):

        @pl.when(place == parity)
        def _():
            for at in range(experts_all):
                for target, which in ((mine_ref, parity), (other_ref, 1 - parity)):
                    first = (2 * at + which) * pieces
                    target[at] = source_ref[first : first + pieces, :].astype(BF16)


def weights_body(
    experts,
    place_ref,
    branch_ref,
    attended_ref,
    normed_ref,
    logits_ref,
    gain_ref,
    mine_ref,
    other_ref,
    packed_ref,
):
    features = branch_ref.shape[1]
    extra = logits_ref.shape[1]
    branch = jnp.transpose(branch_ref[...].astype(F32)).astype(BF16)
    packed_ref[:, :features] = nt(branch, attended_ref[...])
    normed = jnp.transpose(normed_ref[...].astype(F32)).astype(BF16)
    column = jnp.transpose(gain_ref[...])[:, :1]
    packed_ref[:, features:] = nn(normed, logits_ref[...]) + jnp.where(
        iota((features, extra), 1) == experts, column, 0.0
    )
    split_rows(place_ref[0], packed_ref, mine_ref, other_ref)


def qkv_body(groups, heads, place_ref, *refs):
    normed_refs = refs[:groups]
    kv_refs = refs[groups : groups + groups * heads]
    dq_refs = refs[groups + groups * heads : groups + 2 * groups * heads]
    mine_ref, other_ref, total_ref, rows_ref = refs[groups + 2 * groups * heads :]
    head_size, height = dq_refs[0].shape
    width = heads * head_size
    for at in range(groups):
        turned = jnp.concatenate(
            [dq_refs[head * groups + at][...].astype(F32) for head in range(heads)], axis=0
        )
        rows_ref[:, :width] = jnp.transpose(turned).astype(BF16)
        for head in range(heads):
            both = kv_refs[head * groups + at][...]
            for part in range(2):
                first = (part + 1) * width + head * head_size
                rows_ref[:, first : first + head_size] = both[
                    :, part * head_size : (part + 1) * head_size
                ]
        product = nn(normed_refs[at][...], rows_ref[...])
        if at == 0:
            total_ref[...] = product
        else:
            total_ref[...] = total_ref[...] + product
    split_rows(place_ref[0], total_ref, mine_ref, other_ref)


def finish_body(groups, heads, place_ref, tokens_ref, gain_ref, w_ref, residual_ref, *refs):
    kv_refs = refs[: groups * heads]
    dq_refs = refs[groups * heads : 2 * groups * heads]
    out_ref, turned_ref, k_all, v_all = refs[2 * groups * heads :]
    head_size, height = dq_refs[0].shape
    features = tokens_ref.shape[1]
    width = heads * head_size
    group = place_ref[1]
    for at in range(groups):
        for head in range(heads):
            first = pl.multiple_of(((at ^ group) * heads + head) * head_size, head_size)
            turned_ref[pl.ds(first, head_size), :] = dq_refs[head * groups + at][...].astype(F32)
            both = kv_refs[head * groups + at][...]
            lanes = slice(head * head_size, (head + 1) * head_size)
            k_all[at ^ group, :, lanes] = both[:, :head_size]
            v_all[at ^ group, :, lanes] = both[:, head_size:]
    rows = jnp.transpose(turned_ref[...]).astype(BF16)
    grad_normed = nt(rows, w_ref[:, :features])
    for part, source in ((1, k_all), (2, v_all)):
        joined = jnp.concatenate([source[at] for at in range(groups)], axis=1)
        grad_normed = grad_normed + nt(joined, w_ref[:, part * features : (part + 1) * features])
    tokens = tokens_ref[...].astype(F32)
    inverse = lax.rsqrt(jnp.mean(tokens * tokens, axis=-1, keepdims=True) + EPSILON)
    unit = tokens * inverse
    grad_unit = grad_normed * gain_ref[...].astype(F32)
    grad = inverse * (grad_unit - unit * jnp.mean(grad_unit * unit, axis=-1, keepdims=True))
    out_ref[...] = (residual_ref[...] + grad).astype(BF16)


def expert_forward_body(
    place_ref, rows_ref, up_ref, down_ref, produced_ref, other_ref, mine_ref, slope_ref, total_ref
):
    step, steps = pl.program_id(0), pl.num_programs(0)
    hidden = nn(rows_ref[...], up_ref[...])
    below = 0.5 * (1.0 + lax.erf(hidden * (2.0**-0.5)))
    bell = jnp.exp(-0.5 * hidden * hidden) * 0.3989422804014327
    slope_ref[...] = (below + hidden * bell).astype(BF16)
    active = (hidden * below).astype(BF16)

    @pl.when(step < steps // 2)
    def _():
        other_ref[...] = active

    @pl.when(step >= steps // 2)
    def _():
        mine_ref[...] = active

    product = nn(active, down_ref[...])

    @pl.when(step == 0)
    def _():
        total_ref[...] = product

    @pl.when(step > 0)
    def _():
        total_ref[...] = total_ref[...] + product

    @pl.when(step == steps - 1)
    def _():
        produced_ref[...] = total_ref[...].astype(BF16)


def expert_backward_body(
    place_ref, grads_ref, up_ref, down_ref, slope_ref, back_ref, other_ref, mine_ref, total_ref
):
    step, steps = pl.program_id(0), pl.num_programs(0)
    grad_active = nt(grads_ref[...], down_ref[...])
    grad_hidden = (grad_active * slope_ref[...].astype(F32)).astype(BF16)

    @pl.when(step < steps // 2)
    def _():
        other_ref[...] = grad_hidden

    @pl.when(step >= steps // 2)
    def _():
        mine_ref[...] = grad_hidden

    product = nt(grad_hidden, up_ref[...])

    @pl.when(step == 0)
    def _():
        total_ref[...] = product

    @pl.when(step > 0)
    def _():
        total_ref[...] = total_ref[...] + product

    @pl.when(step == steps - 1)
    def _():
        back_ref[...] = total_ref[...].astype(BF16)


def run_expert(body, place_arg, rows, up, down, slope, chunk):
    slots, features = rows.shape
    hidden_size = up.shape[1]
    steps = hidden_size // chunk
    half = steps // 2

    def piece(step, place):
        return lax.rem(step + half * (1 - place[0]), steps)

    whole = pl.BlockSpec((slots, features), lambda i, p: (0, 0))
    first_half = pl.BlockSpec((slots, chunk), lambda i, p: (0, jnp.minimum(i, half - 1)))
    second_half = pl.BlockSpec((slots, chunk), lambda i, p: (0, jnp.maximum(i - half, 0)))
    sloping = pl.BlockSpec((slots, chunk), lambda i, p: (0, i))
    in_specs = [
        whole,
        pl.BlockSpec((features, chunk), lambda i, p: (0, piece(i, p))),
        pl.BlockSpec((chunk, features), lambda i, p: (piece(i, p), 0)),
    ]
    out_specs = [whole, first_half, second_half]
    out_shape = [shape((slots, features))] + [shape((slots, hidden_size // 2))] * 2
    args = [place_arg, rows, up, down]
    if slope is None:
        out_specs.append(sloping)
        out_shape.append(shape((slots, hidden_size)))
    else:
        in_specs.append(sloping)
        args.append(slope)
    return pl.pallas_call(
        body,
        out_shape=out_shape,
        grid_spec=pltpu.PrefetchScalarGridSpec(
            num_scalar_prefetch=1,
            grid=(steps,),
            in_specs=in_specs,
            out_specs=out_specs,
            scratch_shapes=[pltpu.VMEM((slots, features), F32)],
        ),
        cost_estimate=pl.CostEstimate(
            flops=4 * slots * features * hidden_size,
            bytes_accessed=4 * features * hidden_size + 4 * slots * hidden_size,
            transcendentals=0,
        ),
        compiler_params=pltpu.CompilerParams(vmem_limit_bytes=EXPERT_LIMIT),
    )(*args)


def exchange(moving, axis):
    return lax.all_to_all(moving, axis, split_axis=0, concat_axis=0, tiled=True)


def cross(moving, axis, distance):
    size = lax.axis_size(axis)
    return lax.ppermute(moving, axis, [(i, i ^ distance) for i in range(size)])


def trade(pieces):
    return [
        piece if at == 0 else cross(piece, "context", at) for at, piece in enumerate(pieces)
    ]


def after(values, *others):
    return lax.optimization_barrier((values,) + others)[0]


def per_device(
    tokens_in,
    gain_attn,
    w_qkv,
    rel_bias,
    w_out,
    gain_ffn,
    w_router,
    w_up,
    w_down,
    segments,
    routes,
    cotangent,
):
    groups = lax.axis_size("context")
    tensor_size = lax.axis_size("tensor")
    expert_size = lax.axis_size("expert")
    height, features = tokens_in.shape
    heads = rel_bias.shape[0]
    width = features // groups
    head_size = width // heads
    length = segments.shape[1]
    spans = length // height
    experts_all = expert_size * groups
    capacity = max(2, 5 * height // (4 * experts_all))
    rows_each = -(-capacity // 8) * 8
    slots = experts_all * rows_each
    place = lax.axis_index("tensor")
    context_at = lax.axis_index("context")
    place_arg = jnp.stack([place, context_at]).astype(jnp.int32)
    gain_row = gain_attn.reshape(1, features)
    square = features * features

    projected = run(
        functools.partial(project_body, groups),
        [shape((height, 2 * width))] * groups
        + [shape((width, height))] * groups
        + [shape((height, features))],
        (place_arg, tokens_in, gain_row, w_qkv),
        scratch=[
            pltpu.VMEM((groups, height, 2 * width), BF16),
            pltpu.VMEM((groups, width, height), BF16),
        ],
        smem=(0,),
        flops=6 * height * square,
        moved=8 * square,
    )
    kv_own = trade(projected[:groups])
    q_own = trade(projected[groups : 2 * groups])
    kv_other = [cross(piece, "tensor", 1) for piece in kv_own]
    table = jnp.pad(rel_bias, ((0, 0), (0, LANES - rel_bias.shape[1])))
    table = jnp.broadcast_to(table[:, :, None], (heads, LANES, height))
    strips = run(
        strip_body,
        [shape((5 * height, height), F32)] * heads,
        (table,),
        flops=heads * 2 * 4 * height * LANES * height,
        moved=heads * 4 * 5 * height * height,
    )
    normed_t = projected[2 * groups].T
    bias32 = rel_bias.astype(F32)
    head_flops = 4 * groups * height * length * head_size
    seg_col = segments.reshape(length, 1)
    seg_row = segments.reshape(spans, height)
    attended, held = [], []
    for head in range(heads):
        outs = run(
            functools.partial(forward_body, groups, heads, head),
            [shape((head_size, height))] * groups
            + [
                shape((groups, head_size, height), F32),
                shape((length, LANES)),
                shape((length, LANES)),
                shape((groups, LANES, height)),
            ],
            (place_arg, bias32, *q_own, *kv_own, *kv_other, seg_col, seg_row, strips[head]),
            scratch=[
                pltpu.VMEM((spans, head_size + 16, height), BF16),
                pltpu.VMEM(((spans + 2) * height, height), F32),
                pltpu.VMEM((groups, head_size, height), BF16),
            ],
            smem=(0, 1),
            flops=6 * head_flops,
            moved=8 * square,
        )
        attended += trade(outs[:groups])
        held.append(outs[groups:])
    normed_all = trade([after(normed_t, *q_own)] * groups)
    route_row = routes.reshape(1, height)
    residual, normed_ffn, router, sent, grad_expert, attended_t = run(
        functools.partial(route_body, groups, heads, capacity, rows_each),
        [
            shape((height, features), F32),
            shape((height, features)),
            shape((height, experts_all), F32),
            shape((slots, features)),
            shape((slots, features)),
            shape((features, height)),
        ],
        (
            place_arg,
            tokens_in,
            w_out,
            gain_ffn.reshape(1, features),
            w_router,
            routes,
            route_row,
            cotangent,
            *attended,
        ),
        smem=(0,),
        flops=2 * height * square,
        moved=4 * square,
        limit=SMALL_LIMIT,
    )

    def move_slots(moving):
        return exchange(
            moving.reshape(experts_all, rows_each, features), ("expert", "context")
        ).reshape(slots, features)

    rows_in = move_slots(sent)
    grads_in = move_slots(grad_expert)
    produced, active_other, active_mine, slope = run_expert(
        expert_forward_body, place_arg, rows_in, w_up[0], w_down[0], None, CHUNK
    )
    back_produced = move_slots(produced)
    grad_rows, hidden_other, hidden_mine = run_expert(
        expert_backward_body, place_arg, grads_in, w_up[0], w_down[0], slope, CHUNK
    )
    back_grads = move_slots(grad_rows)

    def both(values, sent_values):
        return jnp.concatenate([values, cross(sent_values, "tensor", 1)], axis=0)

    grad_down = tn(both(active_mine, active_other), both(grads_in, grads_in))
    grad_up = tn(both(rows_in, rows_in), both(hidden_mine, hidden_other))
    extra = -(-(experts_all + 1) // LANES) * LANES
    outs = run(
        functools.partial(combine_body, groups, heads, capacity, rows_each),
        [
            shape((height, features)),
            shape((height, features), F32),
            shape((height, features)),
            shape((height, extra)),
            shape((8, features), F32),
        ]
        + [shape((head_size, height))] * (groups * heads),
        (
            place_arg,
            back_produced,
            back_grads,
            residual,
            router,
            routes,
            cotangent,
            gain_ffn.reshape(1, features),
            w_router,
            w_out,
        ),
        scratch=[pltpu.VMEM((features, height), BF16)],
        smem=(0,),
        flops=4 * height * square,
        moved=8 * square,
        limit=SMALL_LIMIT,
    )
    mixed_out, grad_residual, branch, grad_logits, gain_sums = outs[:5]
    grad_pieces = [trade(outs[5 + h * groups : 5 + (h + 1) * groups]) for h in range(heads)]
    pieces = features // (experts_all * tensor_size)
    mine, other = run(
        functools.partial(weights_body, experts_all),
        [shape((experts_all, pieces, features + extra))] * 2,
        (place_arg, branch, attended_t, normed_ffn, grad_logits, gain_sums),
        scratch=[pltpu.VMEM((features, features + extra), F32)],
        smem=(0,),
        flops=2 * height * square,
        moved=8 * square,
    )

    def pair_sum(kept, received):
        return (kept.astype(F32) + received.astype(F32)).astype(BF16)

    packed = pair_sum(mine, cross(other, "tensor", 1))
    reduced = jnp.sum(exchange(packed, ("expert", "context")).astype(F32), axis=0)
    gates = [other, packed, packed]
    kv_grads, q_grads, diags, fars = [], [], [], []
    for head in range(heads):
        exact, kaug, vaug, qaug = held[head]
        outs = run(
            functools.partial(backward_body, groups),
            [shape((head_size, height))] * groups
            + [shape((groups, height, 2 * head_size))] * 2
            + [shape((5 * height, height), F32), shape((2, spans, height), F32)],
            (
                after(place_arg, gates[min(head, 2)]),
                kaug,
                vaug,
                qaug,
                exact,
                strips[head],
                *grad_pieces[head],
            ),
            scratch=[
                pltpu.VMEM((spans, head_size + 16, height), BF16),
                pltpu.VMEM((length, LANES), F32),
                pltpu.VMEM((groups, head_size, height), BF16),
                pltpu.VMEM((groups, head_size, height), BF16),
            ],
            smem=(0,),
            flops=8 * head_flops,
            moved=8 * square,
        )
        q_grads.append(outs[:groups])
        own, other_half, diag, far = outs[groups:]
        diags.append(diag)
        fars.append(far)
        kv_grads.append(
            run(
                pair_body,
                [shape((height, 2 * head_size))] * groups,
                (own, cross(other_half, "tensor", 1)),
                moved=6 * own.size,
                limit=SMALL_LIMIT,
            )
        )
    q_landed = [piece for head in range(heads) for piece in trade(q_grads[head])]
    kv_landed = [piece for head in range(heads) for piece in trade(kv_grads[head])]
    mine, other = run(
        functools.partial(qkv_body, groups, heads),
        [shape((experts_all, pieces, 3 * width))] * 2,
        (
            place_arg,
            *normed_all,
            *[piece for head in range(heads) for piece in kv_grads[head]],
            *[piece for head in range(heads) for piece in q_grads[head]],
        ),
        scratch=[pltpu.VMEM((features, 3 * width), F32), pltpu.VMEM((height, 3 * width), BF16)],
        smem=(0,),
        flops=6 * groups * height * features * width,
        moved=8 * square,
    )
    summed = pair_sum(mine, cross(other, "tensor", 1))
    landed = exchange(summed, ("expert", "context")).astype(F32)
    own_qkv = jnp.sum(landed.reshape(expert_size, groups, pieces, 3 * width), axis=0)
    grad_qkv = jnp.concatenate(
        [
            own_qkv[c, :, part * width : (part + 1) * width]
            for part in range(3)
            for c in range(groups)
        ],
        axis=1,
    )
    first_piece = (
        (lax.axis_index("expert") * groups + context_at) * tensor_size + place
    ) * pieces
    own_w = lax.dynamic_slice_in_dim(w_qkv, first_piece, pieces, 0).astype(F32)
    own_gain = lax.dynamic_slice_in_dim(gain_attn, first_piece, pieces, 0).astype(F32)
    grad_gain_attn = jnp.sum(own_w * grad_qkv, axis=1) / own_gain
    grad_tokens = run(
        functools.partial(finish_body, groups, heads),
        shape((height, features)),
        (place_arg, tokens_in, gain_row, w_qkv, grad_residual, *kv_landed, *q_landed),
        scratch=[
            pltpu.VMEM((features, height), F32),
            pltpu.VMEM((groups, height, width), BF16),
            pltpu.VMEM((groups, height, width), BF16),
        ],
        smem=(0,),
        flops=6 * height * square,
        moved=8 * square,
        limit=SMALL_LIMIT,
    )
    by_bucket = run(
        functools.partial(diagonal_body, heads),
        shape((heads, 1, LANES), F32),
        (*diags, *fars),
        flops=heads * 8 * 7 * height * height,
        moved=heads * 20 * height * height,
    )
    by_bucket = by_bucket + cross(by_bucket, "tensor", 1)
    distance = 1
    while distance < expert_size:
        by_bucket = by_bucket + cross(by_bucket, "expert", distance)
        distance *= 2
    return (
        mixed_out,
        grad_tokens,
        grad_gain_attn,
        grad_qkv,
        by_bucket[:, 0, : rel_bias.shape[1]],
        reduced[:, :features].T,
        reduced[:, features + experts_all],
        reduced[:, features : features + experts_all],
        grad_up[None],
        grad_down[None],
    )


def solution(mesh):
    rows = ("expert", "context", "tensor")
    in_specs = (
        P(rows, None),
        P(),
        P(),
        P("context", None),
        P(),
        P(),
        P(),
        P(("expert", "context"), None, None),
        P(("expert", "context"), None, None),
        P("expert", None),
        P(rows, None),
        P(rows, None),
    )
    out_specs = (
        P(rows, None),
        P(rows, None),
        P(rows),
        P(rows, None),
        P("context", None),
        P(None, rows),
        P(rows),
        P(rows, None),
        P(("expert", "context"), None, "tensor"),
        P(("expert", "context"), "tensor", None),
    )
    return jax.shard_map(
        per_device, mesh=mesh, in_specs=in_specs, out_specs=out_specs, check_vma=False
    )
```

```python
import functools

import jax
import jax.numpy as jnp
from jax import lax
from jax.experimental import pallas as pl
from jax.experimental.pallas import tpu as pltpu
from jax.sharding import PartitionSpec as P

EPSILON = 1e-06
THRESHOLDS = (12, 16, 23, 32, 46, 64, 91)
FAR_LEFT = 15
FAR_RIGHT = 31
EXCLUDED = -1e30
LANES = 128
BF16 = jnp.bfloat16
F32 = jnp.float32
VMEM_LIMIT = 56 * 1024 * 1024
CHUNK = 512


def bucket_of(offset):
    distance = jnp.abs(offset)
    beyond = jnp.zeros_like(distance)
    for threshold in THRESHOLDS:
        beyond = beyond + (distance >= threshold).astype(jnp.int32)
    nearby = jnp.where(distance < 8, distance, 8 + beyond)
    return nearby + 16 * (offset > 0).astype(jnp.int32)


def nn(left, right):
    return lax.dot_general(left, right, (((1,), (0,)), ((), ())), preferred_element_type=F32)


def nt(left, right):
    return lax.dot_general(left, right, (((1,), (1,)), ((), ())), preferred_element_type=F32)


def tn(left, right):
    return lax.dot_general(left, right, (((0,), (0,)), ((), ())), preferred_element_type=F32)


def iota(shape, axis):
    return lax.broadcasted_iota(jnp.int32, shape, axis)


def three_terms(values):
    high = values.astype(BF16).astype(F32)
    middle = (values - high).astype(BF16).astype(F32)
    return high, middle, values - high - middle


def specs_for(count, smem=()):
    return [
        pl.BlockSpec(memory_space=pltpu.SMEM if i in smem else pltpu.VMEM) for i in range(count)
    ]


def run(body, out_shape, args, scratch=(), smem=(), flops=0, moved=0, limit=VMEM_LIMIT):
    return pl.pallas_call(
        body,
        out_shape=out_shape,
        in_specs=specs_for(len(args), smem),
        scratch_shapes=list(scratch),
        cost_estimate=pl.CostEstimate(flops=flops, bytes_accessed=moved, transcendentals=0),
        compiler_params=pltpu.CompilerParams(vmem_limit_bytes=limit),
    )(*args)


def shape(dims, kind=BF16):
    return jax.ShapeDtypeStruct(dims, kind)


def project_body(heads, place_ref, tokens_ref, gain_ref, w_ref, *refs):
    groups = len(refs) - 2
    piece_refs, normed_ref, all_ref = refs[:groups], refs[groups], refs[groups + 1]
    height, features = tokens_ref.shape
    width = features // groups
    size = width // heads
    group = place_ref[1]
    tokens = tokens_ref[...].astype(F32)
    inverse = lax.rsqrt(jnp.mean(tokens * tokens, axis=-1, keepdims=True) + EPSILON)
    normed = (tokens * inverse * gain_ref[...].astype(F32)).astype(BF16)
    normed_ref[...] = jnp.transpose(normed.astype(F32)).astype(BF16)
    turned = jnp.transpose(nn(normed, w_ref[:, :features])).astype(BF16)
    keys = nn(normed, w_ref[:, features : 2 * features]).astype(BF16)
    values = nn(normed, w_ref[:, 2 * features :]).astype(BF16)
    for at in range(groups):
        for head in range(heads):
            lanes = slice(at * width + head * size, at * width + (head + 1) * size)
            all_ref[at ^ group, head * height : (head + 1) * height, :] = jnp.concatenate(
                [keys[:, lanes], values[:, lanes]], axis=1
            )
        for half in range(height // LANES):
            first = heads * height + half * width
            all_ref[at ^ group, first : first + width, :] = turned[
                at * width : (at + 1) * width, half * LANES : (half + 1) * LANES
            ]
    for at in range(groups):
        piece_refs[at][...] = all_ref[at]


def q_rows(piece_ref, heads, height, size, head):
    width = heads * size
    parts = []
    for half in range(height // LANES):
        first = heads * height + half * width + head * size
        parts.append(piece_ref[pl.ds(pl.multiple_of(first, 16), size), :])
    return jnp.concatenate(parts, axis=1)


def forward_body(groups, heads, place_ref, bias_ref, seg_ref, strip_ref, *refs):
    own_refs, far_refs, out_refs = (refs[i * groups : (i + 1) * groups] for i in range(3))
    exact_ref, inverse_ref, vaug_ref, kt_ref, weight_ref = refs[3 * groups : 3 * groups + 5]
    extra_all, docs_all, kaug_ref, vt_ref, score_ref = refs[3 * groups + 5 :]
    size, height = out_refs[0].shape
    spans = kaug_ref.shape[0] // height
    place, group = place_ref[0], place_ref[1]
    head = pl.program_id(0)
    tall = size + 16
    rest = LANES - size

    @pl.when(head == 0)
    def _():
        row = iota((LANES, height), 0) - size
        for span in range(spans):
            docs = seg_ref[0:1, span * height : (span + 1) * height]
            docs_all[span : span + 1, :] = docs
            extra = jnp.where((row >= 0) & (row < 3) & (docs != row), EXCLUDED, 0.0)
            extra = jnp.where(row - 3 == span, 1.0, extra)
            extra_all[span * height : (span + 1) * height, :] = jnp.transpose(extra).astype(BF16)

    row, column = iota((tall, LANES), 0), iota((tall, LANES), 1)
    pick_v = (((row < size) & (row + size == column)) | ((row == size) & (column == 0))).astype(
        BF16
    )
    pick_k = (
        ((row < size) & (row == column))
        | ((row >= size) & (row < size + spans) & (row + 3 == column))
    ).astype(BF16)
    lane = iota((height, LANES), 1)
    low_half = lane < size
    ones = jnp.where(lane < 3, 1.0, 0.0).astype(BF16)
    extra_row = iota((rest, height), 0)
    queries_all = []
    for at in range(groups):
        block = at ^ group
        for source, parity in ((own_refs[at], place), (far_refs[at], 1 - place)):
            span = 2 * block + parity
            rows = pl.ds(pl.multiple_of(span * height, height), height)
            both = source[pl.ds(pl.multiple_of(head * height, height), height), :]
            keys = jnp.where(low_half, both, extra_all[rows, :])
            values = jnp.where(low_half, ones, both)
            kaug_ref[rows, :] = keys
            vaug_ref[0, rows, :] = values
            vt_ref[span] = nt(pick_v, values).astype(BF16)
            kt_ref[0, span] = nt(pick_k, keys).astype(BF16)
        span = 2 * block + place
        docs = docs_all[pl.ds(span, 1), :]
        apart = extra_row - 3 - span
        far = jnp.where(
            apart <= -2,
            bias_ref[head, FAR_LEFT],
            jnp.where(apart >= 2, bias_ref[head, FAR_RIGHT], 0.0),
        )
        extra = jnp.where(
            extra_row < 3,
            jnp.where(docs == extra_row, 1.0, 0.0),
            jnp.where(extra_row < 3 + spans, far, 0.0),
        )
        queries_all.append(
            jnp.concatenate(
                [q_rows(own_refs[at], heads, height, size, head), extra.astype(BF16)], axis=0
            )
        )
    for at in range(groups):
        span = 2 * (at ^ group) + place
        start = jnp.clip(span - 1, 0, spans - 3)
        queries = queries_all[at]
        slot = at % 2
        row_max = None
        for step in range(spans):
            key_span = (start + step) if step < 3 else ((start + step) & (spans - 1))
            rows = pl.ds(pl.multiple_of(key_span * height, height), height)
            scores = nn(kaug_ref[rows, :], queries)
            if step < 3:
                level = pl.multiple_of((key_span - span + 2) * height, height)
                scores = scores + strip_ref[0, pl.ds(level, height), :]
            score_ref[slot, step] = scores
            best = jnp.max(scores, axis=0, keepdims=True)
            row_max = best if row_max is None else jnp.maximum(row_max, best)
        total = jnp.zeros((tall, height), F32)
        for step in range(spans):
            key_span = (start + step) if step < 3 else ((start + step) & (spans - 1))
            weights = jnp.exp(score_ref[slot, step] - row_max).astype(BF16)
            weight_ref[0, at, step] = weights
            total = total + nn(vt_ref[key_span], weights)
        inverse = 1.0 / total[size : size + 1]
        result = total[:size] * inverse
        out_refs[at][...] = result.astype(BF16)
        exact_ref[0, at] = result
        inverse_ref[0, at] = jnp.broadcast_to(inverse, (8, height))


def backward_body(groups, heads, first_head, place_ref, *refs):
    weight_ref, vaug_ref, kt_ref, exact_ref, inverse_ref = refs[:5]
    own_refs, grad_refs = refs[5 : 5 + groups], refs[5 + groups : 5 + 2 * groups]
    dq_ref, mine_ref, other_ref, diag_ref, far_ref, dkv_ref = refs[5 + 2 * groups :]
    size, height = grad_refs[0].shape
    spans = vaug_ref.shape[1] // height
    place, group = place_ref[0], place_ref[1]
    head = pl.program_id(0) + first_head
    tall = size + 16
    dkv_ref[...] = jnp.zeros_like(dkv_ref)
    diag_ref[...] = jnp.zeros_like(diag_ref)
    far_ref[...] = jnp.zeros_like(far_ref)
    extra_row = iota((LANES - size, height), 0)
    blank = jnp.zeros((size, height), F32)
    span_row = iota((spans, height), 0)
    for at in range(groups):
        span = 2 * (at ^ group) + place
        start = jnp.clip(span - 1, 0, spans - 3)
        queries = q_rows(own_refs[at], heads, height, size, head).astype(F32)
        grads = (grad_refs[at][...].astype(F32) * inverse_ref[0, at, 0:1]).astype(BF16)
        grads32 = grads.astype(F32)
        delta = jnp.sum(grads32 * exact_ref[0, at], axis=0, keepdims=True)
        high, middle, low = three_terms(-delta)
        extra = jnp.where(
            extra_row == 0,
            high,
            jnp.where(extra_row == 1, middle, jnp.where(extra_row == 2, low, 0.0)),
        )
        grads_extra = jnp.concatenate([extra.astype(BF16), grads], axis=0)
        sides = jnp.concatenate(
            [
                jnp.transpose(jnp.concatenate([queries, blank], axis=0)),
                jnp.transpose(jnp.concatenate([blank, grads32], axis=0)),
            ],
            axis=0,
        ).astype(BF16)
        near_total = jnp.zeros((tall, height), F32)
        far_total = jnp.zeros((tall, height), F32)
        for step in range(spans):
            near = step < 3
            key_span = (start + step) if near else ((start + step) & (spans - 1))
            rows = pl.ds(pl.multiple_of(key_span * height, height), height)
            weights = weight_ref[0, at, step]
            grad_probs = nn(vaug_ref[0, rows, :], grads_extra)
            grad_scores = (weights.astype(F32) * grad_probs).astype(BF16)
            if near:
                level = pl.ds(pl.multiple_of((key_span - span + 2) * height, height), height)
                diag_ref[0, level, :] = diag_ref[0, level, :] + grad_scores.astype(F32)
            both = jnp.concatenate([grad_scores, weights], axis=1)
            dkv_ref[rows, :] = dkv_ref[rows, :] + nn(both, sides)
            turned = nn(kt_ref[0, key_span], grad_scores)
            if near:
                near_total = near_total + turned
            else:
                far_total = far_total + turned
        dq_ref[0, at] = (near_total + far_total)[:size].astype(BF16)
        sums = far_total[size : size + spans]
        far_ref[0, 0] = far_ref[0, 0] + jnp.where(span_row < start, sums, 0.0)
        far_ref[0, 1] = far_ref[0, 1] + jnp.where(span_row >= start + 3, sums, 0.0)
    for at in range(groups):
        for target, parity in ((mine_ref, place), (other_ref, 1 - place)):
            first = pl.multiple_of((2 * (at ^ group) + parity) * height, height)
            target[0, at] = dkv_ref[pl.ds(first, height), :].astype(BF16)


def join_body(counts, *refs):
    calls = len(counts)
    mine_refs, got_refs, dq_refs = (refs[i * calls : (i + 1) * calls] for i in range(3))
    piece_refs = refs[3 * calls :]
    size, height = dq_refs[0].shape[2:]
    heads = sum(counts)
    width = heads * size
    for at, piece_ref in enumerate(piece_refs):
        head = 0
        for call_at, count in enumerate(counts):
            for inner in range(count):
                kept = mine_refs[call_at][inner, at].astype(F32)
                piece_ref[head * height : (head + 1) * height, :] = (
                    kept + got_refs[call_at][inner, at].astype(F32)
                ).astype(BF16)
                for half in range(height // LANES):
                    first = heads * height + half * width + head * size
                    piece_ref[first : first + size, :] = dq_refs[call_at][
                        inner, at, :, half * LANES : (half + 1) * LANES
                    ]
                head += 1


def slot_plan(capacity, features):
    base = capacity // 16 * 16
    left = capacity - base
    if base and left and 16 % left == 0 and (2 * features) % (LANES * (16 // left)) == 0:
        return base, left, 16 // left
    return -(-capacity // 8) * 8, 0, 0


def slot_marks(shape_of, axis, chosen, rank, capacity, plan):
    base, left, parts = plan
    position = iota(shape_of, axis)
    limit = base if left else capacity
    marks = [jnp.where(position == jnp.where(rank < limit, chosen * base + rank, -1), 1.0, 0.0)]
    spare = rank - base
    for part in range(parts):
        slot = chosen * 16 + part * left + spare
        slot = jnp.where((spare >= 0) & (spare < left), slot, -1)
        marks.append(jnp.where(position == slot, 1.0, 0.0))
    return [mark.astype(BF16) for mark in marks]


def route_body(
    groups,
    capacity,
    plan,
    place_ref,
    tokens_ref,
    w_out_ref,
    gain_ref,
    w_router_ref,
    route_col_ref,
    route_row_ref,
    cotangent_ref,
    *refs,
):
    pieces = refs[:groups]
    residual_ref, normed_ref, router_ref, sent_ref, attended_ref = refs[groups:]
    height, features = tokens_ref.shape
    experts = w_router_ref.shape[1]
    slots = sent_ref.shape[0]
    width = pieces[0].shape[0]
    group = place_ref[1]
    for at in range(groups):
        first = pl.multiple_of((at ^ group) * width, width)
        attended_ref[pl.ds(first, width), :] = pieces[at][...]
    residual = tokens_ref[...].astype(F32) + tn(attended_ref[...], w_out_ref[...])
    residual_ref[...] = residual
    inverse = lax.rsqrt(jnp.mean(residual * residual, axis=-1, keepdims=True) + EPSILON)
    normed = (residual * inverse * gain_ref[...].astype(F32)).astype(BF16)
    normed_ref[...] = normed
    logits = nn(normed, w_router_ref[...])
    powers = jnp.exp(logits - jnp.max(logits, axis=-1, keepdims=True))
    router = powers / jnp.sum(powers, axis=-1, keepdims=True)
    router_ref[...] = router
    onehot = iota((height, experts), 1) == route_col_ref[...]
    gate = jnp.sum(jnp.where(onehot, router, 0.0), axis=-1, keepdims=True)
    grad_expert = (gate * cotangent_ref[...].astype(F32)).astype(BF16)
    rows = jnp.concatenate([normed, grad_expert], axis=1)
    chosen = route_row_ref[...]
    marks = iota((experts, height), 0) == chosen
    earlier = (iota((height, height), 0) < iota((height, height), 1)).astype(BF16)
    before = nn(jnp.where(marks, 1.0, 0.0).astype(BF16), earlier)
    rank = jnp.sum(jnp.where(marks, before, 0.0), axis=0, keepdims=True).astype(jnp.int32)
    dispatch = slot_marks((slots, height), 0, chosen, rank, capacity, plan)
    sent_ref[:, : 2 * features] = nn(dispatch[0], rows).astype(BF16)
    if plan[1]:
        span = 2 * features // plan[2]
        spare = nn(dispatch[1], rows[:, :span])
        for part in range(1, plan[2]):
            spare = spare + nn(dispatch[1 + part], rows[:, part * span : (part + 1) * span])
        sent_ref[:, 2 * features :] = spare.astype(BF16)


def spare_marks(sources, plan):
    base, left, parts = plan
    target = iota((sources * left, sources * 16), 0)
    origin = iota((sources * left, sources * 16), 1)
    source = target // left
    return [
        (origin == source * 16 + part * left + (target - source * left)).astype(BF16)
        for part in range(parts)
    ]


def expert_body(
    plan,
    place_ref,
    got_ref,
    up_ref,
    down_ref,
    back_ref,
    rows_ref,
    act_other_ref,
    act_mine_ref,
    hid_other_ref,
    hid_mine_ref,
    total_ref,
):
    step, steps = pl.program_id(0), pl.num_programs(0)
    wide = rows_ref.shape[1]
    features = wide // 2
    main = got_ref.shape[0]
    left, parts = plan[1], plan[2]

    @pl.when(step == 0)
    def _():
        rows_ref[:main, :] = got_ref[:, :wide]
        if left:
            span = wide // parts
            packed = got_ref[:, wide:]
            for part, marks in enumerate(spare_marks(main // 16, plan)):
                rows_ref[main:, part * span : (part + 1) * span] = nn(marks, packed).astype(BF16)

    up, down = up_ref[...], down_ref[...]
    hidden = nn(rows_ref[:, :features], up)
    below = 0.5 * (1.0 + lax.erf(hidden * (2.0**-0.5)))
    bell = jnp.exp(-0.5 * hidden * hidden) * 0.3989422804014327
    active = (hidden * below).astype(BF16)
    grad_active = nt(rows_ref[:, features:], down)
    grad_hidden = (grad_active * (below + hidden * bell)).astype(BF16)

    @pl.when(step < steps // 2)
    def _():
        act_other_ref[...] = active
        hid_other_ref[...] = grad_hidden

    @pl.when(step >= steps // 2)
    def _():
        act_mine_ref[...] = active
        hid_mine_ref[...] = grad_hidden

    produced = nn(active, down)
    grad_back = nt(grad_hidden, up)

    @pl.when(step == 0)
    def _():
        total_ref[:, :features] = produced
        total_ref[:, features:] = grad_back

    @pl.when(step > 0)
    def _():
        total_ref[:, :features] = total_ref[:, :features] + produced
        total_ref[:, features:] = total_ref[:, features:] + grad_back

    @pl.when(step == steps - 1)
    def _():
        back_ref[:, :wide] = total_ref[:main, :].astype(BF16)
        if left:
            span = wide // parts
            packed = jnp.zeros((main, span), F32)
            for part, marks in enumerate(spare_marks(main // 16, plan)):
                spare = total_ref[main:, part * span : (part + 1) * span].astype(BF16)
                packed = packed + tn(marks, spare)
            back_ref[:, wide:] = packed.astype(BF16)


def run_expert(place_arg, got, up, down, plan):
    main, columns = got.shape
    features, hidden_size = up.shape
    chunk = CHUNK
    steps = hidden_size // chunk
    half = steps // 2
    slots = main + main // 16 * plan[1]

    def piece(step, place):
        return lax.rem(step + half * (1 - place[0]), steps)

    def fixed(dims):
        return pl.BlockSpec(dims, lambda i, p: (0, 0))

    first_half = pl.BlockSpec((slots, chunk), lambda i, p: (0, jnp.minimum(i, half - 1)))
    second_half = pl.BlockSpec((slots, chunk), lambda i, p: (0, jnp.maximum(i - half, 0)))
    return pl.pallas_call(
        functools.partial(expert_body, plan),
        out_shape=[shape((main, columns)), shape((slots, 2 * features))]
        + [shape((slots, hidden_size // 2))] * 4,
        grid_spec=pltpu.PrefetchScalarGridSpec(
            num_scalar_prefetch=1,
            grid=(steps,),
            in_specs=[
                fixed((main, columns)),
                pl.BlockSpec((features, chunk), lambda i, p: (0, piece(i, p))),
                pl.BlockSpec((chunk, features), lambda i, p: (piece(i, p), 0)),
            ],
            out_specs=[fixed((main, columns)), fixed((slots, 2 * features))]
            + [first_half, second_half] * 2,
            scratch_shapes=[pltpu.VMEM((slots, 2 * features), F32)],
        ),
        cost_estimate=pl.CostEstimate(
            flops=8 * slots * features * hidden_size,
            bytes_accessed=4 * features * hidden_size + 4 * slots * hidden_size,
            transcendentals=0,
        ),
        compiler_params=pltpu.CompilerParams(vmem_limit_bytes=VMEM_LIMIT),
    )(place_arg, got, up, down)


def combine_body(
    groups,
    capacity,
    plan,
    place_ref,
    got_ref,
    residual_ref,
    router_ref,
    route_col_ref,
    cotangent_ref,
    gain_ref,
    w_router_ref,
    w_out_ref,
    mixed_ref,
    grad_residual_ref,
    branch_ref,
    logits_ref,
    gain_out_ref,
    *refs,
):
    pieces, turned_ref = refs[:groups], refs[groups]
    height, experts = router_ref.shape
    features = residual_ref.shape[1]
    slots = got_ref.shape[0]
    width = pieces[0].shape[0]
    group = place_ref[1]
    chosen = route_col_ref[...]
    onehot = iota((height, experts), 1) == chosen
    earlier = (iota((height, height), 0) > iota((height, height), 1)).astype(BF16)
    before = nn(earlier, jnp.where(onehot, 1.0, 0.0).astype(BF16))
    rank = jnp.sum(jnp.where(onehot, before, 0.0), axis=1, keepdims=True).astype(jnp.int32)
    combine = slot_marks((height, slots), 1, chosen, rank, capacity, plan)
    back = nn(combine[0], got_ref[:, : 2 * features])
    if plan[1]:
        spare = got_ref[:, 2 * features :]
        back = back + jnp.concatenate([nn(marks, spare) for marks in combine[1:]], axis=1)
    router = router_ref[...]
    gate = jnp.sum(jnp.where(onehot, router, 0.0), axis=-1, keepdims=True)
    residual = residual_ref[...]
    inverse = lax.rsqrt(jnp.mean(residual * residual, axis=-1, keepdims=True) + EPSILON)
    unit = residual * inverse
    grad_mixed = cotangent_ref[...].astype(F32)
    gathered = back[:, :features]
    mixed_ref[...] = (residual + gate * gathered).astype(BF16)
    grad_gate = jnp.sum(grad_mixed * gathered, axis=-1, keepdims=True)
    grad_logits = (router * (jnp.where(onehot, grad_gate, 0.0) - gate * grad_gate)).astype(BF16)
    grad_normed = back[:, features:] + nt(grad_logits, w_router_ref[...])
    grad_unit = grad_normed * gain_ref[...].astype(F32)
    grad_residual = grad_mixed + inverse * (
        grad_unit - unit * jnp.mean(grad_unit * unit, axis=-1, keepdims=True)
    )
    branch = grad_residual.astype(BF16)
    turned_ref[...] = nt(w_out_ref[...], branch).astype(BF16)
    for at in range(groups):
        first = pl.multiple_of((at ^ group) * width, width)
        pieces[at][...] = turned_ref[pl.ds(first, width), :]
    grad_residual_ref[...] = grad_residual
    branch_ref[...] = branch
    spare_lanes = logits_ref.shape[1] - experts
    logits_ref[...] = jnp.concatenate([grad_logits, jnp.zeros((height, spare_lanes), BF16)], axis=1)
    sums = jnp.sum(grad_normed * unit, axis=0, keepdims=True)
    gain_out_ref[...] = jnp.broadcast_to(sums, gain_out_ref.shape)


def qkv_body(groups, heads, place_ref, *refs):
    normed_refs, piece_refs = refs[:groups], refs[groups : 2 * groups]
    mine_ref, other_ref, total_ref, rows_ref = refs[2 * groups :]
    height = normed_refs[0].shape[1]
    width = rows_ref.shape[1] // 3
    for at in range(groups):
        piece = piece_refs[at]
        for head in range(heads):
            rows_ref[:, head * LANES : (head + 1) * LANES] = piece[
                head * height : (head + 1) * height, :
            ]
        parts = [
            piece[heads * height + half * width : heads * height + (half + 1) * width, :]
            for half in range(height // LANES)
        ]
        turned = jnp.concatenate(parts, axis=1).astype(F32)
        rows_ref[:, 2 * width :] = jnp.transpose(turned).astype(BF16)
        product = nn(normed_refs[at][...], rows_ref[...])
        if at == 0:
            total_ref[...] = product
        else:
            total_ref[...] = total_ref[...] + product
    split_rows(place_ref[0], total_ref, mine_ref, other_ref)


def rows_body(groups, heads, landed_ref, w_ref, gain_ref, out_ref, gain_out_ref):
    sources, _, columns = landed_ref.shape
    width = columns // 3
    size = width // heads
    features = groups * width
    for group in range(groups):
        total = landed_ref[group].astype(F32)
        for expert in range(1, sources // groups):
            total = total + landed_ref[expert * groups + group].astype(F32)
        out_ref[:, group * width : (group + 1) * width] = total[:, 2 * width :]
        for head in range(heads):
            for part in range(2):
                source = head * 2 * size + part * size
                first = (part + 1) * features + group * width + head * size
                out_ref[:, first : first + size] = total[:, source : source + size]
    sums = jnp.sum(w_ref[...].astype(F32) * out_ref[...], axis=1, keepdims=True)
    gain_out_ref[...] = sums / gain_ref[...].astype(F32)


def finish_body(groups, heads, place_ref, tokens_ref, gain_ref, w_ref, residual_ref, *refs):
    piece_refs = refs[:groups]
    out_ref, turned_ref, k_all, v_all = refs[groups:]
    height, features = tokens_ref.shape
    width = features // groups
    size = width // heads
    group = place_ref[1]
    for at in range(groups):
        piece = piece_refs[at]
        first = pl.multiple_of((at ^ group) * width, width)
        for half in range(height // LANES):
            source = heads * height + half * width
            turned_ref[pl.ds(first, width), half * LANES : (half + 1) * LANES] = piece[
                source : source + width, :
            ].astype(F32)
        for head in range(heads):
            both = piece[head * height : (head + 1) * height, :]
            lanes = slice(head * size, (head + 1) * size)
            k_all[at ^ group, :, lanes] = both[:, :size]
            v_all[at ^ group, :, lanes] = both[:, size:]
    grad_normed = nt(jnp.transpose(turned_ref[...]).astype(BF16), w_ref[:, :features])
    for part, source in ((1, k_all), (2, v_all)):
        joined = jnp.concatenate([source[at] for at in range(groups)], axis=1)
        grad_normed = grad_normed + nt(joined, w_ref[:, part * features : (part + 1) * features])
    tokens = tokens_ref[...].astype(F32)
    inverse = lax.rsqrt(jnp.mean(tokens * tokens, axis=-1, keepdims=True) + EPSILON)
    unit = tokens * inverse
    grad_unit = grad_normed * gain_ref[...].astype(F32)
    grad = inverse * (grad_unit - unit * jnp.mean(grad_unit * unit, axis=-1, keepdims=True))
    out_ref[...] = (residual_ref[...] + grad).astype(BF16)


def strip_body(table_ref, strips_ref):
    heads, rows, height = strips_ref.shape
    used = rows - height
    offset = iota((used, LANES), 0) - 2 * height
    onehot = (bucket_of(offset) == iota((used, LANES), 1)).astype(BF16)
    lane = iota((used, height), 1)
    blank = jnp.zeros((height, height), F32)
    for head in range(heads):
        values = nn(onehot, table_ref[head])
        moved = 1
        while moved < height:
            values = jnp.where((lane & moved) != 0, pltpu.roll(values, moved, 0), values)
            moved *= 2
        strips_ref[head, :height] = blank
        strips_ref[head, height:used] = values[height:]
        strips_ref[head, used:] = blank


def diagonal_body(counts, *refs):
    calls = len(counts)
    out_ref = refs[2 * calls]
    places = [(call_at, inner) for call_at in range(calls) for inner in range(counts[call_at])]
    rows, height = refs[0].shape[1:]
    total_rows = rows + 2 * height
    lane = iota((total_rows, height), 1)
    offset = iota((total_rows, LANES), 0) - 3 * height
    table = (bucket_of(offset) == iota((total_rows, LANES), 1)).astype(F32)
    lane_out = iota((1, LANES), 1)
    blank = jnp.zeros((height, height), F32)
    for head, (call_at, inner) in enumerate(places):
        diag_ref, far_ref = refs[call_at].at[inner], refs[calls + call_at].at[inner]
        values = jnp.concatenate([blank, diag_ref[...], blank], axis=0)
        moved = 1
        while moved < height:
            values = jnp.where(
                (lane & moved) != 0, pltpu.roll(values, total_rows - moved, 0), values
            )
            moved *= 2
        sums = jnp.sum(values, axis=1, keepdims=True)
        by_bucket = jnp.sum(sums * table, axis=0, keepdims=True)
        by_bucket = by_bucket + jnp.where(lane_out == FAR_LEFT, jnp.sum(far_ref[0]), 0.0)
        out_ref[head] = by_bucket + jnp.where(lane_out == FAR_RIGHT, jnp.sum(far_ref[1]), 0.0)


def split_rows(place, source_ref, mine_ref, other_ref):
    experts_all, pieces, columns = mine_ref.shape
    for parity in range(2):

        @pl.when(place == parity)
        def _():
            for at in range(experts_all):
                for target, which in ((mine_ref, parity), (other_ref, 1 - parity)):
                    first = (2 * at + which) * pieces
                    target[at] = source_ref[first : first + pieces, :].astype(BF16)


def weights_body(
    experts,
    place_ref,
    branch_ref,
    attended_ref,
    normed_ref,
    logits_ref,
    gain_ref,
    mine_ref,
    other_ref,
    packed_ref,
):
    features = branch_ref.shape[1]
    extra = logits_ref.shape[1]
    branch = jnp.transpose(branch_ref[...].astype(F32)).astype(BF16)
    packed_ref[:, :features] = nt(branch, attended_ref[...])
    normed = jnp.transpose(normed_ref[...].astype(F32)).astype(BF16)
    column = jnp.transpose(gain_ref[...])[:, :1]
    packed_ref[:, features:] = nn(normed, logits_ref[...]) + jnp.where(
        iota((features, extra), 1) == experts, column, 0.0
    )
    split_rows(place_ref[0], packed_ref, mine_ref, other_ref)


def exchange(moving, axis):
    return lax.all_to_all(moving, axis, split_axis=0, concat_axis=0, tiled=True)


def cross(moving, axis, distance):
    size = lax.axis_size(axis)
    return lax.ppermute(moving, axis, [(i, i ^ distance) for i in range(size)])


def trade(pieces):
    return [
        piece if at == 0 else cross(piece, "context", at) for at, piece in enumerate(pieces)
    ]


def after(values, *others):
    return lax.optimization_barrier((values,) + others)[0]


def per_device(
    tokens_in,
    gain_attn,
    w_qkv,
    rel_bias,
    w_out,
    gain_ffn,
    w_router,
    w_up,
    w_down,
    segments,
    routes,
    cotangent,
):
    groups = lax.axis_size("context")
    tensor_size = lax.axis_size("tensor")
    expert_size = lax.axis_size("expert")
    height, features = tokens_in.shape
    heads = rel_bias.shape[0]
    width = features // groups
    size = width // heads
    length = segments.shape[1]
    spans = length // height
    experts_all = expert_size * groups
    capacity = max(2, 5 * height // (4 * experts_all))
    plan = slot_plan(capacity, features)
    slots = experts_all * plan[0]
    columns = 2 * features + (2 * features // plan[2] if plan[1] else 0)
    piece_rows = heads * height + height // LANES * width
    place = lax.axis_index("tensor")
    context_at = lax.axis_index("context")
    place_arg = jnp.stack([place, context_at]).astype(jnp.int32)
    gain_row = gain_attn.reshape(1, features)
    square = features * features

    projected = run(
        functools.partial(project_body, heads),
        [shape((piece_rows, LANES))] * groups + [shape((features, height))],
        (place_arg, tokens_in, gain_row, w_qkv),
        scratch=[pltpu.VMEM((groups, piece_rows, LANES), BF16)],
        smem=(0,),
        flops=6 * height * square,
        moved=8 * square,
    )
    own = trade(projected[:groups])
    far = [cross(piece, "tensor", 1) for piece in own]
    table = jnp.pad(rel_bias, ((0, 0), (0, LANES - rel_bias.shape[1])))
    table = jnp.broadcast_to(table[:, :, None], (heads, LANES, height))
    strips = run(
        strip_body,
        shape((heads, 5 * height, height), F32),
        (table,),
        flops=heads * 2 * 4 * height * LANES * height,
        moved=heads * 4 * 5 * height * height,
    )
    head_flops = 4 * groups * height * length * size

    def fixed(dims):
        return pl.BlockSpec(dims, lambda h, n=len(dims): (0,) * n)

    def by_head(dims, first=0):
        return pl.BlockSpec(
            (1,) + dims, lambda h, n=len(dims), f=first: (h + f,) + (0,) * n
        )

    def head_rows(first=0):
        return pl.BlockSpec((size, height), lambda h, f=first: (h + f, 0))

    smem = pl.BlockSpec(memory_space=pltpu.SMEM)
    held_dims = [
        (groups, size, height),
        (groups, 8, height),
        (length, LANES),
        (spans, size + 16, height),
        (groups, spans, height, height),
    ]
    held_kinds = [F32, F32, BF16, BF16, BF16]
    outs = pl.pallas_call(
        functools.partial(forward_body, groups, heads),
        out_shape=[shape((width, height))] * groups
        + [shape((heads,) + dims, kind) for dims, kind in zip(held_dims, held_kinds)],
        grid=(heads,),
        in_specs=[smem, smem, fixed((1, length)), by_head((5 * height, height))]
        + [fixed((piece_rows, LANES))] * (2 * groups),
        out_specs=[head_rows()] * groups + [by_head(dims) for dims in held_dims],
        scratch_shapes=[
            pltpu.VMEM((length, LANES), BF16),
            pltpu.VMEM((spans, height), jnp.int32),
            pltpu.VMEM((length, LANES), BF16),
            pltpu.VMEM((spans, size + 16, height), BF16),
            pltpu.VMEM((2, spans, height, height), F32),
        ],
        cost_estimate=pl.CostEstimate(
            flops=6 * heads * head_flops, bytes_accessed=20 * square, transcendentals=0
        ),
        compiler_params=pltpu.CompilerParams(vmem_limit_bytes=VMEM_LIMIT),
    )(place_arg, rel_bias.astype(F32), segments, strips, *own, *far)
    attended = trade(outs[:groups])
    exact, inverse, vaug, kt, weights = outs[groups:]
    normed_all = trade([after(projected[groups], *own)] * groups)
    residual, normed_ffn, router, sent, attended_t = run(
        functools.partial(route_body, groups, capacity, plan),
        [
            shape((height, features), F32),
            shape((height, features)),
            shape((height, experts_all), F32),
            shape((slots, columns)),
            shape((features, height)),
        ],
        (
            after(place_arg, *normed_all),
            tokens_in,
            w_out,
            gain_ffn.reshape(1, features),
            w_router,
            routes,
            routes.reshape(1, height),
            cotangent,
            *attended,
        ),
        smem=(0,),
        flops=2 * height * square,
        moved=4 * square,
    )

    def move_slots(moving):
        return exchange(
            moving.reshape(experts_all, plan[0], columns), ("expert", "context")
        ).reshape(slots, columns)

    got = move_slots(sent)
    back, rows_in, act_other, act_mine, hid_other, hid_mine = run_expert(
        place_arg, got, w_up[0], w_down[0], plan
    )
    returned = move_slots(back)

    def both(values, sent_values):
        return jnp.concatenate([values, cross(sent_values, "tensor", 1)], axis=0)

    all_rows = both(rows_in, rows_in)
    grad_down = tn(both(act_mine, act_other), all_rows[:, features:])
    grad_up = tn(all_rows[:, :features], both(hid_mine, hid_other))
    extra = -(-(experts_all + 1) // LANES) * LANES
    outs = run(
        functools.partial(combine_body, groups, capacity, plan),
        [
            shape((height, features)),
            shape((height, features), F32),
            shape((height, features)),
            shape((height, extra)),
            shape((8, features), F32),
        ]
        + [shape((width, height))] * groups,
        (
            after(place_arg, grad_down, grad_up),
            returned,
            residual,
            router,
            routes,
            cotangent,
            gain_ffn.reshape(1, features),
            w_router,
            w_out,
        ),
        scratch=[pltpu.VMEM((features, height), BF16)],
        smem=(0,),
        flops=4 * height * square,
        moved=8 * square,
    )
    mixed_out, grad_residual, branch, grad_logits, gain_sums = outs[:5]
    grad_pieces = trade(outs[5:])
    pieces = features // (experts_all * tensor_size)
    mine, other = run(
        functools.partial(weights_body, experts_all),
        [shape((experts_all, pieces, features + extra))] * 2,
        (place_arg, branch, attended_t, normed_ffn, grad_logits, gain_sums),
        scratch=[pltpu.VMEM((features, features + extra), F32)],
        smem=(0,),
        flops=2 * height * square,
        moved=8 * square,
    )

    def pair_sum(kept, received):
        return (kept.astype(F32) + received.astype(F32)).astype(BF16)

    packed = pair_sum(mine, cross(other, "tensor", 1))
    packed_landed = exchange(packed, ("expert", "context"))
    counts = (1, heads - 1)
    mine_kv, got_kv, q_grads, diags, fars = [], [], [], [], []
    for call_at, gate in enumerate((other, packed)):
        first, count = sum(counts[:call_at]), counts[call_at]
        dims = [
            (groups, size, height),
            (groups, height, 2 * size),
            (groups, height, 2 * size),
            (5 * height, height),
            (2, spans, height),
        ]
        outs = pl.pallas_call(
            functools.partial(backward_body, groups, heads, first),
            out_shape=[
                shape((count,) + of, kind)
                for of, kind in zip(dims, [BF16, BF16, BF16, F32, F32])
            ],
            grid=(count,),
            in_specs=[smem]
            + [
                by_head(of, first)
                for of in (held_dims[4], held_dims[2], held_dims[3], held_dims[0], held_dims[1])
            ]
            + [fixed((piece_rows, LANES))] * groups
            + [head_rows(first)] * groups,
            out_specs=[by_head(of) for of in dims],
            scratch_shapes=[pltpu.VMEM((length, LANES), F32)],
            cost_estimate=pl.CostEstimate(
                flops=8 * count * head_flops, bytes_accessed=20 * square, transcendentals=0
            ),
            compiler_params=pltpu.CompilerParams(vmem_limit_bytes=VMEM_LIMIT),
        )(after(place_arg, gate), weights, vaug, kt, exact, inverse, *own, *grad_pieces)
        q_grads.append(outs[0])
        mine_kv.append(outs[1])
        got_kv.append(cross(outs[2], "tensor", 1))
        diags.append(outs[3])
        fars.append(outs[4])
    joined = run(
        functools.partial(join_body, counts),
        [shape((piece_rows, LANES))] * groups,
        (*mine_kv, after(got_kv[0], packed_landed), *got_kv[1:], *q_grads),
        moved=4 * groups * piece_rows * LANES,
    )
    landed_pieces = trade(joined)
    mine, other = run(
        functools.partial(qkv_body, groups, heads),
        [shape((experts_all, pieces, 3 * width))] * 2,
        (place_arg, *normed_all, *joined),
        scratch=[pltpu.VMEM((features, 3 * width), F32), pltpu.VMEM((height, 3 * width), BF16)],
        smem=(0,),
        flops=6 * groups * height * features * width,
        moved=8 * square,
    )
    landed = exchange(pair_sum(mine, cross(other, "tensor", 1)), ("expert", "context"))
    first_piece = (
        (lax.axis_index("expert") * groups + context_at) * tensor_size + place
    ) * pieces
    own_w = lax.dynamic_slice_in_dim(w_qkv, first_piece, pieces, 0)
    own_gain = lax.dynamic_slice_in_dim(gain_attn, first_piece, pieces, 0).reshape(pieces, 1)
    grad_qkv, grad_gain_attn = run(
        functools.partial(rows_body, groups, heads),
        [shape((pieces, 3 * features), F32), shape((pieces, 1), F32)],
        (landed, own_w, own_gain),
        moved=2 * landed.size,
    )
    grad_tokens = run(
        functools.partial(finish_body, groups, heads),
        shape((height, features)),
        (place_arg, tokens_in, gain_row, w_qkv, grad_residual, *landed_pieces),
        scratch=[
            pltpu.VMEM((features, height), F32),
            pltpu.VMEM((groups, height, width), BF16),
            pltpu.VMEM((groups, height, width), BF16),
        ],
        smem=(0,),
        flops=6 * height * square,
        moved=8 * square,
    )
    by_bucket = run(
        functools.partial(diagonal_body, counts),
        shape((heads, 1, LANES), F32),
        (*diags, *fars),
        flops=heads * 8 * 7 * height * height,
        moved=heads * 20 * height * height,
    )
    by_bucket = by_bucket + cross(by_bucket, "tensor", 1)
    distance = 1
    while distance < expert_size:
        by_bucket = by_bucket + cross(by_bucket, "expert", distance)
        distance *= 2
    reduced = jnp.sum(packed_landed.astype(F32), axis=0)
    return (
        mixed_out,
        grad_tokens,
        grad_gain_attn[:, 0],
        grad_qkv,
        by_bucket[:, 0, : rel_bias.shape[1]],
        reduced[:, :features].T,
        reduced[:, features + experts_all],
        reduced[:, features : features + experts_all],
        grad_up[None],
        grad_down[None],
    )


def solution(mesh):
    rows = ("expert", "context", "tensor")
    in_specs = (
        P(rows, None),
        P(),
        P(),
        P("context", None),
        P(),
        P(),
        P(),
        P(("expert", "context"), None, None),
        P(("expert", "context"), None, None),
        P("expert", None),
        P(rows, None),
        P(rows, None),
    )
    out_specs = (
        P(rows, None),
        P(rows, None),
        P(rows),
        P(rows, None),
        P("context", None),
        P(None, rows),
        P(rows),
        P(rows, None),
        P(("expert", "context"), None, "tensor"),
        P(("expert", "context"), "tensor", None),
    )
    return jax.shard_map(
        per_device, mesh=mesh, in_specs=in_specs, out_specs=out_specs, check_vma=False
    )
```

```python
import functools

import jax
import jax.numpy as jnp
from jax import lax
from jax.experimental import pallas as pl
from jax.experimental.pallas import tpu as pltpu
from jax.sharding import PartitionSpec as P

EPSILON = 1e-06
THRESHOLDS = (12, 16, 23, 32, 46, 64, 91)
FAR_LEFT = 15
FAR_RIGHT = 31
EXCLUDED = -1e30
LANES = 128
BF16 = jnp.bfloat16
F32 = jnp.float32
VMEM_LIMIT = 56 * 1024 * 1024
CHUNK = 768
PART = 256


def bucket_of(offset):
    distance = jnp.abs(offset)
    beyond = jnp.zeros_like(distance)
    for threshold in THRESHOLDS:
        beyond = beyond + (distance >= threshold).astype(jnp.int32)
    nearby = jnp.where(distance < 8, distance, 8 + beyond)
    return nearby + 16 * (offset > 0).astype(jnp.int32)


def nn(left, right):
    return lax.dot_general(left, right, (((1,), (0,)), ((), ())), preferred_element_type=F32)


def nt(left, right):
    return lax.dot_general(left, right, (((1,), (1,)), ((), ())), preferred_element_type=F32)


def tn(left, right):
    return lax.dot_general(left, right, (((0,), (0,)), ((), ())), preferred_element_type=F32)


def iota(shape, axis):
    return lax.broadcasted_iota(jnp.int32, shape, axis)


def three_terms(values):
    high = values.astype(BF16).astype(F32)
    middle = (values - high).astype(BF16).astype(F32)
    return high, middle, values - high - middle


def specs_for(count, smem=()):
    return [
        pl.BlockSpec(memory_space=pltpu.SMEM if i in smem else pltpu.VMEM) for i in range(count)
    ]


def run(body, out_shape, args, scratch=(), smem=(), flops=0, moved=0, limit=VMEM_LIMIT):
    return pl.pallas_call(
        body,
        out_shape=out_shape,
        in_specs=specs_for(len(args), smem),
        scratch_shapes=list(scratch),
        cost_estimate=pl.CostEstimate(flops=flops, bytes_accessed=moved, transcendentals=0),
        compiler_params=pltpu.CompilerParams(vmem_limit_bytes=limit),
    )(*args)


def shape(dims, kind=BF16):
    return jax.ShapeDtypeStruct(dims, kind)


def project_body(heads, place_ref, tokens_ref, gain_ref, w_ref, *refs):
    groups = len(refs) - 2
    piece_refs, normed_ref, all_ref = refs[:groups], refs[groups], refs[groups + 1]
    height, features = tokens_ref.shape
    width = features // groups
    size = width // heads
    group = place_ref[1]
    tokens = tokens_ref[...].astype(F32)
    inverse = lax.rsqrt(jnp.mean(tokens * tokens, axis=-1, keepdims=True) + EPSILON)
    normed = (tokens * inverse * gain_ref[...].astype(F32)[None, :]).astype(BF16)
    normed_ref[...] = jnp.transpose(normed.astype(F32)).astype(BF16)
    turned = jnp.transpose(nn(normed, w_ref[:, :features])).astype(BF16)
    keys = nn(normed, w_ref[:, features : 2 * features]).astype(BF16)
    values = nn(normed, w_ref[:, 2 * features :]).astype(BF16)
    for at in range(groups):
        for head in range(heads):
            lanes = slice(at * width + head * size, at * width + (head + 1) * size)
            all_ref[at ^ group, head * height : (head + 1) * height, :] = jnp.concatenate(
                [keys[:, lanes], values[:, lanes]], axis=1
            )
        for half in range(height // LANES):
            first = heads * height + half * width
            all_ref[at ^ group, first : first + width, :] = turned[
                at * width : (at + 1) * width, half * LANES : (half + 1) * LANES
            ]
    for at in range(groups):
        piece_refs[at][...] = all_ref[at]


def q_rows(piece_ref, heads, height, size, head):
    width = heads * size
    parts = []
    for half in range(height // LANES):
        first = heads * height + half * width + head * size
        parts.append(piece_ref[pl.ds(pl.multiple_of(first, 16), size), :])
    return jnp.concatenate(parts, axis=1)


def forward_body(groups, heads, place_ref, bias_ref, seg_ref, strip_ref, *refs):
    own_refs, far_refs, out_refs = (refs[i * groups : (i + 1) * groups] for i in range(3))
    exact_ref, inverse_ref, vaug_ref, kt_ref, weight_ref = refs[3 * groups : 3 * groups + 5]
    extra_all, docs_all, kaug_ref, vt_ref, *score_refs = refs[3 * groups + 5 :]
    size, height = out_refs[0].shape
    spans = kaug_ref.shape[0] // height
    place, group = place_ref[0], place_ref[1]
    head = pl.program_id(0)
    tall = size + 16
    rest = LANES - size

    @pl.when(head == 0)
    def _():
        row = iota((LANES, height), 0) - size
        for span in range(spans):
            docs = seg_ref[0:1, span * height : (span + 1) * height]
            docs_all[span : span + 1, :] = docs
            extra = jnp.where((row >= 0) & (row < 3) & (docs != row), EXCLUDED, 0.0)
            extra = jnp.where(row - 3 == span, 1.0, extra)
            extra_all[span * height : (span + 1) * height, :] = jnp.transpose(extra).astype(BF16)

    row, column = iota((tall, LANES), 0), iota((tall, LANES), 1)
    pick_v = (((row < size) & (row + size == column)) | ((row == size) & (column == 0))).astype(
        BF16
    )
    pick_k = (
        ((row < size) & (row == column))
        | ((row >= size) & (row < size + spans) & (row + 3 == column))
    ).astype(BF16)
    lane = iota((height, LANES), 1)
    low_half = lane < size
    ones = jnp.where(lane < 3, 1.0, 0.0).astype(BF16)
    extra_row = iota((rest, height), 0)
    queries_all = []
    for at in range(groups):
        block = at ^ group
        for source, parity in ((own_refs[at], place), (far_refs[at], 1 - place)):
            span = 2 * block + parity
            rows = pl.ds(pl.multiple_of(span * height, height), height)
            both = source[pl.ds(pl.multiple_of(head * height, height), height), :]
            keys = jnp.where(low_half, both, extra_all[rows, :])
            values = jnp.where(low_half, ones, both)
            kaug_ref[rows, :] = keys
            vaug_ref[0, rows, :] = values
            vt_ref[:, rows] = nt(pick_v, values).astype(BF16)
            kt_ref[0, :, rows] = nt(pick_k, keys).astype(BF16)
        span = 2 * block + place
        docs = docs_all[pl.ds(span, 1), :]
        apart = extra_row - 3 - span
        far = jnp.where(
            apart <= -2,
            bias_ref[head, FAR_LEFT],
            jnp.where(apart >= 2, bias_ref[head, FAR_RIGHT], 0.0),
        )
        extra = jnp.where(
            extra_row < 3,
            jnp.where(docs == extra_row, 1.0, 0.0),
            jnp.where(extra_row < 3 + spans, far, 0.0),
        )
        queries_all.append(
            jnp.concatenate(
                [q_rows(own_refs[at], heads, height, size, head), extra.astype(BF16)], axis=0
            )
        )
    for at in range(groups):
        span = 2 * (at ^ group) + place
        start = jnp.clip(span - 1, 0, spans - 3)
        score_ref = score_refs[at % 2]
        score_ref[...] = nn(kaug_ref[...], queries_all[at])
        rows = pl.ds(pl.multiple_of(start * height, height), 3 * height)
        level = pl.ds(pl.multiple_of((start - span + 2) * height, height), 3 * height)
        score_ref[rows, :] = score_ref[rows, :] + strip_ref[0, level, :]
        row_max = jnp.max(score_ref[...], axis=0, keepdims=True)
        for key in range(spans):
            weight_ref[0, at, key] = jnp.exp(
                score_ref[key * height : (key + 1) * height, :] - row_max
            ).astype(BF16)
        total = nn(vt_ref[...], weight_ref[0, at].reshape(spans * height, height))
        inverse = 1.0 / total[size : size + 1]
        result = total[:size] * inverse
        out_refs[at][...] = result.astype(BF16)
        exact_ref[0, at] = result
        inverse_ref[0, at] = jnp.broadcast_to(inverse, (8, height))


def turn_body(groups, heads, *refs):
    piece_refs, out_ref = refs[:groups], refs[groups]
    height = out_ref.shape[2]
    size = out_ref.shape[3] // 2
    blank = jnp.zeros((size, height), F32)
    for at in range(groups):
        for head in range(heads):
            queries = q_rows(piece_refs[at], heads, height, size, head).astype(F32)
            out_ref[head, at] = jnp.transpose(jnp.concatenate([queries, blank], axis=0)).astype(
                BF16
            )


def backward_body(groups, place_ref, *refs):
    weight_ref, vaug_ref, kt_ref, exact_ref, inverse_ref, q_ref = refs[:6]
    grad_refs = refs[6 : 6 + groups]
    dq_ref, mine_ref, other_ref, diag_ref, far_ref, dkv_ref = refs[6 + groups : 12 + groups]
    slope_refs, score_refs = refs[12 + groups : 14 + groups], refs[14 + groups :]
    size, height = grad_refs[0].shape
    length = vaug_ref.shape[1]
    spans = length // height
    place, group = place_ref[0], place_ref[1]
    diag_ref[...] = jnp.zeros_like(diag_ref)
    extra_row = iota((LANES - size, height), 0)
    blank = jnp.zeros((size, height), F32)
    span_row = iota((spans, height), 0)
    left_total = jnp.zeros((spans, height), F32)
    right_total = jnp.zeros((spans, height), F32)
    for at in range(groups):
        span = 2 * (at ^ group) + place
        start = jnp.clip(span - 1, 0, spans - 3)
        slope_ref, score_ref = slope_refs[at % 2], score_refs[at % 2]
        grads = (grad_refs[at][...].astype(F32) * inverse_ref[0, at, 0:1]).astype(BF16)
        grads32 = grads.astype(F32)
        delta = jnp.sum(grads32 * exact_ref[0, at], axis=0, keepdims=True)
        high, middle, low = three_terms(-delta)
        extra = jnp.where(
            extra_row == 0,
            high,
            jnp.where(extra_row == 1, middle, jnp.where(extra_row == 2, low, 0.0)),
        )
        slope_ref[...] = nn(
            vaug_ref[0], jnp.concatenate([extra.astype(BF16), grads], axis=0)
        )
        turned = jnp.transpose(jnp.concatenate([blank, grads32], axis=0)).astype(BF16)
        sides = jnp.concatenate([q_ref[0, at], turned], axis=0)
        for key in range(spans):
            rows = slice(key * height, (key + 1) * height)
            score_ref[rows, :] = (
                weight_ref[0, at, key].astype(F32) * slope_ref[rows, :]
            ).astype(BF16)
        both = jnp.concatenate(
            [score_ref[...], weight_ref[0, at].reshape(length, height)], axis=1
        )
        product = nn(both, sides)
        if at == 0:
            dkv_ref[...] = product
        else:
            dkv_ref[...] = dkv_ref[...] + product
        total = nn(kt_ref[0], score_ref[...])
        dq_ref[0, at] = total[:size].astype(BF16)
        sums = total[size : size + spans]
        left_total = left_total + jnp.where(span_row < start, sums, 0.0)
        right_total = right_total + jnp.where(span_row >= start + 3, sums, 0.0)
        rows = pl.ds(pl.multiple_of(start * height, height), 3 * height)
        level = pl.ds(pl.multiple_of((start - span + 2) * height, height), 3 * height)
        diag_ref[0, level, :] = diag_ref[0, level, :] + score_ref[rows, :].astype(F32)
    far_ref[0, 0] = left_total
    far_ref[0, 1] = right_total
    for at in range(groups):
        for target, parity in ((mine_ref, place), (other_ref, 1 - place)):
            first = pl.multiple_of((2 * (at ^ group) + parity) * height, height)
            target[0, at] = dkv_ref[pl.ds(first, height), :].astype(BF16)


def join_body(counts, *refs):
    calls = len(counts)
    mine_refs, got_refs, dq_refs = (refs[i * calls : (i + 1) * calls] for i in range(3))
    piece_refs = refs[3 * calls :]
    size, height = dq_refs[0].shape[2:]
    heads = sum(counts)
    width = heads * size
    for at, piece_ref in enumerate(piece_refs):
        head = 0
        for call_at, count in enumerate(counts):
            for inner in range(count):
                kept = mine_refs[call_at][inner, at].astype(F32)
                piece_ref[head * height : (head + 1) * height, :] = (
                    kept + got_refs[call_at][inner, at].astype(F32)
                ).astype(BF16)
                for half in range(height // LANES):
                    first = heads * height + half * width + head * size
                    piece_ref[first : first + size, :] = dq_refs[call_at][
                        inner, at, :, half * LANES : (half + 1) * LANES
                    ]
                head += 1


def slot_plan(capacity, features):
    base = capacity // 16 * 16
    left = capacity - base
    if base and left and 16 % left == 0 and (2 * features) % (LANES * (16 // left)) == 0:
        return base, left, 16 // left
    return -(-capacity // 8) * 8, 0, 0


def slot_marks(shape_of, axis, chosen, rank, capacity, plan):
    base, left, parts = plan
    position = iota(shape_of, axis)
    limit = base if left else capacity
    marks = [jnp.where(position == jnp.where(rank < limit, chosen * base + rank, -1), 1.0, 0.0)]
    spare = rank - base
    for part in range(parts):
        slot = chosen * 16 + part * left + spare
        slot = jnp.where((spare >= 0) & (spare < left), slot, -1)
        marks.append(jnp.where(position == slot, 1.0, 0.0))
    return [mark.astype(BF16) for mark in marks]


def route_body(
    groups,
    capacity,
    plan,
    place_ref,
    tokens_ref,
    w_out_ref,
    gain_ref,
    w_router_ref,
    route_row_ref,
    cotangent_ref,
    *refs,
):
    pieces = refs[:groups]
    residual_ref, normed_ref, router_ref, sent_ref, attended_ref = refs[groups:]
    height, features = tokens_ref.shape
    experts = w_router_ref.shape[0]
    slots = sent_ref.shape[0]
    width = pieces[0].shape[0]
    group = place_ref[1]
    for at in range(groups):
        first = pl.multiple_of((at ^ group) * width, width)
        attended_ref[pl.ds(first, width), :] = pieces[at][...]
    residual = tokens_ref[...].astype(F32) + tn(attended_ref[...], w_out_ref[...])
    residual_ref[...] = residual
    inverse = lax.rsqrt(jnp.mean(residual * residual, axis=-1, keepdims=True) + EPSILON)
    normed = (residual * inverse * gain_ref[...].astype(F32)[None, :]).astype(BF16)
    normed_ref[...] = normed
    logits = nt(normed, w_router_ref[...])
    powers = jnp.exp(logits - jnp.max(logits, axis=-1, keepdims=True))
    router = powers / jnp.sum(powers, axis=-1, keepdims=True)
    router_ref[...] = router
    chosen = route_row_ref[...]
    marks = iota((experts, height), 0) == chosen
    onehot = jnp.transpose(jnp.where(marks, 1.0, 0.0))
    gate = jnp.sum(onehot * router, axis=-1, keepdims=True)
    grad_expert = (gate * cotangent_ref[...].astype(F32)).astype(BF16)
    rows = jnp.concatenate([normed, grad_expert], axis=1)
    earlier = (iota((height, height), 0) < iota((height, height), 1)).astype(BF16)
    before = nn(jnp.where(marks, 1.0, 0.0).astype(BF16), earlier)
    rank = jnp.sum(jnp.where(marks, before, 0.0), axis=0, keepdims=True).astype(jnp.int32)
    dispatch = slot_marks((slots, height), 0, chosen, rank, capacity, plan)
    sent_ref[:, : 2 * features] = nn(dispatch[0], rows).astype(BF16)
    if plan[1]:
        span = 2 * features // plan[2]
        spare = nn(dispatch[1], rows[:, :span])
        for part in range(1, plan[2]):
            spare = spare + nn(dispatch[1 + part], rows[:, part * span : (part + 1) * span])
        sent_ref[:, 2 * features :] = spare.astype(BF16)


def spare_marks(sources, plan):
    base, left, parts = plan
    target = iota((sources * left, sources * 16), 0)
    origin = iota((sources * left, sources * 16), 1)
    source = target // left
    return [
        (origin == source * 16 + part * left + (target - source * left)).astype(BF16)
        for part in range(parts)
    ]


def expert_body(
    plan,
    place_ref,
    got_ref,
    up_ref,
    down_ref,
    back_ref,
    rows_ref,
    act_other_ref,
    act_mine_ref,
    hid_other_ref,
    hid_mine_ref,
    total_ref,
    active_ref,
    hidden_ref,
):
    step, steps = pl.program_id(0), pl.num_programs(0)
    wide = rows_ref.shape[1]
    features = wide // 2
    main = got_ref.shape[0]
    left, parts = plan[1], plan[2]

    @pl.when(step == 0)
    def _():
        rows_ref[:main, :] = got_ref[:, :wide]
        if left:
            span = wide // parts
            packed = got_ref[:, wide:]
            for part, marks in enumerate(spare_marks(main // 16, plan)):
                rows_ref[main:, part * span : (part + 1) * span] = nn(marks, packed).astype(BF16)

    chunk = up_ref.shape[1]
    for first in range(0, chunk, PART):
        lanes = slice(first, first + PART)
        hidden = nn(rows_ref[:, :features], up_ref[:, lanes])
        below = 0.5 * (1.0 + lax.erf(hidden * (2.0**-0.5)))
        bell = jnp.exp(-0.5 * hidden * hidden) * 0.3989422804014327
        active_ref[:, lanes] = (hidden * below).astype(BF16)
        grad_active = nt(rows_ref[:, features:], down_ref[lanes, :])
        hidden_ref[:, lanes] = (grad_active * (below + hidden * bell)).astype(BF16)
    produced = nn(active_ref[...], down_ref[...])
    grad_back = nt(hidden_ref[...], up_ref[...])

    @pl.when(step < steps // 2)
    def _():
        act_other_ref[...] = active_ref[...]
        hid_other_ref[...] = hidden_ref[...]

    @pl.when(step >= steps // 2)
    def _():
        act_mine_ref[...] = active_ref[...]
        hid_mine_ref[...] = hidden_ref[...]

    @pl.when(step == 0)
    def _():
        total_ref[:, :features] = produced
        total_ref[:, features:] = grad_back

    @pl.when(step > 0)
    def _():
        total_ref[:, :features] = total_ref[:, :features] + produced
        total_ref[:, features:] = total_ref[:, features:] + grad_back

    @pl.when(step == steps - 1)
    def _():
        back_ref[:, :wide] = total_ref[:main, :].astype(BF16)
        if left:
            span = wide // parts
            packed = jnp.zeros((main, span), F32)
            for part, marks in enumerate(spare_marks(main // 16, plan)):
                spare = total_ref[main:, part * span : (part + 1) * span].astype(BF16)
                packed = packed + tn(marks, spare)
            back_ref[:, wide:] = packed.astype(BF16)


def run_expert(place_arg, got, up, down, plan):
    main, columns = got.shape
    features, hidden_size = up.shape
    chunk = CHUNK
    steps = hidden_size // chunk
    half = steps // 2
    slots = main + main // 16 * plan[1]

    def piece(step, place):
        return lax.rem(step + half * (1 - place[0]), steps)

    def fixed(dims):
        return pl.BlockSpec(dims, lambda i, p: (0, 0))

    first_half = pl.BlockSpec((slots, chunk), lambda i, p: (0, jnp.minimum(i, half - 1)))
    second_half = pl.BlockSpec((slots, chunk), lambda i, p: (0, jnp.maximum(i - half, 0)))
    return pl.pallas_call(
        functools.partial(expert_body, plan),
        out_shape=[shape((main, columns)), shape((slots, 2 * features))]
        + [shape((slots, hidden_size // 2))] * 4,
        grid_spec=pltpu.PrefetchScalarGridSpec(
            num_scalar_prefetch=1,
            grid=(steps,),
            in_specs=[
                fixed((main, columns)),
                pl.BlockSpec((features, chunk), lambda i, p: (0, piece(i, p))),
                pl.BlockSpec((chunk, features), lambda i, p: (piece(i, p), 0)),
            ],
            out_specs=[fixed((main, columns)), fixed((slots, 2 * features))]
            + [first_half, second_half] * 2,
            scratch_shapes=[
                pltpu.VMEM((slots, 2 * features), F32),
                pltpu.VMEM((slots, chunk), BF16),
                pltpu.VMEM((slots, chunk), BF16),
            ],
        ),
        cost_estimate=pl.CostEstimate(
            flops=8 * slots * features * hidden_size,
            bytes_accessed=4 * features * hidden_size + 4 * slots * hidden_size,
            transcendentals=0,
        ),
        compiler_params=pltpu.CompilerParams(vmem_limit_bytes=VMEM_LIMIT),
    )(place_arg, got, up, down)


def combine_body(
    groups,
    capacity,
    plan,
    place_ref,
    got_ref,
    residual_ref,
    router_ref,
    route_row_ref,
    cotangent_ref,
    gain_ref,
    w_router_ref,
    w_out_ref,
    mixed_ref,
    grad_residual_ref,
    branch_ref,
    logits_ref,
    gain_out_ref,
    *refs,
):
    pieces, turned_ref = refs[:groups], refs[groups]
    height, experts = router_ref.shape
    features = residual_ref.shape[1]
    slots = got_ref.shape[0]
    width = pieces[0].shape[0]
    group = place_ref[1]
    chosen_row = route_row_ref[...]
    marks = jnp.where(iota((experts, height), 0) == chosen_row, 1.0, 0.0)
    earlier = (iota((height, height), 0) < iota((height, height), 1)).astype(BF16)
    before = nn(marks.astype(BF16), earlier)
    rank_row = jnp.sum(marks * before, axis=0, keepdims=True)
    onehot = jnp.transpose(marks) > 0.5
    pair_row = iota((8, height), 0)
    pairs = jnp.transpose(jnp.where(pair_row == 0, chosen_row.astype(F32), rank_row))
    chosen = pairs[:, 0:1].astype(jnp.int32)
    rank = pairs[:, 1:2].astype(jnp.int32)
    combine = slot_marks((height, slots), 1, chosen, rank, capacity, plan)
    back = nn(combine[0], got_ref[:, : 2 * features])
    if plan[1]:
        spare = got_ref[:, 2 * features :]
        back = back + jnp.concatenate([nn(marks, spare) for marks in combine[1:]], axis=1)
    router = router_ref[...]
    gate = jnp.sum(jnp.where(onehot, router, 0.0), axis=-1, keepdims=True)
    residual = residual_ref[...]
    inverse = lax.rsqrt(jnp.mean(residual * residual, axis=-1, keepdims=True) + EPSILON)
    unit = residual * inverse
    grad_mixed = cotangent_ref[...].astype(F32)
    gathered = back[:, :features]
    mixed_ref[...] = (residual + gate * gathered).astype(BF16)
    grad_gate = jnp.sum(grad_mixed * gathered, axis=-1, keepdims=True)
    grad_logits = (router * (jnp.where(onehot, grad_gate, 0.0) - gate * grad_gate)).astype(BF16)
    grad_normed = back[:, features:] + nn(grad_logits, w_router_ref[...])
    grad_unit = grad_normed * gain_ref[...].astype(F32)[None, :]
    grad_residual = grad_mixed + inverse * (
        grad_unit - unit * jnp.mean(grad_unit * unit, axis=-1, keepdims=True)
    )
    branch = grad_residual.astype(BF16)
    turned_ref[...] = nt(w_out_ref[...], branch).astype(BF16)
    for at in range(groups):
        first = pl.multiple_of((at ^ group) * width, width)
        pieces[at][...] = turned_ref[pl.ds(first, width), :]
    grad_residual_ref[...] = grad_residual
    branch_ref[...] = branch
    spare_lanes = logits_ref.shape[1] - experts
    logits_ref[...] = jnp.concatenate([grad_logits, jnp.zeros((height, spare_lanes), BF16)], axis=1)
    sums = jnp.sum(grad_normed * unit, axis=0, keepdims=True)
    gain_out_ref[...] = jnp.broadcast_to(sums, gain_out_ref.shape)


def qkv_body(groups, heads, place_ref, *refs):
    normed_refs, piece_refs = refs[:groups], refs[groups : 2 * groups]
    mine_ref, other_ref, total_ref, rows_ref = refs[2 * groups :]
    height = normed_refs[0].shape[1]
    width = rows_ref.shape[1] // 3
    for at in range(groups):
        piece = piece_refs[at]
        for head in range(heads):
            rows_ref[:, head * LANES : (head + 1) * LANES] = piece[
                head * height : (head + 1) * height, :
            ]
        parts = [
            piece[heads * height + half * width : heads * height + (half + 1) * width, :]
            for half in range(height // LANES)
        ]
        turned = jnp.concatenate(parts, axis=1).astype(F32)
        rows_ref[:, 2 * width :] = jnp.transpose(turned).astype(BF16)
        product = nn(normed_refs[at][...], rows_ref[...])
        if at == 0:
            total_ref[...] = product
        else:
            total_ref[...] = total_ref[...] + product
    split_rows(place_ref[0], total_ref, mine_ref, other_ref)


def rows_body(groups, heads, landed_ref, w_ref, gain_ref, out_ref, gain_out_ref):
    sources, _, columns = landed_ref.shape
    width = columns // 3
    size = width // heads
    features = groups * width
    for group in range(groups):
        total = landed_ref[group].astype(F32)
        for expert in range(1, sources // groups):
            total = total + landed_ref[expert * groups + group].astype(F32)
        out_ref[:, group * width : (group + 1) * width] = total[:, 2 * width :]
        for head in range(heads):
            for part in range(2):
                source = head * 2 * size + part * size
                first = (part + 1) * features + group * width + head * size
                out_ref[:, first : first + size] = total[:, source : source + size]
    sums = jnp.sum(w_ref[...].astype(F32) * out_ref[...], axis=1, keepdims=True)
    gain_out_ref[...] = sums / gain_ref[...].astype(F32)


def finish_body(groups, heads, place_ref, tokens_ref, gain_ref, w_ref, residual_ref, *refs):
    piece_refs = refs[:groups]
    out_ref, turned_ref, k_all, v_all = refs[groups:]
    height, features = tokens_ref.shape
    width = features // groups
    size = width // heads
    group = place_ref[1]
    for at in range(groups):
        piece = piece_refs[at]
        first = pl.multiple_of((at ^ group) * width, width)
        for half in range(height // LANES):
            source = heads * height + half * width
            turned_ref[pl.ds(first, width), half * LANES : (half + 1) * LANES] = piece[
                source : source + width, :
            ].astype(F32)
        for head in range(heads):
            both = piece[head * height : (head + 1) * height, :]
            lanes = slice(head * size, (head + 1) * size)
            k_all[at ^ group, :, lanes] = both[:, :size]
            v_all[at ^ group, :, lanes] = both[:, size:]
    grad_normed = nt(jnp.transpose(turned_ref[...]).astype(BF16), w_ref[:, :features])
    for part, source in ((1, k_all), (2, v_all)):
        joined = jnp.concatenate([source[at] for at in range(groups)], axis=1)
        grad_normed = grad_normed + nt(joined, w_ref[:, part * features : (part + 1) * features])
    tokens = tokens_ref[...].astype(F32)
    inverse = lax.rsqrt(jnp.mean(tokens * tokens, axis=-1, keepdims=True) + EPSILON)
    unit = tokens * inverse
    grad_unit = grad_normed * gain_ref[...].astype(F32)[None, :]
    grad = inverse * (grad_unit - unit * jnp.mean(grad_unit * unit, axis=-1, keepdims=True))
    out_ref[...] = (residual_ref[...] + grad).astype(BF16)


def strip_body(table_ref, strips_ref):
    heads, rows, height = strips_ref.shape
    used = rows - height
    offset = iota((used, LANES), 0) - 2 * height
    onehot = (bucket_of(offset) == iota((used, LANES), 1)).astype(BF16)
    lane = iota((used, height), 1)
    blank = jnp.zeros((height, height), F32)
    for head in range(heads):
        values = nn(onehot, table_ref[head])
        moved = 1
        while moved < height:
            values = jnp.where((lane & moved) != 0, pltpu.roll(values, moved, 0), values)
            moved *= 2
        strips_ref[head, :height] = blank
        strips_ref[head, height:used] = values[height:]
        strips_ref[head, used:] = blank


def diagonal_body(counts, *refs):
    calls = len(counts)
    out_ref = refs[2 * calls]
    places = [(call_at, inner) for call_at in range(calls) for inner in range(counts[call_at])]
    rows, height = refs[0].shape[1:]
    total_rows = rows + 2 * height
    lane = iota((total_rows, height), 1)
    offset = iota((total_rows, LANES), 0) - 3 * height
    table = (bucket_of(offset) == iota((total_rows, LANES), 1)).astype(F32)
    lane_out = iota((1, LANES), 1)
    blank = jnp.zeros((height, height), F32)
    for head, (call_at, inner) in enumerate(places):
        diag_ref, far_ref = refs[call_at].at[inner], refs[calls + call_at].at[inner]
        values = jnp.concatenate([blank, diag_ref[...], blank], axis=0)
        moved = 1
        while moved < height:
            values = jnp.where(
                (lane & moved) != 0, pltpu.roll(values, total_rows - moved, 0), values
            )
            moved *= 2
        sums = jnp.sum(values, axis=1, keepdims=True)
        by_bucket = jnp.sum(sums * table, axis=0, keepdims=True)
        by_bucket = by_bucket + jnp.where(lane_out == FAR_LEFT, jnp.sum(far_ref[0]), 0.0)
        out_ref[head] = by_bucket + jnp.where(lane_out == FAR_RIGHT, jnp.sum(far_ref[1]), 0.0)


def split_rows(place, source_ref, mine_ref, other_ref):
    experts_all, pieces, columns = mine_ref.shape
    for parity in range(2):

        @pl.when(place == parity)
        def _():
            for at in range(experts_all):
                for target, which in ((mine_ref, parity), (other_ref, 1 - parity)):
                    first = (2 * at + which) * pieces
                    target[at] = source_ref[first : first + pieces, :].astype(BF16)


def weights_body(
    experts,
    place_ref,
    branch_ref,
    attended_ref,
    normed_ref,
    logits_ref,
    gain_ref,
    out_ref,
    packed_ref,
):
    features = branch_ref.shape[1]
    extra = logits_ref.shape[1]
    branch = jnp.transpose(branch_ref[...].astype(F32)).astype(BF16)
    packed_ref[:, :features] = nt(branch, attended_ref[...])
    normed = jnp.transpose(normed_ref[...].astype(F32)).astype(BF16)
    column = jnp.transpose(gain_ref[...])[:, :1]
    packed_ref[:, features:] = nn(normed, logits_ref[...]) + jnp.where(
        iota((features, extra), 1) == experts, column, 0.0
    )
    count, padded = out_ref.shape[:2]
    pieces = features // count
    blank = jnp.zeros((padded - pieces, out_ref.shape[2]), F32)
    for row in range(count):
        source = (row % (count // 2)) * 2 + row // (count // 2)
        rows = packed_ref[source * pieces : (source + 1) * pieces, :]
        out_ref[row] = jnp.concatenate([rows, blank], axis=0).astype(BF16)


def exchange(moving, axis):
    return lax.all_to_all(moving, axis, split_axis=0, concat_axis=0, tiled=True)


def cross(moving, axis, distance):
    size = lax.axis_size(axis)
    return lax.ppermute(moving, axis, [(i, i ^ distance) for i in range(size)])


def trade(pieces):
    return [
        piece if at == 0 else cross(piece, "context", at) for at, piece in enumerate(pieces)
    ]


def after(values, *others):
    return lax.optimization_barrier((values,) + others)[0]


def per_device(
    tokens_in,
    gain_attn,
    w_qkv,
    rel_bias,
    w_out,
    gain_ffn,
    w_router,
    w_up,
    w_down,
    segments,
    routes,
    cotangent,
):
    groups = lax.axis_size("context")
    tensor_size = lax.axis_size("tensor")
    expert_size = lax.axis_size("expert")
    height, features = tokens_in.shape
    heads = rel_bias.shape[0]
    width = features // groups
    size = width // heads
    length = segments.shape[1]
    spans = length // height
    experts_all = expert_size * groups
    capacity = max(2, 5 * height // (4 * experts_all))
    plan = slot_plan(capacity, features)
    slots = experts_all * plan[0]
    columns = 2 * features + (2 * features // plan[2] if plan[1] else 0)
    piece_rows = heads * height + height // LANES * width
    place = lax.axis_index("tensor")
    context_at = lax.axis_index("context")
    place_arg = jnp.stack([place, context_at]).astype(jnp.int32)
    square = features * features

    projected = run(
        functools.partial(project_body, heads),
        [shape((piece_rows, LANES))] * groups + [shape((features, height))],
        (place_arg, tokens_in, gain_attn, w_qkv),
        scratch=[pltpu.VMEM((groups, piece_rows, LANES), BF16)],
        smem=(0,),
        flops=6 * height * square,
        moved=8 * square,
    )
    own = trade(projected[:groups])
    table = jnp.pad(rel_bias, ((0, 0), (0, LANES - rel_bias.shape[1])))
    table = jnp.broadcast_to(table[:, :, None], (heads, LANES, height))
    strips = run(
        strip_body,
        shape((heads, 5 * height, height), F32),
        (table,),
        flops=heads * 2 * 4 * height * LANES * height,
        moved=heads * 4 * 5 * height * height,
    )
    far = [cross(after(piece, strips), "tensor", 1) for piece in own]
    head_flops = 4 * groups * height * length * size

    def fixed(dims):
        return pl.BlockSpec(dims, lambda h, n=len(dims): (0,) * n)

    def by_head(dims, first=0):
        return pl.BlockSpec(
            (1,) + dims, lambda h, n=len(dims), f=first: (h + f,) + (0,) * n
        )

    def head_rows(first=0):
        return pl.BlockSpec((size, height), lambda h, f=first: (h + f, 0))

    smem = pl.BlockSpec(memory_space=pltpu.SMEM)
    held_dims = [
        (groups, size, height),
        (groups, 8, height),
        (length, LANES),
        (size + 16, length),
        (groups, spans, height, height),
    ]
    held_kinds = [F32, F32, BF16, BF16, BF16]
    outs = pl.pallas_call(
        functools.partial(forward_body, groups, heads),
        out_shape=[shape((width, height))] * groups
        + [shape((heads,) + dims, kind) for dims, kind in zip(held_dims, held_kinds)],
        grid=(heads,),
        in_specs=[smem, smem, fixed((1, length)), by_head((5 * height, height))]
        + [fixed((piece_rows, LANES))] * (2 * groups),
        out_specs=[head_rows()] * groups + [by_head(dims) for dims in held_dims],
        scratch_shapes=[
            pltpu.VMEM((length, LANES), BF16),
            pltpu.VMEM((spans, height), jnp.int32),
            pltpu.VMEM((length, LANES), BF16),
            pltpu.VMEM((size + 16, length), BF16),
            pltpu.VMEM((length, height), F32),
            pltpu.VMEM((length, height), F32),
        ],
        cost_estimate=pl.CostEstimate(
            flops=6 * heads * head_flops, bytes_accessed=20 * square, transcendentals=0
        ),
        compiler_params=pltpu.CompilerParams(vmem_limit_bytes=VMEM_LIMIT),
    )(place_arg, rel_bias.astype(F32), segments, strips, *own, *far)
    attended = trade(outs[:groups])
    exact, inverse, vaug, kt, weights = outs[groups:]
    route_row = routes.reshape(1, height)
    normed_all = trade([after(projected[groups], *own)] * groups)
    residual, normed_ffn, router, sent, attended_t = run(
        functools.partial(route_body, groups, capacity, plan),
        [
            shape((height, features), F32),
            shape((height, features)),
            shape((height, experts_all), F32),
            shape((slots, columns)),
            shape((features, height)),
        ],
        (
            after(place_arg, *normed_all),
            tokens_in,
            w_out,
            gain_ffn,
            w_router.T,
            route_row,
            cotangent,
            *attended,
        ),
        smem=(0,),
        flops=2 * height * square,
        moved=4 * square,
    )

    def move_slots(moving):
        return exchange(
            moving.reshape(experts_all, plan[0], columns), ("expert", "context")
        ).reshape(slots, columns)

    got = move_slots(sent)
    pieces = features // (experts_all * tensor_size)
    first_piece = (
        (lax.axis_index("expert") * groups + context_at) * tensor_size + place
    ) * pieces
    first_piece = after(first_piece, sent)
    own_w = lax.dynamic_slice_in_dim(w_qkv, first_piece, pieces, 0)
    own_gain = lax.dynamic_slice_in_dim(gain_attn, first_piece, pieces, 0).reshape(pieces, 1)
    turned = run(
        functools.partial(turn_body, groups, heads),
        shape((heads, groups, height, LANES)),
        (after(own[0], sent), *own[1:]),
        flops=2 * square,
        moved=4 * square,
    )
    back, rows_in, act_other, act_mine, hid_other, hid_mine = run_expert(
        after(place_arg, turned, own_w, own_gain), got, w_up[0], w_down[0], plan
    )
    returned = move_slots(back)

    def both(values, sent_values):
        return jnp.concatenate([values, cross(sent_values, "tensor", 1)], axis=0)

    all_rows = both(rows_in, rows_in)
    grad_down = tn(both(act_mine, act_other), all_rows[:, features:])
    grad_up = tn(all_rows[:, :features], both(hid_mine, hid_other))
    extra = -(-(experts_all + 1) // LANES) * LANES
    outs = run(
        functools.partial(combine_body, groups, capacity, plan),
        [
            shape((height, features)),
            shape((height, features), F32),
            shape((height, features)),
            shape((height, extra)),
            shape((8, features), F32),
        ]
        + [shape((width, height))] * groups,
        (
            after(place_arg, grad_down, grad_up),
            returned,
            residual,
            router,
            route_row,
            cotangent,
            gain_ffn,
            w_router.T,
            w_out,
        ),
        scratch=[pltpu.VMEM((features, height), BF16)],
        smem=(0,),
        flops=4 * height * square,
        moved=8 * square,
    )
    mixed_out, grad_residual, branch, grad_logits, gain_sums = outs[:5]
    grad_pieces = trade(outs[5:])
    padded = -(-pieces // 16) * 16
    packed = run(
        functools.partial(weights_body, experts_all),
        shape((experts_all * tensor_size, padded, features + extra)),
        (
            after(place_arg, *grad_pieces[1:3]),
            branch,
            attended_t,
            normed_ffn,
            grad_logits,
            gain_sums,
        ),
        scratch=[pltpu.VMEM((features, features + extra), F32)],
        smem=(0,),
        flops=2 * height * square,
        moved=8 * square,
    )
    reduced = packed.reshape(-1, features + extra)
    for axis in ("tensor", "expert", "context"):
        reduced = lax.psum_scatter(reduced, axis, scatter_dimension=0, tiled=True)

    def pair_sum(kept, received):
        return (kept.astype(F32) + received.astype(F32)).astype(BF16)

    counts = (1, heads - 1)
    mine_kv, got_kv, q_grads, diags, fars = [], [], [], [], []
    for call_at in range(len(counts)):
        first, count = sum(counts[:call_at]), counts[call_at]
        dims = [
            (groups, size, height),
            (groups, height, 2 * size),
            (groups, height, 2 * size),
            (5 * height, height),
            (2, spans, height),
        ]
        outs = pl.pallas_call(
            functools.partial(backward_body, groups),
            out_shape=[
                shape((count,) + of, kind)
                for of, kind in zip(dims, [BF16, BF16, BF16, F32, F32])
            ],
            grid=(count,),
            in_specs=[smem]
            + [
                by_head(of, first)
                for of in (held_dims[4], held_dims[2], held_dims[3], held_dims[0], held_dims[1])
            ]
            + [by_head((groups, height, LANES), first)]
            + [head_rows(first)] * groups,
            out_specs=[by_head(of) for of in dims],
            scratch_shapes=[pltpu.VMEM((length, LANES), F32)]
            + [pltpu.VMEM((length, height), F32)] * 2
            + [pltpu.VMEM((length, height), BF16)] * 2,
            cost_estimate=pl.CostEstimate(
                flops=8 * count * head_flops, bytes_accessed=20 * square, transcendentals=0
            ),
            compiler_params=pltpu.CompilerParams(vmem_limit_bytes=VMEM_LIMIT),
        )(after(place_arg, packed), weights, vaug, kt, exact, inverse, turned, *grad_pieces)
        q_grads.append(outs[0])
        mine_kv.append(outs[1])
        got_kv.append(cross(outs[2], "tensor", 1))
        diags.append(outs[3])
        fars.append(outs[4])
    joined = run(
        functools.partial(join_body, counts),
        [shape((piece_rows, LANES))] * groups,
        (*mine_kv, *got_kv, *q_grads),
        moved=4 * groups * piece_rows * LANES,
    )
    landed_pieces = trade(joined)
    mine, other = run(
        functools.partial(qkv_body, groups, heads),
        [shape((experts_all, pieces, 3 * width))] * 2,
        (place_arg, *normed_all, *joined),
        scratch=[pltpu.VMEM((features, 3 * width), F32), pltpu.VMEM((height, 3 * width), BF16)],
        smem=(0,),
        flops=6 * groups * height * features * width,
        moved=8 * square,
    )
    summed = pair_sum(mine, cross(other, "tensor", 1))
    landed = exchange(after(summed, *landed_pieces), ("expert", "context"))
    grad_qkv, grad_gain_attn = run(
        functools.partial(rows_body, groups, heads),
        [shape((pieces, 3 * features), F32), shape((pieces, 1), F32)],
        (landed, own_w, own_gain),
        moved=2 * landed.size,
    )
    grad_tokens = run(
        functools.partial(finish_body, groups, heads),
        shape((height, features)),
        (place_arg, tokens_in, gain_attn, w_qkv, grad_residual, *landed_pieces),
        scratch=[
            pltpu.VMEM((features, height), F32),
            pltpu.VMEM((groups, height, width), BF16),
            pltpu.VMEM((groups, height, width), BF16),
        ],
        smem=(0,),
        flops=6 * height * square,
        moved=8 * square,
    )
    by_bucket = run(
        functools.partial(diagonal_body, counts),
        shape((heads, 1, LANES), F32),
        (*diags, *fars),
        flops=heads * 8 * 7 * height * height,
        moved=heads * 20 * height * height,
    )
    by_bucket = by_bucket + cross(by_bucket, "tensor", 1)
    distance = 1
    while distance < expert_size:
        by_bucket = by_bucket + cross(by_bucket, "expert", distance)
        distance *= 2
    reduced = reduced[:pieces].astype(F32)
    return (
        mixed_out,
        grad_tokens,
        grad_gain_attn[:, 0],
        grad_qkv,
        by_bucket[:, 0, : rel_bias.shape[1]],
        reduced[:, :features].T,
        reduced[:, features + experts_all],
        reduced[:, features : features + experts_all],
        grad_up[None],
        grad_down[None],
    )


def solution(mesh):
    rows = ("expert", "context", "tensor")
    in_specs = (
        P(rows, None),
        P(),
        P(),
        P("context", None),
        P(),
        P(),
        P(),
        P(("expert", "context"), None, None),
        P(("expert", "context"), None, None),
        P("expert", None),
        P(rows, None),
        P(rows, None),
    )
    out_specs = (
        P(rows, None),
        P(rows, None),
        P(rows),
        P(rows, None),
        P("context", None),
        P(None, rows),
        P(rows),
        P(rows, None),
        P(("expert", "context"), None, "tensor"),
        P(("expert", "context"), "tensor", None),
    )
    return jax.shard_map(
        per_device, mesh=mesh, in_specs=in_specs, out_specs=out_specs, check_vma=False
    )
```

```python
import functools

import jax
import jax.numpy as jnp
from jax import lax
from jax.experimental import pallas as pl
from jax.experimental.pallas import tpu as pltpu
from jax.sharding import PartitionSpec as P

EPSILON = 1e-06
THRESHOLDS = (12, 16, 23, 32, 46, 64, 91)
FAR_LEFT = 15
FAR_RIGHT = 31
EXCLUDED = -1e30
LANES = 128
BF16 = jnp.bfloat16
F32 = jnp.float32
VMEM_LIMIT = 56 * 1024 * 1024
BUCKETS = 32
CHUNK = 768
PART = 256


def bucket_of(offset):
    distance = jnp.abs(offset)
    beyond = jnp.zeros_like(distance)
    for threshold in THRESHOLDS:
        beyond = beyond + (distance >= threshold).astype(jnp.int32)
    nearby = jnp.where(distance < 8, distance, 8 + beyond)
    return nearby + 16 * (offset > 0).astype(jnp.int32)


def nn(left, right):
    return lax.dot_general(left, right, (((1,), (0,)), ((), ())), preferred_element_type=F32)


def nt(left, right):
    return lax.dot_general(left, right, (((1,), (1,)), ((), ())), preferred_element_type=F32)


def tn(left, right):
    return lax.dot_general(left, right, (((0,), (0,)), ((), ())), preferred_element_type=F32)


def iota(shape, axis):
    return lax.broadcasted_iota(jnp.int32, shape, axis)


def three_terms(values):
    high = values.astype(BF16).astype(F32)
    middle = (values - high).astype(BF16).astype(F32)
    return high, middle, values - high - middle


def specs_for(count, smem=()):
    return [
        pl.BlockSpec(memory_space=pltpu.SMEM if i in smem else pltpu.VMEM) for i in range(count)
    ]


def run(body, out_shape, args, scratch=(), smem=(), flops=0, moved=0, limit=VMEM_LIMIT):
    return pl.pallas_call(
        body,
        out_shape=out_shape,
        in_specs=specs_for(len(args), smem),
        scratch_shapes=list(scratch),
        cost_estimate=pl.CostEstimate(flops=flops, bytes_accessed=moved, transcendentals=0),
        compiler_params=pltpu.CompilerParams(vmem_limit_bytes=limit),
    )(*args)


def shape(dims, kind=BF16):
    return jax.ShapeDtypeStruct(dims, kind)


def project_body(heads, place_ref, tokens_ref, gain_ref, w_ref, *refs):
    groups = len(refs) - 2
    piece_refs, normed_ref, all_ref = refs[:groups], refs[groups], refs[groups + 1]
    height, features = tokens_ref.shape
    width = features // groups
    size = width // heads
    group = place_ref[1]
    tokens = tokens_ref[...].astype(F32)
    inverse = lax.rsqrt(jnp.mean(tokens * tokens, axis=-1, keepdims=True) + EPSILON)
    normed = (tokens * inverse * gain_ref[...].astype(F32)[None, :]).astype(BF16)
    normed_ref[...] = jnp.transpose(normed.astype(F32)).astype(BF16)
    turned = jnp.transpose(nn(normed, w_ref[:, :features])).astype(BF16)
    keys = nn(normed, w_ref[:, features : 2 * features]).astype(BF16)
    values = nn(normed, w_ref[:, 2 * features :]).astype(BF16)
    for at in range(groups):
        for head in range(heads):
            lanes = slice(at * width + head * size, at * width + (head + 1) * size)
            all_ref[at ^ group, head * height : (head + 1) * height, :] = jnp.concatenate(
                [keys[:, lanes], values[:, lanes]], axis=1
            )
        for half in range(height // LANES):
            first = heads * height + half * width
            all_ref[at ^ group, first : first + width, :] = turned[
                at * width : (at + 1) * width, half * LANES : (half + 1) * LANES
            ]
    for at in range(groups):
        piece_refs[at][...] = all_ref[at]


def q_rows(piece_ref, heads, height, size, head):
    width = heads * size
    parts = []
    for half in range(height // LANES):
        first = heads * height + half * width + head * size
        parts.append(piece_ref[pl.ds(pl.multiple_of(first, 16), size), :])
    return jnp.concatenate(parts, axis=1)


def forward_body(groups, heads, place_ref, bias_ref, seg_ref, strip_ref, *refs):
    own_refs, far_refs, out_refs = (refs[i * groups : (i + 1) * groups] for i in range(3))
    exact_ref, inverse_ref, vaug_ref, kaug_ref, weight_ref = refs[3 * groups : 3 * groups + 5]
    extra_all, docs_all, vt_ref, score_ref = refs[3 * groups + 5 :]
    size, height = out_refs[0].shape
    spans = kaug_ref.shape[1] // height
    place, group = place_ref[0], place_ref[1]
    head = pl.program_id(0)
    tall = size + 16
    rest = LANES - size

    @pl.when(head == 0)
    def _():
        row = iota((LANES, height), 0) - size
        for span in range(spans):
            docs = seg_ref[0:1, span * height : (span + 1) * height]
            docs_all[span : span + 1, :] = docs
            extra = jnp.where((row >= 0) & (row < 3) & (docs != row), EXCLUDED, 0.0)
            extra = jnp.where(row - 3 == span, 1.0, extra)
            extra_all[span * height : (span + 1) * height, :] = jnp.transpose(extra).astype(BF16)

    row, column = iota((tall, LANES), 0), iota((tall, LANES), 1)
    pick_v = (((row < size) & (row + size == column)) | ((row == size) & (column == 0))).astype(
        BF16
    )
    lane = iota((height, LANES), 1)
    low_half = lane < size
    ones = jnp.where(lane < 3, 1.0, 0.0).astype(BF16)
    extra_row = iota((rest, height), 0)
    queries_all = []
    for at in range(groups):
        block = at ^ group
        for source, parity in ((own_refs[at], place), (far_refs[at], 1 - place)):
            span = 2 * block + parity
            rows = pl.ds(pl.multiple_of(span * height, height), height)
            both = source[pl.ds(pl.multiple_of(head * height, height), height), :]
            keys = jnp.where(low_half, both, extra_all[rows, :])
            values = jnp.where(low_half, ones, both)
            kaug_ref[0, rows, :] = keys
            vaug_ref[0, rows, :] = values
            vt_ref[span] = nt(pick_v, values).astype(BF16)
        span = 2 * block + place
        docs = docs_all[pl.ds(span, 1), :]
        apart = extra_row - 3 - span
        far = jnp.where(
            apart <= -2,
            bias_ref[head, FAR_LEFT],
            jnp.where(apart >= 2, bias_ref[head, FAR_RIGHT], 0.0),
        )
        extra = jnp.where(
            extra_row < 3,
            jnp.where(docs == extra_row, 1.0, 0.0),
            jnp.where(extra_row < 3 + spans, far, 0.0),
        )
        queries_all.append(
            jnp.concatenate(
                [q_rows(own_refs[at], heads, height, size, head), extra.astype(BF16)], axis=0
            )
        )
    for at in range(groups):
        span = 2 * (at ^ group) + place
        start = jnp.clip(span - 1, 0, spans - 3)
        queries = queries_all[at]
        slot = at % 2
        row_max = None
        for step in range(spans):
            key_span = (start + step) if step < 3 else ((start + step) & (spans - 1))
            rows = pl.ds(pl.multiple_of(key_span * height, height), height)
            scores = nn(kaug_ref[0, rows, :], queries)
            if step < 3:
                level = pl.multiple_of((key_span - span + 2) * height, height)
                scores = scores + strip_ref[0, pl.ds(level, height), :]
            score_ref[slot, step] = scores
            best = jnp.max(scores, axis=0, keepdims=True)
            row_max = best if row_max is None else jnp.maximum(row_max, best)
        total = jnp.zeros((tall, height), F32)
        for step in range(spans):
            key_span = (start + step) if step < 3 else ((start + step) & (spans - 1))
            weights = jnp.exp(score_ref[slot, step] - row_max).astype(BF16)
            weight_ref[0, at, key_span] = weights
            total = total + nn(vt_ref[key_span], weights)
        inverse = 1.0 / total[size : size + 1]
        result = total[:size] * inverse
        out_refs[at][...] = result.astype(BF16)
        exact_ref[0, at] = result
        inverse_ref[0, at] = jnp.broadcast_to(inverse, (8, height))


def turn_body(groups, heads, kaug_ref, *refs):
    piece_refs, out_ref, kt_ref = refs[:groups], refs[groups], refs[groups + 1]
    height = out_ref.shape[2]
    size = out_ref.shape[3] // 2
    spans = kaug_ref.shape[1] // height
    row, column = iota((size + 16, LANES), 0), iota((size + 16, LANES), 1)
    pick_k = (
        ((row < size) & (row == column))
        | ((row >= size) & (row < size + spans) & (row + 3 == column))
    ).astype(BF16)
    blank = jnp.zeros((size, height), F32)
    for head in range(heads):
        kt_ref[head] = nt(pick_k, kaug_ref[head]).astype(BF16)
        for at in range(groups):
            queries = q_rows(piece_refs[at], heads, height, size, head).astype(F32)
            out_ref[head, at] = jnp.transpose(jnp.concatenate([queries, blank], axis=0)).astype(
                BF16
            )


def backward_body(groups, place_ref, *refs):
    weight_ref, vaug_ref, kt_ref, exact_ref, inverse_ref, q_ref = refs[:6]
    grad_refs = refs[6 : 6 + groups]
    dq_ref, mine_ref, other_ref, diag_ref, far_ref, dkv_ref = refs[6 + groups : 12 + groups]
    slope_refs, score_refs = refs[12 + groups : 14 + groups], refs[14 + groups :]
    size, height = grad_refs[0].shape
    length = vaug_ref.shape[1]
    spans = length // height
    place, group = place_ref[0], place_ref[1]
    diag_ref[...] = jnp.zeros_like(diag_ref)
    extra_row = iota((LANES - size, height), 0)
    blank = jnp.zeros((size, height), F32)
    span_row = iota((spans, height), 0)
    left_total = jnp.zeros((spans, height), F32)
    right_total = jnp.zeros((spans, height), F32)
    for at in range(groups):
        span = 2 * (at ^ group) + place
        start = jnp.clip(span - 1, 0, spans - 3)
        slope_ref, score_ref = slope_refs[at % 2], score_refs[at % 2]
        grads = (grad_refs[at][...].astype(F32) * inverse_ref[0, at, 0:1]).astype(BF16)
        grads32 = grads.astype(F32)
        delta = jnp.sum(grads32 * exact_ref[0, at], axis=0, keepdims=True)
        high, middle, low = three_terms(-delta)
        extra = jnp.where(
            extra_row == 0,
            high,
            jnp.where(extra_row == 1, middle, jnp.where(extra_row == 2, low, 0.0)),
        )
        slope_ref[...] = nn(
            vaug_ref[0], jnp.concatenate([extra.astype(BF16), grads], axis=0)
        )
        turned = jnp.transpose(jnp.concatenate([blank, grads32], axis=0)).astype(BF16)
        sides = jnp.concatenate([q_ref[0, at], turned], axis=0)
        for key in range(spans):
            rows = slice(key * height, (key + 1) * height)
            score_ref[rows, :] = (
                weight_ref[0, at, key].astype(F32) * slope_ref[rows, :]
            ).astype(BF16)
        both = jnp.concatenate(
            [score_ref[...], weight_ref[0, at].reshape(length, height)], axis=1
        )
        product = nn(both, sides)
        if at == 0:
            dkv_ref[...] = product
        else:
            dkv_ref[...] = dkv_ref[...] + product
        total = nn(kt_ref[0], score_ref[...])
        dq_ref[0, at] = total[:size].astype(BF16)
        sums = total[size : size + spans]
        left_total = left_total + jnp.where(span_row < start, sums, 0.0)
        right_total = right_total + jnp.where(span_row >= start + 3, sums, 0.0)
        rows = pl.ds(pl.multiple_of(start * height, height), 3 * height)
        level = pl.ds(pl.multiple_of((start - span + 2) * height, height), 3 * height)
        diag_ref[0, level, :] = diag_ref[0, level, :] + score_ref[rows, :].astype(F32)
    far_ref[0, 0] = left_total
    far_ref[0, 1] = right_total
    for at in range(groups):
        for target, parity in ((mine_ref, place), (other_ref, 1 - place)):
            first = pl.multiple_of((2 * (at ^ group) + parity) * height, height)
            target[0, at] = dkv_ref[pl.ds(first, height), :].astype(BF16)


def join_body(counts, *refs):
    calls = len(counts)
    mine_refs, got_refs, dq_refs = (refs[i * calls : (i + 1) * calls] for i in range(3))
    piece_refs = refs[3 * calls :]
    size, height = dq_refs[0].shape[2:]
    heads = sum(counts)
    width = heads * size
    for at, piece_ref in enumerate(piece_refs):
        head = 0
        for call_at, count in enumerate(counts):
            for inner in range(count):
                kept = mine_refs[call_at][inner, at].astype(F32)
                piece_ref[head * height : (head + 1) * height, :] = (
                    kept + got_refs[call_at][inner, at].astype(F32)
                ).astype(BF16)
                for half in range(height // LANES):
                    first = heads * height + half * width + head * size
                    piece_ref[first : first + size, :] = dq_refs[call_at][
                        inner, at, :, half * LANES : (half + 1) * LANES
                    ]
                head += 1


def slot_plan(capacity, features):
    base = capacity // 16 * 16
    left = capacity - base
    if base and left and 16 % left == 0 and (2 * features) % (LANES * (16 // left)) == 0:
        return base, left, 16 // left
    return -(-capacity // 8) * 8, 0, 0


def slot_marks(shape_of, axis, chosen, rank, capacity, plan):
    base, left, parts = plan
    position = iota(shape_of, axis)
    limit = base if left else capacity
    marks = [jnp.where(position == jnp.where(rank < limit, chosen * base + rank, -1), 1.0, 0.0)]
    spare = rank - base
    for part in range(parts):
        slot = chosen * 16 + part * left + spare
        slot = jnp.where((spare >= 0) & (spare < left), slot, -1)
        marks.append(jnp.where(position == slot, 1.0, 0.0))
    return [mark.astype(BF16) for mark in marks]


def route_body(
    groups,
    capacity,
    plan,
    place_ref,
    tokens_ref,
    w_out_ref,
    gain_ref,
    w_router_ref,
    route_row_ref,
    cotangent_ref,
    *refs,
):
    pieces = refs[:groups]
    residual_ref, normed_ref, router_ref, sent_ref, attended_ref = refs[groups:]
    height, features = tokens_ref.shape
    experts = w_router_ref.shape[0]
    slots = sent_ref.shape[0]
    width = pieces[0].shape[0]
    group = place_ref[1]
    for at in range(groups):
        first = pl.multiple_of((at ^ group) * width, width)
        attended_ref[pl.ds(first, width), :] = pieces[at][...]
    residual = tokens_ref[...].astype(F32) + tn(attended_ref[...], w_out_ref[...])
    residual_ref[...] = residual
    inverse = lax.rsqrt(jnp.mean(residual * residual, axis=-1, keepdims=True) + EPSILON)
    normed = (residual * inverse * gain_ref[...].astype(F32)[None, :]).astype(BF16)
    normed_ref[...] = normed
    logits = nt(normed, w_router_ref[...])
    powers = jnp.exp(logits - jnp.max(logits, axis=-1, keepdims=True))
    router = powers / jnp.sum(powers, axis=-1, keepdims=True)
    router_ref[...] = router
    chosen = route_row_ref[...]
    marks = iota((experts, height), 0) == chosen
    onehot = jnp.transpose(jnp.where(marks, 1.0, 0.0))
    gate = jnp.sum(onehot * router, axis=-1, keepdims=True)
    grad_expert = (gate * cotangent_ref[...].astype(F32)).astype(BF16)
    rows = jnp.concatenate([normed, grad_expert], axis=1)
    earlier = (iota((height, height), 0) < iota((height, height), 1)).astype(BF16)
    before = nn(jnp.where(marks, 1.0, 0.0).astype(BF16), earlier)
    rank = jnp.sum(jnp.where(marks, before, 0.0), axis=0, keepdims=True).astype(jnp.int32)
    dispatch = slot_marks((slots, height), 0, chosen, rank, capacity, plan)
    sent_ref[:, : 2 * features] = nn(dispatch[0], rows).astype(BF16)
    if plan[1]:
        span = 2 * features // plan[2]
        spare = nn(dispatch[1], rows[:, :span])
        for part in range(1, plan[2]):
            spare = spare + nn(dispatch[1 + part], rows[:, part * span : (part + 1) * span])
        sent_ref[:, 2 * features :] = spare.astype(BF16)


def spare_marks(sources, plan):
    base, left, parts = plan
    target = iota((sources * left, sources * 16), 0)
    origin = iota((sources * left, sources * 16), 1)
    source = target // left
    return [
        (origin == source * 16 + part * left + (target - source * left)).astype(BF16)
        for part in range(parts)
    ]


def expert_body(
    plan,
    place_ref,
    got_ref,
    up_ref,
    down_ref,
    back_ref,
    rows_ref,
    act_other_ref,
    act_mine_ref,
    hid_other_ref,
    hid_mine_ref,
    total_ref,
    active_ref,
    hidden_ref,
):
    step, steps = pl.program_id(0), pl.num_programs(0)
    wide = rows_ref.shape[1]
    features = wide // 2
    main = got_ref.shape[0]
    left, parts = plan[1], plan[2]

    @pl.when(step == 0)
    def _():
        rows_ref[:main, :] = got_ref[:, :wide]
        if left:
            span = wide // parts
            packed = got_ref[:, wide:]
            for part, marks in enumerate(spare_marks(main // 16, plan)):
                rows_ref[main:, part * span : (part + 1) * span] = nn(marks, packed).astype(BF16)

    chunk = up_ref.shape[1]
    for first in range(0, chunk, PART):
        lanes = slice(first, first + PART)
        hidden = nn(rows_ref[:, :features], up_ref[:, lanes])
        below = 0.5 * (1.0 + lax.erf(hidden * (2.0**-0.5)))
        bell = jnp.exp(-0.5 * hidden * hidden) * 0.3989422804014327
        active_ref[:, lanes] = (hidden * below).astype(BF16)
        grad_active = nt(rows_ref[:, features:], down_ref[lanes, :])
        hidden_ref[:, lanes] = (grad_active * (below + hidden * bell)).astype(BF16)
    produced = nn(active_ref[...], down_ref[...])
    grad_back = nt(hidden_ref[...], up_ref[...])

    @pl.when(step < steps // 2)
    def _():
        act_other_ref[...] = active_ref[...]
        hid_other_ref[...] = hidden_ref[...]

    @pl.when(step >= steps // 2)
    def _():
        act_mine_ref[...] = active_ref[...]
        hid_mine_ref[...] = hidden_ref[...]

    @pl.when(step == 0)
    def _():
        total_ref[:, :features] = produced
        total_ref[:, features:] = grad_back

    @pl.when(step > 0)
    def _():
        total_ref[:, :features] = total_ref[:, :features] + produced
        total_ref[:, features:] = total_ref[:, features:] + grad_back

    @pl.when(step == steps - 1)
    def _():
        back_ref[:, :wide] = total_ref[:main, :].astype(BF16)
        if left:
            span = wide // parts
            packed = jnp.zeros((main, span), F32)
            for part, marks in enumerate(spare_marks(main // 16, plan)):
                spare = total_ref[main:, part * span : (part + 1) * span].astype(BF16)
                packed = packed + tn(marks, spare)
            back_ref[:, wide:] = packed.astype(BF16)


def run_expert(place_arg, got, up, down, plan):
    main, columns = got.shape
    features, hidden_size = up.shape
    chunk = CHUNK
    steps = hidden_size // chunk
    half = steps // 2
    slots = main + main // 16 * plan[1]

    def piece(step, place):
        return lax.rem(step + half * (1 - place[0]), steps)

    def fixed(dims):
        return pl.BlockSpec(dims, lambda i, p: (0, 0))

    first_half = pl.BlockSpec((slots, chunk), lambda i, p: (0, jnp.minimum(i, half - 1)))
    second_half = pl.BlockSpec((slots, chunk), lambda i, p: (0, jnp.maximum(i - half, 0)))
    return pl.pallas_call(
        functools.partial(expert_body, plan),
        out_shape=[shape((main, columns)), shape((slots, 2 * features))]
        + [shape((slots, hidden_size // 2))] * 4,
        grid_spec=pltpu.PrefetchScalarGridSpec(
            num_scalar_prefetch=1,
            grid=(steps,),
            in_specs=[
                fixed((main, columns)),
                pl.BlockSpec((features, chunk), lambda i, p: (0, piece(i, p))),
                pl.BlockSpec((chunk, features), lambda i, p: (piece(i, p), 0)),
            ],
            out_specs=[fixed((main, columns)), fixed((slots, 2 * features))]
            + [first_half, second_half] * 2,
            scratch_shapes=[
                pltpu.VMEM((slots, 2 * features), F32),
                pltpu.VMEM((slots, chunk), BF16),
                pltpu.VMEM((slots, chunk), BF16),
            ],
        ),
        cost_estimate=pl.CostEstimate(
            flops=8 * slots * features * hidden_size,
            bytes_accessed=4 * features * hidden_size + 4 * slots * hidden_size,
            transcendentals=0,
        ),
        compiler_params=pltpu.CompilerParams(vmem_limit_bytes=VMEM_LIMIT),
    )(place_arg, got, up, down)


def combine_body(
    groups,
    capacity,
    plan,
    place_ref,
    got_ref,
    residual_ref,
    router_ref,
    route_row_ref,
    cotangent_ref,
    gain_ref,
    w_router_ref,
    w_out_ref,
    mixed_ref,
    grad_residual_ref,
    branch_ref,
    logits_ref,
    gain_out_ref,
    *refs,
):
    pieces, turned_ref = refs[:groups], refs[groups]
    height, experts = router_ref.shape
    features = residual_ref.shape[1]
    slots = got_ref.shape[0]
    width = pieces[0].shape[0]
    group = place_ref[1]
    chosen_row = route_row_ref[...]
    marks = jnp.where(iota((experts, height), 0) == chosen_row, 1.0, 0.0)
    earlier = (iota((height, height), 0) < iota((height, height), 1)).astype(BF16)
    before = nn(marks.astype(BF16), earlier)
    rank_row = jnp.sum(marks * before, axis=0, keepdims=True)
    onehot = jnp.transpose(marks) > 0.5
    pair_row = iota((8, height), 0)
    pairs = jnp.transpose(jnp.where(pair_row == 0, chosen_row.astype(F32), rank_row))
    chosen = pairs[:, 0:1].astype(jnp.int32)
    rank = pairs[:, 1:2].astype(jnp.int32)
    combine = slot_marks((height, slots), 1, chosen, rank, capacity, plan)
    back = nn(combine[0], got_ref[:, : 2 * features])
    if plan[1]:
        spare = got_ref[:, 2 * features :]
        back = back + jnp.concatenate([nn(marks, spare) for marks in combine[1:]], axis=1)
    router = router_ref[...]
    gate = jnp.sum(jnp.where(onehot, router, 0.0), axis=-1, keepdims=True)
    residual = residual_ref[...]
    inverse = lax.rsqrt(jnp.mean(residual * residual, axis=-1, keepdims=True) + EPSILON)
    unit = residual * inverse
    grad_mixed = cotangent_ref[...].astype(F32)
    gathered = back[:, :features]
    mixed_ref[...] = (residual + gate * gathered).astype(BF16)
    grad_gate = jnp.sum(grad_mixed * gathered, axis=-1, keepdims=True)
    grad_logits = (router * (jnp.where(onehot, grad_gate, 0.0) - gate * grad_gate)).astype(BF16)
    grad_normed = back[:, features:] + nn(grad_logits, w_router_ref[...])
    grad_unit = grad_normed * gain_ref[...].astype(F32)[None, :]
    grad_residual = grad_mixed + inverse * (
        grad_unit - unit * jnp.mean(grad_unit * unit, axis=-1, keepdims=True)
    )
    branch = grad_residual.astype(BF16)
    turned_ref[...] = nt(w_out_ref[...], branch).astype(BF16)
    for at in range(groups):
        first = pl.multiple_of((at ^ group) * width, width)
        pieces[at][...] = turned_ref[pl.ds(first, width), :]
    grad_residual_ref[...] = grad_residual
    branch_ref[...] = branch
    spare_lanes = logits_ref.shape[1] - experts
    logits_ref[...] = jnp.concatenate([grad_logits, jnp.zeros((height, spare_lanes), BF16)], axis=1)
    sums = jnp.sum(grad_normed * unit, axis=0, keepdims=True)
    gain_out_ref[...] = jnp.broadcast_to(sums, gain_out_ref.shape)


def qkv_body(groups, heads, place_ref, *refs):
    normed_refs, piece_refs = refs[:groups], refs[groups : 2 * groups]
    bucket_ref, mine_ref, other_ref, total_ref, rows_ref = refs[2 * groups :]
    pieces = mine_ref.shape[1]
    wide = rows_ref.shape[1]
    height = normed_refs[0].shape[1]
    width = rows_ref.shape[1] // 3
    for at in range(groups):
        piece = piece_refs[at]
        for head in range(heads):
            rows_ref[:, head * LANES : (head + 1) * LANES] = piece[
                head * height : (head + 1) * height, :
            ]
        parts = [
            piece[heads * height + half * width : heads * height + (half + 1) * width, :]
            for half in range(height // LANES)
        ]
        turned = jnp.concatenate(parts, axis=1).astype(F32)
        rows_ref[:, 2 * width :] = jnp.transpose(turned).astype(BF16)
        product = nn(normed_refs[at][...], rows_ref[...])
        if at == 0:
            total_ref[:, :wide] = product
        else:
            total_ref[:, :wide] = total_ref[:, :wide] + product
    row = iota((total_ref.shape[0], BUCKETS), 0) % pieces
    buckets = jnp.zeros((total_ref.shape[0], BUCKETS), F32)
    for head in range(heads):
        buckets = jnp.where(row == head, bucket_ref[head, :, :BUCKETS], buckets)
    total_ref[:, wide:] = buckets
    split_rows(place_ref[0], total_ref, mine_ref, other_ref)


def rows_body(
    groups, heads, place_ref, landed_ref, w_ref, gain_ref, out_ref, gain_out_ref, bucket_ref
):
    sources, _, columns = landed_ref.shape
    width = (columns - BUCKETS) // 3
    size = width // heads
    features = groups * width
    for group in range(groups):
        total = landed_ref[group].astype(F32)
        for expert in range(1, sources // groups):
            total = total + landed_ref[expert * groups + group].astype(F32)
        out_ref[:, group * width : (group + 1) * width] = total[:, 2 * width : 3 * width]
        for head in range(heads):
            for part in range(2):
                source = head * 2 * size + part * size
                first = (part + 1) * features + group * width + head * size
                out_ref[:, first : first + size] = total[:, source : source + size]
    sums = jnp.sum(w_ref[...].astype(F32) * out_ref[...], axis=1, keepdims=True)
    gain_out_ref[...] = sums / gain_ref[...].astype(F32)
    buckets = jnp.zeros((landed_ref.shape[1], BUCKETS), F32)
    for expert in range(sources // groups):
        buckets = buckets + landed_ref[expert * groups + place_ref[1]][:, 3 * width :].astype(F32)
    bucket_ref[...] = buckets[:heads]


def finish_body(groups, heads, place_ref, tokens_ref, gain_ref, w_ref, residual_ref, *refs):
    piece_refs = refs[:groups]
    out_ref, turned_ref, k_all, v_all = refs[groups:]
    height, features = tokens_ref.shape
    width = features // groups
    size = width // heads
    group = place_ref[1]
    for at in range(groups):
        piece = piece_refs[at]
        first = pl.multiple_of((at ^ group) * width, width)
        for half in range(height // LANES):
            source = heads * height + half * width
            turned_ref[pl.ds(first, width), half * LANES : (half + 1) * LANES] = piece[
                source : source + width, :
            ].astype(F32)
        for head in range(heads):
            both = piece[head * height : (head + 1) * height, :]
            lanes = slice(head * size, (head + 1) * size)
            k_all[at ^ group, :, lanes] = both[:, :size]
            v_all[at ^ group, :, lanes] = both[:, size:]
    grad_normed = nt(jnp.transpose(turned_ref[...]).astype(BF16), w_ref[:, :features])
    for part, source in ((1, k_all), (2, v_all)):
        joined = jnp.concatenate([source[at] for at in range(groups)], axis=1)
        grad_normed = grad_normed + nt(joined, w_ref[:, part * features : (part + 1) * features])
    tokens = tokens_ref[...].astype(F32)
    inverse = lax.rsqrt(jnp.mean(tokens * tokens, axis=-1, keepdims=True) + EPSILON)
    unit = tokens * inverse
    grad_unit = grad_normed * gain_ref[...].astype(F32)[None, :]
    grad = inverse * (grad_unit - unit * jnp.mean(grad_unit * unit, axis=-1, keepdims=True))
    out_ref[...] = (residual_ref[...] + grad).astype(BF16)


def strip_body(table_ref, strips_ref):
    heads, rows, height = strips_ref.shape
    used = rows - height
    offset = iota((used, LANES), 0) - 2 * height
    onehot = (bucket_of(offset) == iota((used, LANES), 1)).astype(BF16)
    lane = iota((used, height), 1)
    blank = jnp.zeros((height, height), F32)
    for head in range(heads):
        values = nn(onehot, table_ref[head])
        moved = 1
        while moved < height:
            values = jnp.where((lane & moved) != 0, pltpu.roll(values, moved, 0), values)
            moved *= 2
        strips_ref[head, :height] = blank
        strips_ref[head, height:used] = values[height:]
        strips_ref[head, used:] = blank


def diagonal_body(counts, *refs):
    calls = len(counts)
    out_ref = refs[2 * calls]
    places = [(call_at, inner) for call_at in range(calls) for inner in range(counts[call_at])]
    height = refs[0].shape[2]
    total_rows = 5 * height
    lane = iota((total_rows, height), 1)
    offset = iota((total_rows, LANES), 0) - 2 * height
    table = (bucket_of(offset) == iota((total_rows, LANES), 1)).astype(F32)
    lane_out = iota((1, LANES), 1)
    blank = jnp.zeros((height, height), F32)
    for head, (call_at, inner) in enumerate(places):
        diag_ref, far_ref = refs[call_at].at[inner], refs[calls + call_at].at[inner]
        values = jnp.concatenate([blank, diag_ref[height : 4 * height, :], blank], axis=0)
        moved = 1
        while moved < height:
            values = jnp.where(
                (lane & moved) != 0, pltpu.roll(values, total_rows - moved, 0), values
            )
            moved *= 2
        sums = jnp.sum(values, axis=1, keepdims=True)
        by_bucket = jnp.sum(sums * table, axis=0, keepdims=True)
        by_bucket = by_bucket + jnp.where(
            lane_out == FAR_LEFT, jnp.sum(far_ref[0]) + jnp.sum(diag_ref[:height, :]), 0.0
        )
        out_ref[head] = by_bucket + jnp.where(
            lane_out == FAR_RIGHT, jnp.sum(far_ref[1]) + jnp.sum(diag_ref[4 * height :, :]), 0.0
        )


def split_rows(place, source_ref, mine_ref, other_ref):
    experts_all, pieces, columns = mine_ref.shape
    for parity in range(2):

        @pl.when(place == parity)
        def _():
            for at in range(experts_all):
                for target, which in ((mine_ref, parity), (other_ref, 1 - parity)):
                    first = (2 * at + which) * pieces
                    target[at] = source_ref[first : first + pieces, :].astype(BF16)


def weights_body(
    experts,
    place_ref,
    branch_ref,
    attended_ref,
    normed_ref,
    logits_ref,
    gain_ref,
    mine_ref,
    other_ref,
    packed_ref,
):
    features = branch_ref.shape[1]
    extra = logits_ref.shape[1]
    branch = jnp.transpose(branch_ref[...].astype(F32)).astype(BF16)
    packed_ref[:, :features] = nt(branch, attended_ref[...])
    normed = jnp.transpose(normed_ref[...].astype(F32)).astype(BF16)
    column = jnp.transpose(gain_ref[...])[:, :1]
    packed_ref[:, features:] = nn(normed, logits_ref[...]) + jnp.where(
        iota((features, extra), 1) == experts, column, 0.0
    )
    split_rows(place_ref[0], packed_ref, mine_ref, other_ref)


def exchange(moving, axis):
    return lax.all_to_all(moving, axis, split_axis=0, concat_axis=0, tiled=True)


def cross(moving, axis, distance):
    size = lax.axis_size(axis)
    return lax.ppermute(moving, axis, [(i, i ^ distance) for i in range(size)])


def trade(pieces):
    return [
        piece if at == 0 else cross(piece, "context", at) for at, piece in enumerate(pieces)
    ]


def after(values, *others):
    return lax.optimization_barrier((values,) + others)[0]


def per_device(
    tokens_in,
    gain_attn,
    w_qkv,
    rel_bias,
    w_out,
    gain_ffn,
    w_router,
    w_up,
    w_down,
    segments,
    routes,
    cotangent,
):
    groups = lax.axis_size("context")
    tensor_size = lax.axis_size("tensor")
    expert_size = lax.axis_size("expert")
    height, features = tokens_in.shape
    heads = rel_bias.shape[0]
    width = features // groups
    size = width // heads
    length = segments.shape[1]
    spans = length // height
    experts_all = expert_size * groups
    capacity = max(2, 5 * height // (4 * experts_all))
    plan = slot_plan(capacity, features)
    slots = experts_all * plan[0]
    columns = 2 * features + (2 * features // plan[2] if plan[1] else 0)
    piece_rows = heads * height + height // LANES * width
    place = lax.axis_index("tensor")
    context_at = lax.axis_index("context")
    place_arg = jnp.stack([place, context_at]).astype(jnp.int32)
    square = features * features

    projected = run(
        functools.partial(project_body, heads),
        [shape((piece_rows, LANES))] * groups + [shape((features, height))],
        (place_arg, tokens_in, gain_attn, w_qkv),
        scratch=[pltpu.VMEM((groups, piece_rows, LANES), BF16)],
        smem=(0,),
        flops=6 * height * square,
        moved=8 * square,
    )
    own = trade(projected[:groups])
    table = jnp.pad(rel_bias, ((0, 0), (0, LANES - rel_bias.shape[1])))
    table = jnp.broadcast_to(table[:, :, None], (heads, LANES, height))
    strips = run(
        strip_body,
        shape((heads, 5 * height, height), F32),
        (table,),
        flops=heads * 2 * 4 * height * LANES * height,
        moved=heads * 4 * 5 * height * height,
    )
    far = [cross(after(piece, strips), "tensor", 1) for piece in own]
    head_flops = 4 * groups * height * length * size

    def fixed(dims):
        return pl.BlockSpec(dims, lambda h, n=len(dims): (0,) * n)

    def by_head(dims, first=0):
        return pl.BlockSpec(
            (1,) + dims, lambda h, n=len(dims), f=first: (h + f,) + (0,) * n
        )

    def head_rows(first=0):
        return pl.BlockSpec((size, height), lambda h, f=first: (h + f, 0))

    smem = pl.BlockSpec(memory_space=pltpu.SMEM)
    held_dims = [
        (groups, size, height),
        (groups, 8, height),
        (length, LANES),
        (length, LANES),
        (groups, spans, height, height),
    ]
    held_kinds = [F32, F32, BF16, BF16, BF16]
    outs = pl.pallas_call(
        functools.partial(forward_body, groups, heads),
        out_shape=[shape((width, height))] * groups
        + [shape((heads,) + dims, kind) for dims, kind in zip(held_dims, held_kinds)],
        grid=(heads,),
        in_specs=[smem, smem, fixed((1, length)), by_head((5 * height, height))]
        + [fixed((piece_rows, LANES))] * (2 * groups),
        out_specs=[head_rows()] * groups + [by_head(dims) for dims in held_dims],
        scratch_shapes=[
            pltpu.VMEM((length, LANES), BF16),
            pltpu.VMEM((spans, height), jnp.int32),
            pltpu.VMEM((spans, size + 16, height), BF16),
            pltpu.VMEM((2, spans, height, height), F32),
        ],
        cost_estimate=pl.CostEstimate(
            flops=6 * heads * head_flops, bytes_accessed=20 * square, transcendentals=0
        ),
        compiler_params=pltpu.CompilerParams(vmem_limit_bytes=VMEM_LIMIT),
    )(place_arg, rel_bias.astype(F32), segments, strips, *own, *far)
    attended = trade(outs[:groups])
    exact, inverse, vaug, kaug, weights = outs[groups:]
    route_row = routes.reshape(1, height)
    normed_all = trade([after(projected[groups], *own)] * groups)
    residual, normed_ffn, router, sent, attended_t = run(
        functools.partial(route_body, groups, capacity, plan),
        [
            shape((height, features), F32),
            shape((height, features)),
            shape((height, experts_all), F32),
            shape((slots, columns)),
            shape((features, height)),
        ],
        (
            after(place_arg, *normed_all),
            tokens_in,
            w_out,
            gain_ffn,
            w_router.T,
            route_row,
            cotangent,
            *attended,
        ),
        smem=(0,),
        flops=2 * height * square,
        moved=4 * square,
    )

    def move_slots(moving):
        return exchange(
            moving.reshape(experts_all, plan[0], columns), ("expert", "context")
        ).reshape(slots, columns)

    got = move_slots(sent)
    pieces = features // (experts_all * tensor_size)
    first_piece = (
        (lax.axis_index("expert") * groups + context_at) * tensor_size + place
    ) * pieces
    first_piece = after(first_piece, sent)
    own_w = lax.dynamic_slice_in_dim(w_qkv, first_piece, pieces, 0)
    own_gain = lax.dynamic_slice_in_dim(gain_attn, first_piece, pieces, 0).reshape(pieces, 1)
    turned, kt = run(
        functools.partial(turn_body, groups, heads),
        [shape((heads, groups, height, LANES)), shape((heads, size + 16, length))],
        (after(kaug, sent), *own),
        flops=2 * square,
        moved=4 * square,
    )
    back, rows_in, act_other, act_mine, hid_other, hid_mine = run_expert(
        after(place_arg, turned, own_w, own_gain), got, w_up[0], w_down[0], plan
    )
    returned = move_slots(back)

    def both(values, sent_values):
        return jnp.concatenate([values, cross(sent_values, "tensor", 1)], axis=0)

    all_rows = both(rows_in, rows_in)
    grad_down = tn(both(act_mine, act_other), all_rows[:, features:])
    grad_up = tn(all_rows[:, :features], both(hid_mine, hid_other))
    extra = -(-(experts_all + 1) // LANES) * LANES
    outs = run(
        functools.partial(combine_body, groups, capacity, plan),
        [
            shape((height, features)),
            shape((height, features), F32),
            shape((height, features)),
            shape((height, extra)),
            shape((8, features), F32),
        ]
        + [shape((width, height))] * groups,
        (
            after(place_arg, grad_down, grad_up),
            returned,
            residual,
            router,
            route_row,
            cotangent,
            gain_ffn,
            w_router.T,
            w_out,
        ),
        scratch=[pltpu.VMEM((features, height), BF16)],
        smem=(0,),
        flops=4 * height * square,
        moved=8 * square,
    )
    mixed_out, grad_residual, branch, grad_logits, gain_sums = outs[:5]
    grad_pieces = trade(outs[5:])
    mine, other = run(
        functools.partial(weights_body, experts_all),
        [shape((experts_all, pieces, features + extra))] * 2,
        (place_arg, branch, attended_t, normed_ffn, grad_logits, gain_sums),
        scratch=[pltpu.VMEM((features, features + extra), F32)],
        smem=(0,),
        flops=2 * height * square,
        moved=8 * square,
    )

    def pair_sum(kept, received):
        return (kept.astype(F32) + received.astype(F32)).astype(BF16)

    packed = pair_sum(mine, cross(other, "tensor", 1))
    packed_landed = exchange(packed, ("expert", "context"))
    counts = (heads - 1, 1)
    mine_kv, got_kv, q_grads, diags, fars = [], [], [], [], []
    for call_at in range(len(counts)):
        first, count = sum(counts[:call_at]), counts[call_at]
        dims = [
            (groups, size, height),
            (groups, height, 2 * size),
            (groups, height, 2 * size),
            (5 * height, height),
            (2, spans, height),
        ]
        outs = pl.pallas_call(
            functools.partial(backward_body, groups),
            out_shape=[
                shape((count,) + of, kind)
                for of, kind in zip(dims, [BF16, BF16, BF16, F32, F32])
            ],
            grid=(count,),
            in_specs=[smem]
            + [
                by_head(of, first)
                for of in (
                    held_dims[4],
                    held_dims[2],
                    (size + 16, length),
                    held_dims[0],
                    held_dims[1],
                )
            ]
            + [by_head((groups, height, LANES), first)]
            + [head_rows(first)] * groups,
            out_specs=[by_head(of) for of in dims],
            scratch_shapes=[pltpu.VMEM((length, LANES), F32)]
            + [pltpu.VMEM((length, height), F32)] * 2
            + [pltpu.VMEM((length, height), BF16)] * 2,
            cost_estimate=pl.CostEstimate(
                flops=8 * count * head_flops, bytes_accessed=20 * square, transcendentals=0
            ),
            compiler_params=pltpu.CompilerParams(vmem_limit_bytes=VMEM_LIMIT),
        )(after(place_arg, packed), weights, vaug, kt, exact, inverse, turned, *grad_pieces)
        q_grads.append(outs[0])
        mine_kv.append(outs[1])
        got_kv.append(cross(outs[2], "tensor", 1))
        diags.append(outs[3])
        fars.append(outs[4])
    joined = run(
        functools.partial(join_body, counts),
        [shape((piece_rows, LANES))] * groups,
        (*mine_kv, after(got_kv[0], packed_landed), *got_kv[1:], *q_grads),
        moved=4 * groups * piece_rows * LANES,
    )
    landed_pieces = trade(joined)
    by_bucket = run(
        functools.partial(diagonal_body, counts),
        shape((heads, 1, LANES), F32),
        (*diags, *fars),
        flops=heads * 8 * 7 * height * height,
        moved=heads * 20 * height * height,
    )
    mine, other = run(
        functools.partial(qkv_body, groups, heads),
        [shape((experts_all, pieces, 3 * width + BUCKETS))] * 2,
        (after(place_arg, landed_pieces[1], landed_pieces[3]), *normed_all, *joined, by_bucket),
        scratch=[
            pltpu.VMEM((features, 3 * width + BUCKETS), F32),
            pltpu.VMEM((height, 3 * width), BF16),
        ],
        smem=(0,),
        flops=6 * groups * height * features * width,
        moved=8 * square,
    )
    summed = pair_sum(mine, cross(other, "tensor", 1))
    landed = exchange(after(summed, *landed_pieces), ("expert", "context"))
    grad_qkv, grad_gain_attn, grad_rel = run(
        functools.partial(rows_body, groups, heads),
        [
            shape((pieces, 3 * features), F32),
            shape((pieces, 1), F32),
            shape((heads, BUCKETS), F32),
        ],
        (place_arg, landed, own_w, own_gain),
        smem=(0,),
        moved=2 * landed.size,
    )
    grad_tokens = run(
        functools.partial(finish_body, groups, heads),
        shape((height, features)),
        (place_arg, tokens_in, gain_attn, w_qkv, grad_residual, *landed_pieces),
        scratch=[
            pltpu.VMEM((features, height), F32),
            pltpu.VMEM((groups, height, width), BF16),
            pltpu.VMEM((groups, height, width), BF16),
        ],
        smem=(0,),
        flops=6 * height * square,
        moved=8 * square,
    )
    reduced = jnp.sum(packed_landed.astype(F32), axis=0)
    return (
        mixed_out,
        grad_tokens,
        grad_gain_attn[:, 0],
        grad_qkv,
        grad_rel,
        reduced[:, :features].T,
        reduced[:, features + experts_all],
        reduced[:, features : features + experts_all],
        grad_up[None],
        grad_down[None],
    )


def solution(mesh):
    rows = ("expert", "context", "tensor")
    in_specs = (
        P(rows, None),
        P(),
        P(),
        P("context", None),
        P(),
        P(),
        P(),
        P(("expert", "context"), None, None),
        P(("expert", "context"), None, None),
        P("expert", None),
        P(rows, None),
        P(rows, None),
    )
    out_specs = (
        P(rows, None),
        P(rows, None),
        P(rows),
        P(rows, None),
        P("context", None),
        P(None, rows),
        P(rows),
        P(rows, None),
        P(("expert", "context"), None, "tensor"),
        P(("expert", "context"), "tensor", None),
    )
    return jax.shard_map(
        per_device, mesh=mesh, in_specs=in_specs, out_specs=out_specs, check_vma=False
    )
```

```python
import functools

import jax
import jax.numpy as jnp
from jax import lax
from jax.experimental import pallas as pl
from jax.experimental.pallas import tpu as pltpu
from jax.sharding import PartitionSpec as P

EPSILON = 1e-06
THRESHOLDS = (12, 16, 23, 32, 46, 64, 91)
FAR_LEFT = 15
FAR_RIGHT = 31
EXCLUDED = -1e30
LANES = 128
BF16 = jnp.bfloat16
F32 = jnp.float32
VMEM_LIMIT = 56 * 1024 * 1024
BUCKETS = 32
CHUNK = 768
PART = 256


def bucket_of(offset):
    distance = jnp.abs(offset)
    beyond = jnp.zeros_like(distance)
    for threshold in THRESHOLDS:
        beyond = beyond + (distance >= threshold).astype(jnp.int32)
    nearby = jnp.where(distance < 8, distance, 8 + beyond)
    return nearby + 16 * (offset > 0).astype(jnp.int32)


def nn(left, right):
    return lax.dot_general(left, right, (((1,), (0,)), ((), ())), preferred_element_type=F32)


def nt(left, right):
    return lax.dot_general(left, right, (((1,), (1,)), ((), ())), preferred_element_type=F32)


def tn(left, right):
    return lax.dot_general(left, right, (((0,), (0,)), ((), ())), preferred_element_type=F32)


def iota(shape, axis):
    return lax.broadcasted_iota(jnp.int32, shape, axis)


def three_terms(values):
    high = values.astype(BF16).astype(F32)
    middle = (values - high).astype(BF16).astype(F32)
    return high, middle, values - high - middle


def specs_for(count, smem=()):
    return [
        pl.BlockSpec(memory_space=pltpu.SMEM if i in smem else pltpu.VMEM) for i in range(count)
    ]


def run(body, out_shape, args, scratch=(), smem=(), flops=0, moved=0, limit=VMEM_LIMIT):
    return pl.pallas_call(
        body,
        out_shape=out_shape,
        in_specs=specs_for(len(args), smem),
        scratch_shapes=list(scratch),
        cost_estimate=pl.CostEstimate(flops=flops, bytes_accessed=moved, transcendentals=0),
        compiler_params=pltpu.CompilerParams(vmem_limit_bytes=limit),
    )(*args)


def shape(dims, kind=BF16):
    return jax.ShapeDtypeStruct(dims, kind)


def project_body(heads, place_ref, tokens_ref, gain_ref, w_ref, *refs):
    groups = len(refs) - 2
    piece_refs, normed_ref, all_ref = refs[:groups], refs[groups], refs[groups + 1]
    height, features = tokens_ref.shape
    width = features // groups
    size = width // heads
    group = place_ref[1]
    tokens = tokens_ref[...].astype(F32)
    inverse = lax.rsqrt(jnp.mean(tokens * tokens, axis=-1, keepdims=True) + EPSILON)
    normed = (tokens * inverse * gain_ref[...].astype(F32)[None, :]).astype(BF16)
    normed_ref[...] = jnp.transpose(normed.astype(F32)).astype(BF16)
    turned = jnp.transpose(nn(normed, w_ref[:, :features])).astype(BF16)
    keys = nn(normed, w_ref[:, features : 2 * features]).astype(BF16)
    values = nn(normed, w_ref[:, 2 * features :]).astype(BF16)
    for at in range(groups):
        for head in range(heads):
            lanes = slice(at * width + head * size, at * width + (head + 1) * size)
            all_ref[at ^ group, head * height : (head + 1) * height, :] = jnp.concatenate(
                [keys[:, lanes], values[:, lanes]], axis=1
            )
        for half in range(height // LANES):
            first = heads * height + half * width
            all_ref[at ^ group, first : first + width, :] = turned[
                at * width : (at + 1) * width, half * LANES : (half + 1) * LANES
            ]
    for at in range(groups):
        piece_refs[at][...] = all_ref[at]


def q_rows(piece_ref, heads, height, size, head):
    width = heads * size
    parts = []
    for half in range(height // LANES):
        first = heads * height + half * width + head * size
        parts.append(piece_ref[pl.ds(pl.multiple_of(first, 16), size), :])
    return jnp.concatenate(parts, axis=1)


def forward_body(groups, heads, place_ref, bias_ref, seg_ref, strip_ref, *refs):
    own_refs, far_refs, out_refs = (refs[i * groups : (i + 1) * groups] for i in range(3))
    exact_ref, inverse_ref, vaug_ref, kaug_ref, weight_ref = refs[3 * groups : 3 * groups + 5]
    extra_all, docs_all, vt_ref, score_ref = refs[3 * groups + 5 :]
    size, height = out_refs[0].shape
    spans = kaug_ref.shape[1] // height
    place, group = place_ref[0], place_ref[1]
    head = pl.program_id(0)
    tall = size + 16
    rest = LANES - size

    @pl.when(head == 0)
    def _():
        row = iota((LANES, height), 0) - size
        for span in range(spans):
            docs = seg_ref[0:1, span * height : (span + 1) * height]
            docs_all[span : span + 1, :] = docs
            extra = jnp.where((row >= 0) & (row < 3) & (docs != row), EXCLUDED, 0.0)
            extra = jnp.where(row - 3 == span, 1.0, extra)
            extra_all[span * height : (span + 1) * height, :] = jnp.transpose(extra).astype(BF16)

    row, column = iota((tall, LANES), 0), iota((tall, LANES), 1)
    pick_v = (((row < size) & (row + size == column)) | ((row == size) & (column == 0))).astype(
        BF16
    )
    lane = iota((height, LANES), 1)
    low_half = lane < size
    ones = jnp.where(lane < 3, 1.0, 0.0).astype(BF16)
    extra_row = iota((rest, height), 0)
    queries_all = []
    for at in range(groups):
        block = at ^ group
        for source, parity in ((own_refs[at], place), (far_refs[at], 1 - place)):
            span = 2 * block + parity
            rows = pl.ds(pl.multiple_of(span * height, height), height)
            both = source[pl.ds(pl.multiple_of(head * height, height), height), :]
            keys = jnp.where(low_half, both, extra_all[rows, :])
            values = jnp.where(low_half, ones, both)
            kaug_ref[0, rows, :] = keys
            vaug_ref[0, rows, :] = values
            vt_ref[span] = nt(pick_v, values).astype(BF16)
        span = 2 * block + place
        docs = docs_all[pl.ds(span, 1), :]
        apart = extra_row - 3 - span
        far = jnp.where(
            apart <= -2,
            bias_ref[head, FAR_LEFT],
            jnp.where(apart >= 2, bias_ref[head, FAR_RIGHT], 0.0),
        )
        extra = jnp.where(
            extra_row < 3,
            jnp.where(docs == extra_row, 1.0, 0.0),
            jnp.where(extra_row < 3 + spans, far, 0.0),
        )
        queries_all.append(
            jnp.concatenate(
                [q_rows(own_refs[at], heads, height, size, head), extra.astype(BF16)], axis=0
            )
        )
    for at in range(groups):
        span = 2 * (at ^ group) + place
        start = jnp.clip(span - 1, 0, spans - 3)
        queries = queries_all[at]
        slot = at % 2
        row_max = None
        for step in range(spans):
            key_span = (start + step) if step < 3 else ((start + step) & (spans - 1))
            rows = pl.ds(pl.multiple_of(key_span * height, height), height)
            scores = nn(kaug_ref[0, rows, :], queries)
            if step < 3:
                level = pl.multiple_of((key_span - span + 2) * height, height)
                scores = scores + strip_ref[0, pl.ds(level, height), :]
            score_ref[slot, step] = scores
            best = jnp.max(scores, axis=0, keepdims=True)
            row_max = best if row_max is None else jnp.maximum(row_max, best)
        total = jnp.zeros((tall, height), F32)
        for step in range(spans):
            key_span = (start + step) if step < 3 else ((start + step) & (spans - 1))
            weights = jnp.exp(score_ref[slot, step] - row_max).astype(BF16)
            weight_ref[0, at, key_span] = weights
            total = total + nn(vt_ref[key_span], weights)
        inverse = 1.0 / total[size : size + 1]
        result = total[:size] * inverse
        out_refs[at][...] = result.astype(BF16)
        exact_ref[0, at] = result
        inverse_ref[0, at] = jnp.broadcast_to(inverse, (8, height))


def turn_body(groups, heads, kaug_ref, *refs):
    piece_refs, out_ref, kt_ref = refs[:groups], refs[groups], refs[groups + 1]
    height = out_ref.shape[2]
    size = out_ref.shape[3] // 2
    spans = kaug_ref.shape[1] // height
    row, column = iota((size + 16, LANES), 0), iota((size + 16, LANES), 1)
    pick_k = (
        ((row < size) & (row == column))
        | ((row >= size) & (row < size + spans) & (row + 3 == column))
    ).astype(BF16)
    blank = jnp.zeros((size, height), F32)
    for head in range(heads):
        kt_ref[head] = nt(pick_k, kaug_ref[head]).astype(BF16)
        for at in range(groups):
            queries = q_rows(piece_refs[at], heads, height, size, head).astype(F32)
            out_ref[head, at] = jnp.transpose(jnp.concatenate([queries, blank], axis=0)).astype(
                BF16
            )


def backward_body(groups, place_ref, *refs):
    weight_ref, vaug_ref, kt_ref, exact_ref, inverse_ref, q_ref = refs[:6]
    grad_refs = refs[6 : 6 + groups]
    dq_ref, mine_ref, other_ref, diag_ref, far_ref, dkv_ref = refs[6 + groups : 12 + groups]
    slope_refs, score_refs = refs[12 + groups : 14 + groups], refs[14 + groups :]
    size, height = grad_refs[0].shape
    length = vaug_ref.shape[1]
    spans = length // height
    place, group = place_ref[0], place_ref[1]
    diag_ref[...] = jnp.zeros_like(diag_ref)
    extra_row = iota((LANES - size, height), 0)
    blank = jnp.zeros((size, height), F32)
    span_row = iota((spans, height), 0)
    left_total = jnp.zeros((spans, height), F32)
    right_total = jnp.zeros((spans, height), F32)
    for at in range(groups):
        span = 2 * (at ^ group) + place
        start = jnp.clip(span - 1, 0, spans - 3)
        slope_ref, score_ref = slope_refs[at % 2], score_refs[at % 2]
        grads = (grad_refs[at][...].astype(F32) * inverse_ref[0, at, 0:1]).astype(BF16)
        grads32 = grads.astype(F32)
        delta = jnp.sum(grads32 * exact_ref[0, at], axis=0, keepdims=True)
        high, middle, low = three_terms(-delta)
        extra = jnp.where(
            extra_row == 0,
            high,
            jnp.where(extra_row == 1, middle, jnp.where(extra_row == 2, low, 0.0)),
        )
        slope_ref[...] = nn(
            vaug_ref[0], jnp.concatenate([extra.astype(BF16), grads], axis=0)
        )
        turned = jnp.transpose(jnp.concatenate([blank, grads32], axis=0)).astype(BF16)
        sides = jnp.concatenate([q_ref[0, at], turned], axis=0)
        for key in range(spans):
            rows = slice(key * height, (key + 1) * height)
            score_ref[rows, :] = (
                weight_ref[0, at, key].astype(F32) * slope_ref[rows, :]
            ).astype(BF16)
        both = jnp.concatenate(
            [score_ref[...], weight_ref[0, at].reshape(length, height)], axis=1
        )
        product = nn(both, sides)
        if at == 0:
            dkv_ref[...] = product
        else:
            dkv_ref[...] = dkv_ref[...] + product
        total = nn(kt_ref[0], score_ref[...])
        dq_ref[0, at] = total[:size].astype(BF16)
        sums = total[size : size + spans]
        left_total = left_total + jnp.where(span_row < start, sums, 0.0)
        right_total = right_total + jnp.where(span_row >= start + 3, sums, 0.0)
        rows = pl.ds(pl.multiple_of(start * height, height), 3 * height)
        level = pl.ds(pl.multiple_of((start - span + 2) * height, height), 3 * height)
        diag_ref[0, level, :] = diag_ref[0, level, :] + score_ref[rows, :].astype(F32)
    far_ref[0, 0] = left_total
    far_ref[0, 1] = right_total
    for at in range(groups):
        for target, parity in ((mine_ref, place), (other_ref, 1 - place)):
            first = pl.multiple_of((2 * (at ^ group) + parity) * height, height)
            target[0, at] = dkv_ref[pl.ds(first, height), :].astype(BF16)


def join_body(counts, *refs):
    calls = len(counts)
    mine_refs, got_refs, dq_refs = (refs[i * calls : (i + 1) * calls] for i in range(3))
    piece_refs = refs[3 * calls :]
    size, height = dq_refs[0].shape[2:]
    heads = sum(counts)
    width = heads * size
    for at, piece_ref in enumerate(piece_refs):
        head = 0
        for call_at, count in enumerate(counts):
            for inner in range(count):
                kept = mine_refs[call_at][inner, at].astype(F32)
                piece_ref[head * height : (head + 1) * height, :] = (
                    kept + got_refs[call_at][inner, at].astype(F32)
                ).astype(BF16)
                for half in range(height // LANES):
                    first = heads * height + half * width + head * size
                    piece_ref[first : first + size, :] = dq_refs[call_at][
                        inner, at, :, half * LANES : (half + 1) * LANES
                    ]
                head += 1


def slot_plan(capacity, features):
    base = capacity // 16 * 16
    left = capacity - base
    if base and left and 16 % left == 0 and (2 * features) % (LANES * (16 // left)) == 0:
        return base, left, 16 // left
    return -(-capacity // 8) * 8, 0, 0


def slot_marks(shape_of, axis, chosen, rank, capacity, plan):
    base, left, parts = plan
    position = iota(shape_of, axis)
    limit = base if left else capacity
    marks = [jnp.where(position == jnp.where(rank < limit, chosen * base + rank, -1), 1.0, 0.0)]
    spare = rank - base
    for part in range(parts):
        slot = chosen * 16 + part * left + spare
        slot = jnp.where((spare >= 0) & (spare < left), slot, -1)
        marks.append(jnp.where(position == slot, 1.0, 0.0))
    return [mark.astype(BF16) for mark in marks]


def route_body(
    groups,
    capacity,
    plan,
    place_ref,
    tokens_ref,
    w_out_ref,
    gain_ref,
    w_router_ref,
    route_row_ref,
    cotangent_ref,
    *refs,
):
    pieces = refs[:groups]
    residual_ref, normed_ref, router_ref, sent_ref, grad_sent_ref, attended_ref = refs[groups:]
    height, features = tokens_ref.shape
    experts = w_router_ref.shape[0]
    slots = sent_ref.shape[0]
    width = pieces[0].shape[0]
    group = place_ref[1]
    for at in range(groups):
        first = pl.multiple_of((at ^ group) * width, width)
        attended_ref[pl.ds(first, width), :] = pieces[at][...]
    residual = tokens_ref[...].astype(F32) + tn(attended_ref[...], w_out_ref[...])
    residual_ref[...] = residual
    inverse = lax.rsqrt(jnp.mean(residual * residual, axis=-1, keepdims=True) + EPSILON)
    normed = (residual * inverse * gain_ref[...].astype(F32)[None, :]).astype(BF16)
    normed_ref[...] = normed
    logits = nt(normed, w_router_ref[...])
    powers = jnp.exp(logits - jnp.max(logits, axis=-1, keepdims=True))
    router = powers / jnp.sum(powers, axis=-1, keepdims=True)
    router_ref[...] = router
    chosen = route_row_ref[...]
    marks = iota((experts, height), 0) == chosen
    onehot = jnp.transpose(jnp.where(marks, 1.0, 0.0))
    gate = jnp.sum(onehot * router, axis=-1, keepdims=True)
    grad_expert = (gate * cotangent_ref[...].astype(F32)).astype(BF16)
    rows = jnp.concatenate([normed, grad_expert], axis=1)
    earlier = (iota((height, height), 0) < iota((height, height), 1)).astype(BF16)
    before = nn(jnp.where(marks, 1.0, 0.0).astype(BF16), earlier)
    rank = jnp.sum(jnp.where(marks, before, 0.0), axis=0, keepdims=True).astype(jnp.int32)
    dispatch = slot_marks((slots, height), 0, chosen, rank, capacity, plan)
    sent_ref[:, :features] = nn(dispatch[0], normed).astype(BF16)
    grad_sent_ref[...] = nn(dispatch[0], grad_expert).astype(BF16)
    if plan[1]:
        span = 2 * features // plan[2]
        spare = nn(dispatch[1], rows[:, :span])
        for part in range(1, plan[2]):
            spare = spare + nn(dispatch[1 + part], rows[:, part * span : (part + 1) * span])
        sent_ref[:, features:] = spare.astype(BF16)


def spare_marks(sources, plan):
    base, left, parts = plan
    target = iota((sources * left, sources * 16), 0)
    origin = iota((sources * left, sources * 16), 1)
    source = target // left
    return [
        (origin == source * 16 + part * left + (target - source * left)).astype(BF16)
        for part in range(parts)
    ]


def unpack_spare(rows_ref, packed, plan, first_part):
    main = packed.shape[0]
    marks = spare_marks(main // 16, plan)
    half = plan[2] // 2
    span = rows_ref.shape[1] // half
    for part in range(half):
        rows_ref[main:, part * span : (part + 1) * span] = nn(
            marks[first_part + part], packed
        ).astype(BF16)


def add_up(total_ref, step, product):
    @pl.when(step == 0)
    def _():
        total_ref[...] = product

    @pl.when(step > 0)
    def _():
        total_ref[...] = total_ref[...] + product


def store_half(step, steps, values_ref, other_ref, mine_ref):
    @pl.when(step < steps // 2)
    def _():
        other_ref[...] = values_ref[...]

    @pl.when(step >= steps // 2)
    def _():
        mine_ref[...] = values_ref[...]


def expert_forward_body(
    plan,
    place_ref,
    got_ref,
    up_ref,
    down_ref,
    back_ref,
    spare_ref,
    rows_ref,
    slope_ref,
    other_ref,
    mine_ref,
    total_ref,
    active_ref,
):
    step, steps = pl.program_id(0), pl.num_programs(0)
    main, features = back_ref.shape

    @pl.when(step == 0)
    def _():
        rows_ref[:main, :] = got_ref[:, :features]
        if plan[1]:
            unpack_spare(rows_ref, got_ref[:, features:], plan, 0)

    for first in range(0, up_ref.shape[1], PART):
        lanes = slice(first, first + PART)
        hidden = nn(rows_ref[...], up_ref[:, lanes])
        below = 0.5 * (1.0 + lax.erf(hidden * (2.0**-0.5)))
        bell = jnp.exp(-0.5 * hidden * hidden) * 0.3989422804014327
        active_ref[:, lanes] = (hidden * below).astype(BF16)
        slope_ref[:, lanes] = (below + hidden * bell).astype(BF16)
    add_up(total_ref, step, nn(active_ref[...], down_ref[...]))
    store_half(step, steps, active_ref, other_ref, mine_ref)

    @pl.when(step == steps - 1)
    def _():
        back_ref[...] = total_ref[:main, :].astype(BF16)
        if plan[1]:
            spare_ref[...] = total_ref[main:, :].astype(BF16)
        else:
            spare_ref[...] = jnp.zeros_like(spare_ref)


def expert_backward_body(
    plan,
    place_ref,
    got_ref,
    up_ref,
    down_ref,
    slope_ref,
    packed_ref,
    spare_ref,
    back_ref,
    rows_ref,
    other_ref,
    mine_ref,
    total_ref,
    hidden_ref,
):
    step, steps = pl.program_id(0), pl.num_programs(0)
    main, features = got_ref.shape

    @pl.when(step == 0)
    def _():
        rows_ref[:main, :] = got_ref[...]
        if plan[1]:
            unpack_spare(rows_ref, packed_ref[:, features:], plan, plan[2] // 2)

    for first in range(0, up_ref.shape[1], PART):
        lanes = slice(first, first + PART)
        grad_active = nt(rows_ref[...], down_ref[lanes, :])
        hidden_ref[:, lanes] = (grad_active * slope_ref[:, lanes].astype(F32)).astype(BF16)
    add_up(total_ref, step, nt(hidden_ref[...], up_ref[...]))
    store_half(step, steps, hidden_ref, other_ref, mine_ref)

    @pl.when(step == steps - 1)
    def _():
        back_ref[:, :features] = total_ref[:main, :].astype(BF16)
        if plan[1]:
            spare = jnp.concatenate(
                [spare_ref[...], total_ref[main:, :].astype(BF16)], axis=1
            )
            span = 2 * features // plan[2]
            packed = jnp.zeros((main, span), F32)
            for part, marks in enumerate(spare_marks(main // 16, plan)):
                packed = packed + tn(marks, spare[:, part * span : (part + 1) * span])
            back_ref[:, features:] = packed.astype(BF16)


def run_expert(plan, place_arg, got, up, down, forward):
    main = got.shape[0]
    features, hidden_size = up.shape
    chunk = CHUNK
    steps = hidden_size // chunk
    half = steps // 2
    spare = main // 16 * plan[1]
    slots = main + spare
    columns = features + (2 * features // plan[2] if plan[1] else 0)
    spare = max(spare, 8)

    def piece(step, place):
        return lax.rem(step + half * (1 - place[0]), steps)

    def fixed(dims):
        return pl.BlockSpec(dims, lambda i, p: (0, 0))

    halves = [
        pl.BlockSpec((slots, chunk), lambda i, p: (0, jnp.minimum(i, half - 1))),
        pl.BlockSpec((slots, chunk), lambda i, p: (0, jnp.maximum(i - half, 0))),
    ]
    sloping = pl.BlockSpec((slots, chunk), lambda i, p: (0, i))
    weight_specs = [
        pl.BlockSpec((features, chunk), lambda i, p: (0, piece(i, p))),
        pl.BlockSpec((chunk, features), lambda i, p: (piece(i, p), 0)),
    ]
    half_shapes = [shape((slots, hidden_size // 2))] * 2
    if forward is None:
        body = expert_forward_body
        args = (got, up, down)
        in_specs = [fixed((main, columns))] + weight_specs
        out_specs = [fixed((main, features)), fixed((spare, features)), fixed((slots, features))]
        out_specs += [sloping] + halves
        out_shape = [shape((main, features)), shape((spare, features)), shape((slots, features))]
        out_shape += [shape((slots, hidden_size))] + half_shapes
        flops = 0
    else:
        body = expert_backward_body
        args = (got, up, down) + forward
        in_specs = [fixed((main, features))] + weight_specs
        in_specs += [sloping, fixed((main, columns)), fixed((spare, features))]
        out_specs = [fixed((main, columns)), fixed((slots, features))] + halves
        out_shape = [shape((main, columns)), shape((slots, features))] + half_shapes
        flops = 4 * slots * features * hidden_size
    return pl.pallas_call(
        functools.partial(body, plan),
        out_shape=out_shape,
        grid_spec=pltpu.PrefetchScalarGridSpec(
            num_scalar_prefetch=1,
            grid=(steps,),
            in_specs=in_specs,
            out_specs=out_specs,
            scratch_shapes=[
                pltpu.VMEM((slots, features), F32),
                pltpu.VMEM((slots, chunk), BF16),
            ],
        ),
        cost_estimate=pl.CostEstimate(flops=flops, bytes_accessed=flops // 400, transcendentals=0),
        compiler_params=pltpu.CompilerParams(vmem_limit_bytes=VMEM_LIMIT),
    )(place_arg, *args)


def combine_body(
    groups,
    capacity,
    plan,
    place_ref,
    produced_ref,
    got_ref,
    residual_ref,
    router_ref,
    route_row_ref,
    cotangent_ref,
    gain_ref,
    w_router_ref,
    w_out_ref,
    mixed_ref,
    grad_residual_ref,
    branch_ref,
    logits_ref,
    gain_out_ref,
    *refs,
):
    pieces, turned_ref = refs[:groups], refs[groups]
    height, experts = router_ref.shape
    features = residual_ref.shape[1]
    slots = got_ref.shape[0]
    width = pieces[0].shape[0]
    group = place_ref[1]
    chosen_row = route_row_ref[...]
    marks = jnp.where(iota((experts, height), 0) == chosen_row, 1.0, 0.0)
    earlier = (iota((height, height), 0) < iota((height, height), 1)).astype(BF16)
    before = nn(marks.astype(BF16), earlier)
    rank_row = jnp.sum(marks * before, axis=0, keepdims=True)
    onehot = jnp.transpose(marks) > 0.5
    pair_row = iota((8, height), 0)
    pairs = jnp.transpose(jnp.where(pair_row == 0, chosen_row.astype(F32), rank_row))
    chosen = pairs[:, 0:1].astype(jnp.int32)
    rank = pairs[:, 1:2].astype(jnp.int32)
    combine = slot_marks((height, slots), 1, chosen, rank, capacity, plan)
    back = jnp.concatenate(
        [nn(combine[0], produced_ref[...]), nn(combine[0], got_ref[:, :features])], axis=1
    )
    if plan[1]:
        spare = got_ref[:, features:]
        back = back + jnp.concatenate([nn(marks, spare) for marks in combine[1:]], axis=1)
    router = router_ref[...]
    gate = jnp.sum(jnp.where(onehot, router, 0.0), axis=-1, keepdims=True)
    residual = residual_ref[...]
    inverse = lax.rsqrt(jnp.mean(residual * residual, axis=-1, keepdims=True) + EPSILON)
    unit = residual * inverse
    grad_mixed = cotangent_ref[...].astype(F32)
    gathered = back[:, :features]
    mixed_ref[...] = (residual + gate * gathered).astype(BF16)
    grad_gate = jnp.sum(grad_mixed * gathered, axis=-1, keepdims=True)
    grad_logits = (router * (jnp.where(onehot, grad_gate, 0.0) - gate * grad_gate)).astype(BF16)
    grad_normed = back[:, features:] + nn(grad_logits, w_router_ref[...])
    grad_unit = grad_normed * gain_ref[...].astype(F32)[None, :]
    grad_residual = grad_mixed + inverse * (
        grad_unit - unit * jnp.mean(grad_unit * unit, axis=-1, keepdims=True)
    )
    branch = grad_residual.astype(BF16)
    turned_ref[...] = nt(w_out_ref[...], branch).astype(BF16)
    for at in range(groups):
        first = pl.multiple_of((at ^ group) * width, width)
        pieces[at][...] = turned_ref[pl.ds(first, width), :]
    grad_residual_ref[...] = grad_residual
    branch_ref[...] = branch
    spare_lanes = logits_ref.shape[1] - experts
    logits_ref[...] = jnp.concatenate([grad_logits, jnp.zeros((height, spare_lanes), BF16)], axis=1)
    sums = jnp.sum(grad_normed * unit, axis=0, keepdims=True)
    gain_out_ref[...] = jnp.broadcast_to(sums, gain_out_ref.shape)


def qkv_body(groups, heads, place_ref, *refs):
    normed_refs, piece_refs = refs[:groups], refs[groups : 2 * groups]
    bucket_ref, mine_ref, other_ref, total_ref, rows_ref = refs[2 * groups :]
    pieces = mine_ref.shape[1]
    wide = rows_ref.shape[1]
    height = normed_refs[0].shape[1]
    width = rows_ref.shape[1] // 3
    for at in range(groups):
        piece = piece_refs[at]
        for head in range(heads):
            rows_ref[:, head * LANES : (head + 1) * LANES] = piece[
                head * height : (head + 1) * height, :
            ]
        parts = [
            piece[heads * height + half * width : heads * height + (half + 1) * width, :]
            for half in range(height // LANES)
        ]
        turned = jnp.concatenate(parts, axis=1).astype(F32)
        rows_ref[:, 2 * width :] = jnp.transpose(turned).astype(BF16)
        product = nn(normed_refs[at][...], rows_ref[...])
        if at == 0:
            total_ref[:, :wide] = product
        else:
            total_ref[:, :wide] = total_ref[:, :wide] + product
    row = iota((total_ref.shape[0], BUCKETS), 0) % pieces
    buckets = jnp.zeros((total_ref.shape[0], BUCKETS), F32)
    for head in range(heads):
        buckets = jnp.where(row == head, bucket_ref[head, :, :BUCKETS], buckets)
    total_ref[:, wide:] = buckets
    split_rows(place_ref[0], total_ref, mine_ref, other_ref)


def rows_body(
    groups, heads, place_ref, landed_ref, w_ref, gain_ref, out_ref, gain_out_ref, bucket_ref
):
    sources, _, columns = landed_ref.shape
    width = (columns - BUCKETS) // 3
    size = width // heads
    features = groups * width
    for group in range(groups):
        total = landed_ref[group].astype(F32)
        for expert in range(1, sources // groups):
            total = total + landed_ref[expert * groups + group].astype(F32)
        out_ref[:, group * width : (group + 1) * width] = total[:, 2 * width : 3 * width]
        for head in range(heads):
            for part in range(2):
                source = head * 2 * size + part * size
                first = (part + 1) * features + group * width + head * size
                out_ref[:, first : first + size] = total[:, source : source + size]
    sums = jnp.sum(w_ref[...].astype(F32) * out_ref[...], axis=1, keepdims=True)
    gain_out_ref[...] = sums / gain_ref[...].astype(F32)
    buckets = jnp.zeros((landed_ref.shape[1], BUCKETS), F32)
    for expert in range(sources // groups):
        buckets = buckets + landed_ref[expert * groups + place_ref[1]][:, 3 * width :].astype(F32)
    bucket_ref[...] = buckets[:heads]


def finish_body(groups, heads, place_ref, tokens_ref, gain_ref, w_ref, residual_ref, *refs):
    piece_refs = refs[:groups]
    out_ref, turned_ref, k_all, v_all = refs[groups:]
    height, features = tokens_ref.shape
    width = features // groups
    size = width // heads
    group = place_ref[1]
    for at in range(groups):
        piece = piece_refs[at]
        first = pl.multiple_of((at ^ group) * width, width)
        for half in range(height // LANES):
            source = heads * height + half * width
            turned_ref[pl.ds(first, width), half * LANES : (half + 1) * LANES] = piece[
                source : source + width, :
            ].astype(F32)
        for head in range(heads):
            both = piece[head * height : (head + 1) * height, :]
            lanes = slice(head * size, (head + 1) * size)
            k_all[at ^ group, :, lanes] = both[:, :size]
            v_all[at ^ group, :, lanes] = both[:, size:]
    grad_normed = nt(jnp.transpose(turned_ref[...]).astype(BF16), w_ref[:, :features])
    for part, source in ((1, k_all), (2, v_all)):
        joined = jnp.concatenate([source[at] for at in range(groups)], axis=1)
        grad_normed = grad_normed + nt(joined, w_ref[:, part * features : (part + 1) * features])
    tokens = tokens_ref[...].astype(F32)
    inverse = lax.rsqrt(jnp.mean(tokens * tokens, axis=-1, keepdims=True) + EPSILON)
    unit = tokens * inverse
    grad_unit = grad_normed * gain_ref[...].astype(F32)[None, :]
    grad = inverse * (grad_unit - unit * jnp.mean(grad_unit * unit, axis=-1, keepdims=True))
    out_ref[...] = (residual_ref[...] + grad).astype(BF16)


def strip_body(table_ref, strips_ref):
    heads, rows, height = strips_ref.shape
    used = rows - height
    offset = iota((used, LANES), 0) - 2 * height
    onehot = (bucket_of(offset) == iota((used, LANES), 1)).astype(BF16)
    lane = iota((used, height), 1)
    blank = jnp.zeros((height, height), F32)
    for head in range(heads):
        values = nn(onehot, table_ref[head])
        moved = 1
        while moved < height:
            values = jnp.where((lane & moved) != 0, pltpu.roll(values, moved, 0), values)
            moved *= 2
        strips_ref[head, :height] = blank
        strips_ref[head, height:used] = values[height:]
        strips_ref[head, used:] = blank


def diagonal_body(counts, *refs):
    calls = len(counts)
    out_ref = refs[2 * calls]
    places = [(call_at, inner) for call_at in range(calls) for inner in range(counts[call_at])]
    height = refs[0].shape[2]
    total_rows = 5 * height
    lane = iota((total_rows, height), 1)
    offset = iota((total_rows, LANES), 0) - 2 * height
    table = (bucket_of(offset) == iota((total_rows, LANES), 1)).astype(F32)
    lane_out = iota((1, LANES), 1)
    blank = jnp.zeros((height, height), F32)
    for head, (call_at, inner) in enumerate(places):
        diag_ref, far_ref = refs[call_at].at[inner], refs[calls + call_at].at[inner]
        values = jnp.concatenate([blank, diag_ref[height : 4 * height, :], blank], axis=0)
        moved = 1
        while moved < height:
            values = jnp.where(
                (lane & moved) != 0, pltpu.roll(values, total_rows - moved, 0), values
            )
            moved *= 2
        sums = jnp.sum(values, axis=1, keepdims=True)
        by_bucket = jnp.sum(sums * table, axis=0, keepdims=True)
        by_bucket = by_bucket + jnp.where(
            lane_out == FAR_LEFT, jnp.sum(far_ref[0]) + jnp.sum(diag_ref[:height, :]), 0.0
        )
        out_ref[head] = by_bucket + jnp.where(
            lane_out == FAR_RIGHT, jnp.sum(far_ref[1]) + jnp.sum(diag_ref[4 * height :, :]), 0.0
        )


def split_rows(place, source_ref, mine_ref, other_ref):
    experts_all, pieces, columns = mine_ref.shape
    for parity in range(2):

        @pl.when(place == parity)
        def _():
            for at in range(experts_all):
                for target, which in ((mine_ref, parity), (other_ref, 1 - parity)):
                    first = (2 * at + which) * pieces
                    target[at] = source_ref[first : first + pieces, :].astype(BF16)


def weights_body(
    experts,
    place_ref,
    branch_ref,
    attended_ref,
    normed_ref,
    logits_ref,
    gain_ref,
    mine_ref,
    other_ref,
    packed_ref,
):
    features = branch_ref.shape[1]
    extra = logits_ref.shape[1]
    branch = jnp.transpose(branch_ref[...].astype(F32)).astype(BF16)
    packed_ref[:, :features] = nt(branch, attended_ref[...])
    normed = jnp.transpose(normed_ref[...].astype(F32)).astype(BF16)
    column = jnp.transpose(gain_ref[...])[:, :1]
    packed_ref[:, features:] = nn(normed, logits_ref[...]) + jnp.where(
        iota((features, extra), 1) == experts, column, 0.0
    )
    split_rows(place_ref[0], packed_ref, mine_ref, other_ref)


def exchange(moving, axis):
    return lax.all_to_all(moving, axis, split_axis=0, concat_axis=0, tiled=True)


def cross(moving, axis, distance):
    size = lax.axis_size(axis)
    return lax.ppermute(moving, axis, [(i, i ^ distance) for i in range(size)])


def trade(pieces):
    return [
        piece if at == 0 else cross(piece, "context", at) for at, piece in enumerate(pieces)
    ]


def after(values, *others):
    return lax.optimization_barrier((values,) + others)[0]


def per_device(
    tokens_in,
    gain_attn,
    w_qkv,
    rel_bias,
    w_out,
    gain_ffn,
    w_router,
    w_up,
    w_down,
    segments,
    routes,
    cotangent,
):
    groups = lax.axis_size("context")
    tensor_size = lax.axis_size("tensor")
    expert_size = lax.axis_size("expert")
    height, features = tokens_in.shape
    heads = rel_bias.shape[0]
    width = features // groups
    size = width // heads
    length = segments.shape[1]
    spans = length // height
    experts_all = expert_size * groups
    capacity = max(2, 5 * height // (4 * experts_all))
    plan = slot_plan(capacity, features)
    slots = experts_all * plan[0]
    columns = features + (2 * features // plan[2] if plan[1] else 0)
    piece_rows = heads * height + height // LANES * width
    place = lax.axis_index("tensor")
    context_at = lax.axis_index("context")
    place_arg = jnp.stack([place, context_at]).astype(jnp.int32)
    square = features * features

    projected = run(
        functools.partial(project_body, heads),
        [shape((piece_rows, LANES))] * groups + [shape((features, height))],
        (place_arg, tokens_in, gain_attn, w_qkv),
        scratch=[pltpu.VMEM((groups, piece_rows, LANES), BF16)],
        smem=(0,),
        flops=6 * height * square,
        moved=8 * square,
    )
    own = trade(projected[:groups])
    table = jnp.pad(rel_bias, ((0, 0), (0, LANES - rel_bias.shape[1])))
    table = jnp.broadcast_to(table[:, :, None], (heads, LANES, height))
    strips = run(
        strip_body,
        shape((heads, 5 * height, height), F32),
        (table,),
        flops=heads * 2 * 4 * height * LANES * height,
        moved=heads * 4 * 5 * height * height,
    )
    far = [cross(after(piece, strips), "tensor", 1) for piece in own]
    head_flops = 4 * groups * height * length * size

    def fixed(dims):
        return pl.BlockSpec(dims, lambda h, n=len(dims): (0,) * n)

    def by_head(dims, first=0):
        return pl.BlockSpec(
            (1,) + dims, lambda h, n=len(dims), f=first: (h + f,) + (0,) * n
        )

    def head_rows(first=0):
        return pl.BlockSpec((size, height), lambda h, f=first: (h + f, 0))

    smem = pl.BlockSpec(memory_space=pltpu.SMEM)
    held_dims = [
        (groups, size, height),
        (groups, 8, height),
        (length, LANES),
        (length, LANES),
        (groups, spans, height, height),
    ]
    held_kinds = [F32, F32, BF16, BF16, BF16]
    outs = pl.pallas_call(
        functools.partial(forward_body, groups, heads),
        out_shape=[shape((width, height))] * groups
        + [shape((heads,) + dims, kind) for dims, kind in zip(held_dims, held_kinds)],
        grid=(heads,),
        in_specs=[smem, smem, fixed((1, length)), by_head((5 * height, height))]
        + [fixed((piece_rows, LANES))] * (2 * groups),
        out_specs=[head_rows()] * groups + [by_head(dims) for dims in held_dims],
        scratch_shapes=[
            pltpu.VMEM((length, LANES), BF16),
            pltpu.VMEM((spans, height), jnp.int32),
            pltpu.VMEM((spans, size + 16, height), BF16),
            pltpu.VMEM((2, spans, height, height), F32),
        ],
        cost_estimate=pl.CostEstimate(
            flops=6 * heads * head_flops, bytes_accessed=20 * square, transcendentals=0
        ),
        compiler_params=pltpu.CompilerParams(vmem_limit_bytes=VMEM_LIMIT),
    )(place_arg, rel_bias.astype(F32), segments, strips, *own, *far)
    attended = trade(outs[:groups])
    exact, inverse, vaug, kaug, weights = outs[groups:]
    route_row = routes.reshape(1, height)
    normed_all = trade([after(projected[groups], *own)] * groups)
    residual, normed_ffn, router, sent, grad_sent, attended_t = run(
        functools.partial(route_body, groups, capacity, plan),
        [
            shape((height, features), F32),
            shape((height, features)),
            shape((height, experts_all), F32),
            shape((slots, columns)),
            shape((slots, features)),
            shape((features, height)),
        ],
        (
            after(place_arg, *normed_all),
            tokens_in,
            w_out,
            gain_ffn,
            w_router.T,
            route_row,
            cotangent,
            *attended,
        ),
        smem=(0,),
        flops=2 * height * square,
        moved=4 * square,
    )

    def move_slots(moving):
        return exchange(
            moving.reshape(experts_all, plan[0], -1), ("expert", "context")
        ).reshape(moving.shape)

    got = move_slots(sent)
    grad_got = move_slots(grad_sent)
    pieces = features // (experts_all * tensor_size)
    first_piece = (
        (lax.axis_index("expert") * groups + context_at) * tensor_size + place
    ) * pieces
    first_piece = after(first_piece, sent)
    own_w = lax.dynamic_slice_in_dim(w_qkv, first_piece, pieces, 0)
    own_gain = lax.dynamic_slice_in_dim(gain_attn, first_piece, pieces, 0).reshape(pieces, 1)
    turned, kt = run(
        functools.partial(turn_body, groups, heads),
        [shape((heads, groups, height, LANES)), shape((heads, size + 16, length))],
        (after(kaug, sent), *own),
        flops=2 * square,
        moved=4 * square,
    )
    produced, spare, rows_in, slope, act_other, act_mine = run_expert(
        plan, after(place_arg, turned, own_w, own_gain), got, w_up[0], w_down[0], None
    )
    produced_back = move_slots(produced)
    back, grad_rows, hid_other, hid_mine = run_expert(
        plan, place_arg, grad_got, w_up[0], w_down[0], (slope, got, spare)
    )
    returned = move_slots(back)

    def both(values, sent_values):
        return jnp.concatenate([values, cross(sent_values, "tensor", 1)], axis=0)

    grad_down = tn(both(act_mine, act_other), both(grad_rows, grad_rows))
    grad_up = tn(both(rows_in, rows_in), both(hid_mine, hid_other))
    extra = -(-(experts_all + 1) // LANES) * LANES
    outs = run(
        functools.partial(combine_body, groups, capacity, plan),
        [
            shape((height, features)),
            shape((height, features), F32),
            shape((height, features)),
            shape((height, extra)),
            shape((8, features), F32),
        ]
        + [shape((width, height))] * groups,
        (
            after(place_arg, grad_down, grad_up),
            produced_back,
            returned,
            residual,
            router,
            route_row,
            cotangent,
            gain_ffn,
            w_router.T,
            w_out,
        ),
        scratch=[pltpu.VMEM((features, height), BF16)],
        smem=(0,),
        flops=4 * height * square,
        moved=8 * square,
    )
    mixed_out, grad_residual, branch, grad_logits, gain_sums = outs[:5]
    grad_pieces = trade(outs[5:])
    mine, other = run(
        functools.partial(weights_body, experts_all),
        [shape((experts_all, pieces, features + extra))] * 2,
        (place_arg, branch, attended_t, normed_ffn, grad_logits, gain_sums),
        scratch=[pltpu.VMEM((features, features + extra), F32)],
        smem=(0,),
        flops=2 * height * square,
        moved=8 * square,
    )

    def pair_sum(kept, received):
        return (kept.astype(F32) + received.astype(F32)).astype(BF16)

    packed = pair_sum(mine, cross(other, "tensor", 1))
    packed_landed = exchange(packed, ("expert", "context"))
    counts = (heads - 1, 1)
    mine_kv, got_kv, q_grads, diags, fars = [], [], [], [], []
    for call_at in range(len(counts)):
        first, count = sum(counts[:call_at]), counts[call_at]
        dims = [
            (groups, size, height),
            (groups, height, 2 * size),
            (groups, height, 2 * size),
            (5 * height, height),
            (2, spans, height),
        ]
        outs = pl.pallas_call(
            functools.partial(backward_body, groups),
            out_shape=[
                shape((count,) + of, kind)
                for of, kind in zip(dims, [BF16, BF16, BF16, F32, F32])
            ],
            grid=(count,),
            in_specs=[smem]
            + [
                by_head(of, first)
                for of in (
                    held_dims[4],
                    held_dims[2],
                    (size + 16, length),
                    held_dims[0],
                    held_dims[1],
                )
            ]
            + [by_head((groups, height, LANES), first)]
            + [head_rows(first)] * groups,
            out_specs=[by_head(of) for of in dims],
            scratch_shapes=[pltpu.VMEM((length, LANES), F32)]
            + [pltpu.VMEM((length, height), F32)] * 2
            + [pltpu.VMEM((length, height), BF16)] * 2,
            cost_estimate=pl.CostEstimate(
                flops=8 * count * head_flops, bytes_accessed=20 * square, transcendentals=0
            ),
            compiler_params=pltpu.CompilerParams(vmem_limit_bytes=VMEM_LIMIT),
        )(after(place_arg, packed), weights, vaug, kt, exact, inverse, turned, *grad_pieces)
        q_grads.append(outs[0])
        mine_kv.append(outs[1])
        got_kv.append(cross(outs[2], "tensor", 1))
        diags.append(outs[3])
        fars.append(outs[4])
    joined = run(
        functools.partial(join_body, counts),
        [shape((piece_rows, LANES))] * groups,
        (*mine_kv, after(got_kv[0], packed_landed), *got_kv[1:], *q_grads),
        moved=4 * groups * piece_rows * LANES,
    )
    landed_pieces = trade(joined)
    by_bucket = run(
        functools.partial(diagonal_body, counts),
        shape((heads, 1, LANES), F32),
        (*diags, *fars),
    )
    mine, other = run(
        functools.partial(qkv_body, groups, heads),
        [shape((experts_all, pieces, 3 * width + BUCKETS))] * 2,
        (place_arg, *normed_all, *joined, by_bucket),
        scratch=[
            pltpu.VMEM((features, 3 * width + BUCKETS), F32),
            pltpu.VMEM((height, 3 * width), BF16),
        ],
        smem=(0,),
    )
    summed = pair_sum(mine, cross(after(other, *landed_pieces), "tensor", 1))
    landed = exchange(summed, ("expert", "context"))
    grad_qkv, grad_gain_attn, grad_rel = run(
        functools.partial(rows_body, groups, heads),
        [
            shape((pieces, 3 * features), F32),
            shape((pieces, 1), F32),
            shape((heads, BUCKETS), F32),
        ],
        (place_arg, landed, own_w, own_gain),
        smem=(0,),
        moved=2 * landed.size,
    )
    grad_tokens = run(
        functools.partial(finish_body, groups, heads),
        shape((height, features)),
        (place_arg, tokens_in, gain_attn, w_qkv, grad_residual, *landed_pieces),
        scratch=[
            pltpu.VMEM((features, height), F32),
            pltpu.VMEM((groups, height, width), BF16),
            pltpu.VMEM((groups, height, width), BF16),
        ],
        smem=(0,),
        flops=6 * height * square,
        moved=8 * square,
    )
    reduced = jnp.sum(packed_landed.astype(F32), axis=0)
    return (
        mixed_out,
        grad_tokens,
        grad_gain_attn[:, 0],
        grad_qkv,
        grad_rel,
        reduced[:, :features].T,
        reduced[:, features + experts_all],
        reduced[:, features : features + experts_all],
        grad_up[None],
        grad_down[None],
    )


def solution(mesh):
    rows = ("expert", "context", "tensor")
    in_specs = (
        P(rows, None),
        P(),
        P(),
        P("context", None),
        P(),
        P(),
        P(),
        P(("expert", "context"), None, None),
        P(("expert", "context"), None, None),
        P("expert", None),
        P(rows, None),
        P(rows, None),
    )
    out_specs = (
        P(rows, None),
        P(rows, None),
        P(rows),
        P(rows, None),
        P("context", None),
        P(None, rows),
        P(rows),
        P(rows, None),
        P(("expert", "context"), None, "tensor"),
        P(("expert", "context"), "tensor", None),
    )
    return jax.shard_map(
        per_device, mesh=mesh, in_specs=in_specs, out_specs=out_specs, check_vma=False
    )
```

```python
import functools

import jax
import jax.numpy as jnp
from jax import lax
from jax.experimental import pallas as pl
from jax.experimental.pallas import tpu as pltpu
from jax.sharding import PartitionSpec as P

EPSILON = 1e-06
THRESHOLDS = (12, 16, 23, 32, 46, 64, 91)
FAR_LEFT = 15
FAR_RIGHT = 31
EXCLUDED = -1e30
LANES = 128
BF16 = jnp.bfloat16
F32 = jnp.float32
VMEM_LIMIT = 56 * 1024 * 1024
BUCKETS = 32
EXPERT_LIMIT = 36 * 1024 * 1024
PART = 256


def bucket_of(offset):
    distance = jnp.abs(offset)
    beyond = jnp.zeros_like(distance)
    for threshold in THRESHOLDS:
        beyond = beyond + (distance >= threshold).astype(jnp.int32)
    nearby = jnp.where(distance < 8, distance, 8 + beyond)
    return nearby + 16 * (offset > 0).astype(jnp.int32)


def nn(left, right):
    return lax.dot_general(left, right, (((1,), (0,)), ((), ())), preferred_element_type=F32)


def nt(left, right):
    return lax.dot_general(left, right, (((1,), (1,)), ((), ())), preferred_element_type=F32)


def tn(left, right):
    return lax.dot_general(left, right, (((0,), (0,)), ((), ())), preferred_element_type=F32)


def iota(shape, axis):
    return lax.broadcasted_iota(jnp.int32, shape, axis)


def three_terms(values):
    high = values.astype(BF16).astype(F32)
    middle = (values - high).astype(BF16).astype(F32)
    return high, middle, values - high - middle


def specs_for(count, smem=()):
    return [
        pl.BlockSpec(memory_space=pltpu.SMEM if i in smem else pltpu.VMEM) for i in range(count)
    ]


def run(body, out_shape, args, scratch=(), smem=(), flops=0, moved=0, limit=VMEM_LIMIT):
    return pl.pallas_call(
        body,
        out_shape=out_shape,
        in_specs=specs_for(len(args), smem),
        scratch_shapes=list(scratch),
        cost_estimate=pl.CostEstimate(flops=flops, bytes_accessed=moved, transcendentals=0),
        compiler_params=pltpu.CompilerParams(vmem_limit_bytes=limit),
    )(*args)


def shape(dims, kind=BF16):
    return jax.ShapeDtypeStruct(dims, kind)


def project_body(heads, place_ref, tokens_ref, gain_ref, w_ref, *refs):
    groups = len(refs) - 2
    piece_refs, normed_ref, all_ref = refs[:groups], refs[groups], refs[groups + 1]
    height, features = tokens_ref.shape
    width = features // groups
    size = width // heads
    group = place_ref[1]
    tokens = tokens_ref[...].astype(F32)
    inverse = lax.rsqrt(jnp.mean(tokens * tokens, axis=-1, keepdims=True) + EPSILON)
    normed = (tokens * inverse * gain_ref[...].astype(F32)[None, :]).astype(BF16)
    normed_ref[...] = jnp.transpose(normed.astype(F32)).astype(BF16)
    turned = jnp.transpose(nn(normed, w_ref[:, :features])).astype(BF16)
    keys = nn(normed, w_ref[:, features : 2 * features]).astype(BF16)
    values = nn(normed, w_ref[:, 2 * features :]).astype(BF16)
    for at in range(groups):
        for head in range(heads):
            lanes = slice(at * width + head * size, at * width + (head + 1) * size)
            all_ref[at ^ group, head * height : (head + 1) * height, :] = jnp.concatenate(
                [keys[:, lanes], values[:, lanes]], axis=1
            )
        for half in range(height // LANES):
            first = heads * height + half * width
            all_ref[at ^ group, first : first + width, :] = turned[
                at * width : (at + 1) * width, half * LANES : (half + 1) * LANES
            ]
    for at in range(groups):
        piece_refs[at][...] = all_ref[at]


def q_rows(piece_ref, heads, height, size, head):
    width = heads * size
    parts = []
    for half in range(height // LANES):
        first = heads * height + half * width + head * size
        parts.append(piece_ref[pl.ds(pl.multiple_of(first, 16), size), :])
    return jnp.concatenate(parts, axis=1)


def forward_body(groups, heads, place_ref, bias_ref, seg_ref, strip_ref, *refs):
    own_refs, far_refs, out_refs = (refs[i * groups : (i + 1) * groups] for i in range(3))
    exact_ref, inverse_ref, vaug_ref, kaug_ref, weight_ref = refs[3 * groups : 3 * groups + 5]
    extra_all, docs_all, vt_ref, score_ref = refs[3 * groups + 5 :]
    size, height = out_refs[0].shape
    spans = kaug_ref.shape[1] // height
    place, group = place_ref[0], place_ref[1]
    head = pl.program_id(0)
    tall = size + 16
    rest = LANES - size

    @pl.when(head == 0)
    def _():
        row = iota((LANES, height), 0) - size
        for span in range(spans):
            docs = seg_ref[0:1, span * height : (span + 1) * height]
            docs_all[span : span + 1, :] = docs
            extra = jnp.where((row >= 0) & (row < 3) & (docs != row), EXCLUDED, 0.0)
            extra = jnp.where(row - 3 == span, 1.0, extra)
            extra_all[span * height : (span + 1) * height, :] = jnp.transpose(extra).astype(BF16)

    row, column = iota((tall, LANES), 0), iota((tall, LANES), 1)
    pick_v = (((row < size) & (row + size == column)) | ((row == size) & (column == 0))).astype(
        BF16
    )
    lane = iota((height, LANES), 1)
    low_half = lane < size
    ones = jnp.where(lane < 3, 1.0, 0.0).astype(BF16)
    extra_row = iota((rest, height), 0)
    queries_all = []
    for at in range(groups):
        block = at ^ group
        for source, parity in ((own_refs[at], place), (far_refs[at], 1 - place)):
            span = 2 * block + parity
            rows = pl.ds(pl.multiple_of(span * height, height), height)
            both = source[pl.ds(pl.multiple_of(head * height, height), height), :]
            keys = jnp.where(low_half, both, extra_all[rows, :])
            values = jnp.where(low_half, ones, both)
            kaug_ref[0, rows, :] = keys
            vaug_ref[0, rows, :] = values
            vt_ref[span] = nt(pick_v, values).astype(BF16)
        span = 2 * block + place
        docs = docs_all[pl.ds(span, 1), :]
        apart = extra_row - 3 - span
        far = jnp.where(
            apart <= -2,
            bias_ref[head, FAR_LEFT],
            jnp.where(apart >= 2, bias_ref[head, FAR_RIGHT], 0.0),
        )
        extra = jnp.where(
            extra_row < 3,
            jnp.where(docs == extra_row, 1.0, 0.0),
            jnp.where(extra_row < 3 + spans, far, 0.0),
        )
        queries_all.append(
            jnp.concatenate(
                [q_rows(own_refs[at], heads, height, size, head), extra.astype(BF16)], axis=0
            )
        )
    for at in range(groups):
        span = 2 * (at ^ group) + place
        start = jnp.clip(span - 1, 0, spans - 3)
        queries = queries_all[at]
        slot = at % 2
        row_max = None
        for step in range(spans):
            key_span = (start + step) if step < 3 else ((start + step) & (spans - 1))
            rows = pl.ds(pl.multiple_of(key_span * height, height), height)
            scores = nn(kaug_ref[0, rows, :], queries)
            if step < 3:
                level = pl.multiple_of((key_span - span + 2) * height, height)
                scores = scores + strip_ref[0, pl.ds(level, height), :]
            score_ref[slot, step] = scores
            best = jnp.max(scores, axis=0, keepdims=True)
            row_max = best if row_max is None else jnp.maximum(row_max, best)
        total = jnp.zeros((tall, height), F32)
        for step in range(spans):
            key_span = (start + step) if step < 3 else ((start + step) & (spans - 1))
            weights = jnp.exp(score_ref[slot, step] - row_max).astype(BF16)
            weight_ref[0, at, key_span] = weights
            total = total + nn(vt_ref[key_span], weights)
        inverse = 1.0 / total[size : size + 1]
        result = total[:size] * inverse
        out_refs[at][...] = result.astype(BF16)
        exact_ref[0, at] = result
        inverse_ref[0, at] = jnp.broadcast_to(inverse, (8, height))


def turn_body(groups, heads, kaug_ref, *refs):
    piece_refs, out_ref, kt_ref = refs[:groups], refs[groups], refs[groups + 1]
    height = out_ref.shape[2]
    size = out_ref.shape[3] // 2
    spans = kaug_ref.shape[1] // height
    row, column = iota((size + 16, LANES), 0), iota((size + 16, LANES), 1)
    pick_k = (
        ((row < size) & (row == column))
        | ((row >= size) & (row < size + spans) & (row + 3 == column))
    ).astype(BF16)
    blank = jnp.zeros((size, height), F32)
    for head in range(heads):
        kt_ref[head] = nt(pick_k, kaug_ref[head]).astype(BF16)
        for at in range(groups):
            queries = q_rows(piece_refs[at], heads, height, size, head).astype(F32)
            out_ref[head, at] = jnp.transpose(jnp.concatenate([queries, blank], axis=0)).astype(
                BF16
            )


def backward_body(groups, place_ref, *refs):
    weight_ref, vaug_ref, kt_ref, exact_ref, inverse_ref, q_ref = refs[:6]
    grad_refs = refs[6 : 6 + groups]
    dq_ref, mine_ref, other_ref, diag_ref, far_ref, dkv_ref = refs[6 + groups : 12 + groups]
    slope_refs, score_refs = refs[12 + groups : 14 + groups], refs[14 + groups :]
    size, height = grad_refs[0].shape
    length = vaug_ref.shape[1]
    spans = length // height
    place, group = place_ref[0], place_ref[1]
    diag_ref[...] = jnp.zeros_like(diag_ref)
    extra_row = iota((LANES - size, height), 0)
    blank = jnp.zeros((size, height), F32)
    span_row = iota((spans, height), 0)
    left_total = jnp.zeros((spans, height), F32)
    right_total = jnp.zeros((spans, height), F32)
    for at in range(groups):
        span = 2 * (at ^ group) + place
        start = jnp.clip(span - 1, 0, spans - 3)
        slope_ref, score_ref = slope_refs[at % 2], score_refs[at % 2]
        grads = (grad_refs[at][...].astype(F32) * inverse_ref[0, at, 0:1]).astype(BF16)
        grads32 = grads.astype(F32)
        delta = jnp.sum(grads32 * exact_ref[0, at], axis=0, keepdims=True)
        high, middle, low = three_terms(-delta)
        extra = jnp.where(
            extra_row == 0,
            high,
            jnp.where(extra_row == 1, middle, jnp.where(extra_row == 2, low, 0.0)),
        )
        slope_ref[...] = nn(
            vaug_ref[0], jnp.concatenate([extra.astype(BF16), grads], axis=0)
        )
        turned = jnp.transpose(jnp.concatenate([blank, grads32], axis=0)).astype(BF16)
        sides = jnp.concatenate([q_ref[0, at], turned], axis=0)
        for key in range(spans):
            rows = slice(key * height, (key + 1) * height)
            score_ref[rows, :] = (
                weight_ref[0, at, key].astype(F32) * slope_ref[rows, :]
            ).astype(BF16)
        both = jnp.concatenate(
            [score_ref[...], weight_ref[0, at].reshape(length, height)], axis=1
        )
        product = nn(both, sides)
        if at == 0:
            dkv_ref[...] = product
        else:
            dkv_ref[...] = dkv_ref[...] + product
        total = nn(kt_ref[0], score_ref[...])
        dq_ref[0, at] = total[:size].astype(BF16)
        sums = total[size : size + spans]
        left_total = left_total + jnp.where(span_row < start, sums, 0.0)
        right_total = right_total + jnp.where(span_row >= start + 3, sums, 0.0)
        rows = pl.ds(pl.multiple_of(start * height, height), 3 * height)
        level = pl.ds(pl.multiple_of((start - span + 2) * height, height), 3 * height)
        diag_ref[0, level, :] = diag_ref[0, level, :] + score_ref[rows, :].astype(F32)
    far_ref[0, 0] = left_total
    far_ref[0, 1] = right_total
    for at in range(groups):
        for target, parity in ((mine_ref, place), (other_ref, 1 - place)):
            first = pl.multiple_of((2 * (at ^ group) + parity) * height, height)
            target[0, at] = dkv_ref[pl.ds(first, height), :].astype(BF16)


def join_body(counts, *refs):
    calls = len(counts)
    mine_refs, got_refs, dq_refs = (refs[i * calls : (i + 1) * calls] for i in range(3))
    piece_refs = refs[3 * calls :]
    size, height = dq_refs[0].shape[2:]
    heads = sum(counts)
    width = heads * size
    for at, piece_ref in enumerate(piece_refs):
        head = 0
        for call_at, count in enumerate(counts):
            for inner in range(count):
                kept = mine_refs[call_at][inner, at].astype(F32)
                piece_ref[head * height : (head + 1) * height, :] = (
                    kept + got_refs[call_at][inner, at].astype(F32)
                ).astype(BF16)
                for half in range(height // LANES):
                    first = heads * height + half * width + head * size
                    piece_ref[first : first + size, :] = dq_refs[call_at][
                        inner, at, :, half * LANES : (half + 1) * LANES
                    ]
                head += 1


def slot_plan(capacity, features):
    base = capacity // 16 * 16
    left = capacity - base
    if base and left and 16 % left == 0 and (2 * features) % (LANES * (16 // left)) == 0:
        return base, left, 16 // left
    return -(-capacity // 8) * 8, 0, 0


def slot_marks(shape_of, axis, chosen, rank, capacity, plan):
    base, left, parts = plan
    position = iota(shape_of, axis)
    limit = base if left else capacity
    marks = [jnp.where(position == jnp.where(rank < limit, chosen * base + rank, -1), 1.0, 0.0)]
    spare = rank - base
    for part in range(parts):
        slot = chosen * 16 + part * left + spare
        slot = jnp.where((spare >= 0) & (spare < left), slot, -1)
        marks.append(jnp.where(position == slot, 1.0, 0.0))
    return [mark.astype(BF16) for mark in marks]


def route_body(
    groups,
    capacity,
    plan,
    place_ref,
    tokens_ref,
    w_out_ref,
    gain_ref,
    w_router_ref,
    route_row_ref,
    cotangent_ref,
    *refs,
):
    pieces = refs[:groups]
    residual_ref, normed_ref, router_ref, sent_ref, grad_sent_ref, attended_ref = refs[groups:]
    height, features = tokens_ref.shape
    experts = w_router_ref.shape[0]
    slots = sent_ref.shape[0]
    width = pieces[0].shape[0]
    group = place_ref[1]
    for at in range(groups):
        first = pl.multiple_of((at ^ group) * width, width)
        attended_ref[pl.ds(first, width), :] = pieces[at][...]
    residual = tokens_ref[...].astype(F32) + tn(attended_ref[...], w_out_ref[...])
    residual_ref[...] = residual
    inverse = lax.rsqrt(jnp.mean(residual * residual, axis=-1, keepdims=True) + EPSILON)
    normed = (residual * inverse * gain_ref[...].astype(F32)[None, :]).astype(BF16)
    normed_ref[...] = normed
    logits = nt(normed, w_router_ref[...])
    powers = jnp.exp(logits - jnp.max(logits, axis=-1, keepdims=True))
    router = powers / jnp.sum(powers, axis=-1, keepdims=True)
    router_ref[...] = router
    chosen = route_row_ref[...]
    marks = iota((experts, height), 0) == chosen
    onehot = jnp.transpose(jnp.where(marks, 1.0, 0.0))
    gate = jnp.sum(onehot * router, axis=-1, keepdims=True)
    grad_expert = (gate * cotangent_ref[...].astype(F32)).astype(BF16)
    rows = jnp.concatenate([normed, grad_expert], axis=1)
    earlier = (iota((height, height), 0) < iota((height, height), 1)).astype(BF16)
    before = nn(jnp.where(marks, 1.0, 0.0).astype(BF16), earlier)
    rank = jnp.sum(jnp.where(marks, before, 0.0), axis=0, keepdims=True).astype(jnp.int32)
    dispatch = slot_marks((slots, height), 0, chosen, rank, capacity, plan)
    sent_ref[:, :features] = nn(dispatch[0], normed).astype(BF16)
    grad_sent_ref[...] = nn(dispatch[0], grad_expert).astype(BF16)
    if plan[1]:
        span = 2 * features // plan[2]
        spare = nn(dispatch[1], rows[:, :span])
        for part in range(1, plan[2]):
            spare = spare + nn(dispatch[1 + part], rows[:, part * span : (part + 1) * span])
        sent_ref[:, features:] = spare.astype(BF16)


def spare_marks(sources, plan):
    base, left, parts = plan
    target = iota((sources * left, sources * 16), 0)
    origin = iota((sources * left, sources * 16), 1)
    source = target // left
    return [
        (origin == source * 16 + part * left + (target - source * left)).astype(BF16)
        for part in range(parts)
    ]


def unpack_spare(rows_ref, packed, plan, first_part):
    main = packed.shape[0]
    marks = spare_marks(main // 16, plan)
    half = plan[2] // 2
    span = rows_ref.shape[1] // half
    for part in range(half):
        rows_ref[main:, part * span : (part + 1) * span] = nn(
            marks[first_part + part], packed
        ).astype(BF16)


def expert_forward_body(
    plan,
    place_ref,
    got_ref,
    up_ref,
    down_ref,
    back_ref,
    spare_ref,
    rows_ref,
    slope_ref,
    other_ref,
    mine_ref,
    total_ref,
):
    main, features = back_ref.shape
    hidden_size = up_ref.shape[1]
    half = hidden_size // 2
    rows_ref[:main, :] = got_ref[:, :features]
    if plan[1]:
        unpack_spare(rows_ref, got_ref[:, features:], plan, 0)
    for at, active_ref in enumerate((other_ref, mine_ref)):
        start = (1 - place_ref[0]) * half if at == 0 else place_ref[0] * half
        for first in range(0, half, PART):
            lanes = pl.ds(pl.multiple_of(start + first, PART), PART)
            hidden = nn(rows_ref[...], up_ref[:, lanes])
            below = 0.5 * (1.0 + lax.erf(hidden * (2.0**-0.5)))
            bell = jnp.exp(-0.5 * hidden * hidden) * 0.3989422804014327
            active_ref[:, first : first + PART] = (hidden * below).astype(BF16)
            slope_ref[at, :, first : first + PART] = (below + hidden * bell).astype(BF16)
        rows = pl.ds(pl.multiple_of(start, PART), half)
        product = nn(active_ref[...], down_ref[rows, :])
        if at == 0:
            total_ref[...] = product
        else:
            total_ref[...] = total_ref[...] + product
    back_ref[...] = total_ref[:main, :].astype(BF16)
    if plan[1]:
        spare_ref[...] = total_ref[main:, :].astype(BF16)
    else:
        spare_ref[...] = jnp.zeros_like(spare_ref)


def expert_backward_body(
    plan,
    place_ref,
    got_ref,
    up_ref,
    down_ref,
    slope_ref,
    packed_ref,
    spare_ref,
    back_ref,
    rows_ref,
    other_ref,
    mine_ref,
    total_ref,
):
    main, features = got_ref.shape
    half = up_ref.shape[1] // 2
    rows_ref[:main, :] = got_ref[...]
    if plan[1]:
        unpack_spare(rows_ref, packed_ref[:, features:], plan, plan[2] // 2)
    for at, hidden_ref in enumerate((other_ref, mine_ref)):
        start = (1 - place_ref[0]) * half if at == 0 else place_ref[0] * half
        for first in range(0, half, PART):
            rows = pl.ds(pl.multiple_of(start + first, PART), PART)
            grad_active = nt(rows_ref[...], down_ref[rows, :])
            slope = slope_ref[at, :, first : first + PART].astype(F32)
            hidden_ref[:, first : first + PART] = (grad_active * slope).astype(BF16)
        lanes = pl.ds(pl.multiple_of(start, PART), half)
        product = nt(hidden_ref[...], up_ref[:, lanes])
        if at == 0:
            total_ref[...] = product
        else:
            total_ref[...] = total_ref[...] + product
    back_ref[:, :features] = total_ref[:main, :].astype(BF16)
    if plan[1]:
        spare = jnp.concatenate([spare_ref[...], total_ref[main:, :].astype(BF16)], axis=1)
        span = 2 * features // plan[2]
        packed = jnp.zeros((main, span), F32)
        for part, marks in enumerate(spare_marks(main // 16, plan)):
            packed = packed + tn(marks, spare[:, part * span : (part + 1) * span])
        back_ref[:, features:] = packed.astype(BF16)


def run_expert(plan, place_arg, got, up, down, forward):
    main = got.shape[0]
    features, hidden_size = up.shape
    spare = main // 16 * plan[1]
    slots = main + spare
    columns = features + (2 * features // plan[2] if plan[1] else 0)
    spare = max(spare, 8)
    halves = [shape((slots, hidden_size // 2))] * 2
    if forward is None:
        body = expert_forward_body
        out_shape = [shape((main, features)), shape((spare, features)), shape((slots, features))]
        out_shape += [shape((2, slots, hidden_size // 2))] + halves
        args, flops = (got, up, down), 0
    else:
        body = expert_backward_body
        out_shape = [shape((main, columns)), shape((slots, features))] + halves
        args, flops = (got, up, down) + forward, 4 * slots * features * hidden_size
    return run(
        functools.partial(body, plan),
        out_shape,
        (place_arg,) + args,
        scratch=[pltpu.VMEM((slots, features), F32)],
        smem=(0,),
        flops=flops,
        moved=flops // 400,
        limit=EXPERT_LIMIT,
    )


def combine_body(
    groups,
    capacity,
    plan,
    place_ref,
    produced_ref,
    got_ref,
    residual_ref,
    router_ref,
    route_row_ref,
    cotangent_ref,
    gain_ref,
    w_router_ref,
    w_out_ref,
    mixed_ref,
    grad_residual_ref,
    branch_ref,
    logits_ref,
    gain_out_ref,
    *refs,
):
    pieces, turned_ref = refs[:groups], refs[groups]
    height, experts = router_ref.shape
    features = residual_ref.shape[1]
    slots = got_ref.shape[0]
    width = pieces[0].shape[0]
    group = place_ref[1]
    chosen_row = route_row_ref[...]
    marks = jnp.where(iota((experts, height), 0) == chosen_row, 1.0, 0.0)
    earlier = (iota((height, height), 0) < iota((height, height), 1)).astype(BF16)
    before = nn(marks.astype(BF16), earlier)
    rank_row = jnp.sum(marks * before, axis=0, keepdims=True)
    onehot = jnp.transpose(marks) > 0.5
    pair_row = iota((8, height), 0)
    pairs = jnp.transpose(jnp.where(pair_row == 0, chosen_row.astype(F32), rank_row))
    chosen = pairs[:, 0:1].astype(jnp.int32)
    rank = pairs[:, 1:2].astype(jnp.int32)
    combine = slot_marks((height, slots), 1, chosen, rank, capacity, plan)
    back = jnp.concatenate(
        [nn(combine[0], produced_ref[...]), nn(combine[0], got_ref[:, :features])], axis=1
    )
    if plan[1]:
        spare = got_ref[:, features:]
        back = back + jnp.concatenate([nn(marks, spare) for marks in combine[1:]], axis=1)
    router = router_ref[...]
    gate = jnp.sum(jnp.where(onehot, router, 0.0), axis=-1, keepdims=True)
    residual = residual_ref[...]
    inverse = lax.rsqrt(jnp.mean(residual * residual, axis=-1, keepdims=True) + EPSILON)
    unit = residual * inverse
    grad_mixed = cotangent_ref[...].astype(F32)
    gathered = back[:, :features]
    mixed_ref[...] = (residual + gate * gathered).astype(BF16)
    grad_gate = jnp.sum(grad_mixed * gathered, axis=-1, keepdims=True)
    grad_logits = (router * (jnp.where(onehot, grad_gate, 0.0) - gate * grad_gate)).astype(BF16)
    grad_normed = back[:, features:] + nn(grad_logits, w_router_ref[...])
    grad_unit = grad_normed * gain_ref[...].astype(F32)[None, :]
    grad_residual = grad_mixed + inverse * (
        grad_unit - unit * jnp.mean(grad_unit * unit, axis=-1, keepdims=True)
    )
    branch = grad_residual.astype(BF16)
    turned_ref[...] = nt(w_out_ref[...], branch).astype(BF16)
    for at in range(groups):
        first = pl.multiple_of((at ^ group) * width, width)
        pieces[at][...] = turned_ref[pl.ds(first, width), :]
    grad_residual_ref[...] = grad_residual
    branch_ref[...] = branch
    spare_lanes = logits_ref.shape[1] - experts
    logits_ref[...] = jnp.concatenate([grad_logits, jnp.zeros((height, spare_lanes), BF16)], axis=1)
    sums = jnp.sum(grad_normed * unit, axis=0, keepdims=True)
    gain_out_ref[...] = jnp.broadcast_to(sums, gain_out_ref.shape)


def qkv_body(groups, heads, place_ref, *refs):
    normed_refs, piece_refs = refs[:groups], refs[groups : 2 * groups]
    bucket_ref, mine_ref, other_ref, total_ref, rows_ref = refs[2 * groups :]
    pieces = mine_ref.shape[1]
    wide = rows_ref.shape[1]
    height = normed_refs[0].shape[1]
    width = rows_ref.shape[1] // 3
    for at in range(groups):
        piece = piece_refs[at]
        for head in range(heads):
            rows_ref[:, head * LANES : (head + 1) * LANES] = piece[
                head * height : (head + 1) * height, :
            ]
        parts = [
            piece[heads * height + half * width : heads * height + (half + 1) * width, :]
            for half in range(height // LANES)
        ]
        turned = jnp.concatenate(parts, axis=1).astype(F32)
        rows_ref[:, 2 * width :] = jnp.transpose(turned).astype(BF16)
        product = nn(normed_refs[at][...], rows_ref[...])
        if at == 0:
            total_ref[:, :wide] = product
        else:
            total_ref[:, :wide] = total_ref[:, :wide] + product
    row = iota((total_ref.shape[0], BUCKETS), 0) % pieces
    buckets = jnp.zeros((total_ref.shape[0], BUCKETS), F32)
    for head in range(heads):
        buckets = jnp.where(row == head, bucket_ref[head, :, :BUCKETS], buckets)
    total_ref[:, wide:] = buckets
    split_rows(place_ref[0], total_ref, mine_ref, other_ref)


def rows_body(
    groups, heads, place_ref, landed_ref, w_ref, gain_ref, out_ref, gain_out_ref, bucket_ref
):
    sources, _, columns = landed_ref.shape
    width = (columns - BUCKETS) // 3
    size = width // heads
    features = groups * width
    for group in range(groups):
        total = landed_ref[group].astype(F32)
        for expert in range(1, sources // groups):
            total = total + landed_ref[expert * groups + group].astype(F32)
        out_ref[:, group * width : (group + 1) * width] = total[:, 2 * width : 3 * width]
        for head in range(heads):
            for part in range(2):
                source = head * 2 * size + part * size
                first = (part + 1) * features + group * width + head * size
                out_ref[:, first : first + size] = total[:, source : source + size]
    sums = jnp.sum(w_ref[...].astype(F32) * out_ref[...], axis=1, keepdims=True)
    gain_out_ref[...] = sums / gain_ref[...].astype(F32)
    buckets = jnp.zeros((landed_ref.shape[1], BUCKETS), F32)
    for expert in range(sources // groups):
        buckets = buckets + landed_ref[expert * groups + place_ref[1]][:, 3 * width :].astype(F32)
    bucket_ref[...] = buckets[:heads]


def finish_body(groups, heads, place_ref, tokens_ref, gain_ref, w_ref, residual_ref, *refs):
    piece_refs = refs[:groups]
    out_ref, turned_ref, k_all, v_all = refs[groups:]
    height, features = tokens_ref.shape
    width = features // groups
    size = width // heads
    group = place_ref[1]
    for at in range(groups):
        piece = piece_refs[at]
        first = pl.multiple_of((at ^ group) * width, width)
        for half in range(height // LANES):
            source = heads * height + half * width
            turned_ref[pl.ds(first, width), half * LANES : (half + 1) * LANES] = piece[
                source : source + width, :
            ].astype(F32)
        for head in range(heads):
            both = piece[head * height : (head + 1) * height, :]
            lanes = slice(head * size, (head + 1) * size)
            k_all[at ^ group, :, lanes] = both[:, :size]
            v_all[at ^ group, :, lanes] = both[:, size:]
    grad_normed = nt(jnp.transpose(turned_ref[...]).astype(BF16), w_ref[:, :features])
    for part, source in ((1, k_all), (2, v_all)):
        joined = jnp.concatenate([source[at] for at in range(groups)], axis=1)
        grad_normed = grad_normed + nt(joined, w_ref[:, part * features : (part + 1) * features])
    tokens = tokens_ref[...].astype(F32)
    inverse = lax.rsqrt(jnp.mean(tokens * tokens, axis=-1, keepdims=True) + EPSILON)
    unit = tokens * inverse
    grad_unit = grad_normed * gain_ref[...].astype(F32)[None, :]
    grad = inverse * (grad_unit - unit * jnp.mean(grad_unit * unit, axis=-1, keepdims=True))
    out_ref[...] = (residual_ref[...] + grad).astype(BF16)


def strip_body(table_ref, strips_ref):
    heads, rows, height = strips_ref.shape
    used = rows - height
    offset = iota((used, LANES), 0) - 2 * height
    onehot = (bucket_of(offset) == iota((used, LANES), 1)).astype(BF16)
    lane = iota((used, height), 1)
    blank = jnp.zeros((height, height), F32)
    for head in range(heads):
        values = nn(onehot, table_ref[head])
        moved = 1
        while moved < height:
            values = jnp.where((lane & moved) != 0, pltpu.roll(values, moved, 0), values)
            moved *= 2
        strips_ref[head, :height] = blank
        strips_ref[head, height:used] = values[height:]
        strips_ref[head, used:] = blank


def diagonal_body(counts, *refs):
    calls = len(counts)
    out_ref = refs[2 * calls]
    places = [(call_at, inner) for call_at in range(calls) for inner in range(counts[call_at])]
    height = refs[0].shape[2]
    total_rows = 5 * height
    lane = iota((total_rows, height), 1)
    offset = iota((total_rows, LANES), 0) - 2 * height
    table = (bucket_of(offset) == iota((total_rows, LANES), 1)).astype(F32)
    lane_out = iota((1, LANES), 1)
    blank = jnp.zeros((height, height), F32)
    for head, (call_at, inner) in enumerate(places):
        diag_ref, far_ref = refs[call_at].at[inner], refs[calls + call_at].at[inner]
        values = jnp.concatenate([blank, diag_ref[height : 4 * height, :], blank], axis=0)
        moved = 1
        while moved < height:
            values = jnp.where(
                (lane & moved) != 0, pltpu.roll(values, total_rows - moved, 0), values
            )
            moved *= 2
        sums = jnp.sum(values, axis=1, keepdims=True)
        by_bucket = jnp.sum(sums * table, axis=0, keepdims=True)
        by_bucket = by_bucket + jnp.where(
            lane_out == FAR_LEFT, jnp.sum(far_ref[0]) + jnp.sum(diag_ref[:height, :]), 0.0
        )
        out_ref[head] = by_bucket + jnp.where(
            lane_out == FAR_RIGHT, jnp.sum(far_ref[1]) + jnp.sum(diag_ref[4 * height :, :]), 0.0
        )


def split_rows(place, source_ref, mine_ref, other_ref):
    experts_all, pieces, columns = mine_ref.shape
    for parity in range(2):

        @pl.when(place == parity)
        def _():
            for at in range(experts_all):
                for target, which in ((mine_ref, parity), (other_ref, 1 - parity)):
                    first = (2 * at + which) * pieces
                    target[at] = source_ref[first : first + pieces, :].astype(BF16)


def weights_body(
    experts,
    place_ref,
    branch_ref,
    attended_ref,
    normed_ref,
    logits_ref,
    gain_ref,
    mine_ref,
    other_ref,
    packed_ref,
):
    features = branch_ref.shape[1]
    extra = logits_ref.shape[1]
    branch = jnp.transpose(branch_ref[...].astype(F32)).astype(BF16)
    packed_ref[:, :features] = nt(branch, attended_ref[...])
    normed = jnp.transpose(normed_ref[...].astype(F32)).astype(BF16)
    column = jnp.transpose(gain_ref[...])[:, :1]
    packed_ref[:, features:] = nn(normed, logits_ref[...]) + jnp.where(
        iota((features, extra), 1) == experts, column, 0.0
    )
    split_rows(place_ref[0], packed_ref, mine_ref, other_ref)


def exchange(moving, axis):
    return lax.all_to_all(moving, axis, split_axis=0, concat_axis=0, tiled=True)


def cross(moving, axis, distance):
    size = lax.axis_size(axis)
    return lax.ppermute(moving, axis, [(i, i ^ distance) for i in range(size)])


def trade(pieces):
    return [
        piece if at == 0 else cross(piece, "context", at) for at, piece in enumerate(pieces)
    ]


def after(values, *others):
    return lax.optimization_barrier((values,) + others)[0]


def per_device(
    tokens_in,
    gain_attn,
    w_qkv,
    rel_bias,
    w_out,
    gain_ffn,
    w_router,
    w_up,
    w_down,
    segments,
    routes,
    cotangent,
):
    groups = lax.axis_size("context")
    tensor_size = lax.axis_size("tensor")
    expert_size = lax.axis_size("expert")
    height, features = tokens_in.shape
    heads = rel_bias.shape[0]
    width = features // groups
    size = width // heads
    length = segments.shape[1]
    spans = length // height
    experts_all = expert_size * groups
    capacity = max(2, 5 * height // (4 * experts_all))
    plan = slot_plan(capacity, features)
    slots = experts_all * plan[0]
    columns = features + (2 * features // plan[2] if plan[1] else 0)
    piece_rows = heads * height + height // LANES * width
    place = lax.axis_index("tensor")
    context_at = lax.axis_index("context")
    place_arg = jnp.stack([place, context_at]).astype(jnp.int32)
    square = features * features

    projected = run(
        functools.partial(project_body, heads),
        [shape((piece_rows, LANES))] * groups + [shape((features, height))],
        (place_arg, tokens_in, gain_attn, w_qkv),
        scratch=[pltpu.VMEM((groups, piece_rows, LANES), BF16)],
        smem=(0,),
        flops=6 * height * square,
        moved=8 * square,
    )
    own = trade(projected[:groups])
    table = jnp.pad(rel_bias, ((0, 0), (0, LANES - rel_bias.shape[1])))
    table = jnp.broadcast_to(table[:, :, None], (heads, LANES, height))
    strips = run(
        strip_body,
        shape((heads, 5 * height, height), F32),
        (table,),
        flops=heads * 2 * 4 * height * LANES * height,
        moved=heads * 4 * 5 * height * height,
    )
    far = [cross(after(piece, strips), "tensor", 1) for piece in own]
    head_flops = 4 * groups * height * length * size

    def fixed(dims):
        return pl.BlockSpec(dims, lambda h, n=len(dims): (0,) * n)

    def by_head(dims, first=0):
        return pl.BlockSpec(
            (1,) + dims, lambda h, n=len(dims), f=first: (h + f,) + (0,) * n
        )

    def head_rows(first=0):
        return pl.BlockSpec((size, height), lambda h, f=first: (h + f, 0))

    smem = pl.BlockSpec(memory_space=pltpu.SMEM)
    held_dims = [
        (groups, size, height),
        (groups, 8, height),
        (length, LANES),
        (length, LANES),
        (groups, spans, height, height),
    ]
    held_kinds = [F32, F32, BF16, BF16, BF16]
    outs = pl.pallas_call(
        functools.partial(forward_body, groups, heads),
        out_shape=[shape((width, height))] * groups
        + [shape((heads,) + dims, kind) for dims, kind in zip(held_dims, held_kinds)],
        grid=(heads,),
        in_specs=[smem, smem, fixed((1, length)), by_head((5 * height, height))]
        + [fixed((piece_rows, LANES))] * (2 * groups),
        out_specs=[head_rows()] * groups + [by_head(dims) for dims in held_dims],
        scratch_shapes=[
            pltpu.VMEM((length, LANES), BF16),
            pltpu.VMEM((spans, height), jnp.int32),
            pltpu.VMEM((spans, size + 16, height), BF16),
            pltpu.VMEM((2, spans, height, height), F32),
        ],
        cost_estimate=pl.CostEstimate(
            flops=6 * heads * head_flops, bytes_accessed=20 * square, transcendentals=0
        ),
        compiler_params=pltpu.CompilerParams(vmem_limit_bytes=VMEM_LIMIT),
    )(place_arg, rel_bias.astype(F32), segments, strips, *own, *far)
    attended = trade(outs[:groups])
    exact, inverse, vaug, kaug, weights = outs[groups:]
    route_row = routes.reshape(1, height)
    normed_all = trade([after(projected[groups], *own)] * groups)
    residual, normed_ffn, router, sent, grad_sent, attended_t = run(
        functools.partial(route_body, groups, capacity, plan),
        [
            shape((height, features), F32),
            shape((height, features)),
            shape((height, experts_all), F32),
            shape((slots, columns)),
            shape((slots, features)),
            shape((features, height)),
        ],
        (
            after(place_arg, *normed_all),
            tokens_in,
            w_out,
            gain_ffn,
            w_router.T,
            route_row,
            cotangent,
            *attended,
        ),
        smem=(0,),
        flops=2 * height * square,
        moved=4 * square,
    )

    def move_slots(moving):
        return exchange(
            moving.reshape(experts_all, plan[0], -1), ("expert", "context")
        ).reshape(moving.shape)

    got = move_slots(sent)
    pieces = features // (experts_all * tensor_size)
    first_piece = (
        (lax.axis_index("expert") * groups + context_at) * tensor_size + place
    ) * pieces
    first_piece = after(first_piece, sent)
    own_w = lax.dynamic_slice_in_dim(w_qkv, first_piece, pieces, 0)
    own_gain = lax.dynamic_slice_in_dim(gain_attn, first_piece, pieces, 0).reshape(pieces, 1)
    turned, kt = run(
        functools.partial(turn_body, groups, heads),
        [shape((heads, groups, height, LANES)), shape((heads, size + 16, length))],
        (after(kaug, sent), *own),
        flops=2 * square,
        moved=4 * square,
    )
    grad_got = move_slots(after(grad_sent, turned, own_w, own_gain))
    produced, spare, rows_in, slope, act_other, act_mine = run_expert(
        plan, place_arg, got, w_up[0], w_down[0], None
    )
    produced_back = move_slots(produced)
    back, grad_rows, hid_other, hid_mine = run_expert(
        plan, place_arg, grad_got, w_up[0], w_down[0], (slope, got, spare)
    )
    returned = move_slots(back)

    def both(values, sent_values):
        return jnp.concatenate([values, cross(sent_values, "tensor", 1)], axis=0)

    grad_down = tn(both(act_mine, act_other), both(grad_rows, grad_rows))
    grad_up = tn(both(rows_in, rows_in), both(hid_mine, hid_other))
    extra = -(-(experts_all + 1) // LANES) * LANES
    outs = run(
        functools.partial(combine_body, groups, capacity, plan),
        [
            shape((height, features)),
            shape((height, features), F32),
            shape((height, features)),
            shape((height, extra)),
            shape((8, features), F32),
        ]
        + [shape((width, height))] * groups,
        (
            after(place_arg, grad_down, grad_up),
            produced_back,
            returned,
            residual,
            router,
            route_row,
            cotangent,
            gain_ffn,
            w_router.T,
            w_out,
        ),
        scratch=[pltpu.VMEM((features, height), BF16)],
        smem=(0,),
        flops=4 * height * square,
        moved=8 * square,
    )
    mixed_out, grad_residual, branch, grad_logits, gain_sums = outs[:5]
    grad_pieces = trade(outs[5:])
    mine, other = run(
        functools.partial(weights_body, experts_all),
        [shape((experts_all, pieces, features + extra))] * 2,
        (place_arg, branch, attended_t, normed_ffn, grad_logits, gain_sums),
        scratch=[pltpu.VMEM((features, features + extra), F32)],
        smem=(0,),
        flops=2 * height * square,
        moved=8 * square,
    )

    def pair_sum(kept, received):
        return (kept.astype(F32) + received.astype(F32)).astype(BF16)

    packed = pair_sum(mine, cross(other, "tensor", 1))
    packed_landed = exchange(packed, ("expert", "context"))
    counts = (heads - 1, 1)
    mine_kv, got_kv, q_grads, diags, fars = [], [], [], [], []
    for call_at in range(len(counts)):
        first, count = sum(counts[:call_at]), counts[call_at]
        dims = [
            (groups, size, height),
            (groups, height, 2 * size),
            (groups, height, 2 * size),
            (5 * height, height),
            (2, spans, height),
        ]
        outs = pl.pallas_call(
            functools.partial(backward_body, groups),
            out_shape=[
                shape((count,) + of, kind)
                for of, kind in zip(dims, [BF16, BF16, BF16, F32, F32])
            ],
            grid=(count,),
            in_specs=[smem]
            + [
                by_head(of, first)
                for of in (
                    held_dims[4],
                    held_dims[2],
                    (size + 16, length),
                    held_dims[0],
                    held_dims[1],
                )
            ]
            + [by_head((groups, height, LANES), first)]
            + [head_rows(first)] * groups,
            out_specs=[by_head(of) for of in dims],
            scratch_shapes=[pltpu.VMEM((length, LANES), F32)]
            + [pltpu.VMEM((length, height), F32)] * 2
            + [pltpu.VMEM((length, height), BF16)] * 2,
            cost_estimate=pl.CostEstimate(
                flops=8 * count * head_flops, bytes_accessed=20 * square, transcendentals=0
            ),
            compiler_params=pltpu.CompilerParams(vmem_limit_bytes=VMEM_LIMIT),
        )(after(place_arg, packed), weights, vaug, kt, exact, inverse, turned, *grad_pieces)
        q_grads.append(outs[0])
        mine_kv.append(outs[1])
        got_kv.append(cross(outs[2], "tensor", 1))
        diags.append(outs[3])
        fars.append(outs[4])
    joined = run(
        functools.partial(join_body, counts),
        [shape((piece_rows, LANES))] * groups,
        (*mine_kv, after(got_kv[0], packed_landed), *got_kv[1:], *q_grads),
        moved=4 * groups * piece_rows * LANES,
    )
    landed_pieces = trade(joined)
    by_bucket = run(
        functools.partial(diagonal_body, counts),
        shape((heads, 1, LANES), F32),
        (*diags, *fars),
    )
    mine, other = run(
        functools.partial(qkv_body, groups, heads),
        [shape((experts_all, pieces, 3 * width + BUCKETS))] * 2,
        (place_arg, *normed_all, *joined, by_bucket),
        scratch=[
            pltpu.VMEM((features, 3 * width + BUCKETS), F32),
            pltpu.VMEM((height, 3 * width), BF16),
        ],
        smem=(0,),
    )
    summed = pair_sum(mine, cross(after(other, *landed_pieces), "tensor", 1))
    landed = exchange(summed, ("expert", "context"))
    grad_qkv, grad_gain_attn, grad_rel = run(
        functools.partial(rows_body, groups, heads),
        [
            shape((pieces, 3 * features), F32),
            shape((pieces, 1), F32),
            shape((heads, BUCKETS), F32),
        ],
        (place_arg, landed, own_w, own_gain),
        smem=(0,),
        moved=2 * landed.size,
    )
    grad_tokens = run(
        functools.partial(finish_body, groups, heads),
        shape((height, features)),
        (place_arg, tokens_in, gain_attn, w_qkv, grad_residual, *landed_pieces),
        scratch=[
            pltpu.VMEM((features, height), F32),
            pltpu.VMEM((groups, height, width), BF16),
            pltpu.VMEM((groups, height, width), BF16),
        ],
        smem=(0,),
        flops=6 * height * square,
        moved=8 * square,
    )
    reduced = jnp.sum(packed_landed.astype(F32), axis=0)
    return (
        mixed_out,
        grad_tokens,
        grad_gain_attn[:, 0],
        grad_qkv,
        grad_rel,
        reduced[:, :features].T,
        reduced[:, features + experts_all],
        reduced[:, features : features + experts_all],
        grad_up[None],
        grad_down[None],
    )


def solution(mesh):
    rows = ("expert", "context", "tensor")
    in_specs = (
        P(rows, None),
        P(),
        P(),
        P("context", None),
        P(),
        P(),
        P(),
        P(("expert", "context"), None, None),
        P(("expert", "context"), None, None),
        P("expert", None),
        P(rows, None),
        P(rows, None),
    )
    out_specs = (
        P(rows, None),
        P(rows, None),
        P(rows),
        P(rows, None),
        P("context", None),
        P(None, rows),
        P(rows),
        P(rows, None),
        P(("expert", "context"), None, "tensor"),
        P(("expert", "context"), "tensor", None),
    )
    return jax.shard_map(
        per_device, mesh=mesh, in_specs=in_specs, out_specs=out_specs, check_vma=False
    )
```

```python
import functools

import jax
import jax.numpy as jnp
from jax import lax
from jax.experimental import pallas as pl
from jax.experimental.pallas import tpu as pltpu
from jax.sharding import PartitionSpec as P

EPSILON = 1e-06
THRESHOLDS = (12, 16, 23, 32, 46, 64, 91)
FAR_LEFT = 15
FAR_RIGHT = 31
EXCLUDED = -1e30
LANES = 128
BF16 = jnp.bfloat16
F32 = jnp.float32
VMEM_LIMIT = 56 * 1024 * 1024
BUCKETS = 32
EXPERT_LIMIT = 24 * 1024 * 1024
PART = 256


def bucket_of(offset):
    distance = jnp.abs(offset)
    beyond = jnp.zeros_like(distance)
    for threshold in THRESHOLDS:
        beyond = beyond + (distance >= threshold).astype(jnp.int32)
    nearby = jnp.where(distance < 8, distance, 8 + beyond)
    return nearby + 16 * (offset > 0).astype(jnp.int32)


def nn(left, right):
    return lax.dot_general(left, right, (((1,), (0,)), ((), ())), preferred_element_type=F32)


def nt(left, right):
    return lax.dot_general(left, right, (((1,), (1,)), ((), ())), preferred_element_type=F32)


def tn(left, right):
    return lax.dot_general(left, right, (((0,), (0,)), ((), ())), preferred_element_type=F32)


def iota(shape, axis):
    return lax.broadcasted_iota(jnp.int32, shape, axis)


def three_terms(values):
    high = values.astype(BF16).astype(F32)
    middle = (values - high).astype(BF16).astype(F32)
    return high, middle, values - high - middle


def specs_for(count, smem=()):
    return [
        pl.BlockSpec(memory_space=pltpu.SMEM if i in smem else pltpu.VMEM) for i in range(count)
    ]


def run(body, out_shape, args, scratch=(), smem=(), flops=0, moved=0, limit=VMEM_LIMIT):
    return pl.pallas_call(
        body,
        out_shape=out_shape,
        in_specs=specs_for(len(args), smem),
        scratch_shapes=list(scratch),
        cost_estimate=pl.CostEstimate(flops=flops, bytes_accessed=moved, transcendentals=0),
        compiler_params=pltpu.CompilerParams(vmem_limit_bytes=limit),
    )(*args)


def shape(dims, kind=BF16):
    return jax.ShapeDtypeStruct(dims, kind)


def project_body(heads, place_ref, tokens_ref, gain_ref, w_ref, *refs):
    groups = len(refs) - 2
    piece_refs, normed_ref, all_ref = refs[:groups], refs[groups], refs[groups + 1]
    height, features = tokens_ref.shape
    width = features // groups
    size = width // heads
    group = place_ref[1]
    tokens = tokens_ref[...].astype(F32)
    inverse = lax.rsqrt(jnp.mean(tokens * tokens, axis=-1, keepdims=True) + EPSILON)
    normed = (tokens * inverse * gain_ref[...].astype(F32)[None, :]).astype(BF16)
    normed_ref[...] = jnp.transpose(normed.astype(F32)).astype(BF16)
    turned = jnp.transpose(nn(normed, w_ref[:, :features])).astype(BF16)
    keys = nn(normed, w_ref[:, features : 2 * features]).astype(BF16)
    values = nn(normed, w_ref[:, 2 * features :]).astype(BF16)
    for at in range(groups):
        for head in range(heads):
            lanes = slice(at * width + head * size, at * width + (head + 1) * size)
            all_ref[at ^ group, head * height : (head + 1) * height, :] = jnp.concatenate(
                [keys[:, lanes], values[:, lanes]], axis=1
            )
        for half in range(height // LANES):
            first = heads * height + half * width
            all_ref[at ^ group, first : first + width, :] = turned[
                at * width : (at + 1) * width, half * LANES : (half + 1) * LANES
            ]
    for at in range(groups):
        piece_refs[at][...] = all_ref[at]


def q_rows(piece_ref, heads, height, size, head):
    width = heads * size
    parts = []
    for half in range(height // LANES):
        first = heads * height + half * width + head * size
        parts.append(piece_ref[pl.ds(pl.multiple_of(first, 16), size), :])
    return jnp.concatenate(parts, axis=1)


def forward_body(groups, heads, place_ref, bias_ref, seg_ref, strip_ref, *refs):
    own_refs, far_refs, out_refs = (refs[i * groups : (i + 1) * groups] for i in range(3))
    exact_ref, inverse_ref, vaug_ref, kaug_ref, weight_ref = refs[3 * groups : 3 * groups + 5]
    extra_all, docs_all, vt_ref, score_ref = refs[3 * groups + 5 :]
    size, height = out_refs[0].shape
    spans = kaug_ref.shape[1] // height
    place, group = place_ref[0], place_ref[1]
    head = pl.program_id(0)
    tall = size + 16
    rest = LANES - size

    @pl.when(head == 0)
    def _():
        row = iota((LANES, height), 0) - size
        for span in range(spans):
            docs = seg_ref[0:1, span * height : (span + 1) * height]
            docs_all[span : span + 1, :] = docs
            extra = jnp.where((row >= 0) & (row < 3) & (docs != row), EXCLUDED, 0.0)
            extra = jnp.where(row - 3 == span, 1.0, extra)
            extra_all[span * height : (span + 1) * height, :] = jnp.transpose(extra).astype(BF16)

    row, column = iota((tall, LANES), 0), iota((tall, LANES), 1)
    pick_v = (((row < size) & (row + size == column)) | ((row == size) & (column == 0))).astype(
        BF16
    )
    lane = iota((height, LANES), 1)
    low_half = lane < size
    ones = jnp.where(lane < 3, 1.0, 0.0).astype(BF16)
    extra_row = iota((rest, height), 0)
    queries_all = []
    for at in range(groups):
        block = at ^ group
        for source, parity in ((own_refs[at], place), (far_refs[at], 1 - place)):
            span = 2 * block + parity
            rows = pl.ds(pl.multiple_of(span * height, height), height)
            both = source[pl.ds(pl.multiple_of(head * height, height), height), :]
            keys = jnp.where(low_half, both, extra_all[rows, :])
            values = jnp.where(low_half, ones, both)
            kaug_ref[0, rows, :] = keys
            vaug_ref[0, rows, :] = values
            vt_ref[span] = nt(pick_v, values).astype(BF16)
        span = 2 * block + place
        docs = docs_all[pl.ds(span, 1), :]
        apart = extra_row - 3 - span
        far = jnp.where(
            apart <= -2,
            bias_ref[head, FAR_LEFT],
            jnp.where(apart >= 2, bias_ref[head, FAR_RIGHT], 0.0),
        )
        extra = jnp.where(
            extra_row < 3,
            jnp.where(docs == extra_row, 1.0, 0.0),
            jnp.where(extra_row < 3 + spans, far, 0.0),
        )
        queries_all.append(
            jnp.concatenate(
                [q_rows(own_refs[at], heads, height, size, head), extra.astype(BF16)], axis=0
            )
        )
    for at in range(groups):
        span = 2 * (at ^ group) + place
        start = jnp.clip(span - 1, 0, spans - 3)
        queries = queries_all[at]
        slot = at % 2
        row_max = None
        for step in range(spans):
            key_span = (start + step) if step < 3 else ((start + step) & (spans - 1))
            rows = pl.ds(pl.multiple_of(key_span * height, height), height)
            scores = nn(kaug_ref[0, rows, :], queries)
            if step < 3:
                level = pl.multiple_of((key_span - span + 2) * height, height)
                scores = scores + strip_ref[0, pl.ds(level, height), :]
            score_ref[slot, step] = scores
            best = jnp.max(scores, axis=0, keepdims=True)
            row_max = best if row_max is None else jnp.maximum(row_max, best)
        total = jnp.zeros((tall, height), F32)
        for step in range(spans):
            key_span = (start + step) if step < 3 else ((start + step) & (spans - 1))
            weights = jnp.exp(score_ref[slot, step] - row_max).astype(BF16)
            weight_ref[0, at, key_span] = weights
            total = total + nn(vt_ref[key_span], weights)
        inverse = 1.0 / total[size : size + 1]
        result = total[:size] * inverse
        out_refs[at][...] = result.astype(BF16)
        exact_ref[0, at] = result
        inverse_ref[0, at] = jnp.broadcast_to(inverse, (8, height))


def turn_body(groups, heads, kaug_ref, *refs):
    piece_refs, out_ref, kt_ref = refs[:groups], refs[groups], refs[groups + 1]
    height = out_ref.shape[2]
    size = out_ref.shape[3] // 2
    spans = kaug_ref.shape[1] // height
    row, column = iota((size + 16, LANES), 0), iota((size + 16, LANES), 1)
    pick_k = (
        ((row < size) & (row == column))
        | ((row >= size) & (row < size + spans) & (row + 3 == column))
    ).astype(BF16)
    blank = jnp.zeros((size, height), F32)
    for head in range(heads):
        kt_ref[head] = nt(pick_k, kaug_ref[head]).astype(BF16)
        for at in range(groups):
            queries = q_rows(piece_refs[at], heads, height, size, head).astype(F32)
            out_ref[head, at] = jnp.transpose(jnp.concatenate([queries, blank], axis=0)).astype(
                BF16
            )


def backward_body(groups, place_ref, *refs):
    weight_ref, vaug_ref, kt_ref, exact_ref, inverse_ref, q_ref = refs[:6]
    grad_refs = refs[6 : 6 + groups]
    dq_ref, mine_ref, other_ref, diag_ref, far_ref, dkv_ref = refs[6 + groups : 12 + groups]
    slope_refs, score_refs = refs[12 + groups : 14 + groups], refs[14 + groups :]
    size, height = grad_refs[0].shape
    length = vaug_ref.shape[1]
    spans = length // height
    place, group = place_ref[0], place_ref[1]
    diag_ref[...] = jnp.zeros_like(diag_ref)
    extra_row = iota((LANES - size, height), 0)
    blank = jnp.zeros((size, height), F32)
    span_row = iota((spans, height), 0)
    left_total = jnp.zeros((spans, height), F32)
    right_total = jnp.zeros((spans, height), F32)
    for at in range(groups):
        span = 2 * (at ^ group) + place
        start = jnp.clip(span - 1, 0, spans - 3)
        slope_ref, score_ref = slope_refs[at % 2], score_refs[at % 2]
        grads = (grad_refs[at][...].astype(F32) * inverse_ref[0, at, 0:1]).astype(BF16)
        grads32 = grads.astype(F32)
        delta = jnp.sum(grads32 * exact_ref[0, at], axis=0, keepdims=True)
        high, middle, low = three_terms(-delta)
        extra = jnp.where(
            extra_row == 0,
            high,
            jnp.where(extra_row == 1, middle, jnp.where(extra_row == 2, low, 0.0)),
        )
        slope_ref[...] = nn(
            vaug_ref[0], jnp.concatenate([extra.astype(BF16), grads], axis=0)
        )
        turned = jnp.transpose(jnp.concatenate([blank, grads32], axis=0)).astype(BF16)
        sides = jnp.concatenate([q_ref[0, at], turned], axis=0)
        for key in range(spans):
            rows = slice(key * height, (key + 1) * height)
            score_ref[rows, :] = (
                weight_ref[0, at, key].astype(F32) * slope_ref[rows, :]
            ).astype(BF16)
        both = jnp.concatenate(
            [score_ref[...], weight_ref[0, at].reshape(length, height)], axis=1
        )
        product = nn(both, sides)
        if at == 0:
            dkv_ref[...] = product
        else:
            dkv_ref[...] = dkv_ref[...] + product
        total = nn(kt_ref[0], score_ref[...])
        dq_ref[0, at] = total[:size].astype(BF16)
        sums = total[size : size + spans]
        left_total = left_total + jnp.where(span_row < start, sums, 0.0)
        right_total = right_total + jnp.where(span_row >= start + 3, sums, 0.0)
        rows = pl.ds(pl.multiple_of(start * height, height), 3 * height)
        level = pl.ds(pl.multiple_of((start - span + 2) * height, height), 3 * height)
        diag_ref[0, level, :] = diag_ref[0, level, :] + score_ref[rows, :].astype(F32)
    far_ref[0, 0] = left_total
    far_ref[0, 1] = right_total
    for at in range(groups):
        for target, parity in ((mine_ref, place), (other_ref, 1 - place)):
            first = pl.multiple_of((2 * (at ^ group) + parity) * height, height)
            target[0, at] = dkv_ref[pl.ds(first, height), :].astype(BF16)


def join_body(counts, *refs):
    calls = len(counts)
    mine_refs, got_refs, dq_refs = (refs[i * calls : (i + 1) * calls] for i in range(3))
    piece_refs = refs[3 * calls :]
    size, height = dq_refs[0].shape[2:]
    heads = sum(counts)
    width = heads * size
    for at, piece_ref in enumerate(piece_refs):
        head = 0
        for call_at, count in enumerate(counts):
            for inner in range(count):
                kept = mine_refs[call_at][inner, at].astype(F32)
                piece_ref[head * height : (head + 1) * height, :] = (
                    kept + got_refs[call_at][inner, at].astype(F32)
                ).astype(BF16)
                for half in range(height // LANES):
                    first = heads * height + half * width + head * size
                    piece_ref[first : first + size, :] = dq_refs[call_at][
                        inner, at, :, half * LANES : (half + 1) * LANES
                    ]
                head += 1


def slot_plan(capacity, features):
    base = capacity // 16 * 16
    left = capacity - base
    if base and left and 16 % left == 0 and (2 * features) % (LANES * (16 // left)) == 0:
        return base, left, 16 // left
    return -(-capacity // 8) * 8, 0, 0


def slot_marks(shape_of, axis, chosen, rank, capacity, plan):
    base, left, parts = plan
    position = iota(shape_of, axis)
    limit = base if left else capacity
    marks = [jnp.where(position == jnp.where(rank < limit, chosen * base + rank, -1), 1.0, 0.0)]
    spare = rank - base
    for part in range(parts):
        slot = chosen * 16 + part * left + spare
        slot = jnp.where((spare >= 0) & (spare < left), slot, -1)
        marks.append(jnp.where(position == slot, 1.0, 0.0))
    return [mark.astype(BF16) for mark in marks]


def route_body(
    groups,
    capacity,
    plan,
    place_ref,
    tokens_ref,
    w_out_ref,
    gain_ref,
    w_router_ref,
    route_row_ref,
    cotangent_ref,
    *refs,
):
    pieces = refs[:groups]
    residual_ref, normed_ref, router_ref, sent_ref, grad_sent_ref, attended_ref = refs[groups:]
    height, features = tokens_ref.shape
    experts = w_router_ref.shape[0]
    slots = sent_ref.shape[0]
    width = pieces[0].shape[0]
    group = place_ref[1]
    for at in range(groups):
        first = pl.multiple_of((at ^ group) * width, width)
        attended_ref[pl.ds(first, width), :] = pieces[at][...]
    residual = tokens_ref[...].astype(F32) + tn(attended_ref[...], w_out_ref[...])
    residual_ref[...] = residual
    inverse = lax.rsqrt(jnp.mean(residual * residual, axis=-1, keepdims=True) + EPSILON)
    normed = (residual * inverse * gain_ref[...].astype(F32)[None, :]).astype(BF16)
    normed_ref[...] = normed
    logits = nt(normed, w_router_ref[...])
    powers = jnp.exp(logits - jnp.max(logits, axis=-1, keepdims=True))
    router = powers / jnp.sum(powers, axis=-1, keepdims=True)
    router_ref[...] = router
    chosen = route_row_ref[...]
    marks = iota((experts, height), 0) == chosen
    onehot = jnp.transpose(jnp.where(marks, 1.0, 0.0))
    gate = jnp.sum(onehot * router, axis=-1, keepdims=True)
    grad_expert = (gate * cotangent_ref[...].astype(F32)).astype(BF16)
    rows = jnp.concatenate([normed, grad_expert], axis=1)
    earlier = (iota((height, height), 0) < iota((height, height), 1)).astype(BF16)
    before = nn(jnp.where(marks, 1.0, 0.0).astype(BF16), earlier)
    rank = jnp.sum(jnp.where(marks, before, 0.0), axis=0, keepdims=True).astype(jnp.int32)
    dispatch = slot_marks((slots, height), 0, chosen, rank, capacity, plan)
    sent_ref[:, :features] = nn(dispatch[0], normed).astype(BF16)
    grad_sent_ref[...] = nn(dispatch[0], grad_expert).astype(BF16)
    if plan[1]:
        span = 2 * features // plan[2]
        spare = nn(dispatch[1], rows[:, :span])
        for part in range(1, plan[2]):
            spare = spare + nn(dispatch[1 + part], rows[:, part * span : (part + 1) * span])
        sent_ref[:, features:] = spare.astype(BF16)


def spare_marks(sources, plan):
    base, left, parts = plan
    target = iota((sources * left, sources * 16), 0)
    origin = iota((sources * left, sources * 16), 1)
    source = target // left
    return [
        (origin == source * 16 + part * left + (target - source * left)).astype(BF16)
        for part in range(parts)
    ]


def unpack_spare(rows_ref, packed, plan, first_part):
    main = packed.shape[0]
    marks = spare_marks(main // 16, plan)
    half = plan[2] // 2
    span = rows_ref.shape[1] // half
    for part in range(half):
        rows_ref[main:, part * span : (part + 1) * span] = nn(
            marks[first_part + part], packed
        ).astype(BF16)


def stage_body(place_ref, up_ref, down_ref, up_out, down_out, mark_ref, up_sem, down_sem):
    up_copy = pltpu.make_async_copy(up_ref, up_out, up_sem)
    down_copy = pltpu.make_async_copy(down_ref, down_out, down_sem)
    up_copy.start()
    down_copy.start()
    mark_ref[...] = jnp.zeros_like(mark_ref) + place_ref[0]
    up_copy.wait()
    down_copy.wait()


def stage(place_arg, up, down):
    vmem = pl.BlockSpec(memory_space=pltpu.VMEM)
    return pl.pallas_call(
        stage_body,
        out_shape=[shape(up.shape), shape(down.shape), shape((8, LANES), jnp.int32)],
        in_specs=[
            pl.BlockSpec(memory_space=pltpu.SMEM),
            pl.BlockSpec(memory_space=pl.ANY),
            pl.BlockSpec(memory_space=pl.ANY),
        ],
        out_specs=[vmem, vmem, vmem],
        scratch_shapes=[pltpu.SemaphoreType.DMA, pltpu.SemaphoreType.DMA],
        cost_estimate=pl.CostEstimate(flops=0, bytes_accessed=2 * up.size, transcendentals=0),
        compiler_params=pltpu.CompilerParams(vmem_limit_bytes=EXPERT_LIMIT),
    )(place_arg, up, down)


def expert_forward_body(
    plan,
    place_ref,
    got_ref,
    up_ref,
    down_ref,
    back_ref,
    spare_ref,
    rows_ref,
    slope_ref,
    other_ref,
    mine_ref,
    total_ref,
):
    main, features = back_ref.shape
    hidden_size = up_ref.shape[1]
    half = hidden_size // 2
    rows_ref[:main, :] = got_ref[:, :features]
    if plan[1]:
        unpack_spare(rows_ref, got_ref[:, features:], plan, 0)
    for at, active_ref in enumerate((other_ref, mine_ref)):
        start = (1 - place_ref[0]) * half if at == 0 else place_ref[0] * half
        for first in range(0, half, PART):
            lanes = pl.ds(pl.multiple_of(start + first, PART), PART)
            hidden = nn(rows_ref[...], up_ref[:, lanes])
            below = 0.5 * (1.0 + lax.erf(hidden * (2.0**-0.5)))
            bell = jnp.exp(-0.5 * hidden * hidden) * 0.3989422804014327
            active_ref[:, first : first + PART] = (hidden * below).astype(BF16)
            slope_ref[at, :, first : first + PART] = (below + hidden * bell).astype(BF16)
        rows = pl.ds(pl.multiple_of(start, PART), half)
        product = nn(active_ref[...], down_ref[rows, :])
        if at == 0:
            total_ref[...] = product
        else:
            total_ref[...] = total_ref[...] + product
    back_ref[...] = total_ref[:main, :].astype(BF16)
    if plan[1]:
        spare_ref[...] = total_ref[main:, :].astype(BF16)
    else:
        spare_ref[...] = jnp.zeros_like(spare_ref)


def expert_backward_body(
    plan,
    place_ref,
    got_ref,
    up_ref,
    down_ref,
    slope_ref,
    packed_ref,
    spare_ref,
    back_ref,
    rows_ref,
    other_ref,
    mine_ref,
    total_ref,
):
    main, features = got_ref.shape
    half = up_ref.shape[1] // 2
    rows_ref[:main, :] = got_ref[...]
    if plan[1]:
        unpack_spare(rows_ref, packed_ref[:, features:], plan, plan[2] // 2)
    for at, hidden_ref in enumerate((other_ref, mine_ref)):
        start = (1 - place_ref[0]) * half if at == 0 else place_ref[0] * half
        for first in range(0, half, PART):
            rows = pl.ds(pl.multiple_of(start + first, PART), PART)
            grad_active = nt(rows_ref[...], down_ref[rows, :])
            slope = slope_ref[at, :, first : first + PART].astype(F32)
            hidden_ref[:, first : first + PART] = (grad_active * slope).astype(BF16)
        lanes = pl.ds(pl.multiple_of(start, PART), half)
        product = nt(hidden_ref[...], up_ref[:, lanes])
        if at == 0:
            total_ref[...] = product
        else:
            total_ref[...] = total_ref[...] + product
    back_ref[:, :features] = total_ref[:main, :].astype(BF16)
    if plan[1]:
        spare = jnp.concatenate([spare_ref[...], total_ref[main:, :].astype(BF16)], axis=1)
        span = 2 * features // plan[2]
        packed = jnp.zeros((main, span), F32)
        for part, marks in enumerate(spare_marks(main // 16, plan)):
            packed = packed + tn(marks, spare[:, part * span : (part + 1) * span])
        back_ref[:, features:] = packed.astype(BF16)


def run_expert(plan, place_arg, got, up, down, forward):
    main = got.shape[0]
    features, hidden_size = up.shape
    spare = main // 16 * plan[1]
    slots = main + spare
    columns = features + (2 * features // plan[2] if plan[1] else 0)
    spare = max(spare, 8)
    halves = [shape((slots, hidden_size // 2))] * 2
    if forward is None:
        body = expert_forward_body
        out_shape = [shape((main, features)), shape((spare, features)), shape((slots, features))]
        out_shape += [shape((2, slots, hidden_size // 2))] + halves
        args, flops = (got, up, down), 0
    else:
        body = expert_backward_body
        out_shape = [shape((main, columns)), shape((slots, features))] + halves
        args, flops = (got, up, down) + forward, 4 * slots * features * hidden_size
    return run(
        functools.partial(body, plan),
        out_shape,
        (place_arg,) + args,
        scratch=[pltpu.VMEM((slots, features), F32)],
        smem=(0,),
        flops=flops,
        moved=flops // 400,
        limit=EXPERT_LIMIT,
    )


def combine_body(
    groups,
    capacity,
    plan,
    place_ref,
    produced_ref,
    got_ref,
    residual_ref,
    router_ref,
    route_row_ref,
    cotangent_ref,
    gain_ref,
    w_router_ref,
    w_out_ref,
    mixed_ref,
    grad_residual_ref,
    branch_ref,
    logits_ref,
    gain_out_ref,
    *refs,
):
    pieces, turned_ref = refs[:groups], refs[groups]
    height, experts = router_ref.shape
    features = residual_ref.shape[1]
    slots = got_ref.shape[0]
    width = pieces[0].shape[0]
    group = place_ref[1]
    chosen_row = route_row_ref[...]
    marks = jnp.where(iota((experts, height), 0) == chosen_row, 1.0, 0.0)
    earlier = (iota((height, height), 0) < iota((height, height), 1)).astype(BF16)
    before = nn(marks.astype(BF16), earlier)
    rank_row = jnp.sum(marks * before, axis=0, keepdims=True)
    onehot = jnp.transpose(marks) > 0.5
    pair_row = iota((8, height), 0)
    pairs = jnp.transpose(jnp.where(pair_row == 0, chosen_row.astype(F32), rank_row))
    chosen = pairs[:, 0:1].astype(jnp.int32)
    rank = pairs[:, 1:2].astype(jnp.int32)
    combine = slot_marks((height, slots), 1, chosen, rank, capacity, plan)
    back = jnp.concatenate(
        [nn(combine[0], produced_ref[...]), nn(combine[0], got_ref[:, :features])], axis=1
    )
    if plan[1]:
        spare = got_ref[:, features:]
        back = back + jnp.concatenate([nn(marks, spare) for marks in combine[1:]], axis=1)
    router = router_ref[...]
    gate = jnp.sum(jnp.where(onehot, router, 0.0), axis=-1, keepdims=True)
    residual = residual_ref[...]
    inverse = lax.rsqrt(jnp.mean(residual * residual, axis=-1, keepdims=True) + EPSILON)
    unit = residual * inverse
    grad_mixed = cotangent_ref[...].astype(F32)
    gathered = back[:, :features]
    mixed_ref[...] = (residual + gate * gathered).astype(BF16)
    grad_gate = jnp.sum(grad_mixed * gathered, axis=-1, keepdims=True)
    grad_logits = (router * (jnp.where(onehot, grad_gate, 0.0) - gate * grad_gate)).astype(BF16)
    grad_normed = back[:, features:] + nn(grad_logits, w_router_ref[...])
    grad_unit = grad_normed * gain_ref[...].astype(F32)[None, :]
    grad_residual = grad_mixed + inverse * (
        grad_unit - unit * jnp.mean(grad_unit * unit, axis=-1, keepdims=True)
    )
    branch = grad_residual.astype(BF16)
    turned_ref[...] = nt(w_out_ref[...], branch).astype(BF16)
    for at in range(groups):
        first = pl.multiple_of((at ^ group) * width, width)
        pieces[at][...] = turned_ref[pl.ds(first, width), :]
    grad_residual_ref[...] = grad_residual
    branch_ref[...] = branch
    spare_lanes = logits_ref.shape[1] - experts
    logits_ref[...] = jnp.concatenate([grad_logits, jnp.zeros((height, spare_lanes), BF16)], axis=1)
    sums = jnp.sum(grad_normed * unit, axis=0, keepdims=True)
    gain_out_ref[...] = jnp.broadcast_to(sums, gain_out_ref.shape)


def qkv_body(groups, heads, place_ref, *refs):
    normed_refs, piece_refs = refs[:groups], refs[groups : 2 * groups]
    bucket_ref, mine_ref, other_ref, total_ref, rows_ref = refs[2 * groups :]
    pieces = mine_ref.shape[1]
    wide = rows_ref.shape[1]
    height = normed_refs[0].shape[1]
    width = rows_ref.shape[1] // 3
    for at in range(groups):
        piece = piece_refs[at]
        for head in range(heads):
            rows_ref[:, head * LANES : (head + 1) * LANES] = piece[
                head * height : (head + 1) * height, :
            ]
        parts = [
            piece[heads * height + half * width : heads * height + (half + 1) * width, :]
            for half in range(height // LANES)
        ]
        turned = jnp.concatenate(parts, axis=1).astype(F32)
        rows_ref[:, 2 * width :] = jnp.transpose(turned).astype(BF16)
        product = nn(normed_refs[at][...], rows_ref[...])
        if at == 0:
            total_ref[:, :wide] = product
        else:
            total_ref[:, :wide] = total_ref[:, :wide] + product
    row = iota((total_ref.shape[0], BUCKETS), 0) % pieces
    buckets = jnp.zeros((total_ref.shape[0], BUCKETS), F32)
    for head in range(heads):
        buckets = jnp.where(row == head, bucket_ref[head, :, :BUCKETS], buckets)
    total_ref[:, wide:] = buckets
    split_rows(place_ref[0], total_ref, mine_ref, other_ref)


def rows_body(
    groups, heads, place_ref, landed_ref, w_ref, gain_ref, out_ref, gain_out_ref, bucket_ref
):
    sources, _, columns = landed_ref.shape
    width = (columns - BUCKETS) // 3
    size = width // heads
    features = groups * width
    for group in range(groups):
        total = landed_ref[group].astype(F32)
        for expert in range(1, sources // groups):
            total = total + landed_ref[expert * groups + group].astype(F32)
        out_ref[:, group * width : (group + 1) * width] = total[:, 2 * width : 3 * width]
        for head in range(heads):
            for part in range(2):
                source = head * 2 * size + part * size
                first = (part + 1) * features + group * width + head * size
                out_ref[:, first : first + size] = total[:, source : source + size]
    sums = jnp.sum(w_ref[...].astype(F32) * out_ref[...], axis=1, keepdims=True)
    gain_out_ref[...] = sums / gain_ref[...].astype(F32)
    buckets = jnp.zeros((landed_ref.shape[1], BUCKETS), F32)
    for expert in range(sources // groups):
        buckets = buckets + landed_ref[expert * groups + place_ref[1]][:, 3 * width :].astype(F32)
    bucket_ref[...] = buckets[:heads]


def finish_body(groups, heads, place_ref, tokens_ref, gain_ref, w_ref, residual_ref, *refs):
    piece_refs = refs[:groups]
    out_ref, turned_ref, k_all, v_all = refs[groups:]
    height, features = tokens_ref.shape
    width = features // groups
    size = width // heads
    group = place_ref[1]
    for at in range(groups):
        piece = piece_refs[at]
        first = pl.multiple_of((at ^ group) * width, width)
        for half in range(height // LANES):
            source = heads * height + half * width
            turned_ref[pl.ds(first, width), half * LANES : (half + 1) * LANES] = piece[
                source : source + width, :
            ].astype(F32)
        for head in range(heads):
            both = piece[head * height : (head + 1) * height, :]
            lanes = slice(head * size, (head + 1) * size)
            k_all[at ^ group, :, lanes] = both[:, :size]
            v_all[at ^ group, :, lanes] = both[:, size:]
    grad_normed = nt(jnp.transpose(turned_ref[...]).astype(BF16), w_ref[:, :features])
    for part, source in ((1, k_all), (2, v_all)):
        joined = jnp.concatenate([source[at] for at in range(groups)], axis=1)
        grad_normed = grad_normed + nt(joined, w_ref[:, part * features : (part + 1) * features])
    tokens = tokens_ref[...].astype(F32)
    inverse = lax.rsqrt(jnp.mean(tokens * tokens, axis=-1, keepdims=True) + EPSILON)
    unit = tokens * inverse
    grad_unit = grad_normed * gain_ref[...].astype(F32)[None, :]
    grad = inverse * (grad_unit - unit * jnp.mean(grad_unit * unit, axis=-1, keepdims=True))
    out_ref[...] = (residual_ref[...] + grad).astype(BF16)


def strip_body(table_ref, strips_ref):
    heads, rows, height = strips_ref.shape
    used = rows - height
    offset = iota((used, LANES), 0) - 2 * height
    onehot = (bucket_of(offset) == iota((used, LANES), 1)).astype(BF16)
    lane = iota((used, height), 1)
    blank = jnp.zeros((height, height), F32)
    for head in range(heads):
        values = nn(onehot, table_ref[head])
        moved = 1
        while moved < height:
            values = jnp.where((lane & moved) != 0, pltpu.roll(values, moved, 0), values)
            moved *= 2
        strips_ref[head, :height] = blank
        strips_ref[head, height:used] = values[height:]
        strips_ref[head, used:] = blank


def diagonal_body(counts, *refs):
    calls = len(counts)
    out_ref = refs[2 * calls]
    places = [(call_at, inner) for call_at in range(calls) for inner in range(counts[call_at])]
    height = refs[0].shape[2]
    total_rows = 5 * height
    lane = iota((total_rows, height), 1)
    offset = iota((total_rows, LANES), 0) - 2 * height
    table = (bucket_of(offset) == iota((total_rows, LANES), 1)).astype(F32)
    lane_out = iota((1, LANES), 1)
    blank = jnp.zeros((height, height), F32)
    for head, (call_at, inner) in enumerate(places):
        diag_ref, far_ref = refs[call_at].at[inner], refs[calls + call_at].at[inner]
        values = jnp.concatenate([blank, diag_ref[height : 4 * height, :], blank], axis=0)
        moved = 1
        while moved < height:
            values = jnp.where(
                (lane & moved) != 0, pltpu.roll(values, total_rows - moved, 0), values
            )
            moved *= 2
        sums = jnp.sum(values, axis=1, keepdims=True)
        by_bucket = jnp.sum(sums * table, axis=0, keepdims=True)
        by_bucket = by_bucket + jnp.where(
            lane_out == FAR_LEFT, jnp.sum(far_ref[0]) + jnp.sum(diag_ref[:height, :]), 0.0
        )
        out_ref[head] = by_bucket + jnp.where(
            lane_out == FAR_RIGHT, jnp.sum(far_ref[1]) + jnp.sum(diag_ref[4 * height :, :]), 0.0
        )


def split_rows(place, source_ref, mine_ref, other_ref):
    experts_all, pieces, columns = mine_ref.shape
    for parity in range(2):

        @pl.when(place == parity)
        def _():
            for at in range(experts_all):
                for target, which in ((mine_ref, parity), (other_ref, 1 - parity)):
                    first = (2 * at + which) * pieces
                    target[at] = source_ref[first : first + pieces, :].astype(BF16)


def weights_body(
    experts,
    place_ref,
    branch_ref,
    attended_ref,
    normed_ref,
    logits_ref,
    gain_ref,
    mine_ref,
    other_ref,
    packed_ref,
):
    features = branch_ref.shape[1]
    extra = logits_ref.shape[1]
    branch = jnp.transpose(branch_ref[...].astype(F32)).astype(BF16)
    packed_ref[:, :features] = nt(branch, attended_ref[...])
    normed = jnp.transpose(normed_ref[...].astype(F32)).astype(BF16)
    column = jnp.transpose(gain_ref[...])[:, :1]
    packed_ref[:, features:] = nn(normed, logits_ref[...]) + jnp.where(
        iota((features, extra), 1) == experts, column, 0.0
    )
    split_rows(place_ref[0], packed_ref, mine_ref, other_ref)


def exchange(moving, axis):
    return lax.all_to_all(moving, axis, split_axis=0, concat_axis=0, tiled=True)


def cross(moving, axis, distance):
    size = lax.axis_size(axis)
    return lax.ppermute(moving, axis, [(i, i ^ distance) for i in range(size)])


def trade(pieces):
    return [
        piece if at == 0 else cross(piece, "context", at) for at, piece in enumerate(pieces)
    ]


def after(values, *others):
    return lax.optimization_barrier((values,) + others)[0]


def per_device(
    tokens_in,
    gain_attn,
    w_qkv,
    rel_bias,
    w_out,
    gain_ffn,
    w_router,
    w_up,
    w_down,
    segments,
    routes,
    cotangent,
):
    groups = lax.axis_size("context")
    tensor_size = lax.axis_size("tensor")
    expert_size = lax.axis_size("expert")
    height, features = tokens_in.shape
    heads = rel_bias.shape[0]
    width = features // groups
    size = width // heads
    length = segments.shape[1]
    spans = length // height
    experts_all = expert_size * groups
    capacity = max(2, 5 * height // (4 * experts_all))
    plan = slot_plan(capacity, features)
    slots = experts_all * plan[0]
    columns = features + (2 * features // plan[2] if plan[1] else 0)
    piece_rows = heads * height + height // LANES * width
    place = lax.axis_index("tensor")
    context_at = lax.axis_index("context")
    place_arg = jnp.stack([place, context_at]).astype(jnp.int32)
    square = features * features

    projected = run(
        functools.partial(project_body, heads),
        [shape((piece_rows, LANES))] * groups + [shape((features, height))],
        (place_arg, tokens_in, gain_attn, w_qkv),
        scratch=[pltpu.VMEM((groups, piece_rows, LANES), BF16)],
        smem=(0,),
        flops=6 * height * square,
        moved=8 * square,
    )
    own = trade(projected[:groups])
    table = jnp.pad(rel_bias, ((0, 0), (0, LANES - rel_bias.shape[1])))
    table = jnp.broadcast_to(table[:, :, None], (heads, LANES, height))
    strips = run(
        strip_body,
        shape((heads, 5 * height, height), F32),
        (table,),
        flops=heads * 2 * 4 * height * LANES * height,
        moved=heads * 4 * 5 * height * height,
    )
    far = [cross(after(piece, strips), "tensor", 1) for piece in own]
    head_flops = 4 * groups * height * length * size

    def fixed(dims):
        return pl.BlockSpec(dims, lambda h, n=len(dims): (0,) * n)

    def by_head(dims, first=0):
        return pl.BlockSpec(
            (1,) + dims, lambda h, n=len(dims), f=first: (h + f,) + (0,) * n
        )

    def head_rows(first=0):
        return pl.BlockSpec((size, height), lambda h, f=first: (h + f, 0))

    smem = pl.BlockSpec(memory_space=pltpu.SMEM)
    held_dims = [
        (groups, size, height),
        (groups, 8, height),
        (length, LANES),
        (length, LANES),
        (groups, spans, height, height),
    ]
    held_kinds = [F32, F32, BF16, BF16, BF16]
    outs = pl.pallas_call(
        functools.partial(forward_body, groups, heads),
        out_shape=[shape((width, height))] * groups
        + [shape((heads,) + dims, kind) for dims, kind in zip(held_dims, held_kinds)],
        grid=(heads,),
        in_specs=[smem, smem, fixed((1, length)), by_head((5 * height, height))]
        + [fixed((piece_rows, LANES))] * (2 * groups),
        out_specs=[head_rows()] * groups + [by_head(dims) for dims in held_dims],
        scratch_shapes=[
            pltpu.VMEM((length, LANES), BF16),
            pltpu.VMEM((spans, height), jnp.int32),
            pltpu.VMEM((spans, size + 16, height), BF16),
            pltpu.VMEM((2, spans, height, height), F32),
        ],
        cost_estimate=pl.CostEstimate(
            flops=6 * heads * head_flops, bytes_accessed=20 * square, transcendentals=0
        ),
        compiler_params=pltpu.CompilerParams(vmem_limit_bytes=VMEM_LIMIT),
    )(place_arg, rel_bias.astype(F32), segments, strips, *own, *far)
    attended = trade(outs[:groups])
    exact, inverse, vaug, kaug, weights = outs[groups:]
    route_row = routes.reshape(1, height)
    normed_all = trade([after(projected[groups], *own)] * groups)
    residual, normed_ffn, router, sent, grad_sent, attended_t = run(
        functools.partial(route_body, groups, capacity, plan),
        [
            shape((height, features), F32),
            shape((height, features)),
            shape((height, experts_all), F32),
            shape((slots, columns)),
            shape((slots, features)),
            shape((features, height)),
        ],
        (
            after(place_arg, *normed_all),
            tokens_in,
            w_out,
            gain_ffn,
            w_router.T,
            route_row,
            cotangent,
            *attended,
        ),
        smem=(0,),
        flops=2 * height * square,
        moved=4 * square,
    )

    def move_slots(moving):
        return exchange(
            moving.reshape(experts_all, plan[0], -1), ("expert", "context")
        ).reshape(moving.shape)

    got = move_slots(sent)
    pieces = features // (experts_all * tensor_size)
    first_piece = (
        (lax.axis_index("expert") * groups + context_at) * tensor_size + place
    ) * pieces
    first_piece = after(first_piece, sent)
    own_w = lax.dynamic_slice_in_dim(w_qkv, first_piece, pieces, 0)
    own_gain = lax.dynamic_slice_in_dim(gain_attn, first_piece, pieces, 0).reshape(pieces, 1)
    turned, kt = run(
        functools.partial(turn_body, groups, heads),
        [shape((heads, groups, height, LANES)), shape((heads, size + 16, length))],
        (after(kaug, sent), *own),
        limit=EXPERT_LIMIT,
        flops=2 * square,
        moved=4 * square,
    )
    up, down, mark = stage(after(place_arg, sent), w_up[0], w_down[0])
    grad_got = move_slots(after(grad_sent, turned, own_w, own_gain, mark))
    produced, spare, rows_in, slope, act_other, act_mine = run_expert(
        plan, place_arg, got, up, down, None
    )
    produced_back = move_slots(produced)
    back, grad_rows, hid_other, hid_mine = run_expert(
        plan, place_arg, grad_got, up, down, (slope, got, spare)
    )
    returned = move_slots(back)

    def both(values, sent_values):
        return jnp.concatenate([values, cross(sent_values, "tensor", 1)], axis=0)

    grad_down = tn(both(act_mine, act_other), both(grad_rows, grad_rows))
    grad_up = tn(both(rows_in, rows_in), both(hid_mine, hid_other))
    extra = -(-(experts_all + 1) // LANES) * LANES
    outs = run(
        functools.partial(combine_body, groups, capacity, plan),
        [
            shape((height, features)),
            shape((height, features), F32),
            shape((height, features)),
            shape((height, extra)),
            shape((8, features), F32),
        ]
        + [shape((width, height))] * groups,
        (
            after(place_arg, grad_down, grad_up),
            produced_back,
            returned,
            residual,
            router,
            route_row,
            cotangent,
            gain_ffn,
            w_router.T,
            w_out,
        ),
        scratch=[pltpu.VMEM((features, height), BF16)],
        smem=(0,),
        flops=4 * height * square,
        moved=8 * square,
    )
    mixed_out, grad_residual, branch, grad_logits, gain_sums = outs[:5]
    grad_pieces = trade(outs[5:])
    mine, other = run(
        functools.partial(weights_body, experts_all),
        [shape((experts_all, pieces, features + extra))] * 2,
        (place_arg, branch, attended_t, normed_ffn, grad_logits, gain_sums),
        scratch=[pltpu.VMEM((features, features + extra), F32)],
        smem=(0,),
        flops=2 * height * square,
        moved=8 * square,
    )

    def pair_sum(kept, received):
        return (kept.astype(F32) + received.astype(F32)).astype(BF16)

    packed = pair_sum(mine, cross(other, "tensor", 1))
    packed_landed = exchange(packed, ("expert", "context"))
    counts = (heads - 1, 1)
    mine_kv, got_kv, q_grads, diags, fars = [], [], [], [], []
    for call_at in range(len(counts)):
        first, count = sum(counts[:call_at]), counts[call_at]
        dims = [
            (groups, size, height),
            (groups, height, 2 * size),
            (groups, height, 2 * size),
            (5 * height, height),
            (2, spans, height),
        ]
        outs = pl.pallas_call(
            functools.partial(backward_body, groups),
            out_shape=[
                shape((count,) + of, kind)
                for of, kind in zip(dims, [BF16, BF16, BF16, F32, F32])
            ],
            grid=(count,),
            in_specs=[smem]
            + [
                by_head(of, first)
                for of in (
                    held_dims[4],
                    held_dims[2],
                    (size + 16, length),
                    held_dims[0],
                    held_dims[1],
                )
            ]
            + [by_head((groups, height, LANES), first)]
            + [head_rows(first)] * groups,
            out_specs=[by_head(of) for of in dims],
            scratch_shapes=[pltpu.VMEM((length, LANES), F32)]
            + [pltpu.VMEM((length, height), F32)] * 2
            + [pltpu.VMEM((length, height), BF16)] * 2,
            cost_estimate=pl.CostEstimate(
                flops=8 * count * head_flops, bytes_accessed=20 * square, transcendentals=0
            ),
            compiler_params=pltpu.CompilerParams(vmem_limit_bytes=VMEM_LIMIT),
        )(after(place_arg, packed), weights, vaug, kt, exact, inverse, turned, *grad_pieces)
        q_grads.append(outs[0])
        mine_kv.append(outs[1])
        got_kv.append(cross(outs[2], "tensor", 1))
        diags.append(outs[3])
        fars.append(outs[4])
    joined = run(
        functools.partial(join_body, counts),
        [shape((piece_rows, LANES))] * groups,
        (*mine_kv, after(got_kv[0], packed_landed), *got_kv[1:], *q_grads),
        moved=4 * groups * piece_rows * LANES,
    )
    landed_pieces = trade(joined)
    by_bucket = run(
        functools.partial(diagonal_body, counts),
        shape((heads, 1, LANES), F32),
        (*diags, *fars),
    )
    mine, other = run(
        functools.partial(qkv_body, groups, heads),
        [shape((experts_all, pieces, 3 * width + BUCKETS))] * 2,
        (place_arg, *normed_all, *joined, by_bucket),
        scratch=[
            pltpu.VMEM((features, 3 * width + BUCKETS), F32),
            pltpu.VMEM((height, 3 * width), BF16),
        ],
        smem=(0,),
    )
    summed = pair_sum(mine, cross(after(other, *landed_pieces), "tensor", 1))
    landed = exchange(summed, ("expert", "context"))
    grad_qkv, grad_gain_attn, grad_rel = run(
        functools.partial(rows_body, groups, heads),
        [
            shape((pieces, 3 * features), F32),
            shape((pieces, 1), F32),
            shape((heads, BUCKETS), F32),
        ],
        (place_arg, landed, own_w, own_gain),
        smem=(0,),
        moved=2 * landed.size,
    )
    grad_tokens = run(
        functools.partial(finish_body, groups, heads),
        shape((height, features)),
        (place_arg, tokens_in, gain_attn, w_qkv, grad_residual, *landed_pieces),
        scratch=[
            pltpu.VMEM((features, height), F32),
            pltpu.VMEM((groups, height, width), BF16),
            pltpu.VMEM((groups, height, width), BF16),
        ],
        smem=(0,),
        flops=6 * height * square,
        moved=8 * square,
    )
    reduced = jnp.sum(packed_landed.astype(F32), axis=0)
    return (
        mixed_out,
        grad_tokens,
        grad_gain_attn[:, 0],
        grad_qkv,
        grad_rel,
        reduced[:, :features].T,
        reduced[:, features + experts_all],
        reduced[:, features : features + experts_all],
        grad_up[None],
        grad_down[None],
    )


def solution(mesh):
    rows = ("expert", "context", "tensor")
    in_specs = (
        P(rows, None),
        P(),
        P(),
        P("context", None),
        P(),
        P(),
        P(),
        P(("expert", "context"), None, None),
        P(("expert", "context"), None, None),
        P("expert", None),
        P(rows, None),
        P(rows, None),
    )
    out_specs = (
        P(rows, None),
        P(rows, None),
        P(rows),
        P(rows, None),
        P("context", None),
        P(None, rows),
        P(rows),
        P(rows, None),
        P(("expert", "context"), None, "tensor"),
        P(("expert", "context"), "tensor", None),
    )
    return jax.shard_map(
        per_device, mesh=mesh, in_specs=in_specs, out_specs=out_specs, check_vma=False
    )
```

```python
import functools

import jax
import jax.numpy as jnp
from jax import lax
from jax.experimental import pallas as pl
from jax.experimental.pallas import tpu as pltpu
from jax.sharding import PartitionSpec as P

EPSILON = 1e-06
THRESHOLDS = (12, 16, 23, 32, 46, 64, 91)
FAR_LEFT = 15
FAR_RIGHT = 31
EXCLUDED = -1e30
LANES = 128
BF16 = jnp.bfloat16
F32 = jnp.float32
VMEM_LIMIT = 56 * 1024 * 1024
BUCKETS = 32
CHUNKS = 4
PART = 256


def bucket_of(offset):
    distance = jnp.abs(offset)
    beyond = jnp.zeros_like(distance)
    for threshold in THRESHOLDS:
        beyond = beyond + (distance >= threshold).astype(jnp.int32)
    nearby = jnp.where(distance < 8, distance, 8 + beyond)
    return nearby + 16 * (offset > 0).astype(jnp.int32)


def nn(left, right):
    return lax.dot_general(left, right, (((1,), (0,)), ((), ())), preferred_element_type=F32)


def nt(left, right):
    return lax.dot_general(left, right, (((1,), (1,)), ((), ())), preferred_element_type=F32)


def tn(left, right):
    return lax.dot_general(left, right, (((0,), (0,)), ((), ())), preferred_element_type=F32)


def iota(shape, axis):
    return lax.broadcasted_iota(jnp.int32, shape, axis)


def three_terms(values):
    high = values.astype(BF16).astype(F32)
    middle = (values - high).astype(BF16).astype(F32)
    return high, middle, values - high - middle


def specs_for(count, smem=()):
    return [
        pl.BlockSpec(memory_space=pltpu.SMEM if i in smem else pltpu.VMEM) for i in range(count)
    ]


def run(body, out_shape, args, scratch=(), smem=(), flops=0, moved=0, limit=VMEM_LIMIT):
    return pl.pallas_call(
        body,
        out_shape=out_shape,
        in_specs=specs_for(len(args), smem),
        scratch_shapes=list(scratch),
        cost_estimate=pl.CostEstimate(flops=flops, bytes_accessed=moved, transcendentals=0),
        compiler_params=pltpu.CompilerParams(vmem_limit_bytes=limit),
    )(*args)


def shape(dims, kind=BF16):
    return jax.ShapeDtypeStruct(dims, kind)


def project_body(heads, place_ref, tokens_ref, gain_ref, w_ref, *refs):
    groups = len(refs) - 2
    piece_refs, normed_ref, all_ref = refs[:groups], refs[groups], refs[groups + 1]
    height, features = tokens_ref.shape
    width = features // groups
    size = width // heads
    group = place_ref[1]
    tokens = tokens_ref[...].astype(F32)
    inverse = lax.rsqrt(jnp.mean(tokens * tokens, axis=-1, keepdims=True) + EPSILON)
    normed = (tokens * inverse * gain_ref[...].astype(F32)[None, :]).astype(BF16)
    normed_ref[...] = jnp.transpose(normed.astype(F32)).astype(BF16)
    turned = jnp.transpose(nn(normed, w_ref[:, :features])).astype(BF16)
    keys = nn(normed, w_ref[:, features : 2 * features]).astype(BF16)
    values = nn(normed, w_ref[:, 2 * features :]).astype(BF16)
    for at in range(groups):
        for head in range(heads):
            lanes = slice(at * width + head * size, at * width + (head + 1) * size)
            all_ref[at ^ group, head * height : (head + 1) * height, :] = jnp.concatenate(
                [keys[:, lanes], values[:, lanes]], axis=1
            )
        for half in range(height // LANES):
            first = heads * height + half * width
            all_ref[at ^ group, first : first + width, :] = turned[
                at * width : (at + 1) * width, half * LANES : (half + 1) * LANES
            ]
    for at in range(groups):
        piece_refs[at][...] = all_ref[at]


def q_rows(piece_ref, heads, height, size, head):
    width = heads * size
    parts = []
    for half in range(height // LANES):
        first = heads * height + half * width + head * size
        parts.append(piece_ref[pl.ds(pl.multiple_of(first, 16), size), :])
    return jnp.concatenate(parts, axis=1)


def forward_body(groups, heads, place_ref, bias_ref, seg_ref, strip_ref, *refs):
    own_refs, far_refs, out_refs = (refs[i * groups : (i + 1) * groups] for i in range(3))
    exact_ref, inverse_ref, vaug_ref, kaug_ref, weight_ref = refs[3 * groups : 3 * groups + 5]
    extra_all, docs_all, vt_ref, score_ref = refs[3 * groups + 5 :]
    size, height = out_refs[0].shape
    spans = kaug_ref.shape[1] // height
    place, group = place_ref[0], place_ref[1]
    head = pl.program_id(0)
    tall = size + 16
    rest = LANES - size

    @pl.when(head == 0)
    def _():
        row = iota((LANES, height), 0) - size
        for span in range(spans):
            docs = seg_ref[0:1, span * height : (span + 1) * height]
            docs_all[span : span + 1, :] = docs
            extra = jnp.where((row >= 0) & (row < 3) & (docs != row), EXCLUDED, 0.0)
            extra = jnp.where(row - 3 == span, 1.0, extra)
            extra_all[span * height : (span + 1) * height, :] = jnp.transpose(extra).astype(BF16)

    row, column = iota((tall, LANES), 0), iota((tall, LANES), 1)
    pick_v = (((row < size) & (row + size == column)) | ((row == size) & (column == 0))).astype(
        BF16
    )
    lane = iota((height, LANES), 1)
    low_half = lane < size
    ones = jnp.where(lane < 3, 1.0, 0.0).astype(BF16)
    extra_row = iota((rest, height), 0)
    queries_all = []
    for at in range(groups):
        block = at ^ group
        for source, parity in ((own_refs[at], place), (far_refs[at], 1 - place)):
            span = 2 * block + parity
            rows = pl.ds(pl.multiple_of(span * height, height), height)
            both = source[pl.ds(pl.multiple_of(head * height, height), height), :]
            keys = jnp.where(low_half, both, extra_all[rows, :])
            values = jnp.where(low_half, ones, both)
            kaug_ref[0, rows, :] = keys
            vaug_ref[0, rows, :] = values
            vt_ref[span] = nt(pick_v, values).astype(BF16)
        span = 2 * block + place
        docs = docs_all[pl.ds(span, 1), :]
        apart = extra_row - 3 - span
        far = jnp.where(
            apart <= -2,
            bias_ref[head, FAR_LEFT],
            jnp.where(apart >= 2, bias_ref[head, FAR_RIGHT], 0.0),
        )
        extra = jnp.where(
            extra_row < 3,
            jnp.where(docs == extra_row, 1.0, 0.0),
            jnp.where(extra_row < 3 + spans, far, 0.0),
        )
        queries_all.append(
            jnp.concatenate(
                [q_rows(own_refs[at], heads, height, size, head), extra.astype(BF16)], axis=0
            )
        )
    for at in range(groups):
        span = 2 * (at ^ group) + place
        start = jnp.clip(span - 1, 0, spans - 3)
        queries = queries_all[at]
        slot = at % 2
        row_max = None
        for step in range(spans):
            key_span = (start + step) if step < 3 else ((start + step) & (spans - 1))
            rows = pl.ds(pl.multiple_of(key_span * height, height), height)
            scores = nn(kaug_ref[0, rows, :], queries)
            if step < 3:
                level = pl.multiple_of((key_span - span + 2) * height, height)
                scores = scores + strip_ref[0, pl.ds(level, height), :]
            score_ref[slot, step] = scores
            best = jnp.max(scores, axis=0, keepdims=True)
            row_max = best if row_max is None else jnp.maximum(row_max, best)
        total = jnp.zeros((tall, height), F32)
        for step in range(spans):
            key_span = (start + step) if step < 3 else ((start + step) & (spans - 1))
            weights = jnp.exp(score_ref[slot, step] - row_max).astype(BF16)
            weight_ref[0, at, key_span] = weights
            total = total + nn(vt_ref[key_span], weights)
        inverse = 1.0 / total[size : size + 1]
        result = total[:size] * inverse
        out_refs[at][...] = result.astype(BF16)
        exact_ref[0, at] = result
        inverse_ref[0, at] = jnp.broadcast_to(inverse, (8, height))


def turn_body(groups, heads, kaug_ref, *refs):
    piece_refs, out_ref, kt_ref = refs[:groups], refs[groups], refs[groups + 1]
    height = out_ref.shape[2]
    size = out_ref.shape[3] // 2
    spans = kaug_ref.shape[1] // height
    row, column = iota((size + 16, LANES), 0), iota((size + 16, LANES), 1)
    pick_k = (
        ((row < size) & (row == column))
        | ((row >= size) & (row < size + spans) & (row + 3 == column))
    ).astype(BF16)
    blank = jnp.zeros((size, height), F32)
    for head in range(heads):
        kt_ref[head] = nt(pick_k, kaug_ref[head]).astype(BF16)
        for at in range(groups):
            queries = q_rows(piece_refs[at], heads, height, size, head).astype(F32)
            out_ref[head, at] = jnp.transpose(jnp.concatenate([queries, blank], axis=0)).astype(
                BF16
            )


def backward_body(groups, place_ref, *refs):
    weight_ref, vaug_ref, kt_ref, exact_ref, inverse_ref, q_ref = refs[:6]
    grad_refs = refs[6 : 6 + groups]
    dq_ref, mine_ref, other_ref, diag_ref, far_ref, dkv_ref = refs[6 + groups : 12 + groups]
    slope_refs, score_refs = refs[12 + groups : 14 + groups], refs[14 + groups :]
    size, height = grad_refs[0].shape
    length = vaug_ref.shape[1]
    spans = length // height
    place, group = place_ref[0], place_ref[1]
    diag_ref[...] = jnp.zeros_like(diag_ref)
    extra_row = iota((LANES - size, height), 0)
    blank = jnp.zeros((size, height), F32)
    span_row = iota((spans, height), 0)
    left_total = jnp.zeros((spans, height), F32)
    right_total = jnp.zeros((spans, height), F32)
    for at in range(groups):
        span = 2 * (at ^ group) + place
        start = jnp.clip(span - 1, 0, spans - 3)
        slope_ref, score_ref = slope_refs[at % 2], score_refs[at % 2]
        grads = (grad_refs[at][...].astype(F32) * inverse_ref[0, at, 0:1]).astype(BF16)
        grads32 = grads.astype(F32)
        delta = jnp.sum(grads32 * exact_ref[0, at], axis=0, keepdims=True)
        high, middle, low = three_terms(-delta)
        extra = jnp.where(
            extra_row == 0,
            high,
            jnp.where(extra_row == 1, middle, jnp.where(extra_row == 2, low, 0.0)),
        )
        slope_ref[...] = nn(
            vaug_ref[0], jnp.concatenate([extra.astype(BF16), grads], axis=0)
        )
        turned = jnp.transpose(jnp.concatenate([blank, grads32], axis=0)).astype(BF16)
        sides = jnp.concatenate([q_ref[0, at], turned], axis=0)
        for key in range(spans):
            rows = slice(key * height, (key + 1) * height)
            score_ref[rows, :] = (
                weight_ref[0, at, key].astype(F32) * slope_ref[rows, :]
            ).astype(BF16)
        both = jnp.concatenate(
            [score_ref[...], weight_ref[0, at].reshape(length, height)], axis=1
        )
        product = nn(both, sides)
        if at == 0:
            dkv_ref[...] = product
        else:
            dkv_ref[...] = dkv_ref[...] + product
        total = nn(kt_ref[0], score_ref[...])
        dq_ref[0, at] = total[:size].astype(BF16)
        sums = total[size : size + spans]
        left_total = left_total + jnp.where(span_row < start, sums, 0.0)
        right_total = right_total + jnp.where(span_row >= start + 3, sums, 0.0)
        rows = pl.ds(pl.multiple_of(start * height, height), 3 * height)
        level = pl.ds(pl.multiple_of((start - span + 2) * height, height), 3 * height)
        diag_ref[0, level, :] = diag_ref[0, level, :] + score_ref[rows, :].astype(F32)
    far_ref[0, 0] = left_total
    far_ref[0, 1] = right_total
    for at in range(groups):
        for target, parity in ((mine_ref, place), (other_ref, 1 - place)):
            first = pl.multiple_of((2 * (at ^ group) + parity) * height, height)
            target[0, at] = dkv_ref[pl.ds(first, height), :].astype(BF16)


def join_body(counts, *refs):
    calls = len(counts)
    mine_refs, got_refs, dq_refs = (refs[i * calls : (i + 1) * calls] for i in range(3))
    piece_refs = refs[3 * calls :]
    size, height = dq_refs[0].shape[2:]
    heads = sum(counts)
    width = heads * size
    for at, piece_ref in enumerate(piece_refs):
        head = 0
        for call_at, count in enumerate(counts):
            for inner in range(count):
                kept = mine_refs[call_at][inner, at].astype(F32)
                piece_ref[head * height : (head + 1) * height, :] = (
                    kept + got_refs[call_at][inner, at].astype(F32)
                ).astype(BF16)
                for half in range(height // LANES):
                    first = heads * height + half * width + head * size
                    piece_ref[first : first + size, :] = dq_refs[call_at][
                        inner, at, :, half * LANES : (half + 1) * LANES
                    ]
                head += 1


def slot_plan(capacity, features):
    base = capacity // 16 * 16
    left = capacity - base
    if base and left and 16 % left == 0 and (2 * features) % (LANES * (16 // left)) == 0:
        return base, left, 16 // left
    return -(-capacity // 8) * 8, 0, 0


def slot_marks(shape_of, axis, chosen, rank, capacity, plan):
    base, left, parts = plan
    position = iota(shape_of, axis)
    limit = base if left else capacity
    marks = [jnp.where(position == jnp.where(rank < limit, chosen * base + rank, -1), 1.0, 0.0)]
    spare = rank - base
    for part in range(parts):
        slot = chosen * 16 + part * left + spare
        slot = jnp.where((spare >= 0) & (spare < left), slot, -1)
        marks.append(jnp.where(position == slot, 1.0, 0.0))
    return [mark.astype(BF16) for mark in marks]


def route_body(
    groups,
    capacity,
    plan,
    place_ref,
    tokens_ref,
    w_out_ref,
    gain_ref,
    w_router_ref,
    route_row_ref,
    cotangent_ref,
    *refs,
):
    pieces = refs[:groups]
    residual_ref, normed_ref, router_ref, sent_ref, grad_sent_ref, attended_ref = refs[groups:]
    height, features = tokens_ref.shape
    experts = w_router_ref.shape[0]
    slots = sent_ref.shape[0]
    width = pieces[0].shape[0]
    group = place_ref[1]
    for at in range(groups):
        first = pl.multiple_of((at ^ group) * width, width)
        attended_ref[pl.ds(first, width), :] = pieces[at][...]
    residual = tokens_ref[...].astype(F32) + tn(attended_ref[...], w_out_ref[...])
    residual_ref[...] = residual
    inverse = lax.rsqrt(jnp.mean(residual * residual, axis=-1, keepdims=True) + EPSILON)
    normed = (residual * inverse * gain_ref[...].astype(F32)[None, :]).astype(BF16)
    normed_ref[...] = normed
    logits = nt(normed, w_router_ref[...])
    powers = jnp.exp(logits - jnp.max(logits, axis=-1, keepdims=True))
    router = powers / jnp.sum(powers, axis=-1, keepdims=True)
    router_ref[...] = router
    chosen = route_row_ref[...]
    marks = iota((experts, height), 0) == chosen
    onehot = jnp.transpose(jnp.where(marks, 1.0, 0.0))
    gate = jnp.sum(onehot * router, axis=-1, keepdims=True)
    grad_expert = (gate * cotangent_ref[...].astype(F32)).astype(BF16)
    rows = jnp.concatenate([normed, grad_expert], axis=1)
    earlier = (iota((height, height), 0) < iota((height, height), 1)).astype(BF16)
    before = nn(jnp.where(marks, 1.0, 0.0).astype(BF16), earlier)
    rank = jnp.sum(jnp.where(marks, before, 0.0), axis=0, keepdims=True).astype(jnp.int32)
    dispatch = slot_marks((slots, height), 0, chosen, rank, capacity, plan)
    sent_ref[:, :features] = nn(dispatch[0], normed).astype(BF16)
    grad_sent_ref[...] = nn(dispatch[0], grad_expert).astype(BF16)
    if plan[1]:
        span = 2 * features // plan[2]
        spare = nn(dispatch[1], rows[:, :span])
        for part in range(1, plan[2]):
            spare = spare + nn(dispatch[1 + part], rows[:, part * span : (part + 1) * span])
        sent_ref[:, features:] = spare.astype(BF16)


def spare_marks(sources, plan):
    base, left, parts = plan
    target = iota((sources * left, sources * 16), 0)
    origin = iota((sources * left, sources * 16), 1)
    source = target // left
    return [
        (origin == source * 16 + part * left + (target - source * left)).astype(BF16)
        for part in range(parts)
    ]


def unpack_spare(rows_ref, packed, plan, first_part):
    main = packed.shape[0]
    marks = spare_marks(main // 16, plan)
    half = plan[2] // 2
    span = rows_ref.shape[1] // half
    for part in range(half):
        rows_ref[main:, part * span : (part + 1) * span] = nn(
            marks[first_part + part], packed
        ).astype(BF16)


def bring(place, up_ref, down_ref, up_all, down_all, sems):
    chunk = up_all.shape[2]
    copies = []
    for at in range(CHUNKS):
        half = (1 - place) if at < CHUNKS // 2 else place
        first = half * (chunk * CHUNKS // 2) + at % (CHUNKS // 2) * chunk
        part = pl.ds(pl.multiple_of(first, chunk), chunk)
        copies.append(
            (
                pltpu.make_async_copy(up_ref.at[:, part], up_all.at[at], sems.at[0, at]),
                pltpu.make_async_copy(down_ref.at[part, :], down_all.at[at], sems.at[1, at]),
            )
        )
    return copies


def expert_forward_body(
    plan,
    place_ref,
    got_ref,
    up_ref,
    down_ref,
    back_ref,
    spare_ref,
    rows_ref,
    slope_ref,
    other_ref,
    mine_ref,
    total_ref,
    up_all,
    down_all,
    sems,
):
    main, features = back_ref.shape
    chunk = up_all.shape[2]
    copies = bring(place_ref[0], up_ref, down_ref, up_all, down_all, sems)
    for up_copy, down_copy in copies:
        up_copy.start()
        down_copy.start()
    rows_ref[:main, :] = got_ref[:, :features]
    if plan[1]:
        unpack_spare(rows_ref, got_ref[:, features:], plan, 0)
    for at in range(CHUNKS):
        active_ref = other_ref if at < CHUNKS // 2 else mine_ref
        base = at % (CHUNKS // 2) * chunk
        copies[at][0].wait()
        for first in range(0, chunk, PART):
            lanes = slice(base + first, base + first + PART)
            hidden = nn(rows_ref[...], up_all[at, :, first : first + PART])
            below = 0.5 * (1.0 + lax.erf(hidden * (2.0**-0.5)))
            bell = jnp.exp(-0.5 * hidden * hidden) * 0.3989422804014327
            active_ref[:, lanes] = (hidden * below).astype(BF16)
            slope_ref[at // (CHUNKS // 2), :, lanes] = (below + hidden * bell).astype(BF16)
        copies[at][1].wait()
        product = nn(active_ref[:, base : base + chunk], down_all[at])
        if at == 0:
            total_ref[...] = product
        else:
            total_ref[...] = total_ref[...] + product
    back_ref[...] = total_ref[:main, :].astype(BF16)
    if plan[1]:
        spare_ref[...] = total_ref[main:, :].astype(BF16)
    else:
        spare_ref[...] = jnp.zeros_like(spare_ref)


def expert_backward_body(
    plan,
    place_ref,
    got_ref,
    up_ref,
    down_ref,
    slope_ref,
    packed_ref,
    spare_ref,
    back_ref,
    rows_ref,
    other_ref,
    mine_ref,
    total_ref,
    up_all,
    down_all,
    sems,
):
    main, features = got_ref.shape
    chunk = up_all.shape[2]
    copies = bring(place_ref[0], up_ref, down_ref, up_all, down_all, sems)
    for up_copy, down_copy in copies:
        down_copy.start()
        up_copy.start()
    rows_ref[:main, :] = got_ref[...]
    if plan[1]:
        unpack_spare(rows_ref, packed_ref[:, features:], plan, plan[2] // 2)
    for at in range(CHUNKS):
        hidden_ref = other_ref if at < CHUNKS // 2 else mine_ref
        base = at % (CHUNKS // 2) * chunk
        copies[at][1].wait()
        for first in range(0, chunk, PART):
            lanes = slice(base + first, base + first + PART)
            grad_active = nt(rows_ref[...], down_all[at, first : first + PART, :])
            slope = slope_ref[at // (CHUNKS // 2), :, lanes].astype(F32)
            hidden_ref[:, lanes] = (grad_active * slope).astype(BF16)
        copies[at][0].wait()
        product = nt(hidden_ref[:, base : base + chunk], up_all[at])
        if at == 0:
            total_ref[...] = product
        else:
            total_ref[...] = total_ref[...] + product
    back_ref[:, :features] = total_ref[:main, :].astype(BF16)
    if plan[1]:
        spare = jnp.concatenate([spare_ref[...], total_ref[main:, :].astype(BF16)], axis=1)
        span = 2 * features // plan[2]
        packed = jnp.zeros((main, span), F32)
        for part, marks in enumerate(spare_marks(main // 16, plan)):
            packed = packed + tn(marks, spare[:, part * span : (part + 1) * span])
        back_ref[:, features:] = packed.astype(BF16)


def run_expert(plan, place_arg, got, up, down, forward):
    main = got.shape[0]
    features, hidden_size = up.shape
    spare = main // 16 * plan[1]
    slots = main + spare
    columns = features + (2 * features // plan[2] if plan[1] else 0)
    spare = max(spare, 8)
    halves = [shape((slots, hidden_size // 2))] * 2
    if forward is None:
        body = expert_forward_body
        out_shape = [shape((main, features)), shape((spare, features)), shape((slots, features))]
        out_shape += [shape((2, slots, hidden_size // 2))] + halves
        args, flops = (got, up, down), 0
    else:
        body = expert_backward_body
        out_shape = [shape((main, columns)), shape((slots, features))] + halves
        args, flops = (got, up, down) + forward, 4 * slots * features * hidden_size
    args = (place_arg,) + args
    specs = specs_for(len(args), (0,))
    specs[2] = specs[3] = pl.BlockSpec(memory_space=pl.ANY)
    chunk = hidden_size // CHUNKS
    return pl.pallas_call(
        functools.partial(body, plan),
        out_shape=out_shape,
        in_specs=specs,
        scratch_shapes=[
            pltpu.VMEM((slots, features), F32),
            pltpu.VMEM((CHUNKS, features, chunk), BF16),
            pltpu.VMEM((CHUNKS, chunk, features), BF16),
            pltpu.SemaphoreType.DMA((2, CHUNKS)),
        ],
        cost_estimate=pl.CostEstimate(flops=flops, bytes_accessed=flops // 400, transcendentals=0),
        compiler_params=pltpu.CompilerParams(vmem_limit_bytes=VMEM_LIMIT),
    )(*args)


def combine_body(
    groups,
    capacity,
    plan,
    place_ref,
    produced_ref,
    got_ref,
    residual_ref,
    router_ref,
    route_row_ref,
    cotangent_ref,
    gain_ref,
    w_router_ref,
    w_out_ref,
    mixed_ref,
    grad_residual_ref,
    branch_ref,
    logits_ref,
    gain_out_ref,
    *refs,
):
    pieces, turned_ref = refs[:groups], refs[groups]
    height, experts = router_ref.shape
    features = residual_ref.shape[1]
    slots = got_ref.shape[0]
    width = pieces[0].shape[0]
    group = place_ref[1]
    chosen_row = route_row_ref[...]
    marks = jnp.where(iota((experts, height), 0) == chosen_row, 1.0, 0.0)
    earlier = (iota((height, height), 0) < iota((height, height), 1)).astype(BF16)
    before = nn(marks.astype(BF16), earlier)
    rank_row = jnp.sum(marks * before, axis=0, keepdims=True)
    onehot = jnp.transpose(marks) > 0.5
    pair_row = iota((8, height), 0)
    pairs = jnp.transpose(jnp.where(pair_row == 0, chosen_row.astype(F32), rank_row))
    chosen = pairs[:, 0:1].astype(jnp.int32)
    rank = pairs[:, 1:2].astype(jnp.int32)
    combine = slot_marks((height, slots), 1, chosen, rank, capacity, plan)
    back = jnp.concatenate(
        [nn(combine[0], produced_ref[...]), nn(combine[0], got_ref[:, :features])], axis=1
    )
    if plan[1]:
        spare = got_ref[:, features:]
        back = back + jnp.concatenate([nn(marks, spare) for marks in combine[1:]], axis=1)
    router = router_ref[...]
    gate = jnp.sum(jnp.where(onehot, router, 0.0), axis=-1, keepdims=True)
    residual = residual_ref[...]
    inverse = lax.rsqrt(jnp.mean(residual * residual, axis=-1, keepdims=True) + EPSILON)
    unit = residual * inverse
    grad_mixed = cotangent_ref[...].astype(F32)
    gathered = back[:, :features]
    mixed_ref[...] = (residual + gate * gathered).astype(BF16)
    grad_gate = jnp.sum(grad_mixed * gathered, axis=-1, keepdims=True)
    grad_logits = (router * (jnp.where(onehot, grad_gate, 0.0) - gate * grad_gate)).astype(BF16)
    grad_normed = back[:, features:] + nn(grad_logits, w_router_ref[...])
    grad_unit = grad_normed * gain_ref[...].astype(F32)[None, :]
    grad_residual = grad_mixed + inverse * (
        grad_unit - unit * jnp.mean(grad_unit * unit, axis=-1, keepdims=True)
    )
    branch = grad_residual.astype(BF16)
    turned_ref[...] = nt(w_out_ref[...], branch).astype(BF16)
    for at in range(groups):
        first = pl.multiple_of((at ^ group) * width, width)
        pieces[at][...] = turned_ref[pl.ds(first, width), :]
    grad_residual_ref[...] = grad_residual
    branch_ref[...] = branch
    spare_lanes = logits_ref.shape[1] - experts
    logits_ref[...] = jnp.concatenate([grad_logits, jnp.zeros((height, spare_lanes), BF16)], axis=1)
    sums = jnp.sum(grad_normed * unit, axis=0, keepdims=True)
    gain_out_ref[...] = jnp.broadcast_to(sums, gain_out_ref.shape)


def qkv_body(groups, heads, place_ref, *refs):
    normed_refs, piece_refs = refs[:groups], refs[groups : 2 * groups]
    bucket_ref, mine_ref, other_ref, total_ref, rows_ref = refs[2 * groups :]
    pieces = mine_ref.shape[1]
    wide = rows_ref.shape[1]
    height = normed_refs[0].shape[1]
    width = rows_ref.shape[1] // 3
    for at in range(groups):
        piece = piece_refs[at]
        for head in range(heads):
            rows_ref[:, head * LANES : (head + 1) * LANES] = piece[
                head * height : (head + 1) * height, :
            ]
        parts = [
            piece[heads * height + half * width : heads * height + (half + 1) * width, :]
            for half in range(height // LANES)
        ]
        turned = jnp.concatenate(parts, axis=1).astype(F32)
        rows_ref[:, 2 * width :] = jnp.transpose(turned).astype(BF16)
        product = nn(normed_refs[at][...], rows_ref[...])
        if at == 0:
            total_ref[:, :wide] = product
        else:
            total_ref[:, :wide] = total_ref[:, :wide] + product
    row = iota((total_ref.shape[0], BUCKETS), 0) % pieces
    buckets = jnp.zeros((total_ref.shape[0], BUCKETS), F32)
    for head in range(heads):
        buckets = jnp.where(row == head, bucket_ref[head, :, :BUCKETS], buckets)
    total_ref[:, wide:] = buckets
    split_rows(place_ref[0], total_ref, mine_ref, other_ref)


def rows_body(
    groups, heads, place_ref, landed_ref, w_ref, gain_ref, out_ref, gain_out_ref, bucket_ref
):
    sources, _, columns = landed_ref.shape
    width = (columns - BUCKETS) // 3
    size = width // heads
    features = groups * width
    for group in range(groups):
        total = landed_ref[group].astype(F32)
        for expert in range(1, sources // groups):
            total = total + landed_ref[expert * groups + group].astype(F32)
        out_ref[:, group * width : (group + 1) * width] = total[:, 2 * width : 3 * width]
        for head in range(heads):
            for part in range(2):
                source = head * 2 * size + part * size
                first = (part + 1) * features + group * width + head * size
                out_ref[:, first : first + size] = total[:, source : source + size]
    sums = lax.dot_general(
        jnp.ones((8, 3 * features), F32),
        w_ref[...].astype(F32) * out_ref[...],
        (((1,), (1,)), ((), ())),
        precision=lax.Precision.HIGHEST,
        preferred_element_type=F32,
    )
    gain_out_ref[...] = sums[0] / gain_ref[...].astype(F32)
    buckets = jnp.zeros((landed_ref.shape[1], BUCKETS), F32)
    for expert in range(sources // groups):
        buckets = buckets + landed_ref[expert * groups + place_ref[1]][:, 3 * width :].astype(F32)
    bucket_ref[...] = buckets[:heads]


def finish_body(groups, heads, place_ref, tokens_ref, gain_ref, w_ref, residual_ref, *refs):
    piece_refs = refs[:groups]
    out_ref, turned_ref, k_all, v_all = refs[groups:]
    height, features = tokens_ref.shape
    width = features // groups
    size = width // heads
    group = place_ref[1]
    for at in range(groups):
        piece = piece_refs[at]
        first = pl.multiple_of((at ^ group) * width, width)
        for half in range(height // LANES):
            source = heads * height + half * width
            turned_ref[pl.ds(first, width), half * LANES : (half + 1) * LANES] = piece[
                source : source + width, :
            ].astype(F32)
        for head in range(heads):
            both = piece[head * height : (head + 1) * height, :]
            lanes = slice(head * size, (head + 1) * size)
            k_all[at ^ group, :, lanes] = both[:, :size]
            v_all[at ^ group, :, lanes] = both[:, size:]
    grad_normed = nt(jnp.transpose(turned_ref[...]).astype(BF16), w_ref[:, :features])
    for part, source in ((1, k_all), (2, v_all)):
        joined = jnp.concatenate([source[at] for at in range(groups)], axis=1)
        grad_normed = grad_normed + nt(joined, w_ref[:, part * features : (part + 1) * features])
    tokens = tokens_ref[...].astype(F32)
    inverse = lax.rsqrt(jnp.mean(tokens * tokens, axis=-1, keepdims=True) + EPSILON)
    unit = tokens * inverse
    grad_unit = grad_normed * gain_ref[...].astype(F32)[None, :]
    grad = inverse * (grad_unit - unit * jnp.mean(grad_unit * unit, axis=-1, keepdims=True))
    out_ref[...] = (residual_ref[...] + grad).astype(BF16)


def strip_body(table_ref, strips_ref):
    heads, rows, height = strips_ref.shape
    used = rows - height
    offset = iota((used, LANES), 0) - 2 * height
    onehot = (bucket_of(offset) == iota((used, LANES), 1)).astype(BF16)
    lane = iota((used, height), 1)
    blank = jnp.zeros((height, height), F32)
    for head in range(heads):
        values = nn(onehot, table_ref[head])
        moved = 1
        while moved < height:
            values = jnp.where((lane & moved) != 0, pltpu.roll(values, moved, 0), values)
            moved *= 2
        strips_ref[head, :height] = blank
        strips_ref[head, height:used] = values[height:]
        strips_ref[head, used:] = blank


def diagonal_body(counts, *refs):
    calls = len(counts)
    out_ref = refs[2 * calls]
    places = [(call_at, inner) for call_at in range(calls) for inner in range(counts[call_at])]
    height = refs[0].shape[2]
    total_rows = 5 * height
    lane = iota((total_rows, height), 1)
    offset = iota((total_rows, LANES), 0) - 2 * height
    table = (bucket_of(offset) == iota((total_rows, LANES), 1)).astype(F32)
    lane_out = iota((1, LANES), 1)
    blank = jnp.zeros((height, height), F32)
    for head, (call_at, inner) in enumerate(places):
        diag_ref, far_ref = refs[call_at].at[inner], refs[calls + call_at].at[inner]
        values = jnp.concatenate([blank, diag_ref[height : 4 * height, :], blank], axis=0)
        moved = 1
        while moved < height:
            values = jnp.where(
                (lane & moved) != 0, pltpu.roll(values, total_rows - moved, 0), values
            )
            moved *= 2
        sums = jnp.sum(values, axis=1, keepdims=True)
        by_bucket = jnp.sum(sums * table, axis=0, keepdims=True)
        by_bucket = by_bucket + jnp.where(
            lane_out == FAR_LEFT, jnp.sum(far_ref[0]) + jnp.sum(diag_ref[:height, :]), 0.0
        )
        out_ref[head] = by_bucket + jnp.where(
            lane_out == FAR_RIGHT, jnp.sum(far_ref[1]) + jnp.sum(diag_ref[4 * height :, :]), 0.0
        )


def split_rows(place, source_ref, mine_ref, other_ref):
    experts_all, pieces, columns = mine_ref.shape
    for parity in range(2):

        @pl.when(place == parity)
        def _():
            for at in range(experts_all):
                for target, which in ((mine_ref, parity), (other_ref, 1 - parity)):
                    first = (2 * at + which) * pieces
                    target[at] = source_ref[first : first + pieces, :].astype(BF16)


def weights_body(
    experts,
    place_ref,
    branch_ref,
    attended_ref,
    normed_ref,
    logits_ref,
    gain_ref,
    mine_ref,
    other_ref,
    packed_ref,
):
    features = branch_ref.shape[1]
    extra = logits_ref.shape[1]
    branch = jnp.transpose(branch_ref[...].astype(F32)).astype(BF16)
    packed_ref[:, :features] = nt(branch, attended_ref[...])
    normed = jnp.transpose(normed_ref[...].astype(F32)).astype(BF16)
    column = jnp.transpose(gain_ref[...])[:, :1]
    packed_ref[:, features:] = nn(normed, logits_ref[...]) + jnp.where(
        iota((features, extra), 1) == experts, column, 0.0
    )
    split_rows(place_ref[0], packed_ref, mine_ref, other_ref)


def pair_body(kept_ref, got_ref, out_ref):
    out_ref[...] = (kept_ref[...].astype(F32) + got_ref[...].astype(F32)).astype(BF16)


def exchange(moving, axis):
    return lax.all_to_all(moving, axis, split_axis=0, concat_axis=0, tiled=True)


def cross(moving, axis, distance):
    size = lax.axis_size(axis)
    return lax.ppermute(moving, axis, [(i, i ^ distance) for i in range(size)])


def trade(pieces):
    return [
        piece if at == 0 else cross(piece, "context", at) for at, piece in enumerate(pieces)
    ]


def after(values, *others):
    return lax.optimization_barrier((values,) + others)[0]


def per_device(
    tokens_in,
    gain_attn,
    w_qkv,
    rel_bias,
    w_out,
    gain_ffn,
    w_router,
    w_up,
    w_down,
    segments,
    routes,
    cotangent,
):
    groups = lax.axis_size("context")
    tensor_size = lax.axis_size("tensor")
    expert_size = lax.axis_size("expert")
    height, features = tokens_in.shape
    heads = rel_bias.shape[0]
    width = features // groups
    size = width // heads
    length = segments.shape[1]
    spans = length // height
    experts_all = expert_size * groups
    capacity = max(2, 5 * height // (4 * experts_all))
    plan = slot_plan(capacity, features)
    slots = experts_all * plan[0]
    columns = features + (2 * features // plan[2] if plan[1] else 0)
    piece_rows = heads * height + height // LANES * width
    place = lax.axis_index("tensor")
    context_at = lax.axis_index("context")
    place_arg = jnp.stack([place, context_at]).astype(jnp.int32)
    square = features * features

    projected = run(
        functools.partial(project_body, heads),
        [shape((piece_rows, LANES))] * groups + [shape((features, height))],
        (place_arg, tokens_in, gain_attn, w_qkv),
        scratch=[pltpu.VMEM((groups, piece_rows, LANES), BF16)],
        smem=(0,),
        flops=6 * height * square,
        moved=8 * square,
    )
    own = trade(projected[:groups])
    table = jnp.pad(rel_bias, ((0, 0), (0, LANES - rel_bias.shape[1])))
    table = jnp.broadcast_to(table[:, :, None], (heads, LANES, height))
    strips = run(
        strip_body,
        shape((heads, 5 * height, height), F32),
        (table,),
        flops=heads * 2 * 4 * height * LANES * height,
        moved=heads * 4 * 5 * height * height,
    )
    far = [cross(after(piece, strips), "tensor", 1) for piece in own]
    head_flops = 4 * groups * height * length * size

    def fixed(dims):
        return pl.BlockSpec(dims, lambda h, n=len(dims): (0,) * n)

    def by_head(dims, first=0):
        return pl.BlockSpec(
            (1,) + dims, lambda h, n=len(dims), f=first: (h + f,) + (0,) * n
        )

    def head_rows(first=0):
        return pl.BlockSpec((size, height), lambda h, f=first: (h + f, 0))

    smem = pl.BlockSpec(memory_space=pltpu.SMEM)
    held_dims = [
        (groups, size, height),
        (groups, 8, height),
        (length, LANES),
        (length, LANES),
        (groups, spans, height, height),
    ]
    held_kinds = [F32, F32, BF16, BF16, BF16]
    outs = pl.pallas_call(
        functools.partial(forward_body, groups, heads),
        out_shape=[shape((width, height))] * groups
        + [shape((heads,) + dims, kind) for dims, kind in zip(held_dims, held_kinds)],
        grid=(heads,),
        in_specs=[smem, smem, fixed((1, length)), by_head((5 * height, height))]
        + [fixed((piece_rows, LANES))] * (2 * groups),
        out_specs=[head_rows()] * groups + [by_head(dims) for dims in held_dims],
        scratch_shapes=[
            pltpu.VMEM((length, LANES), BF16),
            pltpu.VMEM((spans, height), jnp.int32),
            pltpu.VMEM((spans, size + 16, height), BF16),
            pltpu.VMEM((2, spans, height, height), F32),
        ],
        cost_estimate=pl.CostEstimate(
            flops=6 * heads * head_flops, bytes_accessed=20 * square, transcendentals=0
        ),
        compiler_params=pltpu.CompilerParams(vmem_limit_bytes=VMEM_LIMIT),
    )(place_arg, rel_bias.astype(F32), segments, strips, *own, *far)
    attended = trade(outs[:groups])
    exact, inverse, vaug, kaug, weights = outs[groups:]
    route_row = routes.reshape(1, height)
    normed_all = trade([after(projected[groups], *own)] * groups)
    residual, normed_ffn, router, sent, grad_sent, attended_t = run(
        functools.partial(route_body, groups, capacity, plan),
        [
            shape((height, features), F32),
            shape((height, features)),
            shape((height, experts_all), F32),
            shape((slots, columns)),
            shape((slots, features)),
            shape((features, height)),
        ],
        (
            after(place_arg, *normed_all),
            tokens_in,
            w_out,
            gain_ffn,
            w_router.T,
            route_row,
            cotangent,
            *attended,
        ),
        smem=(0,),
        flops=2 * height * square,
        moved=4 * square,
    )

    def move_slots(moving):
        return exchange(
            moving.reshape(experts_all, plan[0], -1), ("expert", "context")
        ).reshape(moving.shape)

    got = move_slots(sent)
    pieces = features // (experts_all * tensor_size)
    first_piece = (
        (lax.axis_index("expert") * groups + context_at) * tensor_size + place
    ) * pieces
    first_piece = after(first_piece, sent)
    own_w = lax.dynamic_slice_in_dim(w_qkv, first_piece, pieces, 0)
    own_gain = lax.dynamic_slice_in_dim(gain_attn, first_piece, pieces, 0)
    turned, kt = run(
        functools.partial(turn_body, groups, heads),
        [shape((heads, groups, height, LANES)), shape((heads, size + 16, length))],
        (after(kaug, sent), *own),
        flops=2 * square,
        moved=4 * square,
    )
    grad_got = move_slots(after(grad_sent, turned, own_w, own_gain))
    produced, spare, rows_in, slope, act_other, act_mine = run_expert(
        plan, place_arg, got, w_up[0], w_down[0], None
    )
    produced_back = move_slots(produced)
    back, grad_rows, hid_other, hid_mine = run_expert(
        plan, place_arg, grad_got, w_up[0], w_down[0], (slope, got, spare)
    )
    returned = move_slots(back)

    def both(values, sent_values):
        return jnp.concatenate([values, cross(sent_values, "tensor", 1)], axis=0)

    grad_down = tn(both(act_mine, act_other), both(grad_rows, grad_rows))
    grad_up = tn(both(rows_in, rows_in), both(hid_mine, hid_other))
    extra = -(-(experts_all + 1) // LANES) * LANES
    outs = run(
        functools.partial(combine_body, groups, capacity, plan),
        [
            shape((height, features)),
            shape((height, features), F32),
            shape((height, features)),
            shape((height, extra)),
            shape((8, features), F32),
        ]
        + [shape((width, height))] * groups,
        (
            after(place_arg, grad_down, grad_up),
            produced_back,
            returned,
            residual,
            router,
            route_row,
            cotangent,
            gain_ffn,
            w_router.T,
            w_out,
        ),
        scratch=[pltpu.VMEM((features, height), BF16)],
        smem=(0,),
        flops=4 * height * square,
        moved=8 * square,
    )
    mixed_out, grad_residual, branch, grad_logits, gain_sums = outs[:5]
    grad_pieces = trade(outs[5:])
    mine, other = run(
        functools.partial(weights_body, experts_all),
        [shape((experts_all, pieces, features + extra))] * 2,
        (place_arg, branch, attended_t, normed_ffn, grad_logits, gain_sums),
        scratch=[pltpu.VMEM((features, features + extra), F32)],
        smem=(0,),
        flops=2 * height * square,
        moved=8 * square,
    )

    def pair_sum(kept, received):
        return run(pair_body, shape(kept.shape), (kept, received), moved=6 * kept.size)

    packed = pair_sum(mine, cross(other, "tensor", 1))
    packed_landed = exchange(packed, ("expert", "context"))
    counts = (heads - 1, 1)
    mine_kv, got_kv, q_grads, diags, fars = [], [], [], [], []
    for call_at in range(len(counts)):
        first, count = sum(counts[:call_at]), counts[call_at]
        dims = [
            (groups, size, height),
            (groups, height, 2 * size),
            (groups, height, 2 * size),
            (5 * height, height),
            (2, spans, height),
        ]
        outs = pl.pallas_call(
            functools.partial(backward_body, groups),
            out_shape=[
                shape((count,) + of, kind)
                for of, kind in zip(dims, [BF16, BF16, BF16, F32, F32])
            ],
            grid=(count,),
            in_specs=[smem]
            + [
                by_head(of, first)
                for of in (
                    held_dims[4],
                    held_dims[2],
                    (size + 16, length),
                    held_dims[0],
                    held_dims[1],
                )
            ]
            + [by_head((groups, height, LANES), first)]
            + [head_rows(first)] * groups,
            out_specs=[by_head(of) for of in dims],
            scratch_shapes=[pltpu.VMEM((length, LANES), F32)]
            + [pltpu.VMEM((length, height), F32)] * 2
            + [pltpu.VMEM((length, height), BF16)] * 2,
            cost_estimate=pl.CostEstimate(
                flops=8 * count * head_flops, bytes_accessed=20 * square, transcendentals=0
            ),
            compiler_params=pltpu.CompilerParams(vmem_limit_bytes=VMEM_LIMIT),
        )(after(place_arg, packed), weights, vaug, kt, exact, inverse, turned, *grad_pieces)
        q_grads.append(outs[0])
        mine_kv.append(outs[1])
        got_kv.append(cross(outs[2], "tensor", 1))
        diags.append(outs[3])
        fars.append(outs[4])
    joined = run(
        functools.partial(join_body, counts),
        [shape((piece_rows, LANES))] * groups,
        (*mine_kv, after(got_kv[0], packed_landed), *got_kv[1:], *q_grads),
        moved=4 * groups * piece_rows * LANES,
    )
    landed_pieces = trade(joined)
    by_bucket = run(
        functools.partial(diagonal_body, counts),
        shape((heads, 1, LANES), F32),
        (*diags, *fars),
    )
    mine, other = run(
        functools.partial(qkv_body, groups, heads),
        [shape((experts_all, pieces, 3 * width + BUCKETS))] * 2,
        (place_arg, *normed_all, *joined, by_bucket),
        scratch=[
            pltpu.VMEM((features, 3 * width + BUCKETS), F32),
            pltpu.VMEM((height, 3 * width), BF16),
        ],
        smem=(0,),
    )
    summed = pair_sum(mine, cross(after(other, *landed_pieces), "tensor", 1))
    landed = exchange(summed, ("expert", "context"))
    grad_qkv, grad_gain_attn, grad_rel = run(
        functools.partial(rows_body, groups, heads),
        [
            shape((pieces, 3 * features), F32),
            shape((pieces,), F32),
            shape((heads, BUCKETS), F32),
        ],
        (place_arg, landed, own_w, own_gain),
        smem=(0,),
        moved=2 * landed.size,
    )
    grad_tokens = run(
        functools.partial(finish_body, groups, heads),
        shape((height, features)),
        (place_arg, tokens_in, gain_attn, w_qkv, grad_residual, *landed_pieces),
        scratch=[
            pltpu.VMEM((features, height), F32),
            pltpu.VMEM((groups, height, width), BF16),
            pltpu.VMEM((groups, height, width), BF16),
        ],
        smem=(0,),
        flops=6 * height * square,
        moved=8 * square,
    )
    reduced = jnp.sum(packed_landed.astype(F32), axis=0)
    return (
        mixed_out,
        grad_tokens,
        grad_gain_attn,
        grad_qkv,
        grad_rel,
        reduced[:, :features].T,
        reduced[:, features + experts_all],
        reduced[:, features : features + experts_all],
        grad_up[None],
        grad_down[None],
    )


def solution(mesh):
    rows = ("expert", "context", "tensor")
    in_specs = (
        P(rows, None),
        P(),
        P(),
        P("context", None),
        P(),
        P(),
        P(),
        P(("expert", "context"), None, None),
        P(("expert", "context"), None, None),
        P("expert", None),
        P(rows, None),
        P(rows, None),
    )
    out_specs = (
        P(rows, None),
        P(rows, None),
        P(rows),
        P(rows, None),
        P("context", None),
        P(None, rows),
        P(rows),
        P(rows, None),
        P(("expert", "context"), None, "tensor"),
        P(("expert", "context"), "tensor", None),
    )
    return jax.shard_map(
        per_device, mesh=mesh, in_specs=in_specs, out_specs=out_specs, check_vma=False
    )
```

```python
import functools

import jax
import jax.numpy as jnp
from jax import lax
from jax.experimental import pallas as pl
from jax.experimental.pallas import tpu as pltpu
from jax.sharding import PartitionSpec as P

EPSILON = 1e-06
THRESHOLDS = (12, 16, 23, 32, 46, 64, 91)
FAR_LEFT = 15
FAR_RIGHT = 31
EXCLUDED = -1e30
LANES = 128
BF16 = jnp.bfloat16
F32 = jnp.float32
VMEM_LIMIT = 56 * 1024 * 1024
BUCKETS = 32
CHUNKS = 4
EXPERT_LIMIT = 24 * 1024 * 1024
PART = 256


def bucket_of(offset):
    distance = jnp.abs(offset)
    beyond = jnp.zeros_like(distance)
    for threshold in THRESHOLDS:
        beyond = beyond + (distance >= threshold).astype(jnp.int32)
    nearby = jnp.where(distance < 8, distance, 8 + beyond)
    return nearby + 16 * (offset > 0).astype(jnp.int32)


def nn(left, right):
    return lax.dot_general(left, right, (((1,), (0,)), ((), ())), preferred_element_type=F32)


def nt(left, right):
    return lax.dot_general(left, right, (((1,), (1,)), ((), ())), preferred_element_type=F32)


def tn(left, right):
    return lax.dot_general(left, right, (((0,), (0,)), ((), ())), preferred_element_type=F32)


def iota(shape, axis):
    return lax.broadcasted_iota(jnp.int32, shape, axis)


def three_terms(values):
    high = values.astype(BF16).astype(F32)
    middle = (values - high).astype(BF16).astype(F32)
    return high, middle, values - high - middle


def specs_for(count, smem=()):
    return [
        pl.BlockSpec(memory_space=pltpu.SMEM if i in smem else pltpu.VMEM) for i in range(count)
    ]


def run(body, out_shape, args, scratch=(), smem=(), flops=0, moved=0, limit=VMEM_LIMIT):
    return pl.pallas_call(
        body,
        out_shape=out_shape,
        in_specs=specs_for(len(args), smem),
        scratch_shapes=list(scratch),
        cost_estimate=pl.CostEstimate(flops=flops, bytes_accessed=moved, transcendentals=0),
        compiler_params=pltpu.CompilerParams(vmem_limit_bytes=limit),
    )(*args)


def shape(dims, kind=BF16):
    return jax.ShapeDtypeStruct(dims, kind)


def project_body(heads, place_ref, tokens_ref, gain_ref, w_ref, *refs):
    groups = len(refs) - 2
    piece_refs, normed_ref, all_ref = refs[:groups], refs[groups], refs[groups + 1]
    height, features = tokens_ref.shape
    width = features // groups
    size = width // heads
    group = place_ref[1]
    tokens = tokens_ref[...].astype(F32)
    inverse = lax.rsqrt(jnp.mean(tokens * tokens, axis=-1, keepdims=True) + EPSILON)
    normed = (tokens * inverse * gain_ref[...].astype(F32)[None, :]).astype(BF16)
    normed_ref[...] = jnp.transpose(normed.astype(F32)).astype(BF16)
    turned = jnp.transpose(nn(normed, w_ref[:, :features])).astype(BF16)
    keys = nn(normed, w_ref[:, features : 2 * features]).astype(BF16)
    values = nn(normed, w_ref[:, 2 * features :]).astype(BF16)
    for at in range(groups):
        for head in range(heads):
            lanes = slice(at * width + head * size, at * width + (head + 1) * size)
            all_ref[at ^ group, head * height : (head + 1) * height, :] = jnp.concatenate(
                [keys[:, lanes], values[:, lanes]], axis=1
            )
        for half in range(height // LANES):
            first = heads * height + half * width
            all_ref[at ^ group, first : first + width, :] = turned[
                at * width : (at + 1) * width, half * LANES : (half + 1) * LANES
            ]
    for at in range(groups):
        piece_refs[at][...] = all_ref[at]


def q_rows(piece_ref, heads, height, size, head):
    width = heads * size
    parts = []
    for half in range(height // LANES):
        first = heads * height + half * width + head * size
        parts.append(piece_ref[pl.ds(pl.multiple_of(first, 16), size), :])
    return jnp.concatenate(parts, axis=1)


def forward_body(groups, heads, place_ref, bias_ref, seg_ref, strip_ref, *refs):
    own_refs, far_refs, out_refs = (refs[i * groups : (i + 1) * groups] for i in range(3))
    exact_ref, inverse_ref, vaug_ref, kaug_ref, weight_ref = refs[3 * groups : 3 * groups + 5]
    extra_all, docs_all, vt_ref, score_ref = refs[3 * groups + 5 :]
    size, height = out_refs[0].shape
    spans = kaug_ref.shape[1] // height
    place, group = place_ref[0], place_ref[1]
    head = pl.program_id(0)
    tall = size + 16
    rest = LANES - size

    @pl.when(head == 0)
    def _():
        row = iota((LANES, height), 0) - size
        for span in range(spans):
            docs = seg_ref[0:1, span * height : (span + 1) * height]
            docs_all[span : span + 1, :] = docs
            extra = jnp.where((row >= 0) & (row < 3) & (docs != row), EXCLUDED, 0.0)
            extra = jnp.where(row - 3 == span, 1.0, extra)
            extra_all[span * height : (span + 1) * height, :] = jnp.transpose(extra).astype(BF16)

    row, column = iota((tall, LANES), 0), iota((tall, LANES), 1)
    pick_v = (((row < size) & (row + size == column)) | ((row == size) & (column == 0))).astype(
        BF16
    )
    lane = iota((height, LANES), 1)
    low_half = lane < size
    ones = jnp.where(lane < 3, 1.0, 0.0).astype(BF16)
    extra_row = iota((rest, height), 0)
    queries_all = []
    for at in range(groups):
        block = at ^ group
        for source, parity in ((own_refs[at], place), (far_refs[at], 1 - place)):
            span = 2 * block + parity
            rows = pl.ds(pl.multiple_of(span * height, height), height)
            both = source[pl.ds(pl.multiple_of(head * height, height), height), :]
            keys = jnp.where(low_half, both, extra_all[rows, :])
            values = jnp.where(low_half, ones, both)
            kaug_ref[0, rows, :] = keys
            vaug_ref[0, rows, :] = values
            vt_ref[span] = nt(pick_v, values).astype(BF16)
        span = 2 * block + place
        docs = docs_all[pl.ds(span, 1), :]
        apart = extra_row - 3 - span
        far = jnp.where(
            apart <= -2,
            bias_ref[head, FAR_LEFT],
            jnp.where(apart >= 2, bias_ref[head, FAR_RIGHT], 0.0),
        )
        extra = jnp.where(
            extra_row < 3,
            jnp.where(docs == extra_row, 1.0, 0.0),
            jnp.where(extra_row < 3 + spans, far, 0.0),
        )
        queries_all.append(
            jnp.concatenate(
                [q_rows(own_refs[at], heads, height, size, head), extra.astype(BF16)], axis=0
            )
        )
    for at in range(groups):
        span = 2 * (at ^ group) + place
        start = jnp.clip(span - 1, 0, spans - 3)
        queries = queries_all[at]
        slot = at % 2
        row_max = None
        for step in range(spans):
            key_span = (start + step) if step < 3 else ((start + step) & (spans - 1))
            rows = pl.ds(pl.multiple_of(key_span * height, height), height)
            scores = nn(kaug_ref[0, rows, :], queries)
            if step < 3:
                level = pl.multiple_of((key_span - span + 2) * height, height)
                scores = scores + strip_ref[0, pl.ds(level, height), :]
            score_ref[slot, step] = scores
            best = jnp.max(scores, axis=0, keepdims=True)
            row_max = best if row_max is None else jnp.maximum(row_max, best)
        total = jnp.zeros((tall, height), F32)
        for step in range(spans):
            key_span = (start + step) if step < 3 else ((start + step) & (spans - 1))
            weights = jnp.exp(score_ref[slot, step] - row_max).astype(BF16)
            weight_ref[0, at, key_span] = weights
            total = total + nn(vt_ref[key_span], weights)
        inverse = 1.0 / total[size : size + 1]
        result = total[:size] * inverse
        out_refs[at][...] = result.astype(BF16)
        exact_ref[0, at] = result
        inverse_ref[0, at] = jnp.broadcast_to(inverse, (8, height))


def turn_body(groups, heads, kaug_ref, *refs):
    piece_refs, out_ref, kt_ref = refs[:groups], refs[groups], refs[groups + 1]
    height = out_ref.shape[2]
    size = out_ref.shape[3] // 2
    spans = kaug_ref.shape[1] // height
    row, column = iota((size + 16, LANES), 0), iota((size + 16, LANES), 1)
    pick_k = (
        ((row < size) & (row == column))
        | ((row >= size) & (row < size + spans) & (row + 3 == column))
    ).astype(BF16)
    blank = jnp.zeros((size, height), F32)
    for head in range(heads):
        kt_ref[head] = nt(pick_k, kaug_ref[head]).astype(BF16)
        for at in range(groups):
            queries = q_rows(piece_refs[at], heads, height, size, head).astype(F32)
            out_ref[head, at] = jnp.transpose(jnp.concatenate([queries, blank], axis=0)).astype(
                BF16
            )


def backward_body(groups, place_ref, *refs):
    weight_ref, vaug_ref, kt_ref, exact_ref, inverse_ref, q_ref = refs[:6]
    grad_refs = refs[6 : 6 + groups]
    dq_ref, mine_ref, other_ref, diag_ref, far_ref, dkv_ref = refs[6 + groups : 12 + groups]
    slope_refs, score_refs = refs[12 + groups : 14 + groups], refs[14 + groups : 16 + groups]
    weight_all, sems = refs[16 + groups :]
    head = pl.program_id(0)
    slot = lax.rem(head, 2)

    def bring_weights(which, into):
        return [
            pltpu.make_async_copy(
                weight_ref.at[which, at], weight_all.at[into, at], sems.at[into, at]
            )
            for at in range(groups)
        ]

    @pl.when(head == 0)
    def _():
        for copy in bring_weights(0, 0):
            copy.start()

    @pl.when(head + 1 < pl.num_programs(0))
    def _():
        for copy in bring_weights(head + 1, 1 - slot):
            copy.start()

    arriving = bring_weights(head, slot)
    size, height = grad_refs[0].shape
    length = vaug_ref.shape[1]
    spans = length // height
    place, group = place_ref[0], place_ref[1]
    diag_ref[...] = jnp.zeros_like(diag_ref)
    extra_row = iota((LANES - size, height), 0)
    blank = jnp.zeros((size, height), F32)
    span_row = iota((spans, height), 0)
    left_total = jnp.zeros((spans, height), F32)
    right_total = jnp.zeros((spans, height), F32)
    for at in range(groups):
        span = 2 * (at ^ group) + place
        start = jnp.clip(span - 1, 0, spans - 3)
        slope_ref, score_ref = slope_refs[at % 2], score_refs[at % 2]
        grads = (grad_refs[at][...].astype(F32) * inverse_ref[0, at, 0:1]).astype(BF16)
        grads32 = grads.astype(F32)
        delta = jnp.sum(grads32 * exact_ref[0, at], axis=0, keepdims=True)
        high, middle, low = three_terms(-delta)
        extra = jnp.where(
            extra_row == 0,
            high,
            jnp.where(extra_row == 1, middle, jnp.where(extra_row == 2, low, 0.0)),
        )
        slope_ref[...] = nn(
            vaug_ref[0], jnp.concatenate([extra.astype(BF16), grads], axis=0)
        )
        turned = jnp.transpose(jnp.concatenate([blank, grads32], axis=0)).astype(BF16)
        sides = jnp.concatenate([q_ref[0, at], turned], axis=0)
        arriving[at].wait()
        for key in range(spans):
            rows = slice(key * height, (key + 1) * height)
            score_ref[rows, :] = (
                weight_all[slot, at, key].astype(F32) * slope_ref[rows, :]
            ).astype(BF16)
        both = jnp.concatenate(
            [score_ref[...], weight_all[slot, at].reshape(length, height)], axis=1
        )
        product = nn(both, sides)
        if at == 0:
            dkv_ref[...] = product
        else:
            dkv_ref[...] = dkv_ref[...] + product
        total = nn(kt_ref[0], score_ref[...])
        dq_ref[0, at] = total[:size].astype(BF16)
        sums = total[size : size + spans]
        left_total = left_total + jnp.where(span_row < start, sums, 0.0)
        right_total = right_total + jnp.where(span_row >= start + 3, sums, 0.0)
        rows = pl.ds(pl.multiple_of(start * height, height), 3 * height)
        level = pl.ds(pl.multiple_of((start - span + 2) * height, height), 3 * height)
        diag_ref[0, level, :] = diag_ref[0, level, :] + score_ref[rows, :].astype(F32)
    far_ref[0, 0] = left_total
    far_ref[0, 1] = right_total
    for at in range(groups):
        for target, parity in ((mine_ref, place), (other_ref, 1 - place)):
            first = pl.multiple_of((2 * (at ^ group) + parity) * height, height)
            target[0, at] = dkv_ref[pl.ds(first, height), :].astype(BF16)


def join_body(counts, *refs):
    calls = len(counts)
    mine_refs, got_refs, dq_refs = (refs[i * calls : (i + 1) * calls] for i in range(3))
    piece_refs = refs[3 * calls :]
    size, height = dq_refs[0].shape[2:]
    heads = sum(counts)
    width = heads * size
    for at, piece_ref in enumerate(piece_refs):
        head = 0
        for call_at, count in enumerate(counts):
            for inner in range(count):
                kept = mine_refs[call_at][inner, at].astype(F32)
                piece_ref[head * height : (head + 1) * height, :] = (
                    kept + got_refs[call_at][inner, at].astype(F32)
                ).astype(BF16)
                for half in range(height // LANES):
                    first = heads * height + half * width + head * size
                    piece_ref[first : first + size, :] = dq_refs[call_at][
                        inner, at, :, half * LANES : (half + 1) * LANES
                    ]
                head += 1


def slot_plan(capacity, features):
    base = capacity // 16 * 16
    left = capacity - base
    if base and left and 16 % left == 0 and (2 * features) % (LANES * (16 // left)) == 0:
        return base, left, 16 // left
    return -(-capacity // 8) * 8, 0, 0


def slot_marks(shape_of, axis, chosen, rank, capacity, plan):
    base, left, parts = plan
    position = iota(shape_of, axis)
    limit = base if left else capacity
    marks = [jnp.where(position == jnp.where(rank < limit, chosen * base + rank, -1), 1.0, 0.0)]
    spare = rank - base
    for part in range(parts):
        slot = chosen * 16 + part * left + spare
        slot = jnp.where((spare >= 0) & (spare < left), slot, -1)
        marks.append(jnp.where(position == slot, 1.0, 0.0))
    return [mark.astype(BF16) for mark in marks]


def route_body(
    groups,
    capacity,
    plan,
    place_ref,
    tokens_ref,
    w_out_ref,
    gain_ref,
    w_router_ref,
    route_row_ref,
    cotangent_ref,
    *refs,
):
    pieces = refs[:groups]
    residual_ref, normed_ref, router_ref, sent_ref, grad_sent_ref, attended_ref = refs[groups:]
    height, features = tokens_ref.shape
    experts = w_router_ref.shape[0]
    slots = sent_ref.shape[0]
    width = pieces[0].shape[0]
    group = place_ref[1]
    for at in range(groups):
        first = pl.multiple_of((at ^ group) * width, width)
        attended_ref[pl.ds(first, width), :] = pieces[at][...]
    residual = tokens_ref[...].astype(F32) + tn(attended_ref[...], w_out_ref[...])
    residual_ref[...] = residual
    inverse = lax.rsqrt(jnp.mean(residual * residual, axis=-1, keepdims=True) + EPSILON)
    normed = (residual * inverse * gain_ref[...].astype(F32)[None, :]).astype(BF16)
    normed_ref[...] = normed
    logits = nt(normed, w_router_ref[...])
    powers = jnp.exp(logits - jnp.max(logits, axis=-1, keepdims=True))
    router = powers / jnp.sum(powers, axis=-1, keepdims=True)
    router_ref[...] = router
    chosen = route_row_ref[...]
    marks = iota((experts, height), 0) == chosen
    onehot = jnp.transpose(jnp.where(marks, 1.0, 0.0))
    gate = jnp.sum(onehot * router, axis=-1, keepdims=True)
    grad_expert = (gate * cotangent_ref[...].astype(F32)).astype(BF16)
    rows = jnp.concatenate([normed, grad_expert], axis=1)
    earlier = (iota((height, height), 0) < iota((height, height), 1)).astype(BF16)
    before = nn(jnp.where(marks, 1.0, 0.0).astype(BF16), earlier)
    rank = jnp.sum(jnp.where(marks, before, 0.0), axis=0, keepdims=True).astype(jnp.int32)
    dispatch = slot_marks((slots, height), 0, chosen, rank, capacity, plan)
    sent_ref[:, :features] = nn(dispatch[0], normed).astype(BF16)
    grad_sent_ref[...] = nn(dispatch[0], grad_expert).astype(BF16)
    if plan[1]:
        span = 2 * features // plan[2]
        spare = nn(dispatch[1], rows[:, :span])
        for part in range(1, plan[2]):
            spare = spare + nn(dispatch[1 + part], rows[:, part * span : (part + 1) * span])
        sent_ref[:, features:] = spare.astype(BF16)


def spare_marks(sources, plan):
    base, left, parts = plan
    target = iota((sources * left, sources * 16), 0)
    origin = iota((sources * left, sources * 16), 1)
    source = target // left
    return [
        (origin == source * 16 + part * left + (target - source * left)).astype(BF16)
        for part in range(parts)
    ]


def unpack_spare(rows_ref, packed, plan, first_part):
    main = packed.shape[0]
    marks = spare_marks(main // 16, plan)
    half = plan[2] // 2
    span = rows_ref.shape[1] // half
    for part in range(half):
        rows_ref[main:, part * span : (part + 1) * span] = nn(
            marks[first_part + part], packed
        ).astype(BF16)


def bring(place, up_ref, down_ref, up_all, down_all, sems):
    chunk = up_all.shape[2]
    copies = []
    for at in range(CHUNKS):
        half = (1 - place) if at < CHUNKS // 2 else place
        first = half * (chunk * CHUNKS // 2) + at % (CHUNKS // 2) * chunk
        part = pl.ds(pl.multiple_of(first, chunk), chunk)
        copies.append(
            (
                pltpu.make_async_copy(up_ref.at[:, part], up_all.at[at], sems.at[0, at]),
                pltpu.make_async_copy(down_ref.at[part, :], down_all.at[at], sems.at[1, at]),
            )
        )
    return copies


def expert_forward_body(
    plan,
    place_ref,
    got_ref,
    up_ref,
    down_ref,
    back_ref,
    spare_ref,
    rows_ref,
    slope_ref,
    other_ref,
    mine_ref,
    total_ref,
    up_all,
    down_all,
    sems,
):
    main, features = back_ref.shape
    chunk = up_all.shape[2]
    copies = bring(place_ref[0], up_ref, down_ref, up_all, down_all, sems)
    for up_copy, down_copy in copies:
        up_copy.start()
        down_copy.start()
    rows_ref[:main, :] = got_ref[:, :features]
    if plan[1]:
        unpack_spare(rows_ref, got_ref[:, features:], plan, 0)
    for at in range(CHUNKS):
        active_ref = other_ref if at < CHUNKS // 2 else mine_ref
        base = at % (CHUNKS // 2) * chunk
        copies[at][0].wait()
        for first in range(0, chunk, PART):
            lanes = slice(base + first, base + first + PART)
            hidden = nn(rows_ref[...], up_all[at, :, first : first + PART])
            below = 0.5 * (1.0 + lax.erf(hidden * (2.0**-0.5)))
            bell = jnp.exp(-0.5 * hidden * hidden) * 0.3989422804014327
            active_ref[:, lanes] = (hidden * below).astype(BF16)
            slope_ref[at // (CHUNKS // 2), :, lanes] = (below + hidden * bell).astype(BF16)
        copies[at][1].wait()
        product = nn(active_ref[:, base : base + chunk], down_all[at])
        if at == 0:
            total_ref[...] = product
        else:
            total_ref[...] = total_ref[...] + product
    back_ref[...] = total_ref[:main, :].astype(BF16)
    if plan[1]:
        spare_ref[...] = total_ref[main:, :].astype(BF16)
    else:
        spare_ref[...] = jnp.zeros_like(spare_ref)


def expert_backward_body(
    plan,
    place_ref,
    got_ref,
    up_ref,
    down_ref,
    slope_ref,
    packed_ref,
    spare_ref,
    back_ref,
    rows_ref,
    other_ref,
    mine_ref,
    total_ref,
    up_all,
    down_all,
    sems,
):
    main, features = got_ref.shape
    chunk = up_all.shape[2]
    copies = bring(place_ref[0], up_ref, down_ref, up_all, down_all, sems)
    for up_copy, down_copy in copies:
        down_copy.start()
        up_copy.start()
    rows_ref[:main, :] = got_ref[...]
    if plan[1]:
        unpack_spare(rows_ref, packed_ref[:, features:], plan, plan[2] // 2)
    for at in range(CHUNKS):
        hidden_ref = other_ref if at < CHUNKS // 2 else mine_ref
        base = at % (CHUNKS // 2) * chunk
        copies[at][1].wait()
        for first in range(0, chunk, PART):
            lanes = slice(base + first, base + first + PART)
            grad_active = nt(rows_ref[...], down_all[at, first : first + PART, :])
            slope = slope_ref[at // (CHUNKS // 2), :, lanes].astype(F32)
            hidden_ref[:, lanes] = (grad_active * slope).astype(BF16)
        copies[at][0].wait()
        product = nt(hidden_ref[:, base : base + chunk], up_all[at])
        if at == 0:
            total_ref[...] = product
        else:
            total_ref[...] = total_ref[...] + product
    back_ref[:, :features] = total_ref[:main, :].astype(BF16)
    if plan[1]:
        spare = jnp.concatenate([spare_ref[...], total_ref[main:, :].astype(BF16)], axis=1)
        span = 2 * features // plan[2]
        packed = jnp.zeros((main, span), F32)
        for part, marks in enumerate(spare_marks(main // 16, plan)):
            packed = packed + tn(marks, spare[:, part * span : (part + 1) * span])
        back_ref[:, features:] = packed.astype(BF16)


def run_expert(plan, place_arg, got, up, down, forward):
    main = got.shape[0]
    features, hidden_size = up.shape
    spare = main // 16 * plan[1]
    slots = main + spare
    columns = features + (2 * features // plan[2] if plan[1] else 0)
    spare = max(spare, 8)
    halves = [shape((slots, hidden_size // 2))] * 2
    if forward is None:
        body = expert_forward_body
        out_shape = [shape((main, features)), shape((spare, features)), shape((slots, features))]
        out_shape += [shape((2, slots, hidden_size // 2))] + halves
        args, flops = (got, up, down), 0
    else:
        body = expert_backward_body
        out_shape = [shape((main, columns)), shape((slots, features))] + halves
        args, flops = (got, up, down) + forward, 4 * slots * features * hidden_size
    args = (place_arg,) + args
    specs = specs_for(len(args), (0,))
    specs[2] = specs[3] = pl.BlockSpec(memory_space=pltpu.HBM)
    chunk = hidden_size // CHUNKS
    return pl.pallas_call(
        functools.partial(body, plan),
        out_shape=out_shape,
        in_specs=specs,
        scratch_shapes=[
            pltpu.VMEM((slots, features), F32),
            pltpu.VMEM((CHUNKS, features, chunk), BF16),
            pltpu.VMEM((CHUNKS, chunk, features), BF16),
            pltpu.SemaphoreType.DMA((2, CHUNKS)),
        ],
        cost_estimate=pl.CostEstimate(flops=flops, bytes_accessed=flops // 400, transcendentals=0),
        compiler_params=pltpu.CompilerParams(vmem_limit_bytes=EXPERT_LIMIT),
    )(*args)


def combine_body(
    groups,
    capacity,
    plan,
    place_ref,
    produced_ref,
    got_ref,
    residual_ref,
    router_ref,
    route_row_ref,
    cotangent_ref,
    gain_ref,
    w_router_ref,
    w_out_ref,
    mixed_ref,
    grad_residual_ref,
    branch_ref,
    logits_ref,
    gain_out_ref,
    *refs,
):
    pieces, turned_ref = refs[:groups], refs[groups]
    height, experts = router_ref.shape
    features = residual_ref.shape[1]
    slots = got_ref.shape[0]
    width = pieces[0].shape[0]
    group = place_ref[1]
    chosen_row = route_row_ref[...]
    marks = jnp.where(iota((experts, height), 0) == chosen_row, 1.0, 0.0)
    earlier = (iota((height, height), 0) < iota((height, height), 1)).astype(BF16)
    before = nn(marks.astype(BF16), earlier)
    rank_row = jnp.sum(marks * before, axis=0, keepdims=True)
    onehot = jnp.transpose(marks) > 0.5
    pair_row = iota((8, height), 0)
    pairs = jnp.transpose(jnp.where(pair_row == 0, chosen_row.astype(F32), rank_row))
    chosen = pairs[:, 0:1].astype(jnp.int32)
    rank = pairs[:, 1:2].astype(jnp.int32)
    combine = slot_marks((height, slots), 1, chosen, rank, capacity, plan)
    back = jnp.concatenate(
        [nn(combine[0], produced_ref[...]), nn(combine[0], got_ref[:, :features])], axis=1
    )
    if plan[1]:
        spare = got_ref[:, features:]
        back = back + jnp.concatenate([nn(marks, spare) for marks in combine[1:]], axis=1)
    router = router_ref[...]
    gate = jnp.sum(jnp.where(onehot, router, 0.0), axis=-1, keepdims=True)
    residual = residual_ref[...]
    inverse = lax.rsqrt(jnp.mean(residual * residual, axis=-1, keepdims=True) + EPSILON)
    unit = residual * inverse
    grad_mixed = cotangent_ref[...].astype(F32)
    gathered = back[:, :features]
    mixed_ref[...] = (residual + gate * gathered).astype(BF16)
    grad_gate = jnp.sum(grad_mixed * gathered, axis=-1, keepdims=True)
    grad_logits = (router * (jnp.where(onehot, grad_gate, 0.0) - gate * grad_gate)).astype(BF16)
    grad_normed = back[:, features:] + nn(grad_logits, w_router_ref[...])
    grad_unit = grad_normed * gain_ref[...].astype(F32)[None, :]
    grad_residual = grad_mixed + inverse * (
        grad_unit - unit * jnp.mean(grad_unit * unit, axis=-1, keepdims=True)
    )
    branch = grad_residual.astype(BF16)
    turned_ref[...] = nt(w_out_ref[...], branch).astype(BF16)
    for at in range(groups):
        first = pl.multiple_of((at ^ group) * width, width)
        pieces[at][...] = turned_ref[pl.ds(first, width), :]
    grad_residual_ref[...] = grad_residual
    branch_ref[...] = branch
    spare_lanes = logits_ref.shape[1] - experts
    logits_ref[...] = jnp.concatenate([grad_logits, jnp.zeros((height, spare_lanes), BF16)], axis=1)
    sums = jnp.sum(grad_normed * unit, axis=0, keepdims=True)
    gain_out_ref[...] = jnp.broadcast_to(sums, gain_out_ref.shape)


def qkv_body(groups, heads, place_ref, *refs):
    normed_refs, piece_refs = refs[:groups], refs[groups : 2 * groups]
    bucket_ref, mine_ref, other_ref, total_ref, rows_ref = refs[2 * groups :]
    pieces = mine_ref.shape[1]
    wide = rows_ref.shape[1]
    height = normed_refs[0].shape[1]
    width = rows_ref.shape[1] // 3
    for at in range(groups):
        piece = piece_refs[at]
        for head in range(heads):
            rows_ref[:, head * LANES : (head + 1) * LANES] = piece[
                head * height : (head + 1) * height, :
            ]
        parts = [
            piece[heads * height + half * width : heads * height + (half + 1) * width, :]
            for half in range(height // LANES)
        ]
        turned = jnp.concatenate(parts, axis=1).astype(F32)
        rows_ref[:, 2 * width :] = jnp.transpose(turned).astype(BF16)
        product = nn(normed_refs[at][...], rows_ref[...])
        if at == 0:
            total_ref[:, :wide] = product
        else:
            total_ref[:, :wide] = total_ref[:, :wide] + product
    row = iota((total_ref.shape[0], BUCKETS), 0) % pieces
    buckets = jnp.zeros((total_ref.shape[0], BUCKETS), F32)
    for head in range(heads):
        buckets = jnp.where(row == head, bucket_ref[head, :, :BUCKETS], buckets)
    total_ref[:, wide:] = buckets
    split_rows(place_ref[0], total_ref, mine_ref, other_ref)


def rows_body(
    groups, heads, place_ref, landed_ref, w_ref, gain_ref, out_ref, gain_out_ref, bucket_ref
):
    sources, _, columns = landed_ref.shape
    width = (columns - BUCKETS) // 3
    size = width // heads
    features = groups * width
    for group in range(groups):
        total = landed_ref[group].astype(F32)
        for expert in range(1, sources // groups):
            total = total + landed_ref[expert * groups + group].astype(F32)
        out_ref[:, group * width : (group + 1) * width] = total[:, 2 * width : 3 * width]
        for head in range(heads):
            for part in range(2):
                source = head * 2 * size + part * size
                first = (part + 1) * features + group * width + head * size
                out_ref[:, first : first + size] = total[:, source : source + size]
    sums = lax.dot_general(
        jnp.ones((8, 3 * features), F32),
        w_ref[...].astype(F32) * out_ref[...],
        (((1,), (1,)), ((), ())),
        precision=lax.Precision.HIGHEST,
        preferred_element_type=F32,
    )
    gain_out_ref[...] = sums[0] / gain_ref[...].astype(F32)
    buckets = jnp.zeros((landed_ref.shape[1], BUCKETS), F32)
    for expert in range(sources // groups):
        buckets = buckets + landed_ref[expert * groups + place_ref[1]][:, 3 * width :].astype(F32)
    bucket_ref[...] = buckets[:heads]


def finish_body(groups, heads, place_ref, tokens_ref, gain_ref, w_ref, residual_ref, *refs):
    piece_refs = refs[:groups]
    out_ref, turned_ref, k_all, v_all = refs[groups:]
    height, features = tokens_ref.shape
    width = features // groups
    size = width // heads
    group = place_ref[1]
    for at in range(groups):
        piece = piece_refs[at]
        first = pl.multiple_of((at ^ group) * width, width)
        for half in range(height // LANES):
            source = heads * height + half * width
            turned_ref[pl.ds(first, width), half * LANES : (half + 1) * LANES] = piece[
                source : source + width, :
            ].astype(F32)
        for head in range(heads):
            both = piece[head * height : (head + 1) * height, :]
            lanes = slice(head * size, (head + 1) * size)
            k_all[at ^ group, :, lanes] = both[:, :size]
            v_all[at ^ group, :, lanes] = both[:, size:]
    grad_normed = nt(jnp.transpose(turned_ref[...]).astype(BF16), w_ref[:, :features])
    for part, source in ((1, k_all), (2, v_all)):
        joined = jnp.concatenate([source[at] for at in range(groups)], axis=1)
        grad_normed = grad_normed + nt(joined, w_ref[:, part * features : (part + 1) * features])
    tokens = tokens_ref[...].astype(F32)
    inverse = lax.rsqrt(jnp.mean(tokens * tokens, axis=-1, keepdims=True) + EPSILON)
    unit = tokens * inverse
    grad_unit = grad_normed * gain_ref[...].astype(F32)[None, :]
    grad = inverse * (grad_unit - unit * jnp.mean(grad_unit * unit, axis=-1, keepdims=True))
    out_ref[...] = (residual_ref[...] + grad).astype(BF16)


def strip_body(table_ref, strips_ref):
    heads, rows, height = strips_ref.shape
    used = rows - height
    offset = iota((used, LANES), 0) - 2 * height
    onehot = (bucket_of(offset) == iota((used, LANES), 1)).astype(BF16)
    lane = iota((used, height), 1)
    blank = jnp.zeros((height, height), F32)
    for head in range(heads):
        values = nn(onehot, table_ref[head])
        moved = 1
        while moved < height:
            values = jnp.where((lane & moved) != 0, pltpu.roll(values, moved, 0), values)
            moved *= 2
        strips_ref[head, :height] = blank
        strips_ref[head, height:used] = values[height:]
        strips_ref[head, used:] = blank


def diagonal_body(counts, *refs):
    calls = len(counts)
    out_ref = refs[2 * calls]
    places = [(call_at, inner) for call_at in range(calls) for inner in range(counts[call_at])]
    height = refs[0].shape[2]
    total_rows = 5 * height
    lane = iota((total_rows, height), 1)
    offset = iota((total_rows, LANES), 0) - 2 * height
    table = (bucket_of(offset) == iota((total_rows, LANES), 1)).astype(F32)
    lane_out = iota((1, LANES), 1)
    blank = jnp.zeros((height, height), F32)
    for head, (call_at, inner) in enumerate(places):
        diag_ref, far_ref = refs[call_at].at[inner], refs[calls + call_at].at[inner]
        values = jnp.concatenate([blank, diag_ref[height : 4 * height, :], blank], axis=0)
        moved = 1
        while moved < height:
            values = jnp.where(
                (lane & moved) != 0, pltpu.roll(values, total_rows - moved, 0), values
            )
            moved *= 2
        sums = jnp.sum(values, axis=1, keepdims=True)
        by_bucket = jnp.sum(sums * table, axis=0, keepdims=True)
        by_bucket = by_bucket + jnp.where(
            lane_out == FAR_LEFT, jnp.sum(far_ref[0]) + jnp.sum(diag_ref[:height, :]), 0.0
        )
        out_ref[head] = by_bucket + jnp.where(
            lane_out == FAR_RIGHT, jnp.sum(far_ref[1]) + jnp.sum(diag_ref[4 * height :, :]), 0.0
        )


def split_rows(place, source_ref, mine_ref, other_ref):
    experts_all, pieces, columns = mine_ref.shape
    for parity in range(2):

        @pl.when(place == parity)
        def _():
            for at in range(experts_all):
                for target, which in ((mine_ref, parity), (other_ref, 1 - parity)):
                    first = (2 * at + which) * pieces
                    target[at] = source_ref[first : first + pieces, :].astype(BF16)


def weights_body(
    experts,
    place_ref,
    branch_ref,
    attended_ref,
    normed_ref,
    logits_ref,
    gain_ref,
    mine_ref,
    other_ref,
    packed_ref,
):
    features = branch_ref.shape[1]
    extra = logits_ref.shape[1]
    branch = jnp.transpose(branch_ref[...].astype(F32)).astype(BF16)
    packed_ref[:, :features] = nt(branch, attended_ref[...])
    normed = jnp.transpose(normed_ref[...].astype(F32)).astype(BF16)
    column = jnp.transpose(gain_ref[...])[:, :1]
    packed_ref[:, features:] = nn(normed, logits_ref[...]) + jnp.where(
        iota((features, extra), 1) == experts, column, 0.0
    )
    split_rows(place_ref[0], packed_ref, mine_ref, other_ref)


def pair_body(kept_ref, got_ref, out_ref):
    out_ref[...] = (kept_ref[...].astype(F32) + got_ref[...].astype(F32)).astype(BF16)


def exchange(moving, axis):
    return lax.all_to_all(moving, axis, split_axis=0, concat_axis=0, tiled=True)


def cross(moving, axis, distance):
    size = lax.axis_size(axis)
    return lax.ppermute(moving, axis, [(i, i ^ distance) for i in range(size)])


def trade(pieces):
    return [
        piece if at == 0 else cross(piece, "context", at) for at, piece in enumerate(pieces)
    ]


def after(values, *others):
    return lax.optimization_barrier((values,) + others)[0]


def per_device(
    tokens_in,
    gain_attn,
    w_qkv,
    rel_bias,
    w_out,
    gain_ffn,
    w_router,
    w_up,
    w_down,
    segments,
    routes,
    cotangent,
):
    groups = lax.axis_size("context")
    tensor_size = lax.axis_size("tensor")
    expert_size = lax.axis_size("expert")
    height, features = tokens_in.shape
    heads = rel_bias.shape[0]
    width = features // groups
    size = width // heads
    length = segments.shape[1]
    spans = length // height
    experts_all = expert_size * groups
    capacity = max(2, 5 * height // (4 * experts_all))
    plan = slot_plan(capacity, features)
    slots = experts_all * plan[0]
    columns = features + (2 * features // plan[2] if plan[1] else 0)
    piece_rows = heads * height + height // LANES * width
    place = lax.axis_index("tensor")
    context_at = lax.axis_index("context")
    place_arg = jnp.stack([place, context_at]).astype(jnp.int32)
    square = features * features

    projected = run(
        functools.partial(project_body, heads),
        [shape((piece_rows, LANES))] * groups + [shape((features, height))],
        (place_arg, tokens_in, gain_attn, w_qkv),
        scratch=[pltpu.VMEM((groups, piece_rows, LANES), BF16)],
        smem=(0,),
        flops=6 * height * square,
        moved=8 * square,
    )
    own = trade(projected[:groups])
    table = jnp.pad(rel_bias, ((0, 0), (0, LANES - rel_bias.shape[1])))
    table = jnp.broadcast_to(table[:, :, None], (heads, LANES, height))
    strips = run(
        strip_body,
        shape((heads, 5 * height, height), F32),
        (table,),
        flops=heads * 2 * 4 * height * LANES * height,
        moved=heads * 4 * 5 * height * height,
    )
    far = [cross(after(piece, strips), "tensor", 1) for piece in own]
    head_flops = 4 * groups * height * length * size

    def fixed(dims):
        return pl.BlockSpec(dims, lambda h, n=len(dims): (0,) * n)

    def by_head(dims, first=0):
        return pl.BlockSpec(
            (1,) + dims, lambda h, n=len(dims), f=first: (h + f,) + (0,) * n
        )

    def head_rows(first=0):
        return pl.BlockSpec((size, height), lambda h, f=first: (h + f, 0))

    smem = pl.BlockSpec(memory_space=pltpu.SMEM)
    held_dims = [
        (groups, size, height),
        (groups, 8, height),
        (length, LANES),
        (length, LANES),
        (groups, spans, height, height),
    ]
    held_kinds = [F32, F32, BF16, BF16, BF16]
    outs = pl.pallas_call(
        functools.partial(forward_body, groups, heads),
        out_shape=[shape((width, height))] * groups
        + [shape((heads,) + dims, kind) for dims, kind in zip(held_dims, held_kinds)],
        grid=(heads,),
        in_specs=[smem, smem, fixed((1, length)), by_head((5 * height, height))]
        + [fixed((piece_rows, LANES))] * (2 * groups),
        out_specs=[head_rows()] * groups + [by_head(dims) for dims in held_dims],
        scratch_shapes=[
            pltpu.VMEM((length, LANES), BF16),
            pltpu.VMEM((spans, height), jnp.int32),
            pltpu.VMEM((spans, size + 16, height), BF16),
            pltpu.VMEM((2, spans, height, height), F32),
        ],
        cost_estimate=pl.CostEstimate(
            flops=6 * heads * head_flops, bytes_accessed=20 * square, transcendentals=0
        ),
        compiler_params=pltpu.CompilerParams(vmem_limit_bytes=VMEM_LIMIT),
    )(place_arg, rel_bias.astype(F32), segments, strips, *own, *far)
    attended = trade(outs[:groups])
    exact, inverse, vaug, kaug, weights = outs[groups:]
    route_row = routes.reshape(1, height)
    normed_all = trade([after(projected[groups], *own)] * groups)
    residual, normed_ffn, router, sent, grad_sent, attended_t = run(
        functools.partial(route_body, groups, capacity, plan),
        [
            shape((height, features), F32),
            shape((height, features)),
            shape((height, experts_all), F32),
            shape((slots, columns)),
            shape((slots, features)),
            shape((features, height)),
        ],
        (
            after(place_arg, *normed_all),
            tokens_in,
            w_out,
            gain_ffn,
            w_router.T,
            route_row,
            cotangent,
            *attended,
        ),
        smem=(0,),
        flops=2 * height * square,
        moved=4 * square,
    )

    def move_slots(moving):
        return exchange(
            moving.reshape(experts_all, plan[0], -1), ("expert", "context")
        ).reshape(moving.shape)

    got = move_slots(sent)
    pieces = features // (experts_all * tensor_size)
    first_piece = (
        (lax.axis_index("expert") * groups + context_at) * tensor_size + place
    ) * pieces
    first_piece = after(first_piece, sent)
    own_w = lax.dynamic_slice_in_dim(w_qkv, first_piece, pieces, 0)
    own_gain = lax.dynamic_slice_in_dim(gain_attn, first_piece, pieces, 0)
    turned, kt = run(
        functools.partial(turn_body, groups, heads),
        [shape((heads, groups, height, LANES)), shape((heads, size + 16, length))],
        (after(kaug, sent), *own),
        flops=2 * square,
        moved=4 * square,
    )
    grad_got = move_slots(after(grad_sent, turned, own_w, own_gain))
    produced, spare, rows_in, slope, act_other, act_mine = run_expert(
        plan, place_arg, got, w_up[0], w_down[0], None
    )
    produced_back = move_slots(produced)
    back, grad_rows, hid_other, hid_mine = run_expert(
        plan, place_arg, grad_got, w_up[0], w_down[0], (slope, got, spare)
    )
    returned = move_slots(back)

    def both(values, sent_values):
        return jnp.concatenate([values, cross(sent_values, "tensor", 1)], axis=0)

    grad_down = tn(both(act_mine, act_other), both(grad_rows, grad_rows))
    grad_up = tn(both(rows_in, rows_in), both(hid_mine, hid_other))
    extra = -(-(experts_all + 1) // LANES) * LANES
    outs = run(
        functools.partial(combine_body, groups, capacity, plan),
        [
            shape((height, features)),
            shape((height, features), F32),
            shape((height, features)),
            shape((height, extra)),
            shape((8, features), F32),
        ]
        + [shape((width, height))] * groups,
        (
            after(place_arg, grad_down, grad_up),
            produced_back,
            returned,
            residual,
            router,
            route_row,
            cotangent,
            gain_ffn,
            w_router.T,
            w_out,
        ),
        scratch=[pltpu.VMEM((features, height), BF16)],
        smem=(0,),
        flops=4 * height * square,
        moved=8 * square,
    )
    mixed_out, grad_residual, branch, grad_logits, gain_sums = outs[:5]
    grad_pieces = trade(outs[5:])
    mine, other = run(
        functools.partial(weights_body, experts_all),
        [shape((experts_all, pieces, features + extra))] * 2,
        (place_arg, branch, attended_t, normed_ffn, grad_logits, gain_sums),
        scratch=[pltpu.VMEM((features, features + extra), F32)],
        smem=(0,),
        flops=2 * height * square,
        moved=8 * square,
    )

    def pair_sum(kept, received):
        return run(pair_body, shape(kept.shape), (kept, received), moved=6 * kept.size)

    packed = pair_sum(mine, cross(other, "tensor", 1))
    packed_landed = exchange(packed, ("expert", "context"))
    counts = (heads,)
    mine_kv, got_kv, q_grads, diags, fars = [], [], [], [], []
    for call_at in range(len(counts)):
        first, count = sum(counts[:call_at]), counts[call_at]
        dims = [
            (groups, size, height),
            (groups, height, 2 * size),
            (groups, height, 2 * size),
            (5 * height, height),
            (2, spans, height),
        ]
        outs = pl.pallas_call(
            functools.partial(backward_body, groups),
            out_shape=[
                shape((count,) + of, kind)
                for of, kind in zip(dims, [BF16, BF16, BF16, F32, F32])
            ],
            grid=(count,),
            in_specs=[smem, pl.BlockSpec(memory_space=pltpu.HBM)]
            + [
                by_head(of, first)
                for of in (
                    held_dims[2],
                    (size + 16, length),
                    held_dims[0],
                    held_dims[1],
                )
            ]
            + [by_head((groups, height, LANES), first)]
            + [head_rows(first)] * groups,
            out_specs=[by_head(of) for of in dims],
            scratch_shapes=[pltpu.VMEM((length, LANES), F32)]
            + [pltpu.VMEM((length, height), F32)] * 2
            + [pltpu.VMEM((length, height), BF16)] * 2
            + [
                pltpu.VMEM((2,) + held_dims[4], BF16),
                pltpu.SemaphoreType.DMA((2, groups)),
            ],
            cost_estimate=pl.CostEstimate(
                flops=8 * count * head_flops, bytes_accessed=20 * square, transcendentals=0
            ),
            compiler_params=pltpu.CompilerParams(vmem_limit_bytes=VMEM_LIMIT),
        )(after(place_arg, packed), weights, vaug, kt, exact, inverse, turned, *grad_pieces)
        q_grads.append(outs[0])
        mine_kv.append(outs[1])
        got_kv.append(cross(outs[2], "tensor", 1))
        diags.append(outs[3])
        fars.append(outs[4])
    joined = run(
        functools.partial(join_body, counts),
        [shape((piece_rows, LANES))] * groups,
        (*mine_kv, after(got_kv[0], packed_landed), *got_kv[1:], *q_grads),
        moved=4 * groups * piece_rows * LANES,
    )
    landed_pieces = trade(joined)
    by_bucket = run(
        functools.partial(diagonal_body, counts),
        shape((heads, 1, LANES), F32),
        (*diags, *fars),
    )
    mine, other = run(
        functools.partial(qkv_body, groups, heads),
        [shape((experts_all, pieces, 3 * width + BUCKETS))] * 2,
        (place_arg, *normed_all, *joined, by_bucket),
        scratch=[
            pltpu.VMEM((features, 3 * width + BUCKETS), F32),
            pltpu.VMEM((height, 3 * width), BF16),
        ],
        smem=(0,),
    )
    summed = pair_sum(mine, cross(after(other, *landed_pieces), "tensor", 1))
    landed = exchange(summed, ("expert", "context"))
    grad_qkv, grad_gain_attn, grad_rel = run(
        functools.partial(rows_body, groups, heads),
        [
            shape((pieces, 3 * features), F32),
            shape((pieces,), F32),
            shape((heads, BUCKETS), F32),
        ],
        (place_arg, landed, own_w, own_gain),
        smem=(0,),
        moved=2 * landed.size,
    )
    grad_tokens = run(
        functools.partial(finish_body, groups, heads),
        shape((height, features)),
        (place_arg, tokens_in, gain_attn, w_qkv, grad_residual, *landed_pieces),
        scratch=[
            pltpu.VMEM((features, height), F32),
            pltpu.VMEM((groups, height, width), BF16),
            pltpu.VMEM((groups, height, width), BF16),
        ],
        smem=(0,),
        flops=6 * height * square,
        moved=8 * square,
    )
    reduced = jnp.sum(packed_landed.astype(F32), axis=0)
    return (
        mixed_out,
        grad_tokens,
        grad_gain_attn,
        grad_qkv,
        grad_rel,
        reduced[:, :features].T,
        reduced[:, features + experts_all],
        reduced[:, features : features + experts_all],
        grad_up[None],
        grad_down[None],
    )


def solution(mesh):
    rows = ("expert", "context", "tensor")
    in_specs = (
        P(rows, None),
        P(),
        P(),
        P("context", None),
        P(),
        P(),
        P(),
        P(("expert", "context"), None, None),
        P(("expert", "context"), None, None),
        P("expert", None),
        P(rows, None),
        P(rows, None),
    )
    out_specs = (
        P(rows, None),
        P(rows, None),
        P(rows),
        P(rows, None),
        P("context", None),
        P(None, rows),
        P(rows),
        P(rows, None),
        P(("expert", "context"), None, "tensor"),
        P(("expert", "context"), "tensor", None),
    )
    return jax.shard_map(
        per_device, mesh=mesh, in_specs=in_specs, out_specs=out_specs, check_vma=False
    )
```

```python
import functools

import jax
import jax.numpy as jnp
from jax import lax
from jax.experimental import pallas as pl
from jax.experimental.pallas import tpu as pltpu
from jax.sharding import PartitionSpec as P

EPSILON = 1e-06
THRESHOLDS = (12, 16, 23, 32, 46, 64, 91)
FAR_LEFT = 15
FAR_RIGHT = 31
EXCLUDED = -1e30
LANES = 128
BF16 = jnp.bfloat16
F32 = jnp.float32
VMEM_LIMIT = 56 * 1024 * 1024
BUCKETS = 32
CHUNKS = 4
PART = 256


def bucket_of(offset):
    distance = jnp.abs(offset)
    beyond = jnp.zeros_like(distance)
    for threshold in THRESHOLDS:
        beyond = beyond + (distance >= threshold).astype(jnp.int32)
    nearby = jnp.where(distance < 8, distance, 8 + beyond)
    return nearby + 16 * (offset > 0).astype(jnp.int32)


def nn(left, right):
    return lax.dot_general(left, right, (((1,), (0,)), ((), ())), preferred_element_type=F32)


def nt(left, right):
    return lax.dot_general(left, right, (((1,), (1,)), ((), ())), preferred_element_type=F32)


def tn(left, right):
    return lax.dot_general(left, right, (((0,), (0,)), ((), ())), preferred_element_type=F32)


def iota(shape, axis):
    return lax.broadcasted_iota(jnp.int32, shape, axis)


def three_terms(values):
    high = values.astype(BF16).astype(F32)
    middle = (values - high).astype(BF16).astype(F32)
    return high, middle, values - high - middle


def specs_for(count, smem=()):
    return [
        pl.BlockSpec(memory_space=pltpu.SMEM if i in smem else pltpu.VMEM) for i in range(count)
    ]


def run(body, out_shape, args, scratch=(), smem=(), flops=0, moved=0, limit=VMEM_LIMIT):
    return pl.pallas_call(
        body,
        out_shape=out_shape,
        in_specs=specs_for(len(args), smem),
        scratch_shapes=list(scratch),
        cost_estimate=pl.CostEstimate(flops=flops, bytes_accessed=moved, transcendentals=0),
        compiler_params=pltpu.CompilerParams(vmem_limit_bytes=limit),
    )(*args)


def shape(dims, kind=BF16):
    return jax.ShapeDtypeStruct(dims, kind)


def project_body(heads, place_ref, tokens_ref, gain_ref, w_ref, *refs):
    groups = len(refs) - 2
    piece_refs, normed_ref, all_ref = refs[:groups], refs[groups], refs[groups + 1]
    height, features = tokens_ref.shape
    width = features // groups
    size = width // heads
    group = place_ref[1]
    tokens = tokens_ref[...].astype(F32)
    inverse = lax.rsqrt(jnp.mean(tokens * tokens, axis=-1, keepdims=True) + EPSILON)
    normed = (tokens * inverse * gain_ref[...].astype(F32)[None, :]).astype(BF16)
    normed_ref[...] = jnp.transpose(normed.astype(F32)).astype(BF16)
    turned = jnp.transpose(nn(normed, w_ref[:, :features])).astype(BF16)
    keys = nn(normed, w_ref[:, features : 2 * features]).astype(BF16)
    values = nn(normed, w_ref[:, 2 * features :]).astype(BF16)
    for at in range(groups):
        for head in range(heads):
            lanes = slice(at * width + head * size, at * width + (head + 1) * size)
            all_ref[at ^ group, head * height : (head + 1) * height, :] = jnp.concatenate(
                [keys[:, lanes], values[:, lanes]], axis=1
            )
        for half in range(height // LANES):
            first = heads * height + half * width
            all_ref[at ^ group, first : first + width, :] = turned[
                at * width : (at + 1) * width, half * LANES : (half + 1) * LANES
            ]
    for at in range(groups):
        piece_refs[at][...] = all_ref[at]


def q_rows(piece_ref, heads, height, size, head):
    width = heads * size
    parts = []
    for half in range(height // LANES):
        first = heads * height + half * width + head * size
        parts.append(piece_ref[pl.ds(pl.multiple_of(first, 16), size), :])
    return jnp.concatenate(parts, axis=1)


def forward_body(groups, heads, place_ref, bias_ref, seg_ref, strip_ref, *refs):
    own_refs, far_refs, out_refs = (refs[i * groups : (i + 1) * groups] for i in range(3))
    exact_ref, inverse_ref, vaug_ref, kaug_ref, weight_ref = refs[3 * groups : 3 * groups + 5]
    extra_all, docs_all, vt_ref, score_ref = refs[3 * groups + 5 :]
    size, height = out_refs[0].shape
    spans = kaug_ref.shape[1] // height
    place, group = place_ref[0], place_ref[1]
    head = pl.program_id(0)
    tall = size + 16
    rest = LANES - size

    @pl.when(head == 0)
    def _():
        row = iota((LANES, height), 0) - size
        for span in range(spans):
            docs = seg_ref[0:1, span * height : (span + 1) * height]
            docs_all[span : span + 1, :] = docs
            extra = jnp.where((row >= 0) & (row < 3) & (docs != row), EXCLUDED, 0.0)
            extra = jnp.where(row - 3 == span, 1.0, extra)
            extra_all[span * height : (span + 1) * height, :] = jnp.transpose(extra).astype(BF16)

    row, column = iota((tall, LANES), 0), iota((tall, LANES), 1)
    pick_v = (((row < size) & (row + size == column)) | ((row == size) & (column == 0))).astype(
        BF16
    )
    lane = iota((height, LANES), 1)
    low_half = lane < size
    ones = jnp.where(lane < 3, 1.0, 0.0).astype(BF16)
    extra_row = iota((rest, height), 0)
    queries_all = []
    for at in range(groups):
        block = at ^ group
        for source, parity in ((own_refs[at], place), (far_refs[at], 1 - place)):
            span = 2 * block + parity
            rows = pl.ds(pl.multiple_of(span * height, height), height)
            both = source[pl.ds(pl.multiple_of(head * height, height), height), :]
            keys = jnp.where(low_half, both, extra_all[rows, :])
            values = jnp.where(low_half, ones, both)
            kaug_ref[0, rows, :] = keys
            vaug_ref[0, rows, :] = values
            vt_ref[span] = nt(pick_v, values).astype(BF16)
        span = 2 * block + place
        docs = docs_all[pl.ds(span, 1), :]
        apart = extra_row - 3 - span
        far = jnp.where(
            apart <= -2,
            bias_ref[head, FAR_LEFT],
            jnp.where(apart >= 2, bias_ref[head, FAR_RIGHT], 0.0),
        )
        extra = jnp.where(
            extra_row < 3,
            jnp.where(docs == extra_row, 1.0, 0.0),
            jnp.where(extra_row < 3 + spans, far, 0.0),
        )
        queries_all.append(
            jnp.concatenate(
                [q_rows(own_refs[at], heads, height, size, head), extra.astype(BF16)], axis=0
            )
        )
    for at in range(groups):
        span = 2 * (at ^ group) + place
        start = jnp.clip(span - 1, 0, spans - 3)
        queries = queries_all[at]
        slot = at % 2
        row_max = None
        for step in range(spans):
            key_span = (start + step) if step < 3 else ((start + step) & (spans - 1))
            rows = pl.ds(pl.multiple_of(key_span * height, height), height)
            scores = nn(kaug_ref[0, rows, :], queries)
            if step < 3:
                level = pl.multiple_of((key_span - span + 2) * height, height)
                scores = scores + strip_ref[0, pl.ds(level, height), :]
            score_ref[slot, step] = scores
            best = jnp.max(scores, axis=0, keepdims=True)
            row_max = best if row_max is None else jnp.maximum(row_max, best)
        total = jnp.zeros((tall, height), F32)
        for step in range(spans):
            key_span = (start + step) if step < 3 else ((start + step) & (spans - 1))
            weights = jnp.exp(score_ref[slot, step] - row_max).astype(BF16)
            weight_ref[0, at, key_span] = weights
            total = total + nn(vt_ref[key_span], weights)
        inverse = 1.0 / total[size : size + 1]
        result = total[:size] * inverse
        out_refs[at][...] = result.astype(BF16)
        exact_ref[0, at] = result
        inverse_ref[0, at] = jnp.broadcast_to(inverse, (8, height))


def turn_body(groups, heads, kaug_ref, *refs):
    piece_refs, out_ref, kt_ref = refs[:groups], refs[groups], refs[groups + 1]
    height = out_ref.shape[2]
    size = out_ref.shape[3] // 2
    spans = kaug_ref.shape[1] // height
    row, column = iota((size + 16, LANES), 0), iota((size + 16, LANES), 1)
    pick_k = (
        ((row < size) & (row == column))
        | ((row >= size) & (row < size + spans) & (row + 3 == column))
    ).astype(BF16)
    blank = jnp.zeros((size, height), F32)
    for head in range(heads):
        kt_ref[head] = nt(pick_k, kaug_ref[head]).astype(BF16)
        for at in range(groups):
            queries = q_rows(piece_refs[at], heads, height, size, head).astype(F32)
            out_ref[head, at] = jnp.transpose(jnp.concatenate([queries, blank], axis=0)).astype(
                BF16
            )


def backward_body(groups, place_ref, *refs):
    weight_ref, vaug_ref, kt_ref, exact_ref, inverse_ref, q_ref = refs[:6]
    grad_refs = refs[6 : 6 + groups]
    dq_ref, mine_ref, other_ref, diag_ref, far_ref, dkv_ref = refs[6 + groups : 12 + groups]
    slope_refs, score_refs = refs[12 + groups : 14 + groups], refs[14 + groups :]
    size, height = grad_refs[0].shape
    length = vaug_ref.shape[1]
    spans = length // height
    place, group = place_ref[0], place_ref[1]
    diag_ref[...] = jnp.zeros_like(diag_ref)
    extra_row = iota((LANES - size, height), 0)
    blank = jnp.zeros((size, height), F32)
    span_row = iota((spans, height), 0)
    left_total = jnp.zeros((spans, height), F32)
    right_total = jnp.zeros((spans, height), F32)
    for at in range(groups):
        span = 2 * (at ^ group) + place
        start = jnp.clip(span - 1, 0, spans - 3)
        slope_ref, score_ref = slope_refs[at % 2], score_refs[at % 2]
        grads = (grad_refs[at][...].astype(F32) * inverse_ref[0, at, 0:1]).astype(BF16)
        grads32 = grads.astype(F32)
        delta = jnp.sum(grads32 * exact_ref[0, at], axis=0, keepdims=True)
        high, middle, low = three_terms(-delta)
        extra = jnp.where(
            extra_row == 0,
            high,
            jnp.where(extra_row == 1, middle, jnp.where(extra_row == 2, low, 0.0)),
        )
        slope_ref[...] = nn(
            vaug_ref[0], jnp.concatenate([extra.astype(BF16), grads], axis=0)
        )
        turned = jnp.transpose(jnp.concatenate([blank, grads32], axis=0)).astype(BF16)
        sides = jnp.concatenate([q_ref[0, at], turned], axis=0)
        for key in range(spans):
            rows = slice(key * height, (key + 1) * height)
            score_ref[rows, :] = (
                weight_ref[0, at, key].astype(F32) * slope_ref[rows, :]
            ).astype(BF16)
        both = jnp.concatenate(
            [score_ref[...], weight_ref[0, at].reshape(length, height)], axis=1
        )
        product = nn(both, sides)
        if at == 0:
            dkv_ref[...] = product
        else:
            dkv_ref[...] = dkv_ref[...] + product
        total = nn(kt_ref[0], score_ref[...])
        dq_ref[0, at] = total[:size].astype(BF16)
        sums = total[size : size + spans]
        left_total = left_total + jnp.where(span_row < start, sums, 0.0)
        right_total = right_total + jnp.where(span_row >= start + 3, sums, 0.0)
        rows = pl.ds(pl.multiple_of(start * height, height), 3 * height)
        level = pl.ds(pl.multiple_of((start - span + 2) * height, height), 3 * height)
        diag_ref[0, level, :] = diag_ref[0, level, :] + score_ref[rows, :].astype(F32)
    far_ref[0, 0] = left_total
    far_ref[0, 1] = right_total
    for at in range(groups):
        for target, parity in ((mine_ref, place), (other_ref, 1 - place)):
            first = pl.multiple_of((2 * (at ^ group) + parity) * height, height)
            target[0, at] = dkv_ref[pl.ds(first, height), :].astype(BF16)


def join_body(counts, *refs):
    calls = len(counts)
    mine_refs, got_refs, dq_refs = (refs[i * calls : (i + 1) * calls] for i in range(3))
    piece_refs = refs[3 * calls :]
    size, height = dq_refs[0].shape[2:]
    heads = sum(counts)
    width = heads * size
    for at, piece_ref in enumerate(piece_refs):
        head = 0
        for call_at, count in enumerate(counts):
            for inner in range(count):
                kept = mine_refs[call_at][inner, at].astype(F32)
                piece_ref[head * height : (head + 1) * height, :] = (
                    kept + got_refs[call_at][inner, at].astype(F32)
                ).astype(BF16)
                for half in range(height // LANES):
                    first = heads * height + half * width + head * size
                    piece_ref[first : first + size, :] = dq_refs[call_at][
                        inner, at, :, half * LANES : (half + 1) * LANES
                    ]
                head += 1


def slot_plan(capacity, features):
    base = capacity // 16 * 16
    left = capacity - base
    if base and left and 16 % left == 0 and (2 * features) % (LANES * (16 // left)) == 0:
        return base, left, 16 // left
    return -(-capacity // 8) * 8, 0, 0


def slot_marks(shape_of, axis, chosen, rank, capacity, plan):
    base, left, parts = plan
    position = iota(shape_of, axis)
    limit = base if left else capacity
    marks = [jnp.where(position == jnp.where(rank < limit, chosen * base + rank, -1), 1.0, 0.0)]
    spare = rank - base
    for part in range(parts):
        slot = chosen * 16 + part * left + spare
        slot = jnp.where((spare >= 0) & (spare < left), slot, -1)
        marks.append(jnp.where(position == slot, 1.0, 0.0))
    return [mark.astype(BF16) for mark in marks]


def route_body(
    groups,
    capacity,
    plan,
    place_ref,
    tokens_ref,
    w_out_ref,
    gain_ref,
    w_router_ref,
    route_row_ref,
    cotangent_ref,
    *refs,
):
    pieces = refs[:groups]
    residual_ref, normed_ref, router_ref, sent_ref, grad_sent_ref, attended_ref = refs[groups:]
    height, features = tokens_ref.shape
    experts = w_router_ref.shape[0]
    slots = sent_ref.shape[0]
    width = pieces[0].shape[0]
    group = place_ref[1]
    for at in range(groups):
        first = pl.multiple_of((at ^ group) * width, width)
        attended_ref[pl.ds(first, width), :] = pieces[at][...]
    residual = tokens_ref[...].astype(F32) + tn(attended_ref[...], w_out_ref[...])
    residual_ref[...] = residual
    inverse = lax.rsqrt(jnp.mean(residual * residual, axis=-1, keepdims=True) + EPSILON)
    normed = (residual * inverse * gain_ref[...].astype(F32)[None, :]).astype(BF16)
    normed_ref[...] = normed
    logits = nt(normed, w_router_ref[...])
    powers = jnp.exp(logits - jnp.max(logits, axis=-1, keepdims=True))
    router = powers / jnp.sum(powers, axis=-1, keepdims=True)
    router_ref[...] = router
    chosen = route_row_ref[...]
    marks = iota((experts, height), 0) == chosen
    onehot = jnp.transpose(jnp.where(marks, 1.0, 0.0))
    gate = jnp.sum(onehot * router, axis=-1, keepdims=True)
    grad_expert = (gate * cotangent_ref[...].astype(F32)).astype(BF16)
    rows = jnp.concatenate([normed, grad_expert], axis=1)
    earlier = (iota((height, height), 0) < iota((height, height), 1)).astype(BF16)
    before = nn(jnp.where(marks, 1.0, 0.0).astype(BF16), earlier)
    rank = jnp.sum(jnp.where(marks, before, 0.0), axis=0, keepdims=True).astype(jnp.int32)
    dispatch = slot_marks((slots, height), 0, chosen, rank, capacity, plan)
    sent_ref[:, :features] = nn(dispatch[0], normed).astype(BF16)
    grad_sent_ref[...] = nn(dispatch[0], grad_expert).astype(BF16)
    if plan[1]:
        span = 2 * features // plan[2]
        spare = nn(dispatch[1], rows[:, :span])
        for part in range(1, plan[2]):
            spare = spare + nn(dispatch[1 + part], rows[:, part * span : (part + 1) * span])
        sent_ref[:, features:] = spare.astype(BF16)


def spare_marks(sources, plan):
    base, left, parts = plan
    target = iota((sources * left, sources * 16), 0)
    origin = iota((sources * left, sources * 16), 1)
    source = target // left
    return [
        (origin == source * 16 + part * left + (target - source * left)).astype(BF16)
        for part in range(parts)
    ]


def unpack_spare(rows_ref, packed, plan, first_part):
    main = packed.shape[0]
    marks = spare_marks(main // 16, plan)
    half = plan[2] // 2
    span = rows_ref.shape[1] // half
    for part in range(half):
        rows_ref[main:, part * span : (part + 1) * span] = nn(
            marks[first_part + part], packed
        ).astype(BF16)


def bring(place, up_ref, down_ref, up_all, down_all, sems):
    chunk = up_all.shape[2]
    copies = []
    for at in range(CHUNKS):
        half = (1 - place) if at < CHUNKS // 2 else place
        first = half * (chunk * CHUNKS // 2) + at % (CHUNKS // 2) * chunk
        part = pl.ds(pl.multiple_of(first, chunk), chunk)
        copies.append(
            (
                pltpu.make_async_copy(up_ref.at[:, part], up_all.at[at], sems.at[0, at]),
                pltpu.make_async_copy(down_ref.at[part, :], down_all.at[at], sems.at[1, at]),
            )
        )
    return copies


def expert_forward_body(
    plan,
    place_ref,
    got_ref,
    up_ref,
    down_ref,
    back_ref,
    spare_ref,
    rows_ref,
    slope_ref,
    other_ref,
    mine_ref,
    total_ref,
    up_all,
    down_all,
    sems,
    active_all,
    slope_all,
    out_sems,
):
    main, features = back_ref.shape
    leaving = []
    chunk = up_all.shape[2]
    copies = bring(place_ref[0], up_ref, down_ref, up_all, down_all, sems)
    for up_copy, down_copy in copies:
        up_copy.start()
        down_copy.start()
    rows_ref[:main, :] = got_ref[:, :features]
    if plan[1]:
        unpack_spare(rows_ref, got_ref[:, features:], plan, 0)
    for at in range(CHUNKS):
        half = at // (CHUNKS // 2)
        base = at % (CHUNKS // 2) * chunk
        copies[at][0].wait()
        for first in range(0, chunk, PART):
            lanes = slice(base + first, base + first + PART)
            hidden = nn(rows_ref[...], up_all[at, :, first : first + PART])
            below = 0.5 * (1.0 + lax.erf(hidden * (2.0**-0.5)))
            bell = jnp.exp(-0.5 * hidden * hidden) * 0.3989422804014327
            active_all[half, :, lanes] = (hidden * below).astype(BF16)
            slope_all[half, :, lanes] = (below + hidden * bell).astype(BF16)
        whole = pl.ds(base, chunk)
        for which, (source, target) in enumerate(
            (
                (active_all.at[half, :, whole], (other_ref, mine_ref)[half].at[:, whole]),
                (slope_all.at[half, :, whole], slope_ref.at[half, :, whole]),
            )
        ):
            copy = pltpu.make_async_copy(source, target, out_sems.at[which, at])
            copy.start()
            leaving.append(copy)
        copies[at][1].wait()
        product = nn(active_all[half, :, base : base + chunk], down_all[at])
        if at == 0:
            total_ref[...] = product
        else:
            total_ref[...] = total_ref[...] + product
    back_ref[...] = total_ref[:main, :].astype(BF16)
    if plan[1]:
        spare_ref[...] = total_ref[main:, :].astype(BF16)
    else:
        spare_ref[...] = jnp.zeros_like(spare_ref)
    for copy in leaving:
        copy.wait()


def expert_backward_body(
    plan,
    place_ref,
    got_ref,
    up_ref,
    down_ref,
    slope_ref,
    packed_ref,
    spare_ref,
    back_ref,
    rows_ref,
    other_ref,
    mine_ref,
    total_ref,
    up_all,
    down_all,
    sems,
):
    main, features = got_ref.shape
    chunk = up_all.shape[2]
    copies = bring(place_ref[0], up_ref, down_ref, up_all, down_all, sems)
    for up_copy, down_copy in copies:
        down_copy.start()
        up_copy.start()
    rows_ref[:main, :] = got_ref[...]
    if plan[1]:
        unpack_spare(rows_ref, packed_ref[:, features:], plan, plan[2] // 2)
    for at in range(CHUNKS):
        hidden_ref = other_ref if at < CHUNKS // 2 else mine_ref
        base = at % (CHUNKS // 2) * chunk
        copies[at][1].wait()
        for first in range(0, chunk, PART):
            lanes = slice(base + first, base + first + PART)
            grad_active = nt(rows_ref[...], down_all[at, first : first + PART, :])
            slope = slope_ref[at // (CHUNKS // 2), :, lanes].astype(F32)
            hidden_ref[:, lanes] = (grad_active * slope).astype(BF16)
        copies[at][0].wait()
        product = nt(hidden_ref[:, base : base + chunk], up_all[at])
        if at == 0:
            total_ref[...] = product
        else:
            total_ref[...] = total_ref[...] + product
    back_ref[:, :features] = total_ref[:main, :].astype(BF16)
    if plan[1]:
        spare = jnp.concatenate([spare_ref[...], total_ref[main:, :].astype(BF16)], axis=1)
        span = 2 * features // plan[2]
        packed = jnp.zeros((main, span), F32)
        for part, marks in enumerate(spare_marks(main // 16, plan)):
            packed = packed + tn(marks, spare[:, part * span : (part + 1) * span])
        back_ref[:, features:] = packed.astype(BF16)


def run_expert(plan, place_arg, got, up, down, forward):
    main = got.shape[0]
    features, hidden_size = up.shape
    spare = main // 16 * plan[1]
    slots = main + spare
    columns = features + (2 * features // plan[2] if plan[1] else 0)
    spare = max(spare, 8)
    halves = [shape((slots, hidden_size // 2))] * 2
    if forward is None:
        body = expert_forward_body
        out_shape = [shape((main, features)), shape((spare, features)), shape((slots, features))]
        out_shape += [shape((2, slots, hidden_size // 2))] + halves
        args, flops = (got, up, down), 0
    else:
        body = expert_backward_body
        out_shape = [shape((main, columns)), shape((slots, features))] + halves
        args, flops = (got, up, down) + forward, 4 * slots * features * hidden_size
    args = (place_arg,) + args
    specs = specs_for(len(args), (0,))
    specs[2] = specs[3] = pl.BlockSpec(memory_space=pl.ANY)
    chunk = hidden_size // CHUNKS
    out_specs = [pl.BlockSpec(memory_space=pltpu.VMEM)] * len(out_shape)
    held = []
    if forward is None:
        out_specs[3:] = [pl.BlockSpec(memory_space=pl.ANY)] * 3
        held = [pltpu.VMEM((2, slots, hidden_size // 2), BF16)] * 2
        held.append(pltpu.SemaphoreType.DMA((2, CHUNKS)))
    return pl.pallas_call(
        functools.partial(body, plan),
        out_shape=out_shape,
        in_specs=specs,
        out_specs=out_specs,
        scratch_shapes=[
            pltpu.VMEM((slots, features), F32),
            pltpu.VMEM((CHUNKS, features, chunk), BF16),
            pltpu.VMEM((CHUNKS, chunk, features), BF16),
            pltpu.SemaphoreType.DMA((2, CHUNKS)),
        ]
        + held,
        cost_estimate=pl.CostEstimate(flops=flops, bytes_accessed=flops // 400, transcendentals=0),
        compiler_params=pltpu.CompilerParams(vmem_limit_bytes=VMEM_LIMIT),
    )(*args)


def combine_body(
    groups,
    capacity,
    plan,
    place_ref,
    produced_ref,
    got_ref,
    residual_ref,
    router_ref,
    route_row_ref,
    cotangent_ref,
    gain_ref,
    w_router_ref,
    w_out_ref,
    mixed_ref,
    grad_residual_ref,
    branch_ref,
    logits_ref,
    gain_out_ref,
    *refs,
):
    pieces, turned_ref = refs[:groups], refs[groups]
    height, experts = router_ref.shape
    features = residual_ref.shape[1]
    slots = got_ref.shape[0]
    width = pieces[0].shape[0]
    group = place_ref[1]
    chosen_row = route_row_ref[...]
    marks = jnp.where(iota((experts, height), 0) == chosen_row, 1.0, 0.0)
    earlier = (iota((height, height), 0) < iota((height, height), 1)).astype(BF16)
    before = nn(marks.astype(BF16), earlier)
    rank_row = jnp.sum(marks * before, axis=0, keepdims=True)
    onehot = jnp.transpose(marks) > 0.5
    pair_row = iota((8, height), 0)
    pairs = jnp.transpose(jnp.where(pair_row == 0, chosen_row.astype(F32), rank_row))
    chosen = pairs[:, 0:1].astype(jnp.int32)
    rank = pairs[:, 1:2].astype(jnp.int32)
    combine = slot_marks((height, slots), 1, chosen, rank, capacity, plan)
    back = jnp.concatenate(
        [nn(combine[0], produced_ref[...]), nn(combine[0], got_ref[:, :features])], axis=1
    )
    if plan[1]:
        spare = got_ref[:, features:]
        back = back + jnp.concatenate([nn(marks, spare) for marks in combine[1:]], axis=1)
    router = router_ref[...]
    gate = jnp.sum(jnp.where(onehot, router, 0.0), axis=-1, keepdims=True)
    residual = residual_ref[...]
    inverse = lax.rsqrt(jnp.mean(residual * residual, axis=-1, keepdims=True) + EPSILON)
    unit = residual * inverse
    grad_mixed = cotangent_ref[...].astype(F32)
    gathered = back[:, :features]
    mixed_ref[...] = (residual + gate * gathered).astype(BF16)
    grad_gate = jnp.sum(grad_mixed * gathered, axis=-1, keepdims=True)
    grad_logits = (router * (jnp.where(onehot, grad_gate, 0.0) - gate * grad_gate)).astype(BF16)
    grad_normed = back[:, features:] + nn(grad_logits, w_router_ref[...])
    grad_unit = grad_normed * gain_ref[...].astype(F32)[None, :]
    grad_residual = grad_mixed + inverse * (
        grad_unit - unit * jnp.mean(grad_unit * unit, axis=-1, keepdims=True)
    )
    branch = grad_residual.astype(BF16)
    turned_ref[...] = nt(w_out_ref[...], branch).astype(BF16)
    for at in range(groups):
        first = pl.multiple_of((at ^ group) * width, width)
        pieces[at][...] = turned_ref[pl.ds(first, width), :]
    grad_residual_ref[...] = grad_residual
    branch_ref[...] = branch
    spare_lanes = logits_ref.shape[1] - experts
    logits_ref[...] = jnp.concatenate([grad_logits, jnp.zeros((height, spare_lanes), BF16)], axis=1)
    sums = jnp.sum(grad_normed * unit, axis=0, keepdims=True)
    gain_out_ref[...] = jnp.broadcast_to(sums, gain_out_ref.shape)


def qkv_body(groups, heads, place_ref, *refs):
    normed_refs, piece_refs = refs[:groups], refs[groups : 2 * groups]
    bucket_ref, mine_ref, other_ref, total_ref, rows_ref = refs[2 * groups :]
    pieces = mine_ref.shape[1]
    wide = rows_ref.shape[1]
    height = normed_refs[0].shape[1]
    width = rows_ref.shape[1] // 3
    for at in range(groups):
        piece = piece_refs[at]
        for head in range(heads):
            rows_ref[:, head * LANES : (head + 1) * LANES] = piece[
                head * height : (head + 1) * height, :
            ]
        parts = [
            piece[heads * height + half * width : heads * height + (half + 1) * width, :]
            for half in range(height // LANES)
        ]
        turned = jnp.concatenate(parts, axis=1).astype(F32)
        rows_ref[:, 2 * width :] = jnp.transpose(turned).astype(BF16)
        product = nn(normed_refs[at][...], rows_ref[...])
        if at == 0:
            total_ref[:, :wide] = product
        else:
            total_ref[:, :wide] = total_ref[:, :wide] + product
    row = iota((total_ref.shape[0], BUCKETS), 0) % pieces
    buckets = jnp.zeros((total_ref.shape[0], BUCKETS), F32)
    for head in range(heads):
        buckets = jnp.where(row == head, bucket_ref[head, :, :BUCKETS], buckets)
    total_ref[:, wide:] = buckets
    split_rows(place_ref[0], total_ref, mine_ref, other_ref)


def rows_body(
    groups, heads, place_ref, landed_ref, w_ref, gain_ref, out_ref, gain_out_ref, bucket_ref
):
    sources, _, columns = landed_ref.shape
    width = (columns - BUCKETS) // 3
    size = width // heads
    features = groups * width
    for group in range(groups):
        total = landed_ref[group].astype(F32)
        for expert in range(1, sources // groups):
            total = total + landed_ref[expert * groups + group].astype(F32)
        out_ref[:, group * width : (group + 1) * width] = total[:, 2 * width : 3 * width]
        for head in range(heads):
            for part in range(2):
                source = head * 2 * size + part * size
                first = (part + 1) * features + group * width + head * size
                out_ref[:, first : first + size] = total[:, source : source + size]
    sums = lax.dot_general(
        jnp.ones((8, 3 * features), F32),
        w_ref[...].astype(F32) * out_ref[...],
        (((1,), (1,)), ((), ())),
        precision=lax.Precision.HIGHEST,
        preferred_element_type=F32,
    )
    gain_out_ref[...] = sums[0] / gain_ref[...].astype(F32)
    buckets = jnp.zeros((landed_ref.shape[1], BUCKETS), F32)
    for expert in range(sources // groups):
        buckets = buckets + landed_ref[expert * groups + place_ref[1]][:, 3 * width :].astype(F32)
    bucket_ref[...] = buckets[:heads]


def finish_body(groups, heads, place_ref, tokens_ref, gain_ref, w_ref, residual_ref, *refs):
    piece_refs = refs[:groups]
    out_ref, turned_ref, k_all, v_all = refs[groups:]
    height, features = tokens_ref.shape
    width = features // groups
    size = width // heads
    group = place_ref[1]
    for at in range(groups):
        piece = piece_refs[at]
        first = pl.multiple_of((at ^ group) * width, width)
        for half in range(height // LANES):
            source = heads * height + half * width
            turned_ref[pl.ds(first, width), half * LANES : (half + 1) * LANES] = piece[
                source : source + width, :
            ].astype(F32)
        for head in range(heads):
            both = piece[head * height : (head + 1) * height, :]
            lanes = slice(head * size, (head + 1) * size)
            k_all[at ^ group, :, lanes] = both[:, :size]
            v_all[at ^ group, :, lanes] = both[:, size:]
    grad_normed = nt(jnp.transpose(turned_ref[...]).astype(BF16), w_ref[:, :features])
    for part, source in ((1, k_all), (2, v_all)):
        joined = jnp.concatenate([source[at] for at in range(groups)], axis=1)
        grad_normed = grad_normed + nt(joined, w_ref[:, part * features : (part + 1) * features])
    tokens = tokens_ref[...].astype(F32)
    inverse = lax.rsqrt(jnp.mean(tokens * tokens, axis=-1, keepdims=True) + EPSILON)
    unit = tokens * inverse
    grad_unit = grad_normed * gain_ref[...].astype(F32)[None, :]
    grad = inverse * (grad_unit - unit * jnp.mean(grad_unit * unit, axis=-1, keepdims=True))
    out_ref[...] = (residual_ref[...] + grad).astype(BF16)


def strip_body(table_ref, strips_ref):
    heads, rows, height = strips_ref.shape
    used = rows - height
    offset = iota((used, LANES), 0) - 2 * height
    onehot = (bucket_of(offset) == iota((used, LANES), 1)).astype(BF16)
    lane = iota((used, height), 1)
    blank = jnp.zeros((height, height), F32)
    for head in range(heads):
        values = nn(onehot, table_ref[head])
        moved = 1
        while moved < height:
            values = jnp.where((lane & moved) != 0, pltpu.roll(values, moved, 0), values)
            moved *= 2
        strips_ref[head, :height] = blank
        strips_ref[head, height:used] = values[height:]
        strips_ref[head, used:] = blank


def diagonal_body(counts, *refs):
    calls = len(counts)
    out_ref = refs[2 * calls]
    places = [(call_at, inner) for call_at in range(calls) for inner in range(counts[call_at])]
    height = refs[0].shape[2]
    total_rows = 5 * height
    lane = iota((total_rows, height), 1)
    offset = iota((total_rows, LANES), 0) - 2 * height
    table = (bucket_of(offset) == iota((total_rows, LANES), 1)).astype(F32)
    lane_out = iota((1, LANES), 1)
    blank = jnp.zeros((height, height), F32)
    for head, (call_at, inner) in enumerate(places):
        diag_ref, far_ref = refs[call_at].at[inner], refs[calls + call_at].at[inner]
        values = jnp.concatenate([blank, diag_ref[height : 4 * height, :], blank], axis=0)
        moved = 1
        while moved < height:
            values = jnp.where(
                (lane & moved) != 0, pltpu.roll(values, total_rows - moved, 0), values
            )
            moved *= 2
        sums = jnp.sum(values, axis=1, keepdims=True)
        by_bucket = jnp.sum(sums * table, axis=0, keepdims=True)
        by_bucket = by_bucket + jnp.where(
            lane_out == FAR_LEFT, jnp.sum(far_ref[0]) + jnp.sum(diag_ref[:height, :]), 0.0
        )
        out_ref[head] = by_bucket + jnp.where(
            lane_out == FAR_RIGHT, jnp.sum(far_ref[1]) + jnp.sum(diag_ref[4 * height :, :]), 0.0
        )


def split_rows(place, source_ref, mine_ref, other_ref):
    experts_all, pieces, columns = mine_ref.shape
    for parity in range(2):

        @pl.when(place == parity)
        def _():
            for at in range(experts_all):
                for target, which in ((mine_ref, parity), (other_ref, 1 - parity)):
                    first = (2 * at + which) * pieces
                    target[at] = source_ref[first : first + pieces, :].astype(BF16)


def weights_body(
    experts,
    place_ref,
    branch_ref,
    attended_ref,
    normed_ref,
    logits_ref,
    gain_ref,
    mine_ref,
    other_ref,
    packed_ref,
):
    features = branch_ref.shape[1]
    extra = logits_ref.shape[1]
    branch = jnp.transpose(branch_ref[...].astype(F32)).astype(BF16)
    packed_ref[:, :features] = nt(branch, attended_ref[...])
    normed = jnp.transpose(normed_ref[...].astype(F32)).astype(BF16)
    column = jnp.transpose(gain_ref[...])[:, :1]
    packed_ref[:, features:] = nn(normed, logits_ref[...]) + jnp.where(
        iota((features, extra), 1) == experts, column, 0.0
    )
    split_rows(place_ref[0], packed_ref, mine_ref, other_ref)


def exchange(moving, axis):
    return lax.all_to_all(moving, axis, split_axis=0, concat_axis=0, tiled=True)


def cross(moving, axis, distance):
    size = lax.axis_size(axis)
    return lax.ppermute(moving, axis, [(i, i ^ distance) for i in range(size)])


def trade(pieces):
    return [
        piece if at == 0 else cross(piece, "context", at) for at, piece in enumerate(pieces)
    ]


def after(values, *others):
    return lax.optimization_barrier((values,) + others)[0]


def per_device(
    tokens_in,
    gain_attn,
    w_qkv,
    rel_bias,
    w_out,
    gain_ffn,
    w_router,
    w_up,
    w_down,
    segments,
    routes,
    cotangent,
):
    groups = lax.axis_size("context")
    tensor_size = lax.axis_size("tensor")
    expert_size = lax.axis_size("expert")
    height, features = tokens_in.shape
    heads = rel_bias.shape[0]
    width = features // groups
    size = width // heads
    length = segments.shape[1]
    spans = length // height
    experts_all = expert_size * groups
    capacity = max(2, 5 * height // (4 * experts_all))
    plan = slot_plan(capacity, features)
    slots = experts_all * plan[0]
    columns = features + (2 * features // plan[2] if plan[1] else 0)
    piece_rows = heads * height + height // LANES * width
    place = lax.axis_index("tensor")
    context_at = lax.axis_index("context")
    place_arg = jnp.stack([place, context_at]).astype(jnp.int32)
    square = features * features

    projected = run(
        functools.partial(project_body, heads),
        [shape((piece_rows, LANES))] * groups + [shape((features, height))],
        (place_arg, tokens_in, gain_attn, w_qkv),
        scratch=[pltpu.VMEM((groups, piece_rows, LANES), BF16)],
        smem=(0,),
        flops=6 * height * square,
        moved=8 * square,
    )
    own = trade(projected[:groups])
    table = jnp.pad(rel_bias, ((0, 0), (0, LANES - rel_bias.shape[1])))
    table = jnp.broadcast_to(table[:, :, None], (heads, LANES, height))
    strips = run(
        strip_body,
        shape((heads, 5 * height, height), F32),
        (table,),
        flops=heads * 2 * 4 * height * LANES * height,
        moved=heads * 4 * 5 * height * height,
    )
    far = [cross(after(piece, strips), "tensor", 1) for piece in own]
    head_flops = 4 * groups * height * length * size

    def fixed(dims):
        return pl.BlockSpec(dims, lambda h, n=len(dims): (0,) * n)

    def by_head(dims, first=0):
        return pl.BlockSpec(
            (1,) + dims, lambda h, n=len(dims), f=first: (h + f,) + (0,) * n
        )

    def head_rows(first=0):
        return pl.BlockSpec((size, height), lambda h, f=first: (h + f, 0))

    smem = pl.BlockSpec(memory_space=pltpu.SMEM)
    held_dims = [
        (groups, size, height),
        (groups, 8, height),
        (length, LANES),
        (length, LANES),
        (groups, spans, height, height),
    ]
    held_kinds = [F32, F32, BF16, BF16, BF16]
    outs = pl.pallas_call(
        functools.partial(forward_body, groups, heads),
        out_shape=[shape((width, height))] * groups
        + [shape((heads,) + dims, kind) for dims, kind in zip(held_dims, held_kinds)],
        grid=(heads,),
        in_specs=[smem, smem, fixed((1, length)), by_head((5 * height, height))]
        + [fixed((piece_rows, LANES))] * (2 * groups),
        out_specs=[head_rows()] * groups + [by_head(dims) for dims in held_dims],
        scratch_shapes=[
            pltpu.VMEM((length, LANES), BF16),
            pltpu.VMEM((spans, height), jnp.int32),
            pltpu.VMEM((spans, size + 16, height), BF16),
            pltpu.VMEM((2, spans, height, height), F32),
        ],
        cost_estimate=pl.CostEstimate(
            flops=6 * heads * head_flops, bytes_accessed=20 * square, transcendentals=0
        ),
        compiler_params=pltpu.CompilerParams(vmem_limit_bytes=VMEM_LIMIT),
    )(place_arg, rel_bias.astype(F32), segments, strips, *own, *far)
    attended = trade(outs[:groups])
    exact, inverse, vaug, kaug, weights = outs[groups:]
    route_row = routes.reshape(1, height)
    normed_all = trade([after(projected[groups], *own)] * groups)
    residual, normed_ffn, router, sent, grad_sent, attended_t = run(
        functools.partial(route_body, groups, capacity, plan),
        [
            shape((height, features), F32),
            shape((height, features)),
            shape((height, experts_all), F32),
            shape((slots, columns)),
            shape((slots, features)),
            shape((features, height)),
        ],
        (
            after(place_arg, *normed_all),
            tokens_in,
            w_out,
            gain_ffn,
            w_router.T,
            route_row,
            cotangent,
            *attended,
        ),
        smem=(0,),
        flops=2 * height * square,
        moved=4 * square,
    )

    def move_slots(moving):
        return exchange(
            moving.reshape(experts_all, plan[0], -1), ("expert", "context")
        ).reshape(moving.shape)

    got = move_slots(sent)
    pieces = features // (experts_all * tensor_size)
    first_piece = (
        (lax.axis_index("expert") * groups + context_at) * tensor_size + place
    ) * pieces
    first_piece = after(first_piece, sent)
    own_w = lax.dynamic_slice_in_dim(w_qkv, first_piece, pieces, 0)
    own_gain = lax.dynamic_slice_in_dim(gain_attn, first_piece, pieces, 0)
    turned, kt = run(
        functools.partial(turn_body, groups, heads),
        [shape((heads, groups, height, LANES)), shape((heads, size + 16, length))],
        (after(kaug, sent), *own),
        flops=2 * square,
        moved=4 * square,
    )
    grad_got = move_slots(after(grad_sent, turned, own_w, own_gain))
    produced, spare, rows_in, slope, act_other, act_mine = run_expert(
        plan, place_arg, got, w_up[0], w_down[0], None
    )
    produced_back = move_slots(produced)
    back, grad_rows, hid_other, hid_mine = run_expert(
        plan, place_arg, grad_got, w_up[0], w_down[0], (slope, got, spare)
    )
    returned = move_slots(back)

    def both(values, sent_values):
        return jnp.concatenate([values, cross(sent_values, "tensor", 1)], axis=0)

    grad_down = tn(both(act_mine, act_other), both(grad_rows, grad_rows))
    grad_up = tn(both(rows_in, rows_in), both(hid_mine, hid_other))
    extra = -(-(experts_all + 1) // LANES) * LANES
    outs = run(
        functools.partial(combine_body, groups, capacity, plan),
        [
            shape((height, features)),
            shape((height, features), F32),
            shape((height, features)),
            shape((height, extra)),
            shape((8, features), F32),
        ]
        + [shape((width, height))] * groups,
        (
            after(place_arg, grad_down, grad_up),
            produced_back,
            returned,
            residual,
            router,
            route_row,
            cotangent,
            gain_ffn,
            w_router.T,
            w_out,
        ),
        scratch=[pltpu.VMEM((features, height), BF16)],
        smem=(0,),
        flops=4 * height * square,
        moved=8 * square,
    )
    mixed_out, grad_residual, branch, grad_logits, gain_sums = outs[:5]
    grad_pieces = trade(outs[5:])
    mine, other = run(
        functools.partial(weights_body, experts_all),
        [shape((experts_all, pieces, features + extra))] * 2,
        (place_arg, branch, attended_t, normed_ffn, grad_logits, gain_sums),
        scratch=[pltpu.VMEM((features, features + extra), F32)],
        smem=(0,),
        flops=2 * height * square,
        moved=8 * square,
    )

    def pair_sum(kept, received):
        return (kept.astype(F32) + received.astype(F32)).astype(BF16)

    packed = pair_sum(mine, cross(other, "tensor", 1))
    packed_landed = exchange(packed, ("expert", "context"))
    counts = (heads - 1, 1)
    mine_kv, got_kv, q_grads, diags, fars = [], [], [], [], []
    for call_at in range(len(counts)):
        first, count = sum(counts[:call_at]), counts[call_at]
        dims = [
            (groups, size, height),
            (groups, height, 2 * size),
            (groups, height, 2 * size),
            (5 * height, height),
            (2, spans, height),
        ]
        outs = pl.pallas_call(
            functools.partial(backward_body, groups),
            out_shape=[
                shape((count,) + of, kind)
                for of, kind in zip(dims, [BF16, BF16, BF16, F32, F32])
            ],
            grid=(count,),
            in_specs=[smem]
            + [
                by_head(of, first)
                for of in (
                    held_dims[4],
                    held_dims[2],
                    (size + 16, length),
                    held_dims[0],
                    held_dims[1],
                )
            ]
            + [by_head((groups, height, LANES), first)]
            + [head_rows(first)] * groups,
            out_specs=[by_head(of) for of in dims],
            scratch_shapes=[pltpu.VMEM((length, LANES), F32)]
            + [pltpu.VMEM((length, height), F32)] * 2
            + [pltpu.VMEM((length, height), BF16)] * 2,
            cost_estimate=pl.CostEstimate(
                flops=8 * count * head_flops, bytes_accessed=20 * square, transcendentals=0
            ),
            compiler_params=pltpu.CompilerParams(vmem_limit_bytes=VMEM_LIMIT),
        )(after(place_arg, packed), weights, vaug, kt, exact, inverse, turned, *grad_pieces)
        q_grads.append(outs[0])
        mine_kv.append(outs[1])
        got_kv.append(cross(outs[2], "tensor", 1))
        diags.append(outs[3])
        fars.append(outs[4])
    joined = run(
        functools.partial(join_body, counts),
        [shape((piece_rows, LANES))] * groups,
        (*mine_kv, after(got_kv[0], packed_landed), *got_kv[1:], *q_grads),
        moved=4 * groups * piece_rows * LANES,
    )
    landed_pieces = trade(joined)
    by_bucket = run(
        functools.partial(diagonal_body, counts),
        shape((heads, 1, LANES), F32),
        (*diags, *fars),
    )
    mine, other = run(
        functools.partial(qkv_body, groups, heads),
        [shape((experts_all, pieces, 3 * width + BUCKETS))] * 2,
        (place_arg, *normed_all, *joined, by_bucket),
        scratch=[
            pltpu.VMEM((features, 3 * width + BUCKETS), F32),
            pltpu.VMEM((height, 3 * width), BF16),
        ],
        smem=(0,),
    )
    summed = pair_sum(mine, cross(after(other, *landed_pieces), "tensor", 1))
    landed = exchange(summed, ("expert", "context"))
    grad_qkv, grad_gain_attn, grad_rel = run(
        functools.partial(rows_body, groups, heads),
        [
            shape((pieces, 3 * features), F32),
            shape((pieces,), F32),
            shape((heads, BUCKETS), F32),
        ],
        (place_arg, landed, own_w, own_gain),
        smem=(0,),
        moved=2 * landed.size,
    )
    grad_tokens = run(
        functools.partial(finish_body, groups, heads),
        shape((height, features)),
        (place_arg, tokens_in, gain_attn, w_qkv, grad_residual, *landed_pieces),
        scratch=[
            pltpu.VMEM((features, height), F32),
            pltpu.VMEM((groups, height, width), BF16),
            pltpu.VMEM((groups, height, width), BF16),
        ],
        smem=(0,),
        flops=6 * height * square,
        moved=8 * square,
    )
    reduced = jnp.sum(packed_landed.astype(F32), axis=0)
    return (
        mixed_out,
        grad_tokens,
        grad_gain_attn,
        grad_qkv,
        grad_rel,
        reduced[:, :features].T,
        reduced[:, features + experts_all],
        reduced[:, features : features + experts_all],
        grad_up[None],
        grad_down[None],
    )


def solution(mesh):
    rows = ("expert", "context", "tensor")
    in_specs = (
        P(rows, None),
        P(),
        P(),
        P("context", None),
        P(),
        P(),
        P(),
        P(("expert", "context"), None, None),
        P(("expert", "context"), None, None),
        P("expert", None),
        P(rows, None),
        P(rows, None),
    )
    out_specs = (
        P(rows, None),
        P(rows, None),
        P(rows),
        P(rows, None),
        P("context", None),
        P(None, rows),
        P(rows),
        P(rows, None),
        P(("expert", "context"), None, "tensor"),
        P(("expert", "context"), "tensor", None),
    )
    return jax.shard_map(
        per_device, mesh=mesh, in_specs=in_specs, out_specs=out_specs, check_vma=False
    )
```

```python
import functools

import jax
import jax.numpy as jnp
from jax import lax
from jax.experimental import pallas as pl
from jax.experimental.pallas import tpu as pltpu
from jax.sharding import PartitionSpec as P

EPSILON = 1e-06
THRESHOLDS = (12, 16, 23, 32, 46, 64, 91)
FAR_LEFT = 15
FAR_RIGHT = 31
EXCLUDED = -1e30
LANES = 128
BF16 = jnp.bfloat16
F32 = jnp.float32
VMEM_LIMIT = 56 * 1024 * 1024
BUCKETS = 32
CHUNKS = 6
PART = 256


def bucket_of(offset):
    distance = jnp.abs(offset)
    beyond = jnp.zeros_like(distance)
    for threshold in THRESHOLDS:
        beyond = beyond + (distance >= threshold).astype(jnp.int32)
    nearby = jnp.where(distance < 8, distance, 8 + beyond)
    return nearby + 16 * (offset > 0).astype(jnp.int32)


def nn(left, right):
    return lax.dot_general(left, right, (((1,), (0,)), ((), ())), preferred_element_type=F32)


def nt(left, right):
    return lax.dot_general(left, right, (((1,), (1,)), ((), ())), preferred_element_type=F32)


def tn(left, right):
    return lax.dot_general(left, right, (((0,), (0,)), ((), ())), preferred_element_type=F32)


def iota(shape, axis):
    return lax.broadcasted_iota(jnp.int32, shape, axis)


def three_terms(values):
    high = values.astype(BF16).astype(F32)
    middle = (values - high).astype(BF16).astype(F32)
    return high, middle, values - high - middle


def specs_for(count, smem=()):
    return [
        pl.BlockSpec(memory_space=pltpu.SMEM if i in smem else pltpu.VMEM) for i in range(count)
    ]


def run(body, out_shape, args, scratch=(), smem=(), flops=0, moved=0, limit=VMEM_LIMIT):
    return pl.pallas_call(
        body,
        out_shape=out_shape,
        in_specs=specs_for(len(args), smem),
        scratch_shapes=list(scratch),
        cost_estimate=pl.CostEstimate(flops=flops, bytes_accessed=moved, transcendentals=0),
        compiler_params=pltpu.CompilerParams(vmem_limit_bytes=limit),
    )(*args)


def shape(dims, kind=BF16):
    return jax.ShapeDtypeStruct(dims, kind)


def project_body(heads, place_ref, tokens_ref, gain_ref, w_ref, *refs):
    groups = len(refs) - 2
    piece_refs, normed_ref, all_ref = refs[:groups], refs[groups], refs[groups + 1]
    height, features = tokens_ref.shape
    width = features // groups
    size = width // heads
    group = place_ref[1]
    tokens = tokens_ref[...].astype(F32)
    inverse = lax.rsqrt(jnp.mean(tokens * tokens, axis=-1, keepdims=True) + EPSILON)
    normed = (tokens * inverse * gain_ref[...].astype(F32)[None, :]).astype(BF16)
    normed_ref[...] = jnp.transpose(normed.astype(F32)).astype(BF16)
    turned = jnp.transpose(nn(normed, w_ref[:, :features])).astype(BF16)
    keys = nn(normed, w_ref[:, features : 2 * features]).astype(BF16)
    values = nn(normed, w_ref[:, 2 * features :]).astype(BF16)
    for at in range(groups):
        for head in range(heads):
            lanes = slice(at * width + head * size, at * width + (head + 1) * size)
            all_ref[at ^ group, head * height : (head + 1) * height, :] = jnp.concatenate(
                [keys[:, lanes], values[:, lanes]], axis=1
            )
        for half in range(height // LANES):
            first = heads * height + half * width
            all_ref[at ^ group, first : first + width, :] = turned[
                at * width : (at + 1) * width, half * LANES : (half + 1) * LANES
            ]
    for at in range(groups):
        piece_refs[at][...] = all_ref[at]


def q_rows(piece_ref, heads, height, size, head):
    width = heads * size
    parts = []
    for half in range(height // LANES):
        first = heads * height + half * width + head * size
        parts.append(piece_ref[pl.ds(pl.multiple_of(first, 16), size), :])
    return jnp.concatenate(parts, axis=1)


def forward_body(groups, heads, place_ref, bias_ref, seg_ref, strip_ref, *refs):
    own_refs, far_refs, out_refs = (refs[i * groups : (i + 1) * groups] for i in range(3))
    exact_ref, inverse_ref, vaug_ref, kaug_ref, weight_ref = refs[3 * groups : 3 * groups + 5]
    extra_all, docs_all, vt_ref, score_ref = refs[3 * groups + 5 :]
    size, height = out_refs[0].shape
    spans = kaug_ref.shape[1] // height
    place, group = place_ref[0], place_ref[1]
    head = pl.program_id(0)
    tall = size + 16
    rest = LANES - size

    @pl.when(head == 0)
    def _():
        row = iota((LANES, height), 0) - size
        for span in range(spans):
            docs = seg_ref[0:1, span * height : (span + 1) * height]
            docs_all[span : span + 1, :] = docs
            extra = jnp.where((row >= 0) & (row < 3) & (docs != row), EXCLUDED, 0.0)
            extra = jnp.where(row - 3 == span, 1.0, extra)
            extra_all[span * height : (span + 1) * height, :] = jnp.transpose(extra).astype(BF16)

    row, column = iota((tall, LANES), 0), iota((tall, LANES), 1)
    pick_v = (((row < size) & (row + size == column)) | ((row == size) & (column == 0))).astype(
        BF16
    )
    lane = iota((height, LANES), 1)
    low_half = lane < size
    ones = jnp.where(lane < 3, 1.0, 0.0).astype(BF16)
    extra_row = iota((rest, height), 0)
    queries_all = []
    for at in range(groups):
        block = at ^ group
        for source, parity in ((own_refs[at], place), (far_refs[at], 1 - place)):
            span = 2 * block + parity
            rows = pl.ds(pl.multiple_of(span * height, height), height)
            both = source[pl.ds(pl.multiple_of(head * height, height), height), :]
            keys = jnp.where(low_half, both, extra_all[rows, :])
            values = jnp.where(low_half, ones, both)
            kaug_ref[0, rows, :] = keys
            vaug_ref[0, rows, :] = values
            vt_ref[span] = nt(pick_v, values).astype(BF16)
        span = 2 * block + place
        docs = docs_all[pl.ds(span, 1), :]
        apart = extra_row - 3 - span
        far = jnp.where(
            apart <= -2,
            bias_ref[head, FAR_LEFT],
            jnp.where(apart >= 2, bias_ref[head, FAR_RIGHT], 0.0),
        )
        extra = jnp.where(
            extra_row < 3,
            jnp.where(docs == extra_row, 1.0, 0.0),
            jnp.where(extra_row < 3 + spans, far, 0.0),
        )
        queries_all.append(
            jnp.concatenate(
                [q_rows(own_refs[at], heads, height, size, head), extra.astype(BF16)], axis=0
            )
        )
    for at in range(groups):
        span = 2 * (at ^ group) + place
        start = jnp.clip(span - 1, 0, spans - 3)
        queries = queries_all[at]
        slot = at % 2
        row_max = None
        for step in range(spans):
            key_span = (start + step) if step < 3 else ((start + step) & (spans - 1))
            rows = pl.ds(pl.multiple_of(key_span * height, height), height)
            scores = nn(kaug_ref[0, rows, :], queries)
            if step < 3:
                level = pl.multiple_of((key_span - span + 2) * height, height)
                scores = scores + strip_ref[0, pl.ds(level, height), :]
            score_ref[slot, step] = scores
            best = jnp.max(scores, axis=0, keepdims=True)
            row_max = best if row_max is None else jnp.maximum(row_max, best)
        total = jnp.zeros((tall, height), F32)
        for step in range(spans):
            key_span = (start + step) if step < 3 else ((start + step) & (spans - 1))
            weights = jnp.exp(score_ref[slot, step] - row_max).astype(BF16)
            weight_ref[0, at, key_span] = weights
            total = total + nn(vt_ref[key_span], weights)
        inverse = 1.0 / total[size : size + 1]
        result = total[:size] * inverse
        out_refs[at][...] = result.astype(BF16)
        exact_ref[0, at] = result
        inverse_ref[0, at] = jnp.broadcast_to(inverse, (8, height))


def turn_body(groups, heads, kaug_ref, *refs):
    piece_refs, out_ref, kt_ref = refs[:groups], refs[groups], refs[groups + 1]
    height = out_ref.shape[2]
    size = out_ref.shape[3] // 2
    spans = kaug_ref.shape[1] // height
    row, column = iota((size + 16, LANES), 0), iota((size + 16, LANES), 1)
    pick_k = (
        ((row < size) & (row == column))
        | ((row >= size) & (row < size + spans) & (row + 3 == column))
    ).astype(BF16)
    blank = jnp.zeros((size, height), F32)
    for head in range(heads):
        kt_ref[head] = nt(pick_k, kaug_ref[head]).astype(BF16)
        for at in range(groups):
            queries = q_rows(piece_refs[at], heads, height, size, head).astype(F32)
            out_ref[head, at] = jnp.transpose(jnp.concatenate([queries, blank], axis=0)).astype(
                BF16
            )


def backward_body(groups, place_ref, *refs):
    weight_ref, vaug_ref, kt_ref, exact_ref, inverse_ref, q_ref = refs[:6]
    grad_refs = refs[6 : 6 + groups]
    dq_ref, mine_ref, other_ref, diag_ref, far_ref, dkv_ref = refs[6 + groups : 12 + groups]
    slope_refs, score_refs = refs[12 + groups : 14 + groups], refs[14 + groups :]
    size, height = grad_refs[0].shape
    length = vaug_ref.shape[1]
    spans = length // height
    place, group = place_ref[0], place_ref[1]
    diag_ref[...] = jnp.zeros_like(diag_ref)
    extra_row = iota((LANES - size, height), 0)
    blank = jnp.zeros((size, height), F32)
    span_row = iota((spans, height), 0)
    left_total = jnp.zeros((spans, height), F32)
    right_total = jnp.zeros((spans, height), F32)
    for at in range(groups):
        span = 2 * (at ^ group) + place
        start = jnp.clip(span - 1, 0, spans - 3)
        slope_ref, score_ref = slope_refs[at % 2], score_refs[at % 2]
        grads = (grad_refs[at][...].astype(F32) * inverse_ref[0, at, 0:1]).astype(BF16)
        grads32 = grads.astype(F32)
        delta = jnp.sum(grads32 * exact_ref[0, at], axis=0, keepdims=True)
        high, middle, low = three_terms(-delta)
        extra = jnp.where(
            extra_row == 0,
            high,
            jnp.where(extra_row == 1, middle, jnp.where(extra_row == 2, low, 0.0)),
        )
        slope_ref[...] = nn(
            vaug_ref[0], jnp.concatenate([extra.astype(BF16), grads], axis=0)
        )
        turned = jnp.transpose(jnp.concatenate([blank, grads32], axis=0)).astype(BF16)
        sides = jnp.concatenate([q_ref[0, at], turned], axis=0)
        for key in range(spans):
            rows = slice(key * height, (key + 1) * height)
            score_ref[rows, :] = (
                weight_ref[0, at, key].astype(F32) * slope_ref[rows, :]
            ).astype(BF16)
        both = jnp.concatenate(
            [score_ref[...], weight_ref[0, at].reshape(length, height)], axis=1
        )
        product = nn(both, sides)
        if at == 0:
            dkv_ref[...] = product
        else:
            dkv_ref[...] = dkv_ref[...] + product
        total = nn(kt_ref[0], score_ref[...])
        dq_ref[0, at] = total[:size].astype(BF16)
        sums = total[size : size + spans]
        left_total = left_total + jnp.where(span_row < start, sums, 0.0)
        right_total = right_total + jnp.where(span_row >= start + 3, sums, 0.0)
        rows = pl.ds(pl.multiple_of(start * height, height), 3 * height)
        level = pl.ds(pl.multiple_of((start - span + 2) * height, height), 3 * height)
        diag_ref[0, level, :] = diag_ref[0, level, :] + score_ref[rows, :].astype(F32)
    far_ref[0, 0] = left_total
    far_ref[0, 1] = right_total
    for at in range(groups):
        for target, parity in ((mine_ref, place), (other_ref, 1 - place)):
            first = pl.multiple_of((2 * (at ^ group) + parity) * height, height)
            target[0, at] = dkv_ref[pl.ds(first, height), :].astype(BF16)


def join_body(counts, *refs):
    calls = len(counts)
    mine_refs, got_refs, dq_refs = (refs[i * calls : (i + 1) * calls] for i in range(3))
    piece_refs = refs[3 * calls :]
    size, height = dq_refs[0].shape[2:]
    heads = sum(counts)
    width = heads * size
    for at, piece_ref in enumerate(piece_refs):
        head = 0
        for call_at, count in enumerate(counts):
            for inner in range(count):
                kept = mine_refs[call_at][inner, at].astype(F32)
                piece_ref[head * height : (head + 1) * height, :] = (
                    kept + got_refs[call_at][inner, at].astype(F32)
                ).astype(BF16)
                for half in range(height // LANES):
                    first = heads * height + half * width + head * size
                    piece_ref[first : first + size, :] = dq_refs[call_at][
                        inner, at, :, half * LANES : (half + 1) * LANES
                    ]
                head += 1


def slot_plan(capacity, features):
    base = capacity // 16 * 16
    left = capacity - base
    if base and left and 16 % left == 0 and (2 * features) % (LANES * (16 // left)) == 0:
        return base, left, 16 // left
    return -(-capacity // 8) * 8, 0, 0


def slot_marks(shape_of, axis, chosen, rank, capacity, plan):
    base, left, parts = plan
    position = iota(shape_of, axis)
    limit = base if left else capacity
    marks = [jnp.where(position == jnp.where(rank < limit, chosen * base + rank, -1), 1.0, 0.0)]
    spare = rank - base
    for part in range(parts):
        slot = chosen * 16 + part * left + spare
        slot = jnp.where((spare >= 0) & (spare < left), slot, -1)
        marks.append(jnp.where(position == slot, 1.0, 0.0))
    return [mark.astype(BF16) for mark in marks]


def route_body(
    groups,
    capacity,
    plan,
    place_ref,
    tokens_ref,
    w_out_ref,
    gain_ref,
    w_router_ref,
    route_row_ref,
    cotangent_ref,
    *refs,
):
    pieces = refs[:groups]
    residual_ref, normed_ref, router_ref, sent_ref, grad_sent_ref, attended_ref = refs[groups:]
    height, features = tokens_ref.shape
    experts = w_router_ref.shape[0]
    slots = sent_ref.shape[0]
    width = pieces[0].shape[0]
    group = place_ref[1]
    for at in range(groups):
        first = pl.multiple_of((at ^ group) * width, width)
        attended_ref[pl.ds(first, width), :] = pieces[at][...]
    residual = tokens_ref[...].astype(F32) + tn(attended_ref[...], w_out_ref[...])
    residual_ref[...] = residual
    inverse = lax.rsqrt(jnp.mean(residual * residual, axis=-1, keepdims=True) + EPSILON)
    normed = (residual * inverse * gain_ref[...].astype(F32)[None, :]).astype(BF16)
    normed_ref[...] = normed
    logits = nt(normed, w_router_ref[...])
    powers = jnp.exp(logits - jnp.max(logits, axis=-1, keepdims=True))
    router = powers / jnp.sum(powers, axis=-1, keepdims=True)
    router_ref[...] = router
    chosen = route_row_ref[...]
    marks = iota((experts, height), 0) == chosen
    onehot = jnp.transpose(jnp.where(marks, 1.0, 0.0))
    gate = jnp.sum(onehot * router, axis=-1, keepdims=True)
    grad_expert = (gate * cotangent_ref[...].astype(F32)).astype(BF16)
    rows = jnp.concatenate([normed, grad_expert], axis=1)
    earlier = (iota((height, height), 0) < iota((height, height), 1)).astype(BF16)
    before = nn(jnp.where(marks, 1.0, 0.0).astype(BF16), earlier)
    rank = jnp.sum(jnp.where(marks, before, 0.0), axis=0, keepdims=True).astype(jnp.int32)
    dispatch = slot_marks((slots, height), 0, chosen, rank, capacity, plan)
    sent_ref[:, :features] = nn(dispatch[0], normed).astype(BF16)
    grad_sent_ref[...] = nn(dispatch[0], grad_expert).astype(BF16)
    if plan[1]:
        span = 2 * features // plan[2]
        spare = nn(dispatch[1], rows[:, :span])
        for part in range(1, plan[2]):
            spare = spare + nn(dispatch[1 + part], rows[:, part * span : (part + 1) * span])
        sent_ref[:, features:] = spare.astype(BF16)


def spare_marks(sources, plan):
    base, left, parts = plan
    target = iota((sources * left, sources * 16), 0)
    origin = iota((sources * left, sources * 16), 1)
    source = target // left
    return [
        (origin == source * 16 + part * left + (target - source * left)).astype(BF16)
        for part in range(parts)
    ]


def unpack_spare(rows_ref, packed, plan, first_part):
    main = packed.shape[0]
    marks = spare_marks(main // 16, plan)
    half = plan[2] // 2
    span = rows_ref.shape[1] // half
    for part in range(half):
        rows_ref[main:, part * span : (part + 1) * span] = nn(
            marks[first_part + part], packed
        ).astype(BF16)


def bring(place, up_ref, down_ref, up_all, down_all, sems):
    chunk = up_all.shape[2]
    copies = []
    for at in range(CHUNKS):
        half = (1 - place) if at < CHUNKS // 2 else place
        first = half * (chunk * CHUNKS // 2) + at % (CHUNKS // 2) * chunk
        part = pl.ds(pl.multiple_of(first, chunk), chunk)
        copies.append(
            (
                pltpu.make_async_copy(up_ref.at[:, part], up_all.at[at], sems.at[0, at]),
                pltpu.make_async_copy(down_ref.at[part, :], down_all.at[at], sems.at[1, at]),
            )
        )
    return copies


def expert_forward_body(
    plan,
    place_ref,
    got_ref,
    up_ref,
    down_ref,
    back_ref,
    spare_ref,
    rows_ref,
    slope_ref,
    other_ref,
    mine_ref,
    total_ref,
    up_all,
    down_all,
    sems,
    active_all,
    slope_all,
    out_sems,
):
    main, features = back_ref.shape
    leaving = []
    chunk = up_all.shape[2]
    copies = bring(place_ref[0], up_ref, down_ref, up_all, down_all, sems)
    for up_copy, down_copy in copies:
        up_copy.start()
        down_copy.start()
    rows_ref[:main, :] = got_ref[:, :features]
    if plan[1]:
        unpack_spare(rows_ref, got_ref[:, features:], plan, 0)
    for at in range(CHUNKS):
        half = at // (CHUNKS // 2)
        base = at % (CHUNKS // 2) * chunk
        copies[at][0].wait()
        for first in range(0, chunk, PART):
            lanes = slice(base + first, base + first + PART)
            hidden = nn(rows_ref[...], up_all[at, :, first : first + PART])
            below = 0.5 * (1.0 + lax.erf(hidden * (2.0**-0.5)))
            bell = jnp.exp(-0.5 * hidden * hidden) * 0.3989422804014327
            active_all[half, :, lanes] = (hidden * below).astype(BF16)
            slope_all[half, :, lanes] = (below + hidden * bell).astype(BF16)
        whole = pl.ds(base, chunk)
        for which, (source, target) in enumerate(
            (
                (active_all.at[half, :, whole], (other_ref, mine_ref)[half].at[:, whole]),
                (slope_all.at[half, :, whole], slope_ref.at[half, :, whole]),
            )
        ):
            copy = pltpu.make_async_copy(source, target, out_sems.at[which, at])
            copy.start()
            leaving.append(copy)
        copies[at][1].wait()
        product = nn(active_all[half, :, base : base + chunk], down_all[at])
        if at == 0:
            total_ref[...] = product
        else:
            total_ref[...] = total_ref[...] + product
    back_ref[...] = total_ref[:main, :].astype(BF16)
    if plan[1]:
        spare_ref[...] = total_ref[main:, :].astype(BF16)
    else:
        spare_ref[...] = jnp.zeros_like(spare_ref)
    for copy in leaving:
        copy.wait()


def expert_backward_body(
    plan,
    place_ref,
    got_ref,
    up_ref,
    down_ref,
    slope_ref,
    packed_ref,
    spare_ref,
    back_ref,
    rows_ref,
    other_ref,
    mine_ref,
    total_ref,
    up_all,
    down_all,
    sems,
):
    main, features = got_ref.shape
    chunk = up_all.shape[2]
    copies = bring(place_ref[0], up_ref, down_ref, up_all, down_all, sems)
    for up_copy, down_copy in copies:
        down_copy.start()
        up_copy.start()
    rows_ref[:main, :] = got_ref[...]
    if plan[1]:
        unpack_spare(rows_ref, packed_ref[:, features:], plan, plan[2] // 2)
    for at in range(CHUNKS):
        hidden_ref = other_ref if at < CHUNKS // 2 else mine_ref
        base = at % (CHUNKS // 2) * chunk
        copies[at][1].wait()
        for first in range(0, chunk, PART):
            lanes = slice(base + first, base + first + PART)
            grad_active = nt(rows_ref[...], down_all[at, first : first + PART, :])
            slope = slope_ref[at // (CHUNKS // 2), :, lanes].astype(F32)
            hidden_ref[:, lanes] = (grad_active * slope).astype(BF16)
        copies[at][0].wait()
        product = nt(hidden_ref[:, base : base + chunk], up_all[at])
        if at == 0:
            total_ref[...] = product
        else:
            total_ref[...] = total_ref[...] + product
    back_ref[:, :features] = total_ref[:main, :].astype(BF16)
    if plan[1]:
        spare = jnp.concatenate([spare_ref[...], total_ref[main:, :].astype(BF16)], axis=1)
        span = 2 * features // plan[2]
        packed = jnp.zeros((main, span), F32)
        for part, marks in enumerate(spare_marks(main // 16, plan)):
            packed = packed + tn(marks, spare[:, part * span : (part + 1) * span])
        back_ref[:, features:] = packed.astype(BF16)


def run_expert(plan, place_arg, got, up, down, forward):
    main = got.shape[0]
    features, hidden_size = up.shape
    spare = main // 16 * plan[1]
    slots = main + spare
    columns = features + (2 * features // plan[2] if plan[1] else 0)
    spare = max(spare, 8)
    halves = [shape((slots, hidden_size // 2))] * 2
    if forward is None:
        body = expert_forward_body
        out_shape = [shape((main, features)), shape((spare, features)), shape((slots, features))]
        out_shape += [shape((2, slots, hidden_size // 2))] + halves
        args, flops = (got, up, down), 0
    else:
        body = expert_backward_body
        out_shape = [shape((main, columns)), shape((slots, features))] + halves
        args, flops = (got, up, down) + forward, 4 * slots * features * hidden_size
    args = (place_arg,) + args
    specs = specs_for(len(args), (0,))
    specs[2] = specs[3] = pl.BlockSpec(memory_space=pl.ANY)
    chunk = hidden_size // CHUNKS
    out_specs = [pl.BlockSpec(memory_space=pltpu.VMEM)] * len(out_shape)
    held = []
    if forward is None:
        out_specs[3:] = [pl.BlockSpec(memory_space=pl.ANY)] * 3
        held = [pltpu.VMEM((2, slots, hidden_size // 2), BF16)] * 2
        held.append(pltpu.SemaphoreType.DMA((2, CHUNKS)))
    return pl.pallas_call(
        functools.partial(body, plan),
        out_shape=out_shape,
        in_specs=specs,
        out_specs=out_specs,
        scratch_shapes=[
            pltpu.VMEM((slots, features), F32),
            pltpu.VMEM((CHUNKS, features, chunk), BF16),
            pltpu.VMEM((CHUNKS, chunk, features), BF16),
            pltpu.SemaphoreType.DMA((2, CHUNKS)),
        ]
        + held,
        cost_estimate=pl.CostEstimate(flops=flops, bytes_accessed=flops // 400, transcendentals=0),
        compiler_params=pltpu.CompilerParams(vmem_limit_bytes=VMEM_LIMIT),
    )(*args)


def combine_body(
    groups,
    capacity,
    plan,
    place_ref,
    produced_ref,
    got_ref,
    residual_ref,
    router_ref,
    route_row_ref,
    cotangent_ref,
    gain_ref,
    w_router_ref,
    w_out_ref,
    mixed_ref,
    grad_residual_ref,
    branch_ref,
    logits_ref,
    gain_out_ref,
    *refs,
):
    pieces, turned_ref = refs[:groups], refs[groups]
    height, experts = router_ref.shape
    features = residual_ref.shape[1]
    slots = got_ref.shape[0]
    width = pieces[0].shape[0]
    group = place_ref[1]
    chosen_row = route_row_ref[...]
    marks = jnp.where(iota((experts, height), 0) == chosen_row, 1.0, 0.0)
    earlier = (iota((height, height), 0) < iota((height, height), 1)).astype(BF16)
    before = nn(marks.astype(BF16), earlier)
    rank_row = jnp.sum(marks * before, axis=0, keepdims=True)
    onehot = jnp.transpose(marks) > 0.5
    pair_row = iota((8, height), 0)
    pairs = jnp.transpose(jnp.where(pair_row == 0, chosen_row.astype(F32), rank_row))
    chosen = pairs[:, 0:1].astype(jnp.int32)
    rank = pairs[:, 1:2].astype(jnp.int32)
    combine = slot_marks((height, slots), 1, chosen, rank, capacity, plan)
    back = jnp.concatenate(
        [nn(combine[0], produced_ref[...]), nn(combine[0], got_ref[:, :features])], axis=1
    )
    if plan[1]:
        spare = got_ref[:, features:]
        back = back + jnp.concatenate([nn(marks, spare) for marks in combine[1:]], axis=1)
    router = router_ref[...]
    gate = jnp.sum(jnp.where(onehot, router, 0.0), axis=-1, keepdims=True)
    residual = residual_ref[...]
    inverse = lax.rsqrt(jnp.mean(residual * residual, axis=-1, keepdims=True) + EPSILON)
    unit = residual * inverse
    grad_mixed = cotangent_ref[...].astype(F32)
    gathered = back[:, :features]
    mixed_ref[...] = (residual + gate * gathered).astype(BF16)
    grad_gate = jnp.sum(grad_mixed * gathered, axis=-1, keepdims=True)
    grad_logits = (router * (jnp.where(onehot, grad_gate, 0.0) - gate * grad_gate)).astype(BF16)
    grad_normed = back[:, features:] + nn(grad_logits, w_router_ref[...])
    grad_unit = grad_normed * gain_ref[...].astype(F32)[None, :]
    grad_residual = grad_mixed + inverse * (
        grad_unit - unit * jnp.mean(grad_unit * unit, axis=-1, keepdims=True)
    )
    branch = grad_residual.astype(BF16)
    turned_ref[...] = nt(w_out_ref[...], branch).astype(BF16)
    for at in range(groups):
        first = pl.multiple_of((at ^ group) * width, width)
        pieces[at][...] = turned_ref[pl.ds(first, width), :]
    grad_residual_ref[...] = grad_residual
    branch_ref[...] = branch
    spare_lanes = logits_ref.shape[1] - experts
    logits_ref[...] = jnp.concatenate([grad_logits, jnp.zeros((height, spare_lanes), BF16)], axis=1)
    sums = jnp.sum(grad_normed * unit, axis=0, keepdims=True)
    gain_out_ref[...] = jnp.broadcast_to(sums, gain_out_ref.shape)


def qkv_body(groups, heads, place_ref, *refs):
    normed_refs, piece_refs = refs[:groups], refs[groups : 2 * groups]
    bucket_ref, mine_ref, other_ref, total_ref, rows_ref = refs[2 * groups :]
    pieces = mine_ref.shape[1]
    wide = rows_ref.shape[1]
    height = normed_refs[0].shape[1]
    width = rows_ref.shape[1] // 3
    for at in range(groups):
        piece = piece_refs[at]
        for head in range(heads):
            rows_ref[:, head * LANES : (head + 1) * LANES] = piece[
                head * height : (head + 1) * height, :
            ]
        parts = [
            piece[heads * height + half * width : heads * height + (half + 1) * width, :]
            for half in range(height // LANES)
        ]
        turned = jnp.concatenate(parts, axis=1).astype(F32)
        rows_ref[:, 2 * width :] = jnp.transpose(turned).astype(BF16)
        product = nn(normed_refs[at][...], rows_ref[...])
        if at == 0:
            total_ref[:, :wide] = product
        else:
            total_ref[:, :wide] = total_ref[:, :wide] + product
    row = iota((total_ref.shape[0], BUCKETS), 0) % pieces
    buckets = jnp.zeros((total_ref.shape[0], BUCKETS), F32)
    for head in range(heads):
        buckets = jnp.where(row == head, bucket_ref[head, :, :BUCKETS], buckets)
    total_ref[:, wide:] = buckets
    split_rows(place_ref[0], total_ref, mine_ref, other_ref)


def rows_body(
    groups, heads, place_ref, landed_ref, w_ref, gain_ref, out_ref, gain_out_ref, bucket_ref
):
    sources, _, columns = landed_ref.shape
    width = (columns - BUCKETS) // 3
    size = width // heads
    features = groups * width
    for group in range(groups):
        total = landed_ref[group].astype(F32)
        for expert in range(1, sources // groups):
            total = total + landed_ref[expert * groups + group].astype(F32)
        out_ref[:, group * width : (group + 1) * width] = total[:, 2 * width : 3 * width]
        for head in range(heads):
            for part in range(2):
                source = head * 2 * size + part * size
                first = (part + 1) * features + group * width + head * size
                out_ref[:, first : first + size] = total[:, source : source + size]
    sums = lax.dot_general(
        jnp.ones((8, 3 * features), F32),
        w_ref[...].astype(F32) * out_ref[...],
        (((1,), (1,)), ((), ())),
        precision=lax.Precision.HIGHEST,
        preferred_element_type=F32,
    )
    gain_out_ref[...] = sums[0] / gain_ref[...].astype(F32)
    buckets = jnp.zeros((landed_ref.shape[1], BUCKETS), F32)
    for expert in range(sources // groups):
        buckets = buckets + landed_ref[expert * groups + place_ref[1]][:, 3 * width :].astype(F32)
    bucket_ref[...] = buckets[:heads]


def finish_body(groups, heads, place_ref, tokens_ref, gain_ref, w_ref, residual_ref, *refs):
    piece_refs = refs[:groups]
    out_ref, turned_ref, k_all, v_all = refs[groups:]
    height, features = tokens_ref.shape
    width = features // groups
    size = width // heads
    group = place_ref[1]
    for at in range(groups):
        piece = piece_refs[at]
        first = pl.multiple_of((at ^ group) * width, width)
        for half in range(height // LANES):
            source = heads * height + half * width
            turned_ref[pl.ds(first, width), half * LANES : (half + 1) * LANES] = piece[
                source : source + width, :
            ].astype(F32)
        for head in range(heads):
            both = piece[head * height : (head + 1) * height, :]
            lanes = slice(head * size, (head + 1) * size)
            k_all[at ^ group, :, lanes] = both[:, :size]
            v_all[at ^ group, :, lanes] = both[:, size:]
    grad_normed = nt(jnp.transpose(turned_ref[...]).astype(BF16), w_ref[:, :features])
    for part, source in ((1, k_all), (2, v_all)):
        joined = jnp.concatenate([source[at] for at in range(groups)], axis=1)
        grad_normed = grad_normed + nt(joined, w_ref[:, part * features : (part + 1) * features])
    tokens = tokens_ref[...].astype(F32)
    inverse = lax.rsqrt(jnp.mean(tokens * tokens, axis=-1, keepdims=True) + EPSILON)
    unit = tokens * inverse
    grad_unit = grad_normed * gain_ref[...].astype(F32)[None, :]
    grad = inverse * (grad_unit - unit * jnp.mean(grad_unit * unit, axis=-1, keepdims=True))
    out_ref[...] = (residual_ref[...] + grad).astype(BF16)


def strip_body(table_ref, strips_ref):
    heads, rows, height = strips_ref.shape
    used = rows - height
    offset = iota((used, LANES), 0) - 2 * height
    onehot = (bucket_of(offset) == iota((used, LANES), 1)).astype(BF16)
    lane = iota((used, height), 1)
    blank = jnp.zeros((height, height), F32)
    for head in range(heads):
        values = nn(onehot, table_ref[head])
        moved = 1
        while moved < height:
            values = jnp.where((lane & moved) != 0, pltpu.roll(values, moved, 0), values)
            moved *= 2
        strips_ref[head, :height] = blank
        strips_ref[head, height:used] = values[height:]
        strips_ref[head, used:] = blank


def diagonal_body(counts, *refs):
    calls = len(counts)
    out_ref = refs[2 * calls]
    places = [(call_at, inner) for call_at in range(calls) for inner in range(counts[call_at])]
    height = refs[0].shape[2]
    total_rows = 5 * height
    lane = iota((total_rows, height), 1)
    offset = iota((total_rows, LANES), 0) - 2 * height
    table = (bucket_of(offset) == iota((total_rows, LANES), 1)).astype(F32)
    lane_out = iota((1, LANES), 1)
    blank = jnp.zeros((height, height), F32)
    for head, (call_at, inner) in enumerate(places):
        diag_ref, far_ref = refs[call_at].at[inner], refs[calls + call_at].at[inner]
        values = jnp.concatenate([blank, diag_ref[height : 4 * height, :], blank], axis=0)
        moved = 1
        while moved < height:
            values = jnp.where(
                (lane & moved) != 0, pltpu.roll(values, total_rows - moved, 0), values
            )
            moved *= 2
        sums = jnp.sum(values, axis=1, keepdims=True)
        by_bucket = jnp.sum(sums * table, axis=0, keepdims=True)
        by_bucket = by_bucket + jnp.where(
            lane_out == FAR_LEFT, jnp.sum(far_ref[0]) + jnp.sum(diag_ref[:height, :]), 0.0
        )
        out_ref[head] = by_bucket + jnp.where(
            lane_out == FAR_RIGHT, jnp.sum(far_ref[1]) + jnp.sum(diag_ref[4 * height :, :]), 0.0
        )


def split_rows(place, source_ref, mine_ref, other_ref):
    experts_all, pieces, columns = mine_ref.shape
    for parity in range(2):

        @pl.when(place == parity)
        def _():
            for at in range(experts_all):
                for target, which in ((mine_ref, parity), (other_ref, 1 - parity)):
                    first = (2 * at + which) * pieces
                    target[at] = source_ref[first : first + pieces, :].astype(BF16)


def weights_body(
    experts,
    place_ref,
    branch_ref,
    attended_ref,
    normed_ref,
    logits_ref,
    gain_ref,
    mine_ref,
    other_ref,
    packed_ref,
):
    features = branch_ref.shape[1]
    extra = logits_ref.shape[1]
    branch = jnp.transpose(branch_ref[...].astype(F32)).astype(BF16)
    packed_ref[:, :features] = nt(branch, attended_ref[...])
    normed = jnp.transpose(normed_ref[...].astype(F32)).astype(BF16)
    column = jnp.transpose(gain_ref[...])[:, :1]
    packed_ref[:, features:] = nn(normed, logits_ref[...]) + jnp.where(
        iota((features, extra), 1) == experts, column, 0.0
    )
    split_rows(place_ref[0], packed_ref, mine_ref, other_ref)


def exchange(moving, axis):
    return lax.all_to_all(moving, axis, split_axis=0, concat_axis=0, tiled=True)


def cross(moving, axis, distance):
    size = lax.axis_size(axis)
    return lax.ppermute(moving, axis, [(i, i ^ distance) for i in range(size)])


def trade(pieces):
    return [
        piece if at == 0 else cross(piece, "context", at) for at, piece in enumerate(pieces)
    ]


def after(values, *others):
    return lax.optimization_barrier((values,) + others)[0]


def per_device(
    tokens_in,
    gain_attn,
    w_qkv,
    rel_bias,
    w_out,
    gain_ffn,
    w_router,
    w_up,
    w_down,
    segments,
    routes,
    cotangent,
):
    groups = lax.axis_size("context")
    tensor_size = lax.axis_size("tensor")
    expert_size = lax.axis_size("expert")
    height, features = tokens_in.shape
    heads = rel_bias.shape[0]
    width = features // groups
    size = width // heads
    length = segments.shape[1]
    spans = length // height
    experts_all = expert_size * groups
    capacity = max(2, 5 * height // (4 * experts_all))
    plan = slot_plan(capacity, features)
    slots = experts_all * plan[0]
    columns = features + (2 * features // plan[2] if plan[1] else 0)
    piece_rows = heads * height + height // LANES * width
    place = lax.axis_index("tensor")
    context_at = lax.axis_index("context")
    place_arg = jnp.stack([place, context_at]).astype(jnp.int32)
    square = features * features

    projected = run(
        functools.partial(project_body, heads),
        [shape((piece_rows, LANES))] * groups + [shape((features, height))],
        (place_arg, tokens_in, gain_attn, w_qkv),
        scratch=[pltpu.VMEM((groups, piece_rows, LANES), BF16)],
        smem=(0,),
        flops=6 * height * square,
        moved=8 * square,
    )
    own = trade(projected[:groups])
    table = jnp.pad(rel_bias, ((0, 0), (0, LANES - rel_bias.shape[1])))
    table = jnp.broadcast_to(table[:, :, None], (heads, LANES, height))
    strips = run(
        strip_body,
        shape((heads, 5 * height, height), F32),
        (table,),
        flops=heads * 2 * 4 * height * LANES * height,
        moved=heads * 4 * 5 * height * height,
    )
    far = [cross(after(piece, strips), "tensor", 1) for piece in own]
    head_flops = 4 * groups * height * length * size

    def fixed(dims):
        return pl.BlockSpec(dims, lambda h, n=len(dims): (0,) * n)

    def by_head(dims, first=0):
        return pl.BlockSpec(
            (1,) + dims, lambda h, n=len(dims), f=first: (h + f,) + (0,) * n
        )

    def head_rows(first=0):
        return pl.BlockSpec((size, height), lambda h, f=first: (h + f, 0))

    smem = pl.BlockSpec(memory_space=pltpu.SMEM)
    held_dims = [
        (groups, size, height),
        (groups, 8, height),
        (length, LANES),
        (length, LANES),
        (groups, spans, height, height),
    ]
    held_kinds = [F32, F32, BF16, BF16, BF16]
    outs = pl.pallas_call(
        functools.partial(forward_body, groups, heads),
        out_shape=[shape((width, height))] * groups
        + [shape((heads,) + dims, kind) for dims, kind in zip(held_dims, held_kinds)],
        grid=(heads,),
        in_specs=[smem, smem, fixed((1, length)), by_head((5 * height, height))]
        + [fixed((piece_rows, LANES))] * (2 * groups),
        out_specs=[head_rows()] * groups + [by_head(dims) for dims in held_dims],
        scratch_shapes=[
            pltpu.VMEM((length, LANES), BF16),
            pltpu.VMEM((spans, height), jnp.int32),
            pltpu.VMEM((spans, size + 16, height), BF16),
            pltpu.VMEM((2, spans, height, height), F32),
        ],
        cost_estimate=pl.CostEstimate(
            flops=6 * heads * head_flops, bytes_accessed=20 * square, transcendentals=0
        ),
        compiler_params=pltpu.CompilerParams(vmem_limit_bytes=VMEM_LIMIT),
    )(place_arg, rel_bias.astype(F32), segments, strips, *own, *far)
    attended = trade(outs[:groups])
    exact, inverse, vaug, kaug, weights = outs[groups:]
    route_row = routes.reshape(1, height)
    normed_all = trade([after(projected[groups], *own)] * groups)
    residual, normed_ffn, router, sent, grad_sent, attended_t = run(
        functools.partial(route_body, groups, capacity, plan),
        [
            shape((height, features), F32),
            shape((height, features)),
            shape((height, experts_all), F32),
            shape((slots, columns)),
            shape((slots, features)),
            shape((features, height)),
        ],
        (
            after(place_arg, *normed_all),
            tokens_in,
            w_out,
            gain_ffn,
            w_router.T,
            route_row,
            cotangent,
            *attended,
        ),
        smem=(0,),
        flops=2 * height * square,
        moved=4 * square,
    )

    def move_slots(moving):
        return exchange(
            moving.reshape(experts_all, plan[0], -1), ("expert", "context")
        ).reshape(moving.shape)

    got = move_slots(sent)
    pieces = features // (experts_all * tensor_size)
    first_piece = (
        (lax.axis_index("expert") * groups + context_at) * tensor_size + place
    ) * pieces
    first_piece = after(first_piece, sent)
    own_w = lax.dynamic_slice_in_dim(w_qkv, first_piece, pieces, 0)
    own_gain = lax.dynamic_slice_in_dim(gain_attn, first_piece, pieces, 0)
    turned, kt = run(
        functools.partial(turn_body, groups, heads),
        [shape((heads, groups, height, LANES)), shape((heads, size + 16, length))],
        (after(kaug, sent), *own),
        flops=2 * square,
        moved=4 * square,
    )
    grad_got = move_slots(after(grad_sent, turned, own_w, own_gain))
    produced, spare, rows_in, slope, act_other, act_mine = run_expert(
        plan, place_arg, got, w_up[0], w_down[0], None
    )
    produced_back = move_slots(produced)
    back, grad_rows, hid_other, hid_mine = run_expert(
        plan, place_arg, grad_got, w_up[0], w_down[0], (slope, got, spare)
    )
    returned = move_slots(back)

    def both(values, sent_values):
        return jnp.concatenate([values, cross(sent_values, "tensor", 1)], axis=0)

    grad_down = tn(both(act_mine, act_other), both(grad_rows, grad_rows))
    grad_up = tn(both(rows_in, rows_in), both(hid_mine, hid_other))
    extra = -(-(experts_all + 1) // LANES) * LANES
    outs = run(
        functools.partial(combine_body, groups, capacity, plan),
        [
            shape((height, features)),
            shape((height, features), F32),
            shape((height, features)),
            shape((height, extra)),
            shape((8, features), F32),
        ]
        + [shape((width, height))] * groups,
        (
            after(place_arg, grad_down, grad_up),
            produced_back,
            returned,
            residual,
            router,
            route_row,
            cotangent,
            gain_ffn,
            w_router.T,
            w_out,
        ),
        scratch=[pltpu.VMEM((features, height), BF16)],
        smem=(0,),
        flops=4 * height * square,
        moved=8 * square,
    )
    mixed_out, grad_residual, branch, grad_logits, gain_sums = outs[:5]
    grad_pieces = trade(outs[5:])
    mine, other = run(
        functools.partial(weights_body, experts_all),
        [shape((experts_all, pieces, features + extra))] * 2,
        (place_arg, branch, attended_t, normed_ffn, grad_logits, gain_sums),
        scratch=[pltpu.VMEM((features, features + extra), F32)],
        smem=(0,),
        flops=2 * height * square,
        moved=8 * square,
    )

    def pair_sum(kept, received):
        return (kept.astype(F32) + received.astype(F32)).astype(BF16)

    packed = pair_sum(mine, cross(other, "tensor", 1))
    packed_landed = exchange(packed, ("expert", "context"))
    counts = (heads - 1, 1)
    mine_kv, got_kv, q_grads, diags, fars = [], [], [], [], []
    for call_at in range(len(counts)):
        first, count = sum(counts[:call_at]), counts[call_at]
        dims = [
            (groups, size, height),
            (groups, height, 2 * size),
            (groups, height, 2 * size),
            (5 * height, height),
            (2, spans, height),
        ]
        outs = pl.pallas_call(
            functools.partial(backward_body, groups),
            out_shape=[
                shape((count,) + of, kind)
                for of, kind in zip(dims, [BF16, BF16, BF16, F32, F32])
            ],
            grid=(count,),
            in_specs=[smem]
            + [
                by_head(of, first)
                for of in (
                    held_dims[4],
                    held_dims[2],
                    (size + 16, length),
                    held_dims[0],
                    held_dims[1],
                )
            ]
            + [by_head((groups, height, LANES), first)]
            + [head_rows(first)] * groups,
            out_specs=[by_head(of) for of in dims],
            scratch_shapes=[pltpu.VMEM((length, LANES), F32)]
            + [pltpu.VMEM((length, height), F32)] * 2
            + [pltpu.VMEM((length, height), BF16)] * 2,
            cost_estimate=pl.CostEstimate(
                flops=8 * count * head_flops, bytes_accessed=20 * square, transcendentals=0
            ),
            compiler_params=pltpu.CompilerParams(vmem_limit_bytes=VMEM_LIMIT),
        )(after(place_arg, packed), weights, vaug, kt, exact, inverse, turned, *grad_pieces)
        q_grads.append(outs[0])
        mine_kv.append(outs[1])
        got_kv.append(cross(outs[2], "tensor", 1))
        diags.append(outs[3])
        fars.append(outs[4])
    joined = run(
        functools.partial(join_body, counts),
        [shape((piece_rows, LANES))] * groups,
        (*mine_kv, after(got_kv[0], packed_landed), *got_kv[1:], *q_grads),
        moved=4 * groups * piece_rows * LANES,
    )
    landed_pieces = trade(joined)
    by_bucket = run(
        functools.partial(diagonal_body, counts),
        shape((heads, 1, LANES), F32),
        (*diags, *fars),
    )
    mine, other = run(
        functools.partial(qkv_body, groups, heads),
        [shape((experts_all, pieces, 3 * width + BUCKETS))] * 2,
        (place_arg, *normed_all, *joined, by_bucket),
        scratch=[
            pltpu.VMEM((features, 3 * width + BUCKETS), F32),
            pltpu.VMEM((height, 3 * width), BF16),
        ],
        smem=(0,),
    )
    summed = pair_sum(mine, cross(after(other, *landed_pieces), "tensor", 1))
    landed = exchange(summed, ("expert", "context"))
    grad_qkv, grad_gain_attn, grad_rel = run(
        functools.partial(rows_body, groups, heads),
        [
            shape((pieces, 3 * features), F32),
            shape((pieces,), F32),
            shape((heads, BUCKETS), F32),
        ],
        (place_arg, landed, own_w, own_gain),
        smem=(0,),
        moved=2 * landed.size,
    )
    grad_tokens = run(
        functools.partial(finish_body, groups, heads),
        shape((height, features)),
        (place_arg, tokens_in, gain_attn, w_qkv, grad_residual, *landed_pieces),
        scratch=[
            pltpu.VMEM((features, height), F32),
            pltpu.VMEM((groups, height, width), BF16),
            pltpu.VMEM((groups, height, width), BF16),
        ],
        smem=(0,),
        flops=6 * height * square,
        moved=8 * square,
    )
    reduced = jnp.sum(packed_landed.astype(F32), axis=0)
    return (
        mixed_out,
        grad_tokens,
        grad_gain_attn,
        grad_qkv,
        grad_rel,
        reduced[:, :features].T,
        reduced[:, features + experts_all],
        reduced[:, features : features + experts_all],
        grad_up[None],
        grad_down[None],
    )


def solution(mesh):
    rows = ("expert", "context", "tensor")
    in_specs = (
        P(rows, None),
        P(),
        P(),
        P("context", None),
        P(),
        P(),
        P(),
        P(("expert", "context"), None, None),
        P(("expert", "context"), None, None),
        P("expert", None),
        P(rows, None),
        P(rows, None),
    )
    out_specs = (
        P(rows, None),
        P(rows, None),
        P(rows),
        P(rows, None),
        P("context", None),
        P(None, rows),
        P(rows),
        P(rows, None),
        P(("expert", "context"), None, "tensor"),
        P(("expert", "context"), "tensor", None),
    )
    return jax.shard_map(
        per_device, mesh=mesh, in_specs=in_specs, out_specs=out_specs, check_vma=False
    )
```
